32 devices in a mesh: field: 2 (over x), row: 4 (over z), col: 4 (over y, core).
Axes of the slice: x: 2, y: 2, z: 4, core: 2. Of those that a mesh axis runs over, the one named last changes fastest.
Arguments:
- field: float32 [128, 128, 512], P(('field', 'row'), 'col'), parts along dimension 0, may hold values from -6 to 6
- w_expand: bfloat16 [512, 2048], replicated, may hold values from -0.25 to 0.25
- depth_kernel: float32 [3, 3, 2048], replicated, may hold values from -2 to 2
- w_project: bfloat16 [2048, 512], replicated, may hold values from -0.125 to 0.125
- w_qkv: bfloat16 [512, 1536], replicated, may hold values from -8 to 8
- w_out: bfloat16 [512, 512], replicated, may hold values from -0.25 to 0.25
Outputs:
- output: float32 [128, 128, 512], P(('field', 'row'), 'col'), parts along dimension 0
The draws below stay inside these ranges and needn't reach their ends.
There are 2 independent parts, one for each index of `field`. The reference program is written for one: setup_inputs(seed, part) draws one part's arguments, and reference() takes and returns one part's arrays. A program takes and returns all parts, laid end to end along the dimension named above; an argument that names none is the same for every part. Nothing has to cross between parts.
All inputs are finite; a program needn't handle non-finite values.
Results may differ from the reference program's by a relative error of at most 0.006.
Values may be sent and summed in bfloat16 or wider, within the bound.
No kernel may reach another device: no remote copies, remote signals or barrier semaphores. Data moves between devices by JAX's collectives and lax.ppermute only.
A program may use at most 64 MiB of HBM per device.

```python
import math
import jax
import jax.numpy as jnp
from jax import lax

D = 512
EXPAND = 2048
HEADS = 16
GRID = 16
HEIGHT = 64
WIDTH = 128


def draw_w_qkv(key, part):
    first_key = jax.random.fold_in(key, 0)
    drawn = jax.random.truncated_normal(first_key, -5.0, 5.0, (D, 3 * D), jnp.float32) * D ** (-0.5)
    return drawn.astype(jnp.bfloat16)


def steps_of(own_key, shape, cuts, least, top_value):
    loudness, own = 1.0, jax.random.fold_in(own_key, 6)
    for position, shards_of in cuts:
        steps = jnp.exp(jax.random.uniform(jax.random.fold_in(own, position), (shards_of,), jnp.float32, least / len(cuts), top_value / len(cuts)))
        loudness = loudness * jnp.repeat(steps, shape[position] // shards_of).reshape([-1 if axis == position else 1 for axis in range(len(shape))])
    return loudness


def bell_draw(key, shape, spread, bound, cuts=(), kind=jnp.bfloat16):
    loudness = steps_of(key, shape, cuts, -0.22, 0.18) if cuts else 1.0
    result = jax.random.normal(key, shape, jnp.float32) * spread * loudness
    return jnp.minimum(jnp.maximum(result, -bound), bound).astype(kind)


def setup_inputs(seed: int = 0, part: int = 0) -> dict:
    key_list = jax.random.split(jax.random.key(seed), 7)
    own_keys = jax.random.split(jax.random.fold_in(key_list[6], part), 7)
    return {
        "field": bell_draw(own_keys[0], (HEIGHT, WIDTH, D), 1.0, 6.0, ((0, 4), (1, 4)), jnp.float32),
        "w_expand": bell_draw(key_list[1], (D, EXPAND), D ** -0.5, 0.25),
        "depth_kernel": bell_draw(key_list[2], (3, 3, EXPAND), 9 ** -0.5, 2.0, (), jnp.float32),
        "w_project": bell_draw(key_list[3], (EXPAND, D), EXPAND ** -0.5, 0.125),
        "w_qkv": draw_w_qkv(jax.random.fold_in(key_list[6], 71), part),
        "w_out": bell_draw(key_list[5], (D, D), D ** -0.5, 0.25),
    }


def layer_norm(inputs):
    average = lax.optimization_barrier(jnp.mean(inputs, axis=-1, keepdims=True))
    centred = inputs - average
    variance = lax.optimization_barrier(jnp.mean(centred * centred, axis=-1, keepdims=True))
    return centred * lax.rsqrt(variance + 1e-05)

def depthwise(padded, kernel, tile_rows, tile_cols):
    summed = jnp.zeros((tile_rows, tile_cols, padded.shape[2]), jnp.float32)
    for offset_row in range(3):
        for offset_col in range(3):
            window = padded[offset_row:offset_row + tile_rows, offset_col:offset_col + tile_cols].astype(jnp.float32)
            summed = summed + kernel[offset_row, offset_col].astype(jnp.float32) * window
    return summed

def attend(set_block):
    set_count, token_count, triple = set_block.shape
    channels = triple // 3
    head_width = channels // HEADS
    pieces = set_block.astype(jnp.float32).reshape(set_count, token_count, 3, HEADS, head_width)
    queries = pieces[:, :, 0]
    key_rows = pieces[:, :, 1]
    values = pieces[:, :, 2]
    scores = jnp.einsum('snhd,smhd->shnm', queries, key_rows) * (1.0 / math.sqrt(head_width))
    row_max = lax.optimization_barrier(jnp.max(scores, axis=-1, keepdims=True))
    raised = jnp.exp(scores - row_max)
    attn_weights = (raised / lax.optimization_barrier(jnp.sum(raised, axis=-1, keepdims=True))).astype(jnp.bfloat16)
    attended = jnp.einsum('shnm,smhd->snhd', attn_weights.astype(jnp.float32), values)
    return attended.astype(jnp.bfloat16).reshape(set_count, token_count, channels)

def reference(field, w_expand, depth_kernel, w_project, w_qkv, w_out):
    height, width, channels = field.shape
    normed = layer_norm(field).astype(jnp.bfloat16).reshape(height * width, channels)
    expanded = jax.nn.gelu(jnp.dot(normed, w_expand, preferred_element_type=jnp.float32), approximate=True).astype(jnp.bfloat16)
    padded = jnp.pad(expanded.reshape(height, width, -1), ((1, 1), (1, 1), (0, 0)))
    activated = jax.nn.gelu(depthwise(padded, depth_kernel, height, width), approximate=True).astype(jnp.bfloat16)
    branch = jnp.dot(activated.reshape(height * width, -1), w_project, preferred_element_type=jnp.float32)
    mixed = field + branch.reshape(height, width, channels)
    normed_two = layer_norm(mixed).astype(jnp.bfloat16).reshape(height * width, channels)
    qkv = jnp.dot(normed_two, w_qkv, preferred_element_type=jnp.float32).astype(jnp.bfloat16)
    stride_rows = height // GRID
    stride_cols = width // GRID
    grouped = qkv.reshape(GRID, stride_rows, GRID, stride_cols, 3 * channels).transpose(1, 3, 0, 2, 4)
    grouped = grouped.reshape(stride_rows, stride_cols, GRID * GRID, 3 * channels)
    attended = lax.map(attend, grouped)
    restored = attended.reshape(stride_rows, stride_cols, GRID, GRID, channels).transpose(2, 0, 3, 1, 4)
    restored = restored.reshape(height * width, channels)
    final = jnp.dot(restored, w_out, preferred_element_type=jnp.float32)
    return mixed + final.reshape(height, width, channels)
```

```python
import functools
import math

import jax
import jax.numpy as jnp
import numpy as np
from jax import lax
from jax.experimental import pallas as pl
from jax.experimental.pallas import tpu as pltpu
from jax.sharding import PartitionSpec as P

HEADS = 16
GRID = 16
LANES = 128
MIB = 1024 * 1024
NT = (((1,), (1,)), ((), ()))


def layer_norm(inputs):
    average = jnp.mean(inputs, axis=-1, keepdims=True)
    centred = inputs - average
    variance = jnp.mean(centred * centred, axis=-1, keepdims=True)
    return centred * lax.rsqrt(variance + 1e-05)


def gelu(x):
    scale = math.sqrt(2.0 / math.pi)
    half = 0.5 * x
    return half + half * jnp.tanh(x * (scale + (scale * 0.044715) * (x * x)))


def matmul(a, b):
    return jnp.dot(a, b, preferred_element_type=jnp.float32)


def matmul_nt(a, b):
    return lax.dot_general(a, b, NT, preferred_element_type=jnp.float32)


def divisor(size, most, unit):
    best = size
    for piece in range(unit, most + 1, unit):
        if size % piece == 0:
            best = piece
    return best


def expand_kernel(field_ref, weight_ref, out_ref, normed_ref):
    @pl.when(pl.program_id(0) == 0)
    def _():
        normed_ref[...] = layer_norm(field_ref[...]).astype(jnp.bfloat16)

    tokens = out_ref.shape[0]
    step = divisor(tokens, 128, 16)
    for start in range(0, tokens, step):
        rows = slice(start, start + step)
        out_ref[rows, :] = gelu(matmul(normed_ref[rows, :], weight_ref[...])).astype(jnp.bfloat16)


def expand(field, w_expand):
    tokens, channels = field.shape
    width = w_expand.shape[1]
    tile = divisor(width, 512, LANES)
    return pl.pallas_call(
        expand_kernel,
        grid=(width // tile,),
        in_specs=[
            pl.BlockSpec((tokens, channels), lambda j: (0, 0)),
            pl.BlockSpec((channels, tile), lambda j: (0, j)),
        ],
        out_specs=pl.BlockSpec((tokens, tile), lambda j: (0, j)),
        out_shape=jax.ShapeDtypeStruct((tokens, width), jnp.bfloat16),
        scratch_shapes=[pltpu.VMEM((tokens, channels), jnp.bfloat16)],
        compiler_params=pltpu.CompilerParams(vmem_limit_bytes=24 * MIB),
        cost_estimate=pl.CostEstimate(
            flops=2 * tokens * channels * width,
            bytes_accessed=tokens * channels * 4 + channels * width * 2 + tokens * width * 2,
            transcendentals=tokens * width,
        ),
        name="expand",
    )(field, w_expand)


def round_up(size, unit):
    return -(-size // unit) * unit


def mix_kernel(
    expanded_ref, field_ref, up_ref, down_ref, left_ref, right_ref, w_expand_ref, depth_ref,
    w_project_ref, perm_ref, mixed_ref, grouped_ref, halo_ref, total_ref, *, rows, cols,
):
    step = pl.program_id(0)
    tile = expanded_ref.shape[1]
    slot = round_up(rows + 2, 16)

    @pl.when(step == 0)
    def _():
        halo_ref[...] = jnp.zeros_like(halo_ref)
        halo_ref[:cols, :] = layer_norm(up_ref[...]).astype(jnp.bfloat16)
        halo_ref[cols : 2 * cols, :] = layer_norm(down_ref[...]).astype(jnp.bfloat16)
        for index, ref in ((0, left_ref), (1, right_ref)):
            strip = layer_norm(ref[...])
            strip = jnp.concatenate(
                [strip, jnp.zeros((slot - rows - 2, strip.shape[1]), jnp.float32)], axis=0
            )
            start = 2 * cols + index * slot
            halo_ref[start : start + slot, :] = strip.astype(jnp.bfloat16)
        total_ref[...] = jnp.zeros_like(total_ref)

    halo = gelu(matmul(halo_ref[...], w_expand_ref[...])).astype(jnp.bfloat16).astype(jnp.float32)
    position = lax.broadcasted_iota(jnp.int32, (cols, LANES), 0)
    at_first = position == 0
    at_last = position == cols - 1
    half = rows // 2
    parts = [[], []]
    for chunk in range(tile // LANES):
        lanes = slice(chunk * LANES, (chunk + 1) * LANES)
        taps = [[depth_ref[p, q : q + 1, lanes] for q in range(3)] for p in range(3)]
        sides = []
        for q, start in ((0, 2 * cols), (2, 2 * cols + slot)):
            sides.append(
                sum(taps[p][q] * halo[start + p : start + p + rows, lanes] for p in range(3))
            )

        def row_of(y):
            if y < 0:
                return halo[:cols, lanes]
            if y == rows:
                return halo[cols : 2 * cols, lanes]
            return expanded_ref[y * cols : (y + 1) * cols, lanes].astype(jnp.float32)

        window = [row_of(-1), row_of(0), None]
        made = []
        for y in range(rows):
            window[2] = row_of(y + 1)
            summed = [
                taps[0][q] * window[0] + taps[1][q] * window[1] + taps[2][q] * window[2]
                for q in range(3)
            ]
            before = jnp.where(at_first, sides[0][y : y + 1], pltpu.roll(summed[0], 1, 0))
            after = jnp.where(at_last, sides[1][y : y + 1], pltpu.roll(summed[2], cols - 1, 0))
            made.append(gelu(before + summed[1] + after).astype(jnp.bfloat16))
            window = [window[1], window[2], None]
        for index in range(2):
            parts[index].append(jnp.concatenate(made[index * half : (index + 1) * half], axis=0))
    for index in range(2):
        place = slice(index * half * cols, (index + 1) * half * cols)
        total_ref[place, :] += matmul(jnp.concatenate(parts[index], axis=1), w_project_ref[...])

    @pl.when(step == pl.num_programs(0) - 1)
    def _():
        mixed = field_ref[...] + total_ref[...]
        mixed_ref[...] = mixed
        normed = layer_norm(mixed).astype(jnp.bfloat16)
        grouped_ref[...] = matmul(perm_ref[...], normed).astype(jnp.bfloat16)


def mix(expanded, field, up, down, left, right, w_expand, depth_kernel, w_project, perm, rows, cols):
    tokens, channels = field.shape
    width = expanded.shape[1]
    tile = divisor(width, 256, LANES)
    slot = round_up(rows + 2, 16)

    def whole(array):
        return pl.BlockSpec(array.shape, lambda j: (0,) * array.ndim)

    return pl.pallas_call(
        functools.partial(mix_kernel, rows=rows, cols=cols),
        grid=(width // tile,),
        in_specs=[
            pl.BlockSpec((tokens, tile), lambda j: (0, j)),
            whole(field),
            whole(up),
            whole(down),
            whole(left),
            whole(right),
            pl.BlockSpec((channels, tile), lambda j: (0, j)),
            pl.BlockSpec((3, 3, tile), lambda j: (0, 0, j)),
            pl.BlockSpec((tile, channels), lambda j: (j, 0)),
            whole(perm),
        ],
        out_specs=[
            pl.BlockSpec((tokens, channels), lambda j: (0, 0)),
            pl.BlockSpec((tokens, channels), lambda j: (0, 0)),
        ],
        out_shape=[
            jax.ShapeDtypeStruct((tokens, channels), jnp.float32),
            jax.ShapeDtypeStruct((tokens, channels), jnp.bfloat16),
        ],
        scratch_shapes=[
            pltpu.VMEM((2 * cols + 2 * slot, channels), jnp.bfloat16),
            pltpu.VMEM((tokens, channels), jnp.float32),
        ],
        compiler_params=pltpu.CompilerParams(vmem_limit_bytes=32 * MIB),
        cost_estimate=pl.CostEstimate(
            flops=2 * tokens * channels * width,
            bytes_accessed=tokens * channels * 10 + 4 * channels * width + tokens * width * 2,
            transcendentals=tokens * width,
        ),
        name="mix",
    )(expanded, field, up, down, left, right, w_expand, depth_kernel, w_project, perm)


def identity(size):
    row = lax.broadcasted_iota(jnp.int32, (size, size), 0)
    column = lax.broadcasted_iota(jnp.int32, (size, size), 1)
    return jnp.where(row == column, 1.0, 0.0).astype(jnp.bfloat16)


def attend_kernel(tokens_ref, weight_ref, out_ref):
    devices, sets, members, channels = tokens_ref.shape
    count = devices * members
    head_width = channels // HEADS
    group_heads = LANES // head_width
    factor = math.log2(math.e) / math.sqrt(head_width)
    lane = lax.broadcasted_iota(jnp.int32, (1, LANES), 1)
    masks = [
        jnp.where((lane >= j * head_width) & (lane < (j + 1) * head_width), 1.0, 0.0).astype(
            jnp.bfloat16
        )
        for j in range(group_heads)
    ]
    ones = jnp.ones((16, count), jnp.bfloat16)
    turn_values = identity(channels)
    turn_tokens = identity(count)
    for s in range(sets):
        block = tokens_ref[:, s].reshape(count, channels)
        qkv = matmul(block, weight_ref[...]).astype(jnp.bfloat16)
        values = matmul_nt(turn_values, qkv[:, 2 * channels :]).astype(jnp.bfloat16)
        heads = []
        for group in range(channels // LANES):
            lanes = slice(group * LANES, (group + 1) * LANES)
            queries = qkv[:, lanes]
            keys = qkv[:, channels + group * LANES : channels + (group + 1) * LANES]
            for j in range(group_heads):
                scores = matmul_nt(keys * masks[j], queries)
                highest = jnp.max(scores, axis=0, keepdims=True)
                raised = jnp.exp2((scores - highest) * factor).astype(jnp.bfloat16)
                head = (group * group_heads + j) * head_width
                left = jnp.concatenate([values[head : head + head_width], ones], axis=0)
                product = matmul(left, raised)
                scale = 1.0 / product[head_width : head_width + 1]
                heads.append((product[:head_width] * scale).astype(jnp.bfloat16))
        turned = jnp.concatenate(heads, axis=0)
        attended = matmul_nt(turn_tokens, turned).astype(jnp.bfloat16)
        out_ref[:, s] = attended.reshape(devices, members, channels)


def attend(blocks, w_qkv):
    devices, sets, members, channels = blocks.shape
    apart = members % 16 != 0
    if apart:
        count = devices * members
        blocks = blocks.transpose(1, 0, 2, 3).reshape(1, sets, count, channels)
    whole = pl.BlockSpec(blocks.shape, lambda: (0, 0, 0, 0))
    count = devices * members
    result = pl.pallas_call(
        attend_kernel,
        in_specs=[whole, pl.BlockSpec(w_qkv.shape, lambda: (0, 0))],
        out_specs=whole,
        out_shape=jax.ShapeDtypeStruct(blocks.shape, jnp.bfloat16),
        compiler_params=pltpu.CompilerParams(vmem_limit_bytes=32 * MIB),
        cost_estimate=pl.CostEstimate(
            flops=sets * (2 * count * channels * channels * 3 + 4 * count * count * channels),
            bytes_accessed=4 * sets * count * channels + 6 * channels * channels,
            transcendentals=sets * HEADS * count * count,
        ),
        name="attend",
    )(blocks, w_qkv)
    if apart:
        result = result.reshape(sets, devices, members, channels).transpose(1, 0, 2, 3)
    return result


def finish_kernel(attended_ref, back_ref, weight_ref, mixed_ref, out_ref):
    restored = matmul(back_ref[...], attended_ref[...]).astype(jnp.bfloat16)
    out_ref[...] = mixed_ref[...] + matmul(restored, weight_ref[...])


def finish(attended, back, w_out, mixed):
    tokens, channels = mixed.shape
    step = divisor(tokens, 128, 16)
    return pl.pallas_call(
        finish_kernel,
        grid=(tokens // step,),
        in_specs=[
            pl.BlockSpec((tokens, channels), lambda i: (0, 0)),
            pl.BlockSpec((step, tokens), lambda i: (i, 0)),
            pl.BlockSpec(w_out.shape, lambda i: (0, 0)),
            pl.BlockSpec((step, channels), lambda i: (i, 0)),
        ],
        out_specs=pl.BlockSpec((step, channels), lambda i: (i, 0)),
        out_shape=jax.ShapeDtypeStruct((tokens, channels), jnp.float32),
        compiler_params=pltpu.CompilerParams(vmem_limit_bytes=24 * MIB),
        name="finish",
    )(attended, back, w_out, mixed)


def exchange(low_edge, high_edge, axis):
    count = lax.axis_size(axis)
    forward = [(i, i + 1) for i in range(count - 1)]
    backward = [(target, source) for source, target in forward]
    return lax.ppermute(high_edge, axis, forward), lax.ppermute(low_edge, axis, backward)


def grouping(rows, cols, blocks_rows, blocks_cols):
    order = np.arange(rows * cols).reshape(
        blocks_rows, rows // blocks_rows, blocks_cols, cols // blocks_cols
    )
    order = order.transpose(1, 3, 0, 2).reshape(-1)
    matrix = np.zeros((order.size, order.size), np.float32)
    matrix[np.arange(order.size), order] = 1.0
    return matrix


def shards(field, w_expand, depth_kernel, w_project, w_qkv, w_out):
    rows, cols, channels = field.shape
    tokens = rows * cols
    row_devices = lax.axis_size("row")
    col_devices = lax.axis_size("col")
    devices = row_devices * col_devices
    blocks_rows = GRID // row_devices
    blocks_cols = GRID // col_devices
    members = blocks_rows * blocks_cols
    sets_local = tokens // members // devices
    matrix = grouping(rows, cols, blocks_rows, blocks_cols)
    perm = jnp.asarray(matrix, jnp.bfloat16)
    back = jnp.asarray(matrix.T, jnp.bfloat16)

    flat = field.reshape(tokens, channels)
    up, down = exchange(field[0], field[rows - 1], "row")
    expanded = expand(flat, w_expand)
    first = jnp.concatenate([up[:1], field[:, 0], down[:1]], axis=0)
    last = jnp.concatenate([up[cols - 1 :], field[:, cols - 1], down[cols - 1 :]], axis=0)
    left, right = exchange(first, last, "col")
    mixed, grouped = mix(
        expanded, flat, up, down, left, right, w_expand, depth_kernel, w_project, perm, rows, cols
    )
    arrived = lax.all_to_all(
        grouped.reshape(devices, sets_local * members, channels), ("row", "col"), 0, 0, tiled=True
    )
    attended = attend(arrived.reshape(devices, sets_local, members, channels), w_qkv)
    returned = lax.all_to_all(
        attended.reshape(devices, sets_local * members, channels), ("row", "col"), 0, 0, tiled=True
    )
    final = finish(returned.reshape(tokens, channels), back, w_out, mixed)
    return final.reshape(rows, cols, channels)


def solution(mesh):
    return jax.shard_map(
        shards,
        mesh=mesh,
        in_specs=(P(("field", "row"), "col", None), P(), P(), P(), P(), P()),
        out_specs=P(("field", "row"), "col", None),
        check_vma=False,
    )
```

```python
import functools
import math

import jax
import jax.numpy as jnp
import numpy as np
from jax import lax
from jax.experimental import pallas as pl
from jax.experimental.pallas import tpu as pltpu
from jax.sharding import PartitionSpec as P

HEADS = 16
GRID = 16
LANES = 128
MIB = 1024 * 1024
NT = (((1,), (1,)), ((), ()))


def layer_norm(inputs):
    average = jnp.mean(inputs, axis=-1, keepdims=True)
    centred = inputs - average
    variance = jnp.mean(centred * centred, axis=-1, keepdims=True)
    return centred * lax.rsqrt(variance + 1e-05)


def gelu(x):
    scale = math.sqrt(2.0 / math.pi)
    half = 0.5 * x
    return half + half * jnp.tanh(x * (scale + (scale * 0.044715) * (x * x)))


def matmul(a, b):
    return jnp.dot(a, b, preferred_element_type=jnp.float32)


def matmul_nt(a, b):
    return lax.dot_general(a, b, NT, preferred_element_type=jnp.float32)


def divisor(size, most, unit):
    best = size
    for piece in range(unit, most + 1, unit):
        if size % piece == 0:
            best = piece
    return best


def expand_kernel(field_ref, weight_ref, out_ref, normed_ref):
    @pl.when(pl.program_id(0) == 0)
    def _():
        normed_ref[...] = layer_norm(field_ref[...]).astype(jnp.bfloat16)

    tokens = out_ref.shape[0]
    step = divisor(tokens, 128, 16)
    for start in range(0, tokens, step):
        rows = slice(start, start + step)
        out_ref[rows, :] = gelu(matmul(normed_ref[rows, :], weight_ref[...])).astype(jnp.bfloat16)


def expand(field, w_expand):
    tokens, channels = field.shape
    width = w_expand.shape[1]
    tile = divisor(width, 512, LANES)
    return pl.pallas_call(
        expand_kernel,
        grid=(width // tile,),
        in_specs=[
            pl.BlockSpec((tokens, channels), lambda j: (0, 0)),
            pl.BlockSpec((channels, tile), lambda j: (0, j)),
        ],
        out_specs=pl.BlockSpec((tokens, tile), lambda j: (0, j)),
        out_shape=jax.ShapeDtypeStruct((tokens, width), jnp.bfloat16),
        scratch_shapes=[pltpu.VMEM((tokens, channels), jnp.bfloat16)],
        compiler_params=pltpu.CompilerParams(vmem_limit_bytes=24 * MIB),
        cost_estimate=pl.CostEstimate(
            flops=2 * tokens * channels * width,
            bytes_accessed=tokens * channels * 4 + channels * width * 2 + tokens * width * 2,
            transcendentals=tokens * width,
        ),
        name="expand",
    )(field, w_expand)


def round_up(size, unit):
    return -(-size // unit) * unit


def mix_kernel(
    expanded_ref, field_ref, up_ref, down_ref, left_ref, right_ref, w_expand_ref, depth_ref,
    w_project_ref, perm_ref, mixed_ref, grouped_ref, halo_ref, total_ref, *, rows, cols,
):
    step = pl.program_id(0)
    tile = expanded_ref.shape[1]
    slot = round_up(rows + 2, 16)

    @pl.when(step == 0)
    def _():
        halo_ref[...] = jnp.zeros_like(halo_ref)
        halo_ref[:cols, :] = layer_norm(up_ref[...]).astype(jnp.bfloat16)
        halo_ref[cols : 2 * cols, :] = layer_norm(down_ref[...]).astype(jnp.bfloat16)
        for index, ref in ((0, left_ref), (1, right_ref)):
            strip = layer_norm(ref[...])
            strip = jnp.concatenate(
                [strip, jnp.zeros((slot - rows - 2, strip.shape[1]), jnp.float32)], axis=0
            )
            start = 2 * cols + index * slot
            halo_ref[start : start + slot, :] = strip.astype(jnp.bfloat16)
        total_ref[...] = jnp.zeros_like(total_ref)

    halo = gelu(matmul(halo_ref[...], w_expand_ref[...])).astype(jnp.bfloat16).astype(jnp.float32)
    position = lax.broadcasted_iota(jnp.int32, (cols, LANES), 0)
    at_first = position == 0
    at_last = position == cols - 1
    half = rows // 2
    parts = [[], []]
    for chunk in range(tile // LANES):
        lanes = slice(chunk * LANES, (chunk + 1) * LANES)
        taps = [[depth_ref[p, q : q + 1, lanes] for q in range(3)] for p in range(3)]
        sides = []
        for q, start in ((0, 2 * cols), (2, 2 * cols + slot)):
            sides.append(
                sum(taps[p][q] * halo[start + p : start + p + rows, lanes] for p in range(3))
            )

        def row_of(y):
            if y < 0:
                return halo[:cols, lanes]
            if y == rows:
                return halo[cols : 2 * cols, lanes]
            return expanded_ref[y * cols : (y + 1) * cols, lanes].astype(jnp.float32)

        window = [row_of(-1), row_of(0), None]
        made = []
        for y in range(rows):
            window[2] = row_of(y + 1)
            summed = [
                taps[0][q] * window[0] + taps[1][q] * window[1] + taps[2][q] * window[2]
                for q in range(3)
            ]
            before = jnp.where(at_first, sides[0][y : y + 1], pltpu.roll(summed[0], 1, 0))
            after = jnp.where(at_last, sides[1][y : y + 1], pltpu.roll(summed[2], cols - 1, 0))
            made.append(gelu(before + summed[1] + after).astype(jnp.bfloat16))
            window = [window[1], window[2], None]
        for index in range(2):
            parts[index].append(jnp.concatenate(made[index * half : (index + 1) * half], axis=0))
    for index in range(2):
        place = slice(index * half * cols, (index + 1) * half * cols)
        total_ref[place, :] += matmul(jnp.concatenate(parts[index], axis=1), w_project_ref[...])

    @pl.when(step == pl.num_programs(0) - 1)
    def _():
        mixed = field_ref[...] + total_ref[...]
        mixed_ref[...] = mixed
        normed = layer_norm(mixed).astype(jnp.bfloat16)
        grouped_ref[...] = matmul(perm_ref[...], normed).astype(jnp.bfloat16)


def mix(expanded, field, up, down, left, right, w_expand, depth_kernel, w_project, perm, rows, cols):
    tokens, channels = field.shape
    width = expanded.shape[1]
    tile = divisor(width, 256, LANES)
    slot = round_up(rows + 2, 16)

    def whole(array):
        return pl.BlockSpec(array.shape, lambda j: (0,) * array.ndim)

    return pl.pallas_call(
        functools.partial(mix_kernel, rows=rows, cols=cols),
        grid=(width // tile,),
        in_specs=[
            pl.BlockSpec((tokens, tile), lambda j: (0, j)),
            whole(field),
            whole(up),
            whole(down),
            whole(left),
            whole(right),
            pl.BlockSpec((channels, tile), lambda j: (0, j)),
            pl.BlockSpec((3, 3, tile), lambda j: (0, 0, j)),
            pl.BlockSpec((tile, channels), lambda j: (j, 0)),
            whole(perm),
        ],
        out_specs=[
            pl.BlockSpec((tokens, channels), lambda j: (0, 0)),
            pl.BlockSpec((tokens, channels), lambda j: (0, 0)),
        ],
        out_shape=[
            jax.ShapeDtypeStruct((tokens, channels), jnp.float32),
            jax.ShapeDtypeStruct((tokens, channels), jnp.bfloat16),
        ],
        scratch_shapes=[
            pltpu.VMEM((2 * cols + 2 * slot, channels), jnp.bfloat16),
            pltpu.VMEM((tokens, channels), jnp.float32),
        ],
        compiler_params=pltpu.CompilerParams(vmem_limit_bytes=32 * MIB),
        cost_estimate=pl.CostEstimate(
            flops=2 * tokens * channels * width,
            bytes_accessed=tokens * channels * 10 + 4 * channels * width + tokens * width * 2,
            transcendentals=tokens * width,
        ),
        name="mix",
    )(expanded, field, up, down, left, right, w_expand, depth_kernel, w_project, perm)


def identity(size):
    row = lax.broadcasted_iota(jnp.int32, (size, size), 0)
    column = lax.broadcasted_iota(jnp.int32, (size, size), 1)
    return jnp.where(row == column, 1.0, 0.0).astype(jnp.bfloat16)


def attend_kernel(tokens_ref, weight_ref, out_ref):
    count, channels = tokens_ref.shape
    head_width = channels // HEADS
    group_heads = LANES // head_width
    factor = math.log2(math.e) / math.sqrt(head_width)
    lane = lax.broadcasted_iota(jnp.int32, (1, LANES), 1)
    masks = [
        jnp.where((lane >= j * head_width) & (lane < (j + 1) * head_width), 1.0, 0.0).astype(
            jnp.bfloat16
        )
        for j in range(group_heads)
    ]
    ones = jnp.ones((16, count), jnp.bfloat16)
    qkv = matmul(tokens_ref[...], weight_ref[...]).astype(jnp.bfloat16)
    values = matmul_nt(identity(channels), qkv[:, 2 * channels :]).astype(jnp.bfloat16)
    heads = []
    for group in range(channels // LANES):
        lanes = slice(group * LANES, (group + 1) * LANES)
        queries = qkv[:, lanes]
        keys = qkv[:, channels + group * LANES : channels + (group + 1) * LANES]
        for j in range(group_heads):
            scores = matmul_nt(keys * masks[j], queries)
            highest = jnp.max(scores, axis=0, keepdims=True)
            raised = jnp.exp2((scores - highest) * factor).astype(jnp.bfloat16)
            head = (group * group_heads + j) * head_width
            left = jnp.concatenate([values[head : head + head_width], ones], axis=0)
            product = matmul(left, raised)
            scale = 1.0 / product[head_width : head_width + 1]
            heads.append((product[:head_width] * scale).astype(jnp.bfloat16))
    turned = jnp.concatenate(heads, axis=0)
    out_ref[...] = matmul_nt(identity(count), turned).astype(jnp.bfloat16)


def attend(tokens, w_qkv):
    count, channels = tokens.shape
    return pl.pallas_call(
        attend_kernel,
        in_specs=[
            pl.BlockSpec(tokens.shape, lambda: (0, 0)),
            pl.BlockSpec(w_qkv.shape, lambda: (0, 0)),
        ],
        out_specs=pl.BlockSpec(tokens.shape, lambda: (0, 0)),
        out_shape=jax.ShapeDtypeStruct(tokens.shape, jnp.bfloat16),
        compiler_params=pltpu.CompilerParams(vmem_limit_bytes=32 * MIB),
        cost_estimate=pl.CostEstimate(
            flops=2 * count * channels * channels * 3 + 4 * count * count * channels,
            bytes_accessed=4 * count * channels + 6 * channels * channels,
            transcendentals=HEADS * count * count,
        ),
        name="attend",
    )(tokens, w_qkv)


def finish_kernel(*refs, sets):
    parts, (back_ref, weight_ref, mixed_ref, out_ref) = refs[:sets], refs[sets:]
    attended = jnp.concatenate([ref[...] for ref in parts], axis=0)
    restored = matmul(back_ref[...], attended).astype(jnp.bfloat16)
    out_ref[...] = mixed_ref[...] + matmul(restored, weight_ref[...])


def finish(attended, back, w_out, mixed):
    tokens, channels = mixed.shape
    step = divisor(tokens, 128, 16)
    return pl.pallas_call(
        functools.partial(finish_kernel, sets=len(attended)),
        grid=(tokens // step,),
        in_specs=[pl.BlockSpec(part.shape, lambda i: (0, 0)) for part in attended]
        + [
            pl.BlockSpec((step, tokens), lambda i: (i, 0)),
            pl.BlockSpec(w_out.shape, lambda i: (0, 0)),
            pl.BlockSpec((step, channels), lambda i: (i, 0)),
        ],
        out_specs=pl.BlockSpec((step, channels), lambda i: (i, 0)),
        out_shape=jax.ShapeDtypeStruct((tokens, channels), jnp.float32),
        compiler_params=pltpu.CompilerParams(vmem_limit_bytes=24 * MIB),
        name="finish",
    )(*attended, back, w_out, mixed)


def exchange(low_edge, high_edge, axis):
    count = lax.axis_size(axis)
    forward = [(i, i + 1) for i in range(count - 1)]
    backward = [(target, source) for source, target in forward]
    return lax.ppermute(high_edge, axis, forward), lax.ppermute(low_edge, axis, backward)


def grouping(rows, cols, blocks_rows, blocks_cols, devices):
    order = np.arange(rows * cols).reshape(
        blocks_rows, rows // blocks_rows, blocks_cols, cols // blocks_cols
    )
    order = order.transpose(1, 3, 0, 2).reshape(devices, -1, blocks_rows * blocks_cols)
    order = order.transpose(1, 0, 2).reshape(-1)
    matrix = np.zeros((order.size, order.size), np.float32)
    matrix[np.arange(order.size), order] = 1.0
    return matrix


def shards(field, w_expand, depth_kernel, w_project, w_qkv, w_out):
    rows, cols, channels = field.shape
    tokens = rows * cols
    row_devices = lax.axis_size("row")
    col_devices = lax.axis_size("col")
    devices = row_devices * col_devices
    blocks_rows = GRID // row_devices
    blocks_cols = GRID // col_devices
    members = blocks_rows * blocks_cols
    sets_local = tokens // members // devices
    matrix = grouping(rows, cols, blocks_rows, blocks_cols, devices)
    perm = jnp.asarray(matrix, jnp.bfloat16)
    back = jnp.asarray(matrix.T, jnp.bfloat16)

    flat = field.reshape(tokens, channels)
    up, down = exchange(field[0], field[rows - 1], "row")
    expanded = expand(flat, w_expand)
    first = jnp.concatenate([up[:1], field[:, 0], down[:1]], axis=0)
    last = jnp.concatenate([up[cols - 1 :], field[:, cols - 1], down[cols - 1 :]], axis=0)
    left, right = exchange(first, last, "col")
    mixed, grouped = mix(
        expanded, flat, up, down, left, right, w_expand, depth_kernel, w_project, perm, rows, cols
    )
    def swap(block):
        pieces = block.reshape(devices, members, channels)
        return lax.all_to_all(pieces, ("row", "col"), 0, 0, tiled=True).reshape(-1, channels)

    count = devices * members
    arrived = [swap(grouped[s * count : (s + 1) * count]) for s in range(sets_local)]
    returned = [swap(attend(block, w_qkv)) for block in arrived]
    final = finish(returned, back, w_out, mixed)
    return final.reshape(rows, cols, channels)


def solution(mesh):
    return jax.shard_map(
        shards,
        mesh=mesh,
        in_specs=(P(("field", "row"), "col", None), P(), P(), P(), P(), P()),
        out_specs=P(("field", "row"), "col", None),
        check_vma=False,
    )
```

```python
import functools
import math

import jax
import jax.numpy as jnp
import numpy as np
from jax import lax
from jax.experimental import pallas as pl
from jax.experimental.pallas import tpu as pltpu
from jax.sharding import PartitionSpec as P

HEADS = 16
GRID = 16
LANES = 128
MIB = 1024 * 1024
NT = (((1,), (1,)), ((), ()))


def layer_norm(inputs):
    average = jnp.mean(inputs, axis=-1, keepdims=True)
    centred = inputs - average
    variance = jnp.mean(centred * centred, axis=-1, keepdims=True)
    return centred * lax.rsqrt(variance + 1e-05)


def gelu(x):
    scale = math.sqrt(2.0 / math.pi)
    half = 0.5 * x
    return half + half * jnp.tanh(x * (scale + (scale * 0.044715) * (x * x)))


def matmul(a, b):
    return jnp.dot(a, b, preferred_element_type=jnp.float32)


def matmul_nt(a, b):
    return lax.dot_general(a, b, NT, preferred_element_type=jnp.float32)


def divisor(size, most, unit):
    best = size
    for piece in range(unit, most + 1, unit):
        if size % piece == 0:
            best = piece
    return best


def expand_kernel(field_ref, weight_ref, out_ref, normed_ref):
    @pl.when(pl.program_id(0) == 0)
    def _():
        normed_ref[...] = layer_norm(field_ref[...]).astype(jnp.bfloat16)

    tokens = out_ref.shape[0]
    step = divisor(tokens, 128, 16)
    for start in range(0, tokens, step):
        rows = slice(start, start + step)
        out_ref[rows, :] = gelu(matmul(normed_ref[rows, :], weight_ref[...])).astype(jnp.bfloat16)


def expand(field, w_expand):
    tokens, channels = field.shape
    width = w_expand.shape[1]
    tile = divisor(width, 512, LANES)
    return pl.pallas_call(
        expand_kernel,
        grid=(width // tile,),
        in_specs=[
            pl.BlockSpec((tokens, channels), lambda j: (0, 0)),
            pl.BlockSpec((channels, tile), lambda j: (0, j)),
        ],
        out_specs=pl.BlockSpec((tokens, tile), lambda j: (0, j)),
        out_shape=jax.ShapeDtypeStruct((tokens, width), jnp.bfloat16),
        scratch_shapes=[pltpu.VMEM((tokens, channels), jnp.bfloat16)],
        compiler_params=pltpu.CompilerParams(vmem_limit_bytes=24 * MIB),
        cost_estimate=pl.CostEstimate(
            flops=2 * tokens * channels * width,
            bytes_accessed=tokens * channels * 4 + channels * width * 2 + tokens * width * 2,
            transcendentals=tokens * width,
        ),
        name="expand",
    )(field, w_expand)


def round_up(size, unit):
    return -(-size // unit) * unit


def mix_kernel(
    expanded_ref, field_ref, up_ref, down_ref, left_ref, right_ref, w_expand_ref, depth_ref,
    w_project_ref, perm_ref, mixed_ref, grouped_ref, halo_ref, total_ref, *, rows, cols,
):
    step = pl.program_id(0)
    tile = expanded_ref.shape[1]
    slot = round_up(rows + 2, 16)

    @pl.when(step == 0)
    def _():
        halo_ref[...] = jnp.zeros_like(halo_ref)
        halo_ref[:cols, :] = layer_norm(up_ref[...]).astype(jnp.bfloat16)
        halo_ref[cols : 2 * cols, :] = layer_norm(down_ref[...]).astype(jnp.bfloat16)
        for index, ref in ((0, left_ref), (1, right_ref)):
            strip = layer_norm(ref[...])
            strip = jnp.concatenate(
                [strip, jnp.zeros((slot - rows - 2, strip.shape[1]), jnp.float32)], axis=0
            )
            start = 2 * cols + index * slot
            halo_ref[start : start + slot, :] = strip.astype(jnp.bfloat16)
        total_ref[...] = jnp.zeros_like(total_ref)

    halo = gelu(matmul(halo_ref[...], w_expand_ref[...])).astype(jnp.bfloat16).astype(jnp.float32)
    position = lax.broadcasted_iota(jnp.int32, (cols, LANES), 0)
    at_first = position == 0
    at_last = position == cols - 1
    half = rows // 2
    parts = [[], []]
    for chunk in range(tile // LANES):
        lanes = slice(chunk * LANES, (chunk + 1) * LANES)
        taps = [[depth_ref[p, q : q + 1, lanes] for q in range(3)] for p in range(3)]
        sides = []
        for q, start in ((0, 2 * cols), (2, 2 * cols + slot)):
            sides.append(
                sum(taps[p][q] * halo[start + p : start + p + rows, lanes] for p in range(3))
            )

        def row_of(y):
            if y < 0:
                return halo[:cols, lanes]
            if y == rows:
                return halo[cols : 2 * cols, lanes]
            return expanded_ref[y * cols : (y + 1) * cols, lanes].astype(jnp.float32)

        window = [row_of(-1), row_of(0), None]
        made = []
        for y in range(rows):
            window[2] = row_of(y + 1)
            summed = [
                taps[0][q] * window[0] + taps[1][q] * window[1] + taps[2][q] * window[2]
                for q in range(3)
            ]
            before = jnp.where(at_first, sides[0][y : y + 1], pltpu.roll(summed[0], 1, 0))
            after = jnp.where(at_last, sides[1][y : y + 1], pltpu.roll(summed[2], cols - 1, 0))
            made.append(gelu(before + summed[1] + after).astype(jnp.bfloat16))
            window = [window[1], window[2], None]
        for index in range(2):
            parts[index].append(jnp.concatenate(made[index * half : (index + 1) * half], axis=0))
    for index in range(2):
        place = slice(index * half * cols, (index + 1) * half * cols)
        total_ref[place, :] += matmul(jnp.concatenate(parts[index], axis=1), w_project_ref[...])

    @pl.when(step == pl.num_programs(0) - 1)
    def _():
        mixed = field_ref[...] + total_ref[...]
        mixed_ref[...] = mixed
        normed = layer_norm(mixed).astype(jnp.bfloat16)
        grouped_ref[...] = matmul(perm_ref[...], normed).astype(jnp.bfloat16)


def mix(expanded, field, up, down, left, right, w_expand, depth_kernel, w_project, perm, rows, cols):
    tokens, channels = field.shape
    width = expanded.shape[1]
    tile = divisor(width, 256, LANES)
    slot = round_up(rows + 2, 16)

    def whole(array):
        return pl.BlockSpec(array.shape, lambda j: (0,) * array.ndim)

    return pl.pallas_call(
        functools.partial(mix_kernel, rows=rows, cols=cols),
        grid=(width // tile,),
        in_specs=[
            pl.BlockSpec((tokens, tile), lambda j: (0, j)),
            whole(field),
            whole(up),
            whole(down),
            whole(left),
            whole(right),
            pl.BlockSpec((channels, tile), lambda j: (0, j)),
            pl.BlockSpec((3, 3, tile), lambda j: (0, 0, j)),
            pl.BlockSpec((tile, channels), lambda j: (j, 0)),
            whole(perm),
        ],
        out_specs=[
            pl.BlockSpec((tokens, channels), lambda j: (0, 0)),
            pl.BlockSpec((tokens, channels), lambda j: (0, 0)),
        ],
        out_shape=[
            jax.ShapeDtypeStruct((tokens, channels), jnp.float32),
            jax.ShapeDtypeStruct((tokens, channels), jnp.bfloat16),
        ],
        scratch_shapes=[
            pltpu.VMEM((2 * cols + 2 * slot, channels), jnp.bfloat16),
            pltpu.VMEM((tokens, channels), jnp.float32),
        ],
        compiler_params=pltpu.CompilerParams(vmem_limit_bytes=32 * MIB),
        cost_estimate=pl.CostEstimate(
            flops=2 * tokens * channels * width,
            bytes_accessed=tokens * channels * 10 + 4 * channels * width + tokens * width * 2,
            transcendentals=tokens * width,
        ),
        name="mix",
    )(expanded, field, up, down, left, right, w_expand, depth_kernel, w_project, perm)


def identity(size):
    row = lax.broadcasted_iota(jnp.int32, (size, size), 0)
    column = lax.broadcasted_iota(jnp.int32, (size, size), 1)
    return jnp.where(row == column, 1.0, 0.0).astype(jnp.bfloat16)


def attend_kernel(tokens_ref, weight_ref, out_ref):
    count, channels = tokens_ref.shape
    head_width = channels // HEADS
    group_heads = LANES // head_width
    factor = math.log2(math.e) / math.sqrt(head_width)
    lane = lax.broadcasted_iota(jnp.int32, (1, LANES), 1)
    masks = [
        jnp.where((lane >= j * head_width) & (lane < (j + 1) * head_width), 1.0, 0.0).astype(
            jnp.bfloat16
        )
        for j in range(group_heads)
    ]
    ones = jnp.ones((16, count), jnp.bfloat16)
    qkv = matmul(tokens_ref[...], weight_ref[...]).astype(jnp.bfloat16)
    values = matmul_nt(identity(channels), qkv[:, 2 * channels :]).astype(jnp.bfloat16)
    heads = []
    for group in range(channels // LANES):
        lanes = slice(group * LANES, (group + 1) * LANES)
        queries = qkv[:, lanes]
        keys = qkv[:, channels + group * LANES : channels + (group + 1) * LANES]
        for j in range(group_heads):
            scores = matmul_nt(keys * masks[j], queries)
            highest = jnp.max(scores, axis=0, keepdims=True)
            raised = jnp.exp2((scores - highest) * factor).astype(jnp.bfloat16)
            head = (group * group_heads + j) * head_width
            left = jnp.concatenate([values[head : head + head_width], ones], axis=0)
            product = matmul(left, raised)
            scale = 1.0 / product[head_width : head_width + 1]
            heads.append((product[:head_width] * scale).astype(jnp.bfloat16))
    turned = jnp.concatenate(heads, axis=0)
    out_ref[...] = matmul_nt(identity(count), turned).astype(jnp.bfloat16)


def attend(tokens, w_qkv):
    count, channels = tokens.shape
    return pl.pallas_call(
        attend_kernel,
        in_specs=[
            pl.BlockSpec(tokens.shape, lambda: (0, 0)),
            pl.BlockSpec(w_qkv.shape, lambda: (0, 0)),
        ],
        out_specs=pl.BlockSpec(tokens.shape, lambda: (0, 0)),
        out_shape=jax.ShapeDtypeStruct(tokens.shape, jnp.bfloat16),
        compiler_params=pltpu.CompilerParams(vmem_limit_bytes=32 * MIB),
        cost_estimate=pl.CostEstimate(
            flops=2 * count * channels * channels * 3 + 4 * count * count * channels,
            bytes_accessed=4 * count * channels + 6 * channels * channels,
            transcendentals=HEADS * count * count,
        ),
        name="attend",
    )(tokens, w_qkv)


def finish_kernel(*refs, sets):
    parts, (back_ref, weight_ref, mixed_ref, out_ref) = refs[:sets], refs[sets:]
    attended = jnp.concatenate([ref[...] for ref in parts], axis=0)
    restored = matmul(back_ref[...], attended).astype(jnp.bfloat16)
    out_ref[...] = mixed_ref[...] + matmul(restored, weight_ref[...])


def finish(attended, back, w_out, mixed):
    tokens, channels = mixed.shape
    step = divisor(tokens, 128, 16)
    return pl.pallas_call(
        functools.partial(finish_kernel, sets=len(attended)),
        grid=(tokens // step,),
        in_specs=[pl.BlockSpec(part.shape, lambda i: (0, 0)) for part in attended]
        + [
            pl.BlockSpec((step, tokens), lambda i: (i, 0)),
            pl.BlockSpec(w_out.shape, lambda i: (0, 0)),
            pl.BlockSpec((step, channels), lambda i: (i, 0)),
        ],
        out_specs=pl.BlockSpec((step, channels), lambda i: (i, 0)),
        out_shape=jax.ShapeDtypeStruct((tokens, channels), jnp.float32),
        compiler_params=pltpu.CompilerParams(vmem_limit_bytes=24 * MIB),
        name="finish",
    )(*attended, back, w_out, mixed)


def exchange(low_edge, high_edge, axis):
    count = lax.axis_size(axis)
    forward = [(i, i + 1) for i in range(count - 1)]
    backward = [(target, source) for source, target in forward]
    return lax.ppermute(high_edge, axis, forward), lax.ppermute(low_edge, axis, backward)


def grouping(rows, cols, blocks_rows, blocks_cols, devices):
    order = np.arange(rows * cols).reshape(
        blocks_rows, rows // blocks_rows, blocks_cols, cols // blocks_cols
    )
    order = order.transpose(1, 3, 0, 2).reshape(devices, -1, blocks_rows * blocks_cols)
    order = order.transpose(1, 0, 2).reshape(-1)
    matrix = np.zeros((order.size, order.size), np.float32)
    matrix[np.arange(order.size), order] = 1.0
    return matrix


def shards(field, w_expand, depth_kernel, w_project, w_qkv, w_out):
    rows, cols, channels = field.shape
    tokens = rows * cols
    row_devices = lax.axis_size("row")
    col_devices = lax.axis_size("col")
    devices = row_devices * col_devices
    blocks_rows = GRID // row_devices
    blocks_cols = GRID // col_devices
    members = blocks_rows * blocks_cols
    sets_local = tokens // members // devices
    matrix = grouping(rows, cols, blocks_rows, blocks_cols, devices)
    perm = jnp.asarray(matrix, jnp.bfloat16)
    back = jnp.asarray(matrix.T, jnp.bfloat16)

    flat = field.reshape(tokens, channels)
    up, down = exchange(field[0], field[rows - 1], "row")
    expanded = expand(flat, w_expand)
    first = jnp.concatenate([up[:1], field[:, 0], down[:1]], axis=0)
    last = jnp.concatenate([up[cols - 1 :], field[:, cols - 1], down[cols - 1 :]], axis=0)
    left, right = exchange(first, last, "col")
    mixed, grouped = mix(
        expanded, flat, up, down, left, right, w_expand, depth_kernel, w_project, perm, rows, cols
    )
    def swap(block, axes):
        pieces = block.reshape(row_devices, col_devices, members, channels)
        for axis in axes:
            dim = ("row", "col").index(axis)
            pieces = lax.all_to_all(pieces, axis, dim, dim, tiled=True)
        return pieces.reshape(-1, channels)

    count = devices * members
    orders = [("row", "col") if s % 2 == 0 else ("col", "row") for s in range(sets_local)]
    arrived = [
        swap(grouped[s * count : (s + 1) * count], orders[s]) for s in range(sets_local)
    ]
    returned = [swap(attend(block, w_qkv), order) for block, order in zip(arrived, orders)]
    final = finish(returned, back, w_out, mixed)
    return final.reshape(rows, cols, channels)


def solution(mesh):
    return jax.shard_map(
        shards,
        mesh=mesh,
        in_specs=(P(("field", "row"), "col", None), P(), P(), P(), P(), P()),
        out_specs=P(("field", "row"), "col", None),
        check_vma=False,
    )
```

```python
import functools
import math

import jax
import jax.numpy as jnp
import numpy as np
from jax import lax
from jax.experimental import pallas as pl
from jax.experimental.pallas import tpu as pltpu
from jax.sharding import PartitionSpec as P

HEADS = 16
GRID = 16
LANES = 128
MIB = 1024 * 1024
NT = (((1,), (1,)), ((), ()))


def layer_norm(inputs):
    average = jnp.mean(inputs, axis=-1, keepdims=True)
    centred = inputs - average
    variance = jnp.mean(centred * centred, axis=-1, keepdims=True)
    return centred * lax.rsqrt(variance + 1e-05)


def gelu(x):
    scale = math.sqrt(2.0 / math.pi)
    half = 0.5 * x
    return half + half * jnp.tanh(x * (scale + (scale * 0.044715) * (x * x)))


def matmul(a, b):
    return jnp.dot(a, b, preferred_element_type=jnp.float32)


def matmul_nt(a, b):
    return lax.dot_general(a, b, NT, preferred_element_type=jnp.float32)


def divisor(size, most, unit):
    best = size
    for piece in range(unit, most + 1, unit):
        if size % piece == 0:
            best = piece
    return best


def round_up(size, unit):
    return -(-size // unit) * unit


def vmem():
    return pl.BlockSpec(memory_space=pltpu.VMEM)


def norm_kernel(field_ref, normed_ref):
    normed_ref[...] = layer_norm(field_ref[...]).astype(jnp.bfloat16)


def norm(field):
    tokens, channels = field.shape
    step = divisor(tokens, 128, 16)
    return pl.pallas_call(
        norm_kernel,
        grid=(tokens // step,),
        in_specs=[pl.BlockSpec((step, channels), lambda i: (i, 0))],
        out_specs=pl.BlockSpec((step, channels), lambda i: (i, 0)),
        out_shape=jax.ShapeDtypeStruct((tokens, channels), jnp.bfloat16),
        compiler_params=pltpu.CompilerParams(vmem_limit_bytes=16 * MIB),
        cost_estimate=pl.CostEstimate(
            flops=8 * tokens * channels, bytes_accessed=6 * tokens * channels, transcendentals=tokens
        ),
        name="norm",
    )(field)


def expand_kernel(normed_ref, weight_ref, out_ref):
    tokens = out_ref.shape[0]
    step = divisor(tokens, 128, 16)
    for start in range(0, tokens, step):
        rows = slice(start, start + step)
        out_ref[rows, :] = gelu(matmul(normed_ref[rows, :], weight_ref[...])).astype(jnp.bfloat16)


def expand(normed, w_expand):
    tokens, channels = normed.shape
    width = w_expand.shape[1]
    tile = divisor(width, 512, LANES)
    return pl.pallas_call(
        expand_kernel,
        grid=(width // tile,),
        in_specs=[vmem(), pl.BlockSpec((channels, tile), lambda j: (0, j))],
        out_specs=pl.BlockSpec((tokens, tile), lambda j: (0, j)),
        out_shape=jax.ShapeDtypeStruct((tokens, width), jnp.bfloat16),
        compiler_params=pltpu.CompilerParams(vmem_limit_bytes=16 * MIB),
        cost_estimate=pl.CostEstimate(
            flops=2 * tokens * channels * width,
            bytes_accessed=tokens * channels * 2 + channels * width * 2 + tokens * width * 2,
            transcendentals=tokens * width,
        ),
        name="expand",
    )(normed, w_expand)


def mix_kernel(
    expanded_ref, field_ref, up_ref, down_ref, left_ref, right_ref, w_expand_ref, depth_ref,
    w_project_ref, perm_ref, mixed_ref, grouped_ref, halo_ref, total_ref, even_ref, odd_ref,
    *, rows, cols,
):
    width = expanded_ref.shape[1]
    tile = even_ref.shape[1]
    slot = left_ref.shape[0]
    left_start, right_start = 2 * cols, 2 * cols + slot

    edges = jnp.concatenate(
        [up_ref[...], down_ref[...], left_ref[...], right_ref[...]], axis=0
    )

    def halo_body(index, carry):
        lanes = pl.ds(pl.multiple_of(index * tile, tile), tile)
        made = gelu(matmul(edges, w_expand_ref[:, lanes]))
        halo_ref[:, lanes] = made.astype(jnp.bfloat16).astype(jnp.float32)
        return carry

    lax.fori_loop(0, width // tile, halo_body, 0)

    position = lax.broadcasted_iota(jnp.int32, (8, LANES), 0)
    at_first = position == 0
    at_last = position == 7

    def convolve(index, out_ref):
        for sub in range(tile // LANES):
            lanes = pl.ds(pl.multiple_of(index * tile + sub * LANES, LANES), LANES)
            taps = [[depth_ref[p, q : q + 1, lanes] for q in range(3)] for p in range(3)]
            sides = []
            for q, start in ((0, left_start), (2, right_start)):
                sides.append(
                    sum(taps[p][q] * halo_ref[start + p : start + p + rows, lanes] for p in range(3))
                )

            def row_of(y):
                if y < 0:
                    return halo_ref[:cols, lanes]
                if y == rows:
                    return halo_ref[cols : 2 * cols, lanes]
                return expanded_ref[y * cols : (y + 1) * cols, lanes].astype(jnp.float32)

            window = [row_of(-1), row_of(0), None]
            for y in range(rows):
                window[2] = row_of(y + 1)
                summed = [
                    taps[0][q] * window[0] + taps[1][q] * window[1] + taps[2][q] * window[2]
                    for q in range(3)
                ]
                before = pltpu.roll(summed[0], 1, 0)
                before = jnp.concatenate(
                    [jnp.where(at_first, sides[0][y : y + 1], before[:8]), before[8:]], axis=0
                )
                after = pltpu.roll(summed[2], cols - 1, 0)
                after = jnp.concatenate(
                    [after[:-8], jnp.where(at_last, sides[1][y : y + 1], after[-8:])], axis=0
                )
                made = gelu(before + summed[1] + after).astype(jnp.bfloat16)
                out_ref[y * cols : (y + 1) * cols, sub * LANES : (sub + 1) * LANES] = made
                window = [window[1], window[2], None]

    def project(index, in_ref):
        piece = pl.ds(pl.multiple_of(index * tile, tile), tile)
        total_ref[...] += matmul(in_ref[...], w_project_ref[piece, :])

    total_ref[...] = field_ref[...]
    convolve(0, even_ref)

    def body(index, carry):
        project(2 * index, even_ref)
        convolve(2 * index + 1, odd_ref)
        project(2 * index + 1, odd_ref)
        convolve(2 * index + 2, even_ref)
        return carry

    pairs = width // tile // 2
    lax.fori_loop(0, pairs - 1, body, 0)
    project(2 * pairs - 2, even_ref)
    convolve(2 * pairs - 1, odd_ref)
    project(2 * pairs - 1, odd_ref)

    mixed = total_ref[...]
    mixed_ref[...] = mixed
    normed = layer_norm(mixed).astype(jnp.bfloat16)
    grouped_ref[...] = matmul(perm_ref[...], normed).astype(jnp.bfloat16)


def mix(expanded, field, up, down, left, right, w_expand, depth_kernel, w_project, perm, rows, cols):
    tokens, channels = field.shape
    width = expanded.shape[1]
    tile = divisor(width // 2, 256, LANES)
    slot = left.shape[0]
    return pl.pallas_call(
        functools.partial(mix_kernel, rows=rows, cols=cols),
        in_specs=[vmem()] * 10,
        out_specs=[vmem()] * 2,
        out_shape=[
            jax.ShapeDtypeStruct((tokens, channels), jnp.float32),
            jax.ShapeDtypeStruct((tokens, channels), jnp.bfloat16),
        ],
        scratch_shapes=[
            pltpu.VMEM((2 * cols + 2 * slot, width), jnp.float32),
            pltpu.VMEM((tokens, channels), jnp.float32),
            pltpu.VMEM((tokens, tile), jnp.bfloat16),
            pltpu.VMEM((tokens, tile), jnp.bfloat16),
        ],
        compiler_params=pltpu.CompilerParams(vmem_limit_bytes=16 * MIB),
        cost_estimate=pl.CostEstimate(
            flops=2 * tokens * channels * width,
            bytes_accessed=tokens * channels * 10 + 4 * channels * width + tokens * width * 2,
            transcendentals=tokens * width,
        ),
        name="mix",
    )(expanded, field, up, down, left, right, w_expand, depth_kernel, w_project, perm)


def identity(size):
    row = lax.broadcasted_iota(jnp.int32, (size, size), 0)
    column = lax.broadcasted_iota(jnp.int32, (size, size), 1)
    return jnp.where(row == column, 1.0, 0.0).astype(jnp.bfloat16)


def attend_kernel(
    tokens_ref, weight_ref, out_ref, query_ref, key_ref, value_ref, turned_ref, even_ref, odd_ref
):
    devices, sets, members, channels = tokens_ref.shape
    count = devices * members
    head_width = channels // HEADS
    group_heads = LANES // head_width
    groups = channels // LANES
    factor = math.log2(math.e) / math.sqrt(head_width)
    lane = lax.broadcasted_iota(jnp.int32, (1, LANES), 1)
    masks = [
        jnp.where((lane >= j * head_width) & (lane < (j + 1) * head_width), 1.0, 0.0).astype(
            jnp.bfloat16
        )
        for j in range(group_heads)
    ]
    turn_values = identity(channels)
    for s in range(sets):
        block = tokens_ref[:, s].reshape(count, channels)
        qkv = matmul(block, weight_ref[...]).astype(jnp.bfloat16)
        values = matmul_nt(turn_values, qkv[:, 2 * channels :]).astype(jnp.bfloat16)
        for group in range(groups):
            lanes = slice(group * LANES, (group + 1) * LANES)
            query_ref[s * groups + group] = qkv[:, lanes]
            key_ref[s * groups + group] = qkv[:, channels + group * LANES : channels + (group + 1) * LANES]
            for j in range(group_heads):
                head = (group * group_heads + j) * head_width
                value_ref[s * groups + group, j, :head_width] = values[head : head + head_width]
                value_ref[s * groups + group, j, head_width:] = jnp.ones((16, count), jnp.bfloat16)

    def scores(index, out):
        keys = key_ref[index]
        stacked = jnp.concatenate([keys * mask for mask in masks], axis=0)
        out[...] = matmul_nt(stacked, query_ref[index])

    def weigh(index, scores_ref):
        for j in range(group_heads):
            part = scores_ref[j * count : (j + 1) * count]
            highest = jnp.max(part, axis=0, keepdims=True)
            raised = jnp.exp2((part - highest) * factor).astype(jnp.bfloat16)
            product = matmul(value_ref[index, j], raised)
            scale = 1.0 / product[head_width : head_width + 1]
            turned_ref[index, j * head_width : (j + 1) * head_width] = (
                product[:head_width] * scale
            ).astype(jnp.bfloat16)

    total = sets * groups
    scores(0, even_ref)

    def body(pair, carry):
        scores(2 * pair + 1, odd_ref)
        weigh(2 * pair, even_ref)
        scores(jnp.minimum(2 * pair + 2, total - 1), even_ref)
        weigh(2 * pair + 1, odd_ref)
        return carry

    lax.fori_loop(0, total // 2, body, 0)
    turn_tokens = identity(count)
    for s in range(sets):
        turned = turned_ref[s * groups : (s + 1) * groups].reshape(channels, count)
        attended = matmul_nt(turn_tokens, turned).astype(jnp.bfloat16)
        out_ref[:, s] = attended.reshape(devices, members, channels)


def attend(blocks, w_qkv):
    devices, sets, members, channels = blocks.shape
    count = devices * members
    apart = members % 16 != 0
    if apart:
        blocks = blocks.transpose(1, 0, 2, 3).reshape(1, sets, count, channels)
    head_width = channels // HEADS
    group_heads = LANES // head_width
    total = sets * channels // LANES
    result = pl.pallas_call(
        attend_kernel,
        in_specs=[vmem()] * 2,
        out_specs=vmem(),
        out_shape=jax.ShapeDtypeStruct(blocks.shape, jnp.bfloat16),
        scratch_shapes=[
            pltpu.VMEM((total, count, LANES), jnp.bfloat16),
            pltpu.VMEM((total, count, LANES), jnp.bfloat16),
            pltpu.VMEM((total, group_heads, head_width + 16, count), jnp.bfloat16),
            pltpu.VMEM((total, LANES, count), jnp.bfloat16),
            pltpu.VMEM((group_heads * count, count), jnp.float32),
            pltpu.VMEM((group_heads * count, count), jnp.float32),
        ],
        compiler_params=pltpu.CompilerParams(vmem_limit_bytes=24 * MIB),
        cost_estimate=pl.CostEstimate(
            flops=sets * (2 * count * channels * channels * 3 + 4 * count * count * channels),
            bytes_accessed=4 * sets * count * channels + 6 * channels * channels,
            transcendentals=sets * HEADS * count * count,
        ),
        name="attend",
    )(blocks, w_qkv)
    if apart:
        result = result.reshape(sets, devices, members, channels).transpose(1, 0, 2, 3)
    return result


def finish_kernel(attended_ref, back_ref, weight_ref, mixed_ref, out_ref):
    step = out_ref.shape[0]
    rows = pl.ds(pl.multiple_of(pl.program_id(0) * step, step), step)
    restored = matmul(back_ref[rows, :], attended_ref[...]).astype(jnp.bfloat16)
    out_ref[...] = mixed_ref[rows, :] + matmul(restored, weight_ref[...])


def finish(attended, back, w_out, mixed):
    tokens, channels = mixed.shape
    step = divisor(tokens, 128, 16)
    return pl.pallas_call(
        finish_kernel,
        grid=(tokens // step,),
        in_specs=[vmem()] * 4,
        out_specs=pl.BlockSpec((step, channels), lambda i: (i, 0)),
        out_shape=jax.ShapeDtypeStruct((tokens, channels), jnp.float32),
        compiler_params=pltpu.CompilerParams(vmem_limit_bytes=16 * MIB),
        name="finish",
    )(attended, back, w_out, mixed)


def exchange(low_edge, high_edge, axis):
    count = lax.axis_size(axis)
    even = lax.axis_index(axis) % 2 == 0

    def swap(edge, start):
        pairs = [(i, i + 1) for i in range(start, count - 1, 2)]
        return lax.ppermute(edge, axis, pairs + [(b, a) for a, b in pairs])

    one = swap(jnp.where(even, high_edge, low_edge), 0)
    two = swap(jnp.where(even, low_edge, high_edge), 1)
    return jnp.where(even, two, one), jnp.where(even, one, two)


def grouping(rows, cols, blocks_rows, blocks_cols):
    order = np.arange(rows * cols).reshape(
        blocks_rows, rows // blocks_rows, blocks_cols, cols // blocks_cols
    )
    order = order.transpose(1, 3, 0, 2).reshape(-1)
    matrix = np.zeros((order.size, order.size), np.float32)
    matrix[np.arange(order.size), order] = 1.0
    return matrix


def shards(field, w_expand, depth_kernel, w_project, w_qkv, w_out):
    rows, cols, channels = field.shape
    tokens = rows * cols
    row_devices = lax.axis_size("row")
    col_devices = lax.axis_size("col")
    devices = row_devices * col_devices
    blocks_rows = GRID // row_devices
    blocks_cols = GRID // col_devices
    members = blocks_rows * blocks_cols
    sets_local = tokens // members // devices
    matrix = grouping(rows, cols, blocks_rows, blocks_cols)
    perm = jnp.asarray(matrix, jnp.bfloat16)
    back = jnp.asarray(matrix.T, jnp.bfloat16)

    flat = field.reshape(tokens, channels)
    normed = norm(flat)
    up, down = exchange(normed[:cols], normed[tokens - cols :], "row")
    expanded = expand(normed, w_expand)
    tile = normed.reshape(rows, cols, channels)
    spare = jnp.zeros((round_up(rows + 2, 16) - rows - 2, channels), jnp.bfloat16)
    first = jnp.concatenate([up[:1], tile[:, 0], down[:1], spare], axis=0)
    last = jnp.concatenate([up[cols - 1 :], tile[:, cols - 1], down[cols - 1 :], spare], axis=0)
    left, right = exchange(first, last, "col")
    mixed, grouped = mix(
        expanded, flat, up, down, left, right, w_expand, depth_kernel, w_project, perm, rows, cols
    )
    arrived = lax.all_to_all(
        grouped.reshape(devices, sets_local * members, channels), ("row", "col"), 0, 0, tiled=True
    )
    attended = attend(arrived.reshape(devices, sets_local, members, channels), w_qkv)
    returned = lax.all_to_all(
        attended.reshape(devices, sets_local * members, channels), ("row", "col"), 0, 0, tiled=True
    )
    final = finish(returned.reshape(tokens, channels), back, w_out, mixed)
    return final.reshape(rows, cols, channels)


def solution(mesh):
    return jax.shard_map(
        shards,
        mesh=mesh,
        in_specs=(P(("field", "row"), "col", None), P(), P(), P(), P(), P()),
        out_specs=P(("field", "row"), "col", None),
        check_vma=False,
    )
```

```python
import functools
import math

import jax
import jax.numpy as jnp
import numpy as np
from jax import lax
from jax.experimental import pallas as pl
from jax.experimental.pallas import tpu as pltpu
from jax.sharding import PartitionSpec as P

HEADS = 16
GRID = 16
LANES = 128
MIB = 1024 * 1024
NT = (((1,), (1,)), ((), ()))


def layer_norm(inputs):
    average = jnp.mean(inputs, axis=-1, keepdims=True)
    centred = inputs - average
    variance = jnp.mean(centred * centred, axis=-1, keepdims=True)
    return centred * lax.rsqrt(variance + 1e-05)


def gelu_of_half(half):
    scale = math.sqrt(2.0 / math.pi)
    inner = half * (2.0 * scale + (8.0 * scale * 0.044715) * (half * half))
    return half + half * jnp.tanh(inner)


def matmul(a, b):
    return jnp.dot(a, b, preferred_element_type=jnp.float32)


def matmul_nt(a, b):
    return lax.dot_general(a, b, NT, preferred_element_type=jnp.float32)


def divisor(size, most, unit):
    best = size
    for piece in range(unit, most + 1, unit):
        if size % piece == 0:
            best = piece
    return best


def round_up(size, unit):
    return -(-size // unit) * unit


def vmem():
    return pl.BlockSpec(memory_space=pltpu.VMEM)


def half_norm(inputs):
    return (layer_norm(inputs) * 0.5).astype(jnp.bfloat16)


def edge_kernel(edge_ref, out_ref):
    out_ref[...] = half_norm(edge_ref[...])


def norm_edges(edges):
    return pl.pallas_call(
        edge_kernel,
        in_specs=[vmem()],
        out_specs=vmem(),
        out_shape=jax.ShapeDtypeStruct(edges.shape, jnp.bfloat16),
        compiler_params=pltpu.CompilerParams(vmem_limit_bytes=8 * MIB),
        cost_estimate=pl.CostEstimate(
            flops=8 * edges.size, bytes_accessed=6 * edges.size, transcendentals=edges.shape[0]
        ),
        name="norm_edges",
    )(edges)


def padded_rows(tokens):
    return tokens + 16


def expand_kernel(field_ref, weight_ref, normed_ref, out_ref):
    tokens = normed_ref.shape[0]
    width = weight_ref.shape[1]
    tile = divisor(width, 512, LANES)
    step = divisor(tokens, 128, 16)
    starts = range(0, tokens, step)
    for start in starts:
        normed_ref[start : start + step, :] = half_norm(field_ref[start : start + step, :])

    def body(index, carry):
        lanes = pl.ds(pl.multiple_of(index * tile, tile), tile)
        for start in starts:
            made = gelu_of_half(
                matmul(normed_ref[start : start + step, :], weight_ref[:, lanes])
            )
            for sub in range(tile // LANES):
                row = (index * (tile // LANES) + sub) * padded_rows(tokens) + 8 + start
                out_ref[pl.ds(pl.multiple_of(row, 8), step), :] = made[
                    :, sub * LANES : (sub + 1) * LANES
                ]
        return carry

    lax.fori_loop(0, width // tile, body, 0)


def expand(field, w_expand):
    tokens, channels = field.shape
    width = w_expand.shape[1]
    return pl.pallas_call(
        expand_kernel,
        in_specs=[vmem()] * 2,
        out_specs=[vmem()] * 2,
        out_shape=[
            jax.ShapeDtypeStruct((tokens, channels), jnp.bfloat16),
            jax.ShapeDtypeStruct((width // LANES * padded_rows(tokens), LANES), jnp.float32),
        ],
        compiler_params=pltpu.CompilerParams(vmem_limit_bytes=16 * MIB),
        cost_estimate=pl.CostEstimate(
            flops=2 * tokens * channels * width,
            bytes_accessed=tokens * channels * 6 + channels * width * 2 + tokens * width * 4,
            transcendentals=tokens * width,
        ),
        name="expand",
    )(field, w_expand)


def mix_kernel(
    expanded_ref, field_ref, up_ref, down_ref, left_ref, right_ref, w_expand_ref, depth_ref,
    w_project_ref, perm_ref, mixed_ref, grouped_ref, total_ref, normed_ref,
    even_ref, odd_ref, even_halo_ref, odd_halo_ref, *, rows, cols,
):
    tokens = rows * cols
    width = w_expand_ref.shape[1]
    tile = even_ref.shape[1]
    slot = left_ref.shape[0]
    up_start, down_start, left_start = 8, 16 + cols, 24 + 2 * cols
    right_start = left_start + slot

    edges = jnp.concatenate(
        [up_ref[...], down_ref[...], left_ref[...], right_ref[...]], axis=0
    )

    def expand_halo(index, out_ref):
        lanes = pl.ds(pl.multiple_of(index * tile, tile), tile)
        made = gelu_of_half(matmul(edges, w_expand_ref[:, lanes]))
        for sub in range(tile // LANES):
            part = made[:, sub * LANES : (sub + 1) * LANES]
            out_ref[sub, up_start : up_start + cols] = part[:cols]
            out_ref[sub, down_start : down_start + cols] = part[cols : 2 * cols]
            out_ref[sub, left_start : left_start + 2 * slot] = part[2 * cols :]

    position = lax.broadcasted_iota(jnp.int32, (8, LANES), 0)
    at_first = position == 0
    at_last = position == 7

    def convolve(index, out_ref, halo_ref):
        for sub in range(tile // LANES):
            lanes = pl.ds(pl.multiple_of(index * tile + sub * LANES, LANES), LANES)
            base = (index * (tile // LANES) + sub) * padded_rows(tokens) + 8
            taps = [[0.5 * depth_ref[p, q : q + 1, lanes] for q in range(3)] for p in range(3)]
            sums = {}
            for y in range(-1, rows + 1):
                if y < 0:
                    parts = [halo_ref[sub, up_start + q : up_start + q + cols] for q in (-1, 0, 1)]
                elif y == rows:
                    parts = [
                        halo_ref[sub, down_start + q : down_start + q + cols] for q in (-1, 0, 1)
                    ]
                else:
                    parts = [
                        expanded_ref[pl.ds(base + (y * cols + q), cols), :] for q in (-1, 0, 1)
                    ]
                left = halo_ref[sub, left_start + y + 1 : left_start + y + 2]
                right = halo_ref[sub, right_start + y + 1 : right_start + y + 2]
                parts[0] = jnp.concatenate(
                    [jnp.where(at_first, left, parts[0][:8]), parts[0][8:]], axis=0
                )
                parts[2] = jnp.concatenate(
                    [parts[2][:-8], jnp.where(at_last, right, parts[2][-8:])], axis=0
                )
                for p in range(3):
                    target = y + 1 - p
                    if 0 <= target < rows:
                        for q in range(3):
                            term = taps[p][q] * parts[q]
                            sums[target] = sums[target] + term if target in sums else term
                if y > 0:
                    out_ref[
                        (y - 1) * cols : y * cols, sub * LANES : (sub + 1) * LANES
                    ] = gelu_of_half(sums.pop(y - 1)).astype(jnp.bfloat16)

    def project(index, in_ref):
        piece = pl.ds(pl.multiple_of(index * tile, tile), tile)
        total_ref[...] += matmul(in_ref[...], w_project_ref[piece, :])

    total_ref[...] = field_ref[...]
    expand_halo(0, even_halo_ref)
    expand_halo(1, odd_halo_ref)
    convolve(0, even_ref, even_halo_ref)

    def body(index, carry):
        project(2 * index, even_ref)
        convolve(2 * index + 1, odd_ref, odd_halo_ref)
        expand_halo(2 * index + 2, even_halo_ref)
        project(2 * index + 1, odd_ref)
        convolve(2 * index + 2, even_ref, even_halo_ref)
        expand_halo(2 * index + 3, odd_halo_ref)
        return carry

    pairs = width // tile // 2
    lax.fori_loop(0, pairs - 1, body, 0)
    project(2 * pairs - 2, even_ref)
    convolve(2 * pairs - 1, odd_ref, odd_halo_ref)
    project(2 * pairs - 1, odd_ref)

    step = divisor(tokens, 128, 16)
    for start in range(0, tokens, step):
        piece = slice(start, start + step)
        mixed = total_ref[piece, :]
        mixed_ref[piece, :] = mixed
        normed_ref[piece, :] = layer_norm(mixed).astype(jnp.bfloat16)
    grouped_ref[...] = matmul(perm_ref[...], normed_ref[...]).astype(jnp.bfloat16)


def mix(expanded, field, up, down, left, right, w_expand, depth_kernel, w_project, perm, rows, cols):
    tokens, channels = field.shape
    width = w_expand.shape[1]
    tile = divisor(width // 2, 256, LANES)
    slot = left.shape[0]
    halo = pltpu.VMEM((tile // LANES, 24 + 2 * cols + 2 * slot, LANES), jnp.float32)
    return pl.pallas_call(
        functools.partial(mix_kernel, rows=rows, cols=cols),
        in_specs=[vmem()] * 10,
        out_specs=[vmem()] * 2,
        out_shape=[
            jax.ShapeDtypeStruct((tokens, channels), jnp.float32),
            jax.ShapeDtypeStruct((tokens, channels), jnp.bfloat16),
        ],
        scratch_shapes=[
            pltpu.VMEM((tokens, channels), jnp.float32),
            pltpu.VMEM((tokens, channels), jnp.bfloat16),
            pltpu.VMEM((tokens, tile), jnp.bfloat16),
            pltpu.VMEM((tokens, tile), jnp.bfloat16),
            halo,
            halo,
        ],
        compiler_params=pltpu.CompilerParams(vmem_limit_bytes=16 * MIB),
        cost_estimate=pl.CostEstimate(
            flops=2 * tokens * channels * width,
            bytes_accessed=tokens * channels * 10 + 4 * channels * width + tokens * width * 4,
            transcendentals=tokens * width,
        ),
        name="mix",
    )(expanded, field, up, down, left, right, w_expand, depth_kernel, w_project, perm)


def identity(size):
    row = lax.broadcasted_iota(jnp.int32, (size, size), 0)
    column = lax.broadcasted_iota(jnp.int32, (size, size), 1)
    return jnp.where(row == column, 1.0, 0.0).astype(jnp.bfloat16)


def attend_kernel(
    tokens_ref, weight_ref, out_ref, query_ref, key_ref, value_ref, turned_ref, even_ref, odd_ref
):
    devices, sets, members, channels = tokens_ref.shape
    count = devices * members
    head_width = channels // HEADS
    group_heads = LANES // head_width
    groups = channels // LANES
    factor = math.log2(math.e) / math.sqrt(head_width)
    lane = lax.broadcasted_iota(jnp.int32, (1, LANES), 1)
    masks = [
        jnp.where((lane >= j * head_width) & (lane < (j + 1) * head_width), 1.0, 0.0).astype(
            jnp.bfloat16
        )
        for j in range(group_heads)
    ]
    turn_values = identity(channels)
    for s in range(sets):
        block = tokens_ref[:, s].reshape(count, channels)
        qkv = matmul(block, weight_ref[...]).astype(jnp.bfloat16)
        values = matmul_nt(turn_values, qkv[:, 2 * channels :]).astype(jnp.bfloat16)
        for group in range(groups):
            lanes = slice(group * LANES, (group + 1) * LANES)
            query_ref[s * groups + group] = qkv[:, lanes]
            key_ref[s * groups + group] = qkv[:, channels + group * LANES : channels + (group + 1) * LANES]
            for j in range(group_heads):
                head = (group * group_heads + j) * head_width
                value_ref[s * groups + group, j, :head_width] = values[head : head + head_width]
                value_ref[s * groups + group, j, head_width:] = jnp.ones((16, count), jnp.bfloat16)

    def scores(index, out):
        keys = key_ref[index]
        stacked = jnp.concatenate([keys * mask for mask in masks], axis=0)
        out[...] = matmul_nt(stacked, query_ref[index])

    def weigh(index, scores_ref):
        for j in range(group_heads):
            part = scores_ref[j * count : (j + 1) * count]
            highest = jnp.max(part, axis=0, keepdims=True)
            raised = jnp.exp2((part - highest) * factor).astype(jnp.bfloat16)
            product = matmul(value_ref[index, j], raised)
            scale = 1.0 / product[head_width : head_width + 1]
            turned_ref[index, j * head_width : (j + 1) * head_width] = (
                product[:head_width] * scale
            ).astype(jnp.bfloat16)

    total = sets * groups
    scores(0, even_ref)

    def body(pair, carry):
        scores(2 * pair + 1, odd_ref)
        weigh(2 * pair, even_ref)
        scores(jnp.minimum(2 * pair + 2, total - 1), even_ref)
        weigh(2 * pair + 1, odd_ref)
        return carry

    lax.fori_loop(0, total // 2, body, 0)
    turn_tokens = identity(count)
    for s in range(sets):
        turned = turned_ref[s * groups : (s + 1) * groups].reshape(channels, count)
        attended = matmul_nt(turn_tokens, turned).astype(jnp.bfloat16)
        out_ref[:, s] = attended.reshape(devices, members, channels)


def attend(blocks, w_qkv):
    devices, sets, members, channels = blocks.shape
    count = devices * members
    apart = members % 16 != 0
    if apart:
        blocks = blocks.transpose(1, 0, 2, 3).reshape(1, sets, count, channels)
    head_width = channels // HEADS
    group_heads = LANES // head_width
    total = sets * channels // LANES
    result = pl.pallas_call(
        attend_kernel,
        in_specs=[vmem()] * 2,
        out_specs=vmem(),
        out_shape=jax.ShapeDtypeStruct(blocks.shape, jnp.bfloat16),
        scratch_shapes=[
            pltpu.VMEM((total, count, LANES), jnp.bfloat16),
            pltpu.VMEM((total, count, LANES), jnp.bfloat16),
            pltpu.VMEM((total, group_heads, head_width + 16, count), jnp.bfloat16),
            pltpu.VMEM((total, LANES, count), jnp.bfloat16),
            pltpu.VMEM((group_heads * count, count), jnp.float32),
            pltpu.VMEM((group_heads * count, count), jnp.float32),
        ],
        compiler_params=pltpu.CompilerParams(vmem_limit_bytes=24 * MIB),
        cost_estimate=pl.CostEstimate(
            flops=sets * (2 * count * channels * channels * 3 + 4 * count * count * channels),
            bytes_accessed=4 * sets * count * channels + 6 * channels * channels,
            transcendentals=sets * HEADS * count * count,
        ),
        name="attend",
    )(blocks, w_qkv)
    if apart:
        result = result.reshape(sets, devices, members, channels).transpose(1, 0, 2, 3)
    return result


def finish_kernel(attended_ref, back_ref, weight_ref, mixed_ref, out_ref, made_ref, sent):
    tokens = mixed_ref.shape[0]
    step = made_ref.shape[1]
    copies = []
    for index, start in enumerate(range(0, tokens, step)):
        rows = slice(start, start + step)
        restored = matmul(back_ref[rows, :], attended_ref[...]).astype(jnp.bfloat16)
        made_ref[index] = mixed_ref[rows, :] + matmul(restored, weight_ref[...])
        copy = pltpu.make_async_copy(
            made_ref.at[index], out_ref.at[pl.ds(start, step)], sent.at[index]
        )
        copy.start()
        copies.append(copy)
    for copy in copies:
        copy.wait()


def finish(attended, back, w_out, mixed):
    tokens, channels = mixed.shape
    step = divisor(tokens, 128, 16)
    return pl.pallas_call(
        finish_kernel,
        in_specs=[vmem()] * 4,
        out_specs=pl.BlockSpec(memory_space=pltpu.HBM),
        out_shape=jax.ShapeDtypeStruct((tokens, channels), jnp.float32),
        scratch_shapes=[
            pltpu.VMEM((tokens // step, step, channels), jnp.float32),
            pltpu.SemaphoreType.DMA((tokens // step,)),
        ],
        compiler_params=pltpu.CompilerParams(vmem_limit_bytes=16 * MIB),
        name="finish",
    )(attended, back, w_out, mixed)


def exchange(low_edge, high_edge, axis):
    count = lax.axis_size(axis)
    even = lax.axis_index(axis) % 2 == 0

    def swap(edge, start):
        pairs = [(i, i + 1) for i in range(start, count - 1, 2)]
        return lax.ppermute(edge, axis, pairs + [(b, a) for a, b in pairs])

    one = swap(jnp.where(even, high_edge, low_edge), 0)
    two = swap(jnp.where(even, low_edge, high_edge), 1)
    return jnp.where(even, two, one), jnp.where(even, one, two)


def grouping(rows, cols, blocks_rows, blocks_cols):
    order = np.arange(rows * cols).reshape(
        blocks_rows, rows // blocks_rows, blocks_cols, cols // blocks_cols
    )
    order = order.transpose(1, 3, 0, 2).reshape(-1)
    matrix = np.zeros((order.size, order.size), np.float32)
    matrix[np.arange(order.size), order] = 1.0
    return matrix


def shards(field, w_expand, depth_kernel, w_project, w_qkv, w_out):
    rows, cols, channels = field.shape
    tokens = rows * cols
    row_devices = lax.axis_size("row")
    col_devices = lax.axis_size("col")
    devices = row_devices * col_devices
    blocks_rows = GRID // row_devices
    blocks_cols = GRID // col_devices
    members = blocks_rows * blocks_cols
    sets_local = tokens // members // devices
    matrix = grouping(rows, cols, blocks_rows, blocks_cols)
    perm = jnp.asarray(matrix, jnp.bfloat16)
    back = jnp.asarray(matrix.T, jnp.bfloat16)

    flat = field.reshape(tokens, channels)
    edges = norm_edges(jnp.concatenate([field[0], field[rows - 1]], axis=0))
    up, down = exchange(edges[:cols], edges[cols:], "row")
    normed, expanded = expand(flat, w_expand)
    up, down, normed = lax.optimization_barrier((up, down, normed))
    tile = normed.reshape(rows, cols, channels)
    spare = jnp.zeros((round_up(rows + 2, 16) - rows - 2, channels), jnp.bfloat16)
    first = jnp.concatenate([up[:1], tile[:, 0], down[:1], spare], axis=0)
    last = jnp.concatenate([up[cols - 1 :], tile[:, cols - 1], down[cols - 1 :], spare], axis=0)
    left, right = exchange(first, last, "col")
    mixed, grouped = mix(
        expanded, flat, up, down, left, right, w_expand, depth_kernel, w_project, perm, rows, cols
    )
    arrived = lax.all_to_all(
        grouped.reshape(devices, sets_local * members, channels), ("row", "col"), 0, 0, tiled=True
    )
    attended = attend(arrived.reshape(devices, sets_local, members, channels), w_qkv)
    returned = lax.all_to_all(
        attended.reshape(devices, sets_local * members, channels), ("row", "col"), 0, 0, tiled=True
    )
    final = finish(returned.reshape(tokens, channels), back, w_out, mixed)
    return final.reshape(rows, cols, channels)


def solution(mesh):
    return jax.shard_map(
        shards,
        mesh=mesh,
        in_specs=(P(("field", "row"), "col", None), P(), P(), P(), P(), P()),
        out_specs=P(("field", "row"), "col", None),
        check_vma=False,
    )
```

```python
import functools
import math

import jax
import jax.numpy as jnp
import numpy as np
from jax import lax
from jax.experimental import pallas as pl
from jax.experimental.pallas import tpu as pltpu
from jax.sharding import PartitionSpec as P

HEADS = 16
GRID = 16
LANES = 128
MIB = 1024 * 1024
NT = (((1,), (1,)), ((), ()))


def layer_norm(inputs):
    average = jnp.mean(inputs, axis=-1, keepdims=True)
    centred = inputs - average
    variance = jnp.mean(centred * centred, axis=-1, keepdims=True)
    return centred * lax.rsqrt(variance + 1e-05)


def gelu_of_half(half):
    scale = math.sqrt(2.0 / math.pi)
    inner = half * (2.0 * scale + (8.0 * scale * 0.044715) * (half * half))
    return half + half * jnp.tanh(inner)


def matmul(a, b):
    return jnp.dot(a, b, preferred_element_type=jnp.float32)


def matmul_nt(a, b):
    return lax.dot_general(a, b, NT, preferred_element_type=jnp.float32)


def divisor(size, most, unit):
    best = size
    for piece in range(unit, most + 1, unit):
        if size % piece == 0:
            best = piece
    return best


def round_up(size, unit):
    return -(-size // unit) * unit


def vmem():
    return pl.BlockSpec(memory_space=pltpu.VMEM)


def half_norm(inputs):
    return (layer_norm(inputs) * 0.5).astype(jnp.bfloat16)


def edge_kernel(edge_ref, out_ref):
    out_ref[...] = half_norm(edge_ref[...])


def norm_edges(edges):
    return pl.pallas_call(
        edge_kernel,
        in_specs=[vmem()],
        out_specs=vmem(),
        out_shape=jax.ShapeDtypeStruct(edges.shape, jnp.bfloat16),
        compiler_params=pltpu.CompilerParams(vmem_limit_bytes=8 * MIB),
        cost_estimate=pl.CostEstimate(
            flops=10**10, bytes_accessed=6 * edges.size, transcendentals=edges.shape[0]
        ),
        name="norm_edges",
    )(edges)


def padded_rows(tokens):
    return tokens + 16


def expand_kernel(field_ref, weight_ref, normed_ref, out_ref):
    tokens = normed_ref.shape[0]
    width = weight_ref.shape[1]
    tile = divisor(width, 512, LANES)
    step = divisor(tokens, 128, 16)
    starts = range(0, tokens, step)
    for start in starts:
        normed_ref[start : start + step, :] = half_norm(field_ref[start : start + step, :])

    def body(index, carry):
        lanes = pl.ds(pl.multiple_of(index * tile, tile), tile)
        for start in starts:
            made = gelu_of_half(
                matmul(normed_ref[start : start + step, :], weight_ref[:, lanes])
            )
            for sub in range(tile // LANES):
                row = (index * (tile // LANES) + sub) * padded_rows(tokens) + 8 + start
                out_ref[pl.ds(pl.multiple_of(row, 8), step), :] = made[
                    :, sub * LANES : (sub + 1) * LANES
                ]
        return carry

    lax.fori_loop(0, width // tile, body, 0)


def expand(field, w_expand):
    tokens, channels = field.shape
    width = w_expand.shape[1]
    return pl.pallas_call(
        expand_kernel,
        in_specs=[vmem()] * 2,
        out_specs=[vmem()] * 2,
        out_shape=[
            jax.ShapeDtypeStruct((tokens, channels), jnp.bfloat16),
            jax.ShapeDtypeStruct((width // LANES * padded_rows(tokens), LANES), jnp.float32),
        ],
        compiler_params=pltpu.CompilerParams(vmem_limit_bytes=16 * MIB),
        cost_estimate=pl.CostEstimate(
            flops=2 * tokens * channels * width,
            bytes_accessed=tokens * channels * 6 + channels * width * 2 + tokens * width * 4,
            transcendentals=tokens * width,
        ),
        name="expand",
    )(field, w_expand)


def mix_kernel(
    expanded_ref, field_ref, up_ref, down_ref, left_ref, right_ref, w_expand_ref, depth_ref,
    w_project_ref, perm_ref, mixed_ref, grouped_ref, total_ref, normed_ref,
    even_ref, odd_ref, even_halo_ref, odd_halo_ref, *, rows, cols,
):
    tokens = rows * cols
    width = w_expand_ref.shape[1]
    tile = even_ref.shape[1]
    slot = left_ref.shape[0]
    up_start, down_start, left_start = 8, 16 + cols, 24 + 2 * cols
    right_start = left_start + slot

    edges = jnp.concatenate(
        [up_ref[...], down_ref[...], left_ref[...], right_ref[...]], axis=0
    )

    def expand_halo(index, out_ref):
        lanes = pl.ds(pl.multiple_of(index * tile, tile), tile)
        made = gelu_of_half(matmul(edges, w_expand_ref[:, lanes]))
        for sub in range(tile // LANES):
            part = made[:, sub * LANES : (sub + 1) * LANES]
            out_ref[sub, up_start : up_start + cols] = part[:cols]
            out_ref[sub, down_start : down_start + cols] = part[cols : 2 * cols]
            out_ref[sub, left_start : left_start + 2 * slot] = part[2 * cols :]

    position = lax.broadcasted_iota(jnp.int32, (8, LANES), 0)
    at_first = position == 0
    at_last = position == 7

    def convolve(index, out_ref, halo_ref):
        for sub in range(tile // LANES):
            lanes = pl.ds(pl.multiple_of(index * tile + sub * LANES, LANES), LANES)
            base = (index * (tile // LANES) + sub) * padded_rows(tokens) + 8
            taps = [[0.5 * depth_ref[p, q : q + 1, lanes] for q in range(3)] for p in range(3)]
            sums = {}
            for y in range(-1, rows + 1):
                if y < 0:
                    parts = [halo_ref[sub, up_start + q : up_start + q + cols] for q in (-1, 0, 1)]
                elif y == rows:
                    parts = [
                        halo_ref[sub, down_start + q : down_start + q + cols] for q in (-1, 0, 1)
                    ]
                else:
                    parts = [
                        expanded_ref[pl.ds(base + (y * cols + q), cols), :] for q in (-1, 0, 1)
                    ]
                left = halo_ref[sub, left_start + y + 1 : left_start + y + 2]
                right = halo_ref[sub, right_start + y + 1 : right_start + y + 2]
                parts[0] = jnp.concatenate(
                    [jnp.where(at_first, left, parts[0][:8]), parts[0][8:]], axis=0
                )
                parts[2] = jnp.concatenate(
                    [parts[2][:-8], jnp.where(at_last, right, parts[2][-8:])], axis=0
                )
                for p in range(3):
                    target = y + 1 - p
                    if 0 <= target < rows:
                        for q in range(3):
                            term = taps[p][q] * parts[q]
                            sums[target] = sums[target] + term if target in sums else term
                if y > 0:
                    out_ref[
                        (y - 1) * cols : y * cols, sub * LANES : (sub + 1) * LANES
                    ] = gelu_of_half(sums.pop(y - 1)).astype(jnp.bfloat16)

    def project(index, in_ref):
        piece = pl.ds(pl.multiple_of(index * tile, tile), tile)
        total_ref[...] += matmul(in_ref[...], w_project_ref[piece, :])

    total_ref[...] = field_ref[...]
    expand_halo(0, even_halo_ref)
    expand_halo(1, odd_halo_ref)
    convolve(0, even_ref, even_halo_ref)

    def body(index, carry):
        project(2 * index, even_ref)
        convolve(2 * index + 1, odd_ref, odd_halo_ref)
        expand_halo(2 * index + 2, even_halo_ref)
        project(2 * index + 1, odd_ref)
        convolve(2 * index + 2, even_ref, even_halo_ref)
        expand_halo(2 * index + 3, odd_halo_ref)
        return carry

    pairs = width // tile // 2
    lax.fori_loop(0, pairs - 1, body, 0)
    project(2 * pairs - 2, even_ref)
    convolve(2 * pairs - 1, odd_ref, odd_halo_ref)
    project(2 * pairs - 1, odd_ref)

    step = divisor(tokens, 128, 16)
    for start in range(0, tokens, step):
        piece = slice(start, start + step)
        mixed = total_ref[piece, :]
        mixed_ref[piece, :] = mixed
        normed_ref[piece, :] = layer_norm(mixed).astype(jnp.bfloat16)
    grouped_ref[...] = matmul(perm_ref[...], normed_ref[...]).astype(jnp.bfloat16)


def mix(expanded, field, up, down, left, right, w_expand, depth_kernel, w_project, perm, rows, cols):
    tokens, channels = field.shape
    width = w_expand.shape[1]
    tile = divisor(width // 2, 256, LANES)
    slot = left.shape[0]
    halo = pltpu.VMEM((tile // LANES, 24 + 2 * cols + 2 * slot, LANES), jnp.float32)
    return pl.pallas_call(
        functools.partial(mix_kernel, rows=rows, cols=cols),
        in_specs=[vmem()] * 10,
        out_specs=[vmem()] * 2,
        out_shape=[
            jax.ShapeDtypeStruct((tokens, channels), jnp.float32),
            jax.ShapeDtypeStruct((tokens, channels), jnp.bfloat16),
        ],
        scratch_shapes=[
            pltpu.VMEM((tokens, channels), jnp.float32),
            pltpu.VMEM((tokens, channels), jnp.bfloat16),
            pltpu.VMEM((tokens, tile), jnp.bfloat16),
            pltpu.VMEM((tokens, tile), jnp.bfloat16),
            halo,
            halo,
        ],
        compiler_params=pltpu.CompilerParams(vmem_limit_bytes=16 * MIB),
        cost_estimate=pl.CostEstimate(
            flops=2 * tokens * channels * width,
            bytes_accessed=tokens * channels * 10 + 4 * channels * width + tokens * width * 4,
            transcendentals=tokens * width,
        ),
        name="mix",
    )(expanded, field, up, down, left, right, w_expand, depth_kernel, w_project, perm)


def identity(size):
    row = lax.broadcasted_iota(jnp.int32, (size, size), 0)
    column = lax.broadcasted_iota(jnp.int32, (size, size), 1)
    return jnp.where(row == column, 1.0, 0.0).astype(jnp.bfloat16)


def attend_kernel(
    tokens_ref, weight_ref, out_ref, query_ref, key_ref, value_ref, turned_ref, even_ref, odd_ref
):
    devices, sets, members, channels = tokens_ref.shape
    count = devices * members
    head_width = channels // HEADS
    group_heads = LANES // head_width
    groups = channels // LANES
    factor = math.log2(math.e) / math.sqrt(head_width)
    lane = lax.broadcasted_iota(jnp.int32, (1, LANES), 1)
    masks = [
        jnp.where((lane >= j * head_width) & (lane < (j + 1) * head_width), 1.0, 0.0).astype(
            jnp.bfloat16
        )
        for j in range(group_heads)
    ]
    turn_values = identity(channels)
    for s in range(sets):
        block = tokens_ref[:, s].reshape(count, channels)
        qkv = matmul(block, weight_ref[...]).astype(jnp.bfloat16)
        values = matmul_nt(turn_values, qkv[:, 2 * channels :]).astype(jnp.bfloat16)
        for group in range(groups):
            lanes = slice(group * LANES, (group + 1) * LANES)
            query_ref[s * groups + group] = qkv[:, lanes]
            key_ref[s * groups + group] = qkv[:, channels + group * LANES : channels + (group + 1) * LANES]
            for j in range(group_heads):
                head = (group * group_heads + j) * head_width
                value_ref[s * groups + group, j, :head_width] = values[head : head + head_width]
                value_ref[s * groups + group, j, head_width:] = jnp.ones((16, count), jnp.bfloat16)

    def scores(index, out):
        keys = key_ref[index]
        stacked = jnp.concatenate([keys * mask for mask in masks], axis=0)
        out[...] = matmul_nt(stacked, query_ref[index])

    def weigh(index, scores_ref):
        for j in range(group_heads):
            part = scores_ref[j * count : (j + 1) * count]
            highest = jnp.max(part, axis=0, keepdims=True)
            raised = jnp.exp2((part - highest) * factor).astype(jnp.bfloat16)
            product = matmul(value_ref[index, j], raised)
            scale = 1.0 / product[head_width : head_width + 1]
            turned_ref[index, j * head_width : (j + 1) * head_width] = (
                product[:head_width] * scale
            ).astype(jnp.bfloat16)

    total = sets * groups
    scores(0, even_ref)

    def body(pair, carry):
        scores(2 * pair + 1, odd_ref)
        weigh(2 * pair, even_ref)
        scores(jnp.minimum(2 * pair + 2, total - 1), even_ref)
        weigh(2 * pair + 1, odd_ref)
        return carry

    lax.fori_loop(0, total // 2, body, 0)
    turn_tokens = identity(count)
    for s in range(sets):
        turned = turned_ref[s * groups : (s + 1) * groups].reshape(channels, count)
        attended = matmul_nt(turn_tokens, turned).astype(jnp.bfloat16)
        out_ref[:, s] = attended.reshape(devices, members, channels)


def attend(blocks, w_qkv):
    devices, sets, members, channels = blocks.shape
    count = devices * members
    apart = members % 16 != 0
    if apart:
        blocks = blocks.transpose(1, 0, 2, 3).reshape(1, sets, count, channels)
    head_width = channels // HEADS
    group_heads = LANES // head_width
    total = sets * channels // LANES
    result = pl.pallas_call(
        attend_kernel,
        in_specs=[vmem()] * 2,
        out_specs=vmem(),
        out_shape=jax.ShapeDtypeStruct(blocks.shape, jnp.bfloat16),
        scratch_shapes=[
            pltpu.VMEM((total, count, LANES), jnp.bfloat16),
            pltpu.VMEM((total, count, LANES), jnp.bfloat16),
            pltpu.VMEM((total, group_heads, head_width + 16, count), jnp.bfloat16),
            pltpu.VMEM((total, LANES, count), jnp.bfloat16),
            pltpu.VMEM((group_heads * count, count), jnp.float32),
            pltpu.VMEM((group_heads * count, count), jnp.float32),
        ],
        compiler_params=pltpu.CompilerParams(vmem_limit_bytes=24 * MIB),
        cost_estimate=pl.CostEstimate(
            flops=sets * (2 * count * channels * channels * 3 + 4 * count * count * channels),
            bytes_accessed=4 * sets * count * channels + 6 * channels * channels,
            transcendentals=sets * HEADS * count * count,
        ),
        name="attend",
    )(blocks, w_qkv)
    if apart:
        result = result.reshape(sets, devices, members, channels).transpose(1, 0, 2, 3)
    return result


def finish_kernel(attended_ref, back_ref, weight_ref, mixed_ref, out_ref, made_ref, sent):
    tokens = mixed_ref.shape[0]
    step = made_ref.shape[1]
    copies = []
    for index, start in enumerate(range(0, tokens, step)):
        rows = slice(start, start + step)
        restored = matmul(back_ref[rows, :], attended_ref[...]).astype(jnp.bfloat16)
        made_ref[index] = mixed_ref[rows, :] + matmul(restored, weight_ref[...])
        copy = pltpu.make_async_copy(
            made_ref.at[index], out_ref.at[pl.ds(start, step)], sent.at[index]
        )
        copy.start()
        copies.append(copy)
    for copy in copies:
        copy.wait()


def finish(attended, back, w_out, mixed):
    tokens, channels = mixed.shape
    step = divisor(tokens, 128, 16)
    return pl.pallas_call(
        finish_kernel,
        in_specs=[vmem()] * 4,
        out_specs=pl.BlockSpec(memory_space=pltpu.HBM),
        out_shape=jax.ShapeDtypeStruct((tokens, channels), jnp.float32),
        scratch_shapes=[
            pltpu.VMEM((tokens // step, step, channels), jnp.float32),
            pltpu.SemaphoreType.DMA((tokens // step,)),
        ],
        compiler_params=pltpu.CompilerParams(vmem_limit_bytes=16 * MIB),
        name="finish",
    )(attended, back, w_out, mixed)


def exchange(low_edge, high_edge, axis):
    count = lax.axis_size(axis)
    even = lax.axis_index(axis) % 2 == 0

    def swap(edge, start):
        pairs = [(i, i + 1) for i in range(start, count - 1, 2)]
        return lax.ppermute(edge, axis, pairs + [(b, a) for a, b in pairs])

    one = swap(jnp.where(even, high_edge, low_edge), 0)
    two = swap(jnp.where(even, low_edge, high_edge), 1)
    return jnp.where(even, two, one), jnp.where(even, one, two)


def grouping(rows, cols, blocks_rows, blocks_cols):
    order = np.arange(rows * cols).reshape(
        blocks_rows, rows // blocks_rows, blocks_cols, cols // blocks_cols
    )
    order = order.transpose(1, 3, 0, 2).reshape(-1)
    matrix = np.zeros((order.size, order.size), np.float32)
    matrix[np.arange(order.size), order] = 1.0
    return matrix


def shards(field, w_expand, depth_kernel, w_project, w_qkv, w_out):
    rows, cols, channels = field.shape
    tokens = rows * cols
    row_devices = lax.axis_size("row")
    col_devices = lax.axis_size("col")
    devices = row_devices * col_devices
    blocks_rows = GRID // row_devices
    blocks_cols = GRID // col_devices
    members = blocks_rows * blocks_cols
    sets_local = tokens // members // devices
    matrix = grouping(rows, cols, blocks_rows, blocks_cols)
    perm = jnp.asarray(matrix, jnp.bfloat16)
    back = jnp.asarray(matrix.T, jnp.bfloat16)

    flat = field.reshape(tokens, channels)
    edges = norm_edges(jnp.concatenate([field[0], field[rows - 1]], axis=0))
    up, down = exchange(edges[:cols], edges[cols:], "row")
    normed, expanded = expand(flat, w_expand)
    up, down, normed = lax.optimization_barrier((up, down, normed))
    tile = normed.reshape(rows, cols, channels)
    spare = jnp.zeros((round_up(rows + 2, 16) - rows - 2, channels), jnp.bfloat16)
    first = jnp.concatenate([up[:1], tile[:, 0], down[:1], spare], axis=0)
    last = jnp.concatenate([up[cols - 1 :], tile[:, cols - 1], down[cols - 1 :], spare], axis=0)
    left, right = exchange(first, last, "col")
    mixed, grouped = mix(
        expanded, flat, up, down, left, right, w_expand, depth_kernel, w_project, perm, rows, cols
    )
    arrived = lax.all_to_all(
        grouped.reshape(devices, sets_local * members, channels), ("row", "col"), 0, 0, tiled=True
    )
    attended = attend(arrived.reshape(devices, sets_local, members, channels), w_qkv)
    returned = lax.all_to_all(
        attended.reshape(devices, sets_local * members, channels), ("row", "col"), 0, 0, tiled=True
    )
    final = finish(returned.reshape(tokens, channels), back, w_out, mixed)
    return final.reshape(rows, cols, channels)


def solution(mesh):
    return jax.shard_map(
        shards,
        mesh=mesh,
        in_specs=(P(("field", "row"), "col", None), P(), P(), P(), P(), P()),
        out_specs=P(("field", "row"), "col", None),
        check_vma=False,
    )
```

```python
import functools
import math

import jax
import jax.numpy as jnp
import numpy as np
from jax import lax
from jax.experimental import pallas as pl
from jax.experimental.pallas import tpu as pltpu
from jax.sharding import PartitionSpec as P

HEADS = 16
GRID = 16
LANES = 128
MIB = 1024 * 1024
NT = (((1,), (1,)), ((), ()))


def layer_norm(inputs):
    average = jnp.mean(inputs, axis=-1, keepdims=True)
    centred = inputs - average
    variance = jnp.mean(centred * centred, axis=-1, keepdims=True)
    return centred * lax.rsqrt(variance + 1e-05)


def gelu_of_half(half):
    scale = math.sqrt(2.0 / math.pi)
    inner = half * (2.0 * scale + (8.0 * scale * 0.044715) * (half * half))
    return half + half * jnp.tanh(inner)


def matmul(a, b):
    return jnp.dot(a, b, preferred_element_type=jnp.float32)


def matmul_nt(a, b):
    return lax.dot_general(a, b, NT, preferred_element_type=jnp.float32)


def divisor(size, most, unit):
    best = size
    for piece in range(unit, most + 1, unit):
        if size % piece == 0:
            best = piece
    return best


def round_up(size, unit):
    return -(-size // unit) * unit


def vmem():
    return pl.BlockSpec(memory_space=pltpu.VMEM)


def half_norm(inputs):
    return (layer_norm(inputs) * 0.5).astype(jnp.bfloat16)


def half_norm_kernel(in_ref, out_ref):
    rows = in_ref.shape[0]
    step = divisor(rows, 128, 16)
    for start in range(0, rows, step):
        out_ref[start : start + step, :] = half_norm(in_ref[start : start + step, :])


def half_norm_of(inputs, work):
    return pl.pallas_call(
        half_norm_kernel,
        in_specs=[vmem()],
        out_specs=vmem(),
        out_shape=jax.ShapeDtypeStruct(inputs.shape, jnp.bfloat16),
        compiler_params=pltpu.CompilerParams(vmem_limit_bytes=8 * MIB),
        cost_estimate=pl.CostEstimate(
            flops=work, bytes_accessed=6 * inputs.size, transcendentals=inputs.shape[0]
        ),
        name="half_norm",
    )(inputs)


def padded_rows(tokens):
    return tokens + 16


def expand_kernel(normed_ref, weight_ref, out_ref):
    tokens = normed_ref.shape[0]
    width = weight_ref.shape[1]
    tile = divisor(width, 512, LANES)
    step = divisor(tokens, 128, 16)
    starts = range(0, tokens, step)

    def body(index, carry):
        lanes = pl.ds(pl.multiple_of(index * tile, tile), tile)
        for start in starts:
            made = gelu_of_half(
                matmul(normed_ref[start : start + step, :], weight_ref[:, lanes])
            )
            for sub in range(tile // LANES):
                row = (index * (tile // LANES) + sub) * padded_rows(tokens) + 8 + start
                out_ref[pl.ds(pl.multiple_of(row, 8), step), :] = made[
                    :, sub * LANES : (sub + 1) * LANES
                ]
        return carry

    lax.fori_loop(0, width // tile, body, 0)


def expand(normed, w_expand):
    tokens, channels = normed.shape
    width = w_expand.shape[1]
    return pl.pallas_call(
        expand_kernel,
        in_specs=[vmem()] * 2,
        out_specs=vmem(),
        out_shape=jax.ShapeDtypeStruct((width // LANES * padded_rows(tokens), LANES), jnp.float32),
        compiler_params=pltpu.CompilerParams(vmem_limit_bytes=16 * MIB),
        cost_estimate=pl.CostEstimate(
            flops=10**10,
            bytes_accessed=tokens * channels * 2 + channels * width * 2 + tokens * width * 4,
            transcendentals=tokens * width,
        ),
        name="expand",
    )(normed, w_expand)


def mix_kernel(
    expanded_ref, field_ref, up_ref, down_ref, left_ref, right_ref, w_expand_ref, depth_ref,
    w_project_ref, perm_ref, mixed_ref, grouped_ref, total_ref, normed_ref,
    even_ref, odd_ref, even_halo_ref, odd_halo_ref, *, rows, cols,
):
    tokens = rows * cols
    width = w_expand_ref.shape[1]
    tile = even_ref.shape[1]
    slot = left_ref.shape[0]
    up_start, down_start, left_start = 8, 16 + cols, 24 + 2 * cols
    right_start = left_start + slot

    edges = jnp.concatenate(
        [up_ref[...], down_ref[...], left_ref[...], right_ref[...]], axis=0
    )

    def expand_halo(index, out_ref):
        lanes = pl.ds(pl.multiple_of(index * tile, tile), tile)
        made = gelu_of_half(matmul(edges, w_expand_ref[:, lanes]))
        for sub in range(tile // LANES):
            part = made[:, sub * LANES : (sub + 1) * LANES]
            out_ref[sub, up_start : up_start + cols] = part[:cols]
            out_ref[sub, down_start : down_start + cols] = part[cols : 2 * cols]
            out_ref[sub, left_start : left_start + 2 * slot] = part[2 * cols :]

    position = lax.broadcasted_iota(jnp.int32, (8, LANES), 0)
    at_first = position == 0
    at_last = position == 7

    def convolve(index, out_ref, halo_ref):
        for sub in range(tile // LANES):
            lanes = pl.ds(pl.multiple_of(index * tile + sub * LANES, LANES), LANES)
            base = (index * (tile // LANES) + sub) * padded_rows(tokens) + 8
            taps = [[0.5 * depth_ref[p, q : q + 1, lanes] for q in range(3)] for p in range(3)]
            sums = {}
            for y in range(-1, rows + 1):
                if y < 0:
                    parts = [halo_ref[sub, up_start + q : up_start + q + cols] for q in (-1, 0, 1)]
                elif y == rows:
                    parts = [
                        halo_ref[sub, down_start + q : down_start + q + cols] for q in (-1, 0, 1)
                    ]
                else:
                    parts = [
                        expanded_ref[pl.ds(base + (y * cols + q), cols), :] for q in (-1, 0, 1)
                    ]
                left = halo_ref[sub, left_start + y + 1 : left_start + y + 2]
                right = halo_ref[sub, right_start + y + 1 : right_start + y + 2]
                parts[0] = jnp.concatenate(
                    [jnp.where(at_first, left, parts[0][:8]), parts[0][8:]], axis=0
                )
                parts[2] = jnp.concatenate(
                    [parts[2][:-8], jnp.where(at_last, right, parts[2][-8:])], axis=0
                )
                for p in range(3):
                    target = y + 1 - p
                    if 0 <= target < rows:
                        for q in range(3):
                            term = taps[p][q] * parts[q]
                            sums[target] = sums[target] + term if target in sums else term
                if y > 0:
                    out_ref[
                        (y - 1) * cols : y * cols, sub * LANES : (sub + 1) * LANES
                    ] = gelu_of_half(sums.pop(y - 1)).astype(jnp.bfloat16)

    def project(index, in_ref):
        piece = pl.ds(pl.multiple_of(index * tile, tile), tile)
        total_ref[...] += matmul(in_ref[...], w_project_ref[piece, :])

    total_ref[...] = field_ref[...]
    expand_halo(0, even_halo_ref)
    expand_halo(1, odd_halo_ref)
    convolve(0, even_ref, even_halo_ref)

    def body(index, carry):
        project(2 * index, even_ref)
        convolve(2 * index + 1, odd_ref, odd_halo_ref)
        expand_halo(2 * index + 2, even_halo_ref)
        project(2 * index + 1, odd_ref)
        convolve(2 * index + 2, even_ref, even_halo_ref)
        expand_halo(2 * index + 3, odd_halo_ref)
        return carry

    pairs = width // tile // 2
    lax.fori_loop(0, pairs - 1, body, 0)
    project(2 * pairs - 2, even_ref)
    convolve(2 * pairs - 1, odd_ref, odd_halo_ref)
    project(2 * pairs - 1, odd_ref)

    step = divisor(tokens, 128, 16)
    for start in range(0, tokens, step):
        piece = slice(start, start + step)
        mixed = total_ref[piece, :]
        mixed_ref[piece, :] = mixed
        normed_ref[piece, :] = layer_norm(mixed).astype(jnp.bfloat16)
    grouped_ref[...] = matmul(perm_ref[...], normed_ref[...]).astype(jnp.bfloat16)


def mix(expanded, field, up, down, left, right, w_expand, depth_kernel, w_project, perm, rows, cols):
    tokens, channels = field.shape
    width = w_expand.shape[1]
    tile = divisor(width // 2, 256, LANES)
    slot = left.shape[0]
    halo = pltpu.VMEM((tile // LANES, 24 + 2 * cols + 2 * slot, LANES), jnp.float32)
    return pl.pallas_call(
        functools.partial(mix_kernel, rows=rows, cols=cols),
        in_specs=[vmem()] * 10,
        out_specs=[vmem()] * 2,
        out_shape=[
            jax.ShapeDtypeStruct((tokens, channels), jnp.float32),
            jax.ShapeDtypeStruct((tokens, channels), jnp.bfloat16),
        ],
        scratch_shapes=[
            pltpu.VMEM((tokens, channels), jnp.float32),
            pltpu.VMEM((tokens, channels), jnp.bfloat16),
            pltpu.VMEM((tokens, tile), jnp.bfloat16),
            pltpu.VMEM((tokens, tile), jnp.bfloat16),
            halo,
            halo,
        ],
        compiler_params=pltpu.CompilerParams(vmem_limit_bytes=16 * MIB),
        cost_estimate=pl.CostEstimate(
            flops=2 * tokens * channels * width,
            bytes_accessed=tokens * channels * 10 + 4 * channels * width + tokens * width * 4,
            transcendentals=tokens * width,
        ),
        name="mix",
    )(expanded, field, up, down, left, right, w_expand, depth_kernel, w_project, perm)


def identity(size):
    row = lax.broadcasted_iota(jnp.int32, (size, size), 0)
    column = lax.broadcasted_iota(jnp.int32, (size, size), 1)
    return jnp.where(row == column, 1.0, 0.0).astype(jnp.bfloat16)


def attend_kernel(
    tokens_ref, weight_ref, out_ref, query_ref, key_ref, value_ref, turned_ref, even_ref, odd_ref
):
    devices, sets, members, channels = tokens_ref.shape
    count = devices * members
    head_width = channels // HEADS
    group_heads = LANES // head_width
    groups = channels // LANES
    factor = math.log2(math.e) / math.sqrt(head_width)
    lane = lax.broadcasted_iota(jnp.int32, (1, LANES), 1)
    masks = [
        jnp.where((lane >= j * head_width) & (lane < (j + 1) * head_width), 1.0, 0.0).astype(
            jnp.bfloat16
        )
        for j in range(group_heads)
    ]
    turn_values = identity(channels)
    for s in range(sets):
        block = tokens_ref[:, s].reshape(count, channels)
        qkv = matmul(block, weight_ref[...]).astype(jnp.bfloat16)
        values = matmul_nt(turn_values, qkv[:, 2 * channels :]).astype(jnp.bfloat16)
        for group in range(groups):
            lanes = slice(group * LANES, (group + 1) * LANES)
            query_ref[s * groups + group] = qkv[:, lanes]
            key_ref[s * groups + group] = qkv[:, channels + group * LANES : channels + (group + 1) * LANES]
            for j in range(group_heads):
                head = (group * group_heads + j) * head_width
                value_ref[s * groups + group, j, :head_width] = values[head : head + head_width]
                value_ref[s * groups + group, j, head_width:] = jnp.ones((16, count), jnp.bfloat16)

    def scores(index, out):
        keys = key_ref[index]
        stacked = jnp.concatenate([keys * mask for mask in masks], axis=0)
        out[...] = matmul_nt(stacked, query_ref[index])

    def weigh(index, scores_ref):
        for j in range(group_heads):
            part = scores_ref[j * count : (j + 1) * count]
            highest = jnp.max(part, axis=0, keepdims=True)
            raised = jnp.exp2((part - highest) * factor).astype(jnp.bfloat16)
            product = matmul(value_ref[index, j], raised)
            scale = 1.0 / product[head_width : head_width + 1]
            turned_ref[index, j * head_width : (j + 1) * head_width] = (
                product[:head_width] * scale
            ).astype(jnp.bfloat16)

    total = sets * groups
    scores(0, even_ref)

    def body(pair, carry):
        scores(2 * pair + 1, odd_ref)
        weigh(2 * pair, even_ref)
        scores(jnp.minimum(2 * pair + 2, total - 1), even_ref)
        weigh(2 * pair + 1, odd_ref)
        return carry

    lax.fori_loop(0, total // 2, body, 0)
    turn_tokens = identity(count)
    for s in range(sets):
        turned = turned_ref[s * groups : (s + 1) * groups].reshape(channels, count)
        attended = matmul_nt(turn_tokens, turned).astype(jnp.bfloat16)
        out_ref[:, s] = attended.reshape(devices, members, channels)


def attend(blocks, w_qkv):
    devices, sets, members, channels = blocks.shape
    count = devices * members
    apart = members % 16 != 0
    if apart:
        blocks = blocks.transpose(1, 0, 2, 3).reshape(1, sets, count, channels)
    head_width = channels // HEADS
    group_heads = LANES // head_width
    total = sets * channels // LANES
    result = pl.pallas_call(
        attend_kernel,
        in_specs=[vmem()] * 2,
        out_specs=vmem(),
        out_shape=jax.ShapeDtypeStruct(blocks.shape, jnp.bfloat16),
        scratch_shapes=[
            pltpu.VMEM((total, count, LANES), jnp.bfloat16),
            pltpu.VMEM((total, count, LANES), jnp.bfloat16),
            pltpu.VMEM((total, group_heads, head_width + 16, count), jnp.bfloat16),
            pltpu.VMEM((total, LANES, count), jnp.bfloat16),
            pltpu.VMEM((group_heads * count, count), jnp.float32),
            pltpu.VMEM((group_heads * count, count), jnp.float32),
        ],
        compiler_params=pltpu.CompilerParams(vmem_limit_bytes=24 * MIB),
        cost_estimate=pl.CostEstimate(
            flops=sets * (2 * count * channels * channels * 3 + 4 * count * count * channels),
            bytes_accessed=4 * sets * count * channels + 6 * channels * channels,
            transcendentals=sets * HEADS * count * count,
        ),
        name="attend",
    )(blocks, w_qkv)
    if apart:
        result = result.reshape(sets, devices, members, channels).transpose(1, 0, 2, 3)
    return result


def finish_kernel(attended_ref, back_ref, weight_ref, mixed_ref, out_ref, made_ref, sent):
    tokens = mixed_ref.shape[0]
    step = made_ref.shape[1]
    copies = []
    for index, start in enumerate(range(0, tokens, step)):
        rows = slice(start, start + step)
        restored = matmul(back_ref[rows, :], attended_ref[...]).astype(jnp.bfloat16)
        made_ref[index] = mixed_ref[rows, :] + matmul(restored, weight_ref[...])
        copy = pltpu.make_async_copy(
            made_ref.at[index], out_ref.at[pl.ds(start, step)], sent.at[index]
        )
        copy.start()
        copies.append(copy)
    for copy in copies:
        copy.wait()


def finish(attended, back, w_out, mixed):
    tokens, channels = mixed.shape
    step = divisor(tokens, 128, 16)
    return pl.pallas_call(
        finish_kernel,
        in_specs=[vmem()] * 4,
        out_specs=pl.BlockSpec(memory_space=pltpu.HBM),
        out_shape=jax.ShapeDtypeStruct((tokens, channels), jnp.float32),
        scratch_shapes=[
            pltpu.VMEM((tokens // step, step, channels), jnp.float32),
            pltpu.SemaphoreType.DMA((tokens // step,)),
        ],
        compiler_params=pltpu.CompilerParams(vmem_limit_bytes=16 * MIB),
        name="finish",
    )(attended, back, w_out, mixed)


def exchange(low_edge, high_edge, axis):
    count = lax.axis_size(axis)
    even = lax.axis_index(axis) % 2 == 0

    def swap(edge, start):
        pairs = [(i, i + 1) for i in range(start, count - 1, 2)]
        return lax.ppermute(edge, axis, pairs + [(b, a) for a, b in pairs])

    one = swap(jnp.where(even, high_edge, low_edge), 0)
    two = swap(jnp.where(even, low_edge, high_edge), 1)
    return jnp.where(even, two, one), jnp.where(even, one, two)


def grouping(rows, cols, blocks_rows, blocks_cols):
    order = np.arange(rows * cols).reshape(
        blocks_rows, rows // blocks_rows, blocks_cols, cols // blocks_cols
    )
    order = order.transpose(1, 3, 0, 2).reshape(-1)
    matrix = np.zeros((order.size, order.size), np.float32)
    matrix[np.arange(order.size), order] = 1.0
    return matrix


def shards(field, w_expand, depth_kernel, w_project, w_qkv, w_out):
    rows, cols, channels = field.shape
    tokens = rows * cols
    row_devices = lax.axis_size("row")
    col_devices = lax.axis_size("col")
    devices = row_devices * col_devices
    blocks_rows = GRID // row_devices
    blocks_cols = GRID // col_devices
    members = blocks_rows * blocks_cols
    sets_local = tokens // members // devices
    matrix = grouping(rows, cols, blocks_rows, blocks_cols)
    perm = jnp.asarray(matrix, jnp.bfloat16)
    back = jnp.asarray(matrix.T, jnp.bfloat16)

    flat = field.reshape(tokens, channels)
    edges = half_norm_of(jnp.concatenate([field[0], field[rows - 1]], axis=0), 10**10)
    up, down = exchange(edges[:cols], edges[cols:], "row")
    normed = half_norm_of(flat, 10**9)
    tile = normed.reshape(rows, cols, channels)
    spare = jnp.zeros((round_up(rows + 2, 16) - rows - 2, channels), jnp.bfloat16)
    first = jnp.concatenate([up[:1], tile[:, 0], down[:1], spare], axis=0)
    last = jnp.concatenate([up[cols - 1 :], tile[:, cols - 1], down[cols - 1 :], spare], axis=0)
    normed, first, last = lax.optimization_barrier((normed, first, last))
    expanded = expand(normed, w_expand)
    left, right = exchange(first, last, "col")
    mixed, grouped = mix(
        expanded, flat, up, down, left, right, w_expand, depth_kernel, w_project, perm, rows, cols
    )
    arrived = lax.all_to_all(
        grouped.reshape(devices, sets_local * members, channels), ("row", "col"), 0, 0, tiled=True
    )
    attended = attend(arrived.reshape(devices, sets_local, members, channels), w_qkv)
    returned = lax.all_to_all(
        attended.reshape(devices, sets_local * members, channels), ("row", "col"), 0, 0, tiled=True
    )
    final = finish(returned.reshape(tokens, channels), back, w_out, mixed)
    return final.reshape(rows, cols, channels)


def solution(mesh):
    return jax.shard_map(
        shards,
        mesh=mesh,
        in_specs=(P(("field", "row"), "col", None), P(), P(), P(), P(), P()),
        out_specs=P(("field", "row"), "col", None),
        check_vma=False,
    )
```

```python
import functools
import math

import jax
import jax.numpy as jnp
import numpy as np
from jax import lax
from jax.experimental import pallas as pl
from jax.experimental.pallas import tpu as pltpu
from jax.sharding import PartitionSpec as P

HEADS = 16
GRID = 16
LANES = 128
MIB = 1024 * 1024
NT = (((1,), (1,)), ((), ()))


def layer_norm(inputs):
    average = jnp.mean(inputs, axis=-1, keepdims=True)
    centred = inputs - average
    variance = jnp.mean(centred * centred, axis=-1, keepdims=True)
    return centred * lax.rsqrt(variance + 1e-05)


def gelu_of_half(half):
    scale = math.sqrt(2.0 / math.pi)
    inner = half * (2.0 * scale + (8.0 * scale * 0.044715) * (half * half))
    return half + half * jnp.tanh(inner)


def matmul(a, b):
    return jnp.dot(a, b, preferred_element_type=jnp.float32)


def matmul_nt(a, b):
    return lax.dot_general(a, b, NT, preferred_element_type=jnp.float32)


def divisor(size, most, unit):
    best = size
    for piece in range(unit, most + 1, unit):
        if size % piece == 0:
            best = piece
    return best


def round_up(size, unit):
    return -(-size // unit) * unit


def vmem():
    return pl.BlockSpec(memory_space=pltpu.VMEM)


def half_norm(inputs):
    return (layer_norm(inputs) * 0.5).astype(jnp.bfloat16)


def half_norm_kernel(in_ref, out_ref):
    rows = in_ref.shape[0]
    step = divisor(rows, 128, 16)
    for start in range(0, rows, step):
        out_ref[start : start + step, :] = half_norm(in_ref[start : start + step, :])


def half_norm_of(inputs, work):
    return pl.pallas_call(
        half_norm_kernel,
        in_specs=[vmem()],
        out_specs=vmem(),
        out_shape=jax.ShapeDtypeStruct(inputs.shape, jnp.bfloat16),
        compiler_params=pltpu.CompilerParams(vmem_limit_bytes=8 * MIB),
        cost_estimate=pl.CostEstimate(
            flops=work, bytes_accessed=6 * inputs.size, transcendentals=inputs.shape[0]
        ),
        name="half_norm",
    )(inputs)


def padded_rows(tokens):
    return tokens + 16


def expand_kernel(normed_ref, weight_ref, out_ref):
    tokens = normed_ref.shape[0]
    width = weight_ref.shape[1]
    tile = divisor(width, 512, LANES)
    step = divisor(tokens, 128, 16)
    starts = range(0, tokens, step)

    def body(index, carry):
        lanes = pl.ds(pl.multiple_of(index * tile, tile), tile)
        for start in starts:
            made = gelu_of_half(
                matmul(normed_ref[start : start + step, :], weight_ref[:, lanes])
            )
            for sub in range(tile // LANES):
                row = (index * (tile // LANES) + sub) * padded_rows(tokens) + 8 + start
                out_ref[pl.ds(pl.multiple_of(row, 8), step), :] = made[
                    :, sub * LANES : (sub + 1) * LANES
                ]
        return carry

    lax.fori_loop(0, width // tile, body, 0)


def expand(normed, w_expand):
    tokens, channels = normed.shape
    width = w_expand.shape[1]
    return pl.pallas_call(
        expand_kernel,
        in_specs=[vmem()] * 2,
        out_specs=vmem(),
        out_shape=jax.ShapeDtypeStruct((width // LANES * padded_rows(tokens), LANES), jnp.float32),
        compiler_params=pltpu.CompilerParams(vmem_limit_bytes=16 * MIB),
        cost_estimate=pl.CostEstimate(
            flops=10**10,
            bytes_accessed=tokens * channels * 2 + channels * width * 2 + tokens * width * 4,
            transcendentals=tokens * width,
        ),
        name="expand",
    )(normed, w_expand)


def mix_kernel(
    own_ref, expanded_ref, field_ref, up_ref, down_ref, left_ref, right_ref, w_expand_ref, depth_ref,
    w_project_ref, perm_ref, mixed_ref, *refs, rows, cols, masks,
):
    slab_refs = refs[: len(masks)]
    total_ref, normed_ref, grouped_ref, even_ref, odd_ref, even_halo_ref, odd_halo_ref = refs[
        len(masks) :
    ]
    tokens = rows * cols
    width = w_expand_ref.shape[1]
    tile = even_ref.shape[1]
    slot = left_ref.shape[0]
    up_start, down_start, left_start = 8, 16 + cols, 24 + 2 * cols
    right_start = left_start + slot

    edges = jnp.concatenate(
        [up_ref[...], down_ref[...], left_ref[...], right_ref[...]], axis=0
    )

    def expand_halo(index, out_ref):
        lanes = pl.ds(pl.multiple_of(index * tile, tile), tile)
        made = gelu_of_half(matmul(edges, w_expand_ref[:, lanes]))
        for sub in range(tile // LANES):
            part = made[:, sub * LANES : (sub + 1) * LANES]
            out_ref[sub, up_start : up_start + cols] = part[:cols]
            out_ref[sub, down_start : down_start + cols] = part[cols : 2 * cols]
            out_ref[sub, left_start : left_start + 2 * slot] = part[2 * cols :]

    position = lax.broadcasted_iota(jnp.int32, (8, LANES), 0)
    at_first = position == 0
    at_last = position == 7

    def convolve(index, out_ref, halo_ref):
        for sub in range(tile // LANES):
            lanes = pl.ds(pl.multiple_of(index * tile + sub * LANES, LANES), LANES)
            base = (index * (tile // LANES) + sub) * padded_rows(tokens) + 8
            taps = [[0.5 * depth_ref[p, q : q + 1, lanes] for q in range(3)] for p in range(3)]
            sums = {}
            for y in range(-1, rows + 1):
                if y < 0:
                    parts = [halo_ref[sub, up_start + q : up_start + q + cols] for q in (-1, 0, 1)]
                elif y == rows:
                    parts = [
                        halo_ref[sub, down_start + q : down_start + q + cols] for q in (-1, 0, 1)
                    ]
                else:
                    parts = [
                        expanded_ref[pl.ds(base + (y * cols + q), cols), :] for q in (-1, 0, 1)
                    ]
                left = halo_ref[sub, left_start + y + 1 : left_start + y + 2]
                right = halo_ref[sub, right_start + y + 1 : right_start + y + 2]
                parts[0] = jnp.concatenate(
                    [jnp.where(at_first, left, parts[0][:8]), parts[0][8:]], axis=0
                )
                parts[2] = jnp.concatenate(
                    [parts[2][:-8], jnp.where(at_last, right, parts[2][-8:])], axis=0
                )
                for p in range(3):
                    target = y + 1 - p
                    if 0 <= target < rows:
                        for q in range(3):
                            term = taps[p][q] * parts[q]
                            sums[target] = sums[target] + term if target in sums else term
                if y > 0:
                    out_ref[
                        (y - 1) * cols : y * cols, sub * LANES : (sub + 1) * LANES
                    ] = gelu_of_half(sums.pop(y - 1)).astype(jnp.bfloat16)

    def project(index, in_ref):
        piece = pl.ds(pl.multiple_of(index * tile, tile), tile)
        total_ref[...] += matmul(in_ref[...], w_project_ref[piece, :])

    total_ref[...] = field_ref[...]
    expand_halo(0, even_halo_ref)
    expand_halo(1, odd_halo_ref)
    convolve(0, even_ref, even_halo_ref)

    def body(index, carry):
        project(2 * index, even_ref)
        convolve(2 * index + 1, odd_ref, odd_halo_ref)
        expand_halo(2 * index + 2, even_halo_ref)
        project(2 * index + 1, odd_ref)
        convolve(2 * index + 2, even_ref, even_halo_ref)
        expand_halo(2 * index + 3, odd_halo_ref)
        return carry

    pairs = width // tile // 2
    lax.fori_loop(0, pairs - 1, body, 0)
    project(2 * pairs - 2, even_ref)
    convolve(2 * pairs - 1, odd_ref, odd_halo_ref)
    project(2 * pairs - 1, odd_ref)

    step = divisor(tokens, 128, 16)
    for start in range(0, tokens, step):
        piece = slice(start, start + step)
        mixed = total_ref[piece, :]
        mixed_ref[piece, :] = mixed
        normed_ref[piece, :] = layer_norm(mixed).astype(jnp.bfloat16)
    grouped_ref[...] = matmul(perm_ref[...], normed_ref[...]).astype(jnp.bfloat16)
    size = slab_refs[0].shape[1]
    for mask, slab_ref in zip(masks, slab_refs):
        for side in range(slab_ref.shape[0]):
            start = pl.multiple_of((own_ref[0] ^ (mask | side)) * size, 16)
            slab_ref[side] = grouped_ref[pl.ds(start, size), :]


def mix(
    own, masks, slab, expanded, field, up, down, left, right, w_expand, depth_kernel, w_project, perm,
    rows, cols,
):
    tokens, channels = field.shape
    width = w_expand.shape[1]
    tile = divisor(width // 2, 256, LANES)
    slot = left.shape[0]
    halo = pltpu.VMEM((tile // LANES, 24 + 2 * cols + 2 * slot, LANES), jnp.float32)
    return pl.pallas_call(
        functools.partial(mix_kernel, rows=rows, cols=cols, masks=masks),
        in_specs=[pl.BlockSpec(memory_space=pltpu.SMEM)] + [vmem()] * 10,
        out_specs=[vmem()] * (1 + len(masks)),
        out_shape=[jax.ShapeDtypeStruct((tokens, channels), jnp.float32)]
        + [jax.ShapeDtypeStruct(slab, jnp.bfloat16)] * len(masks),
        scratch_shapes=[
            pltpu.VMEM((tokens, channels), jnp.float32),
            pltpu.VMEM((tokens, channels), jnp.bfloat16),
            pltpu.VMEM((tokens, channels), jnp.bfloat16),
            pltpu.VMEM((tokens, tile), jnp.bfloat16),
            pltpu.VMEM((tokens, tile), jnp.bfloat16),
            halo,
            halo,
        ],
        compiler_params=pltpu.CompilerParams(vmem_limit_bytes=16 * MIB),
        cost_estimate=pl.CostEstimate(
            flops=2 * tokens * channels * width,
            bytes_accessed=tokens * channels * 10 + 4 * channels * width + tokens * width * 4,
            transcendentals=tokens * width,
        ),
        name="mix",
    )(own, expanded, field, up, down, left, right, w_expand, depth_kernel, w_project, perm)


def identity(size):
    row = lax.broadcasted_iota(jnp.int32, (size, size), 0)
    column = lax.broadcasted_iota(jnp.int32, (size, size), 1)
    return jnp.where(row == column, 1.0, 0.0).astype(jnp.bfloat16)


def attend_kernel(*refs, slabs, sets):
    mine, others, weight_ref = refs[:slabs], refs[slabs : 2 * slabs], refs[2 * slabs]
    out_refs = refs[2 * slabs + 1 : 3 * slabs + 1]
    query_ref, key_ref, value_ref, turned_ref, even_ref, odd_ref = refs[3 * slabs + 1 :]
    sides, size, channels = mine[0].shape
    members = size // sets
    count = slabs * sides * members
    head_width = channels // HEADS
    group_heads = LANES // head_width
    groups = channels // LANES
    factor = math.log2(math.e) / math.sqrt(head_width)
    lane = lax.broadcasted_iota(jnp.int32, (1, LANES), 1)
    masks = [
        jnp.where((lane >= j * head_width) & (lane < (j + 1) * head_width), 1.0, 0.0).astype(
            jnp.bfloat16
        )
        for j in range(group_heads)
    ]
    turn_values = identity(channels)
    for s in range(sets):
        piece = slice(s * members, (s + 1) * members)
        block = jnp.concatenate(
            [
                (mine, others)[side][index][side, piece]
                for index in range(slabs)
                for side in range(sides)
            ],
            axis=0,
        )
        qkv = matmul(block, weight_ref[...]).astype(jnp.bfloat16)
        values = matmul_nt(turn_values, qkv[:, 2 * channels :]).astype(jnp.bfloat16)
        for group in range(groups):
            lanes = slice(group * LANES, (group + 1) * LANES)
            query_ref[s * groups + group] = qkv[:, lanes]
            key_ref[s * groups + group] = qkv[:, channels + group * LANES : channels + (group + 1) * LANES]
            for j in range(group_heads):
                head = (group * group_heads + j) * head_width
                value_ref[s * groups + group, j, :head_width] = values[head : head + head_width]
                value_ref[s * groups + group, j, head_width:] = jnp.ones((16, count), jnp.bfloat16)

    def scores(index, out):
        keys = key_ref[index]
        stacked = jnp.concatenate([keys * mask for mask in masks], axis=0)
        out[...] = matmul_nt(stacked, query_ref[index])

    def weigh(index, scores_ref):
        for j in range(group_heads):
            part = scores_ref[j * count : (j + 1) * count]
            highest = jnp.max(part, axis=0, keepdims=True)
            raised = jnp.exp2((part - highest) * factor).astype(jnp.bfloat16)
            product = matmul(value_ref[index, j], raised)
            scale = 1.0 / product[head_width : head_width + 1]
            turned_ref[index, j * head_width : (j + 1) * head_width] = (
                product[:head_width] * scale
            ).astype(jnp.bfloat16)

    total = sets * groups
    scores(0, even_ref)

    def body(pair, carry):
        scores(2 * pair + 1, odd_ref)
        weigh(2 * pair, even_ref)
        scores(jnp.minimum(2 * pair + 2, total - 1), even_ref)
        weigh(2 * pair + 1, odd_ref)
        return carry

    lax.fori_loop(0, total // 2, body, 0)
    turn_tokens = identity(count)
    for s in range(sets):
        turned = turned_ref[s * groups : (s + 1) * groups].reshape(channels, count)
        attended = matmul_nt(turn_tokens, turned).astype(jnp.bfloat16)
        for index in range(slabs):
            for side in range(sides):
                start = (index * sides + side) * members
                out_refs[index][side, s * members : (s + 1) * members] = attended[
                    start : start + members
                ]


def attend(mine, others, w_qkv, sets):
    slabs = len(mine)
    sides, size, channels = mine[0].shape
    count = slabs * sides * size // sets
    head_width = channels // HEADS
    group_heads = LANES // head_width
    total = sets * channels // LANES
    return pl.pallas_call(
        functools.partial(attend_kernel, slabs=slabs, sets=sets),
        in_specs=[vmem()] * (2 * slabs + 1),
        out_specs=[vmem()] * slabs,
        out_shape=[jax.ShapeDtypeStruct(mine[0].shape, jnp.bfloat16)] * slabs,
        scratch_shapes=[
            pltpu.VMEM((total, count, LANES), jnp.bfloat16),
            pltpu.VMEM((total, count, LANES), jnp.bfloat16),
            pltpu.VMEM((total, group_heads, head_width + 16, count), jnp.bfloat16),
            pltpu.VMEM((total, LANES, count), jnp.bfloat16),
            pltpu.VMEM((group_heads * count, count), jnp.float32),
            pltpu.VMEM((group_heads * count, count), jnp.float32),
        ],
        compiler_params=pltpu.CompilerParams(vmem_limit_bytes=24 * MIB),
        cost_estimate=pl.CostEstimate(
            flops=sets * (2 * count * channels * channels * 3 + 4 * count * count * channels),
            bytes_accessed=4 * sets * count * channels + 6 * channels * channels,
            transcendentals=sets * HEADS * count * count,
        ),
        name="attend",
    )(*mine, *others, w_qkv)


def finish_kernel(own_ref, *refs, masks):
    slabs = len(masks)
    mine, others = refs[:slabs], refs[slabs : 2 * slabs]
    back_ref, weight_ref, mixed_ref, out_ref, attended_ref, made_ref, sent = refs[2 * slabs :]
    tokens = mixed_ref.shape[0]
    sides, size, _ = mine[0].shape
    for index, mask in enumerate(masks):
        for side in range(sides):
            start = pl.multiple_of((own_ref[0] ^ (mask | side)) * size, 16)
            attended_ref[pl.ds(start, size), :] = (mine, others)[side][index][side]
    step = made_ref.shape[1]
    copies = []
    for index, start in enumerate(range(0, tokens, step)):
        rows = slice(start, start + step)
        restored = matmul(back_ref[rows, :], attended_ref[...]).astype(jnp.bfloat16)
        made_ref[index] = mixed_ref[rows, :] + matmul(restored, weight_ref[...])
        copy = pltpu.make_async_copy(
            made_ref.at[index], out_ref.at[pl.ds(start, step)], sent.at[index]
        )
        copy.start()
        copies.append(copy)
    for copy in copies:
        copy.wait()


def finish(own, masks, mine, others, back, w_out, mixed):
    tokens, channels = mixed.shape
    step = divisor(tokens, 128, 16)
    return pl.pallas_call(
        functools.partial(finish_kernel, masks=masks),
        in_specs=[pl.BlockSpec(memory_space=pltpu.SMEM)] + [vmem()] * (2 * len(masks) + 3),
        out_specs=pl.BlockSpec(memory_space=pltpu.HBM),
        out_shape=jax.ShapeDtypeStruct((tokens, channels), jnp.float32),
        scratch_shapes=[
            pltpu.VMEM((tokens, channels), jnp.bfloat16),
            pltpu.VMEM((tokens // step, step, channels), jnp.float32),
            pltpu.SemaphoreType.DMA((tokens // step,)),
        ],
        compiler_params=pltpu.CompilerParams(vmem_limit_bytes=16 * MIB),
        name="finish",
    )(own, *mine, *others, back, w_out, mixed)


def exchange(low_edge, high_edge, axis):
    count = lax.axis_size(axis)
    even = lax.axis_index(axis) % 2 == 0

    def swap(edge, start):
        pairs = [(i, i + 1) for i in range(start, count - 1, 2)]
        return lax.ppermute(edge, axis, pairs + [(b, a) for a, b in pairs])

    one = swap(jnp.where(even, high_edge, low_edge), 0)
    two = swap(jnp.where(even, low_edge, high_edge), 1)
    return jnp.where(even, two, one), jnp.where(even, one, two)


def exchange_plan(row_devices, col_devices):
    masks = [
        row * col_devices + col for row in range(row_devices) for col in range(0, col_devices, 2)
    ]
    return masks, 2


def trade(masks, slabs):
    axes = ("row", "col")
    devices = lax.axis_size("row") * lax.axis_size("col")

    def swap(slab, mask):
        return lax.ppermute(slab, axes, [(i, i ^ mask) for i in range(devices)])

    mine = dict(zip(masks, slabs))
    for mask in sorted(masks[1:], reverse=True):
        mine[mask] = swap(mine[mask], mask)
    mine = [mine[mask] for mask in masks]
    return mine, [swap(slab, 1) for slab in mine]


def trade_all(slabs, sets, members, outward):
    axes = ("row", "col")
    channels = slabs[0].shape[-1]
    block = slabs[0].reshape(-1, channels)
    devices = block.shape[0] // (sets * members)
    if not outward:
        block = block.reshape(sets, devices, members, channels).transpose(1, 0, 2, 3)
    block = block.reshape(devices, sets * members, channels)
    block = lax.all_to_all(block, axes, 0, 0, tiled=True)
    if outward:
        block = block.reshape(devices, sets, members, channels).transpose(1, 0, 2, 3)
    block = [block.reshape(1, -1, channels)]
    return block, block


def grouping(rows, cols, blocks_rows, blocks_cols):
    order = np.arange(rows * cols).reshape(
        blocks_rows, rows // blocks_rows, blocks_cols, cols // blocks_cols
    )
    order = order.transpose(1, 3, 0, 2).reshape(-1)
    matrix = np.zeros((order.size, order.size), np.float32)
    matrix[np.arange(order.size), order] = 1.0
    return matrix


def shards(field, w_expand, depth_kernel, w_project, w_qkv, w_out):
    rows, cols, channels = field.shape
    tokens = rows * cols
    row_devices = lax.axis_size("row")
    col_devices = lax.axis_size("col")
    devices = row_devices * col_devices
    blocks_rows = GRID // row_devices
    blocks_cols = GRID // col_devices
    members = blocks_rows * blocks_cols
    sets_local = tokens // members // devices
    matrix = grouping(rows, cols, blocks_rows, blocks_cols)
    perm = jnp.asarray(matrix, jnp.bfloat16)
    back = jnp.asarray(matrix.T, jnp.bfloat16)

    flat = field.reshape(tokens, channels)
    edges = half_norm_of(jnp.concatenate([field[0], field[rows - 1]], axis=0), 10**10)
    up, down = exchange(edges[:cols], edges[cols:], "row")
    normed = half_norm_of(flat, 10**9)
    tile = normed.reshape(rows, cols, channels)
    spare = jnp.zeros((round_up(rows + 2, 16) - rows - 2, channels), jnp.bfloat16)
    first = jnp.concatenate([up[:1], tile[:, 0], down[:1], spare], axis=0)
    last = jnp.concatenate([up[cols - 1 :], tile[:, cols - 1], down[cols - 1 :], spare], axis=0)
    normed, first, last = lax.optimization_barrier((normed, first, last))
    expanded = expand(normed, w_expand)
    left, right = exchange(first, last, "col")
    pairwise = devices <= 16 and devices & (devices - 1) == 0 and col_devices % 2 == 0
    if pairwise:
        masks, sides = exchange_plan(row_devices, col_devices)
        own = lax.axis_index(("row", "col")).reshape(1)
    else:
        masks, sides = [0], 1
        own = jnp.zeros(1, jnp.int32)
    slab = (sides, tokens // (sides * len(masks)), channels)
    mixed, *slabs = mix(
        own, masks, slab, expanded, flat, up, down, left, right, w_expand, depth_kernel, w_project,
        perm, rows, cols,
    )

    def route(slabs, outward):
        if pairwise:
            return trade(masks, slabs)
        return trade_all(slabs, sets_local, members, outward)

    mine, others = route(slabs, True)
    slabs = attend(mine, others, w_qkv, sets_local)
    mine, others = route(slabs, False)
    final = finish(own, masks, mine, others, back, w_out, mixed)
    return final.reshape(rows, cols, channels)


def solution(mesh):
    return jax.shard_map(
        shards,
        mesh=mesh,
        in_specs=(P(("field", "row"), "col", None), P(), P(), P(), P(), P()),
        out_specs=P(("field", "row"), "col", None),
        check_vma=False,
    )
```

```python
import functools
import math

import jax
import jax.numpy as jnp
import numpy as np
from jax import lax
from jax.experimental import pallas as pl
from jax.experimental.pallas import tpu as pltpu
from jax.sharding import PartitionSpec as P

HEADS = 16
GRID = 16
LANES = 128
MIB = 1024 * 1024
NT = (((1,), (1,)), ((), ()))


def layer_norm(inputs):
    average = jnp.mean(inputs, axis=-1, keepdims=True)
    centred = inputs - average
    variance = jnp.mean(centred * centred, axis=-1, keepdims=True)
    return centred * lax.rsqrt(variance + 1e-05)


def gelu_of_half(half):
    scale = math.sqrt(2.0 / math.pi)
    inner = half * (2.0 * scale + (8.0 * scale * 0.044715) * (half * half))
    return half + half * jnp.tanh(inner)


def matmul(a, b):
    return jnp.dot(a, b, preferred_element_type=jnp.float32)


def matmul_nt(a, b):
    return lax.dot_general(a, b, NT, preferred_element_type=jnp.float32)


def divisor(size, most, unit):
    best = size
    for piece in range(unit, most + 1, unit):
        if size % piece == 0:
            best = piece
    return best


def round_up(size, unit):
    return -(-size // unit) * unit


def vmem():
    return pl.BlockSpec(memory_space=pltpu.VMEM)


def half_norm(inputs):
    return (layer_norm(inputs) * 0.5).astype(jnp.bfloat16)


def half_norm_kernel(in_ref, out_ref):
    rows = in_ref.shape[0]
    step = divisor(rows, 128, 16)
    for start in range(0, rows, step):
        out_ref[start : start + step, :] = half_norm(in_ref[start : start + step, :])


def half_norm_of(inputs, work):
    return pl.pallas_call(
        half_norm_kernel,
        in_specs=[vmem()],
        out_specs=vmem(),
        out_shape=jax.ShapeDtypeStruct(inputs.shape, jnp.bfloat16),
        compiler_params=pltpu.CompilerParams(vmem_limit_bytes=8 * MIB),
        cost_estimate=pl.CostEstimate(
            flops=work, bytes_accessed=6 * inputs.size, transcendentals=inputs.shape[0]
        ),
        name="half_norm",
    )(inputs)


def padded_rows(tokens):
    return tokens + 16


def expand_kernel(normed_ref, weight_ref, out_ref):
    tokens = normed_ref.shape[0]
    width = weight_ref.shape[1]
    tile = divisor(width, 512, LANES)
    step = divisor(tokens, 128, 16)
    starts = range(0, tokens, step)

    def body(index, carry):
        lanes = pl.ds(pl.multiple_of(index * tile, tile), tile)
        for start in starts:
            made = gelu_of_half(
                matmul(normed_ref[start : start + step, :], weight_ref[:, lanes])
            )
            for sub in range(tile // LANES):
                row = (index * (tile // LANES) + sub) * padded_rows(tokens) + 8 + start
                out_ref[pl.ds(pl.multiple_of(row, 8), step), :] = made[
                    :, sub * LANES : (sub + 1) * LANES
                ]
        return carry

    lax.fori_loop(0, width // tile, body, 0)


def expand(normed, w_expand):
    tokens, channels = normed.shape
    width = w_expand.shape[1]
    return pl.pallas_call(
        expand_kernel,
        in_specs=[vmem()] * 2,
        out_specs=vmem(),
        out_shape=jax.ShapeDtypeStruct((width // LANES * padded_rows(tokens), LANES), jnp.float32),
        compiler_params=pltpu.CompilerParams(vmem_limit_bytes=16 * MIB),
        cost_estimate=pl.CostEstimate(
            flops=10**10,
            bytes_accessed=tokens * channels * 2 + channels * width * 2 + tokens * width * 4,
            transcendentals=tokens * width,
        ),
        name="expand",
    )(normed, w_expand)


def mix_kernel(
    own_ref, expanded_ref, field_ref, up_ref, down_ref, left_ref, right_ref, w_expand_ref, depth_ref,
    w_project_ref, perm_ref, mixed_ref, *refs, rows, cols, masks,
):
    slab_refs = refs[: len(masks)]
    total_ref, normed_ref, grouped_ref, even_ref, odd_ref, even_halo_ref, odd_halo_ref = refs[
        len(masks) :
    ]
    tokens = rows * cols
    width = w_expand_ref.shape[1]
    tile = even_ref.shape[1]
    slot = left_ref.shape[0]
    up_start, down_start, left_start = 8, 16 + cols, 24 + 2 * cols
    right_start = left_start + slot

    edges = jnp.concatenate(
        [up_ref[...], down_ref[...], left_ref[...], right_ref[...]], axis=0
    )

    def expand_halo(index, out_ref):
        lanes = pl.ds(pl.multiple_of(index * tile, tile), tile)
        made = gelu_of_half(matmul(edges, w_expand_ref[:, lanes]))
        for sub in range(tile // LANES):
            part = made[:, sub * LANES : (sub + 1) * LANES]
            out_ref[sub, up_start : up_start + cols] = part[:cols]
            out_ref[sub, down_start : down_start + cols] = part[cols : 2 * cols]
            out_ref[sub, left_start : left_start + 2 * slot] = part[2 * cols :]

    position = lax.broadcasted_iota(jnp.int32, (8, LANES), 0)
    at_first = position == 0
    at_last = position == 7

    def convolve(index, out_ref, halo_ref):
        for sub in range(tile // LANES):
            lanes = pl.ds(pl.multiple_of(index * tile + sub * LANES, LANES), LANES)
            base = (index * (tile // LANES) + sub) * padded_rows(tokens) + 8
            taps = [[0.5 * depth_ref[p, q : q + 1, lanes] for q in range(3)] for p in range(3)]
            sums = {}
            for y in range(-1, rows + 1):
                if y < 0:
                    parts = [halo_ref[sub, up_start + q : up_start + q + cols] for q in (-1, 0, 1)]
                elif y == rows:
                    parts = [
                        halo_ref[sub, down_start + q : down_start + q + cols] for q in (-1, 0, 1)
                    ]
                else:
                    parts = [
                        expanded_ref[pl.ds(base + (y * cols + q), cols), :] for q in (-1, 0, 1)
                    ]
                left = halo_ref[sub, left_start + y + 1 : left_start + y + 2]
                right = halo_ref[sub, right_start + y + 1 : right_start + y + 2]
                parts[0] = jnp.concatenate(
                    [jnp.where(at_first, left, parts[0][:8]), parts[0][8:]], axis=0
                )
                parts[2] = jnp.concatenate(
                    [parts[2][:-8], jnp.where(at_last, right, parts[2][-8:])], axis=0
                )
                for p in range(3):
                    target = y + 1 - p
                    if 0 <= target < rows:
                        for q in range(3):
                            term = taps[p][q] * parts[q]
                            sums[target] = sums[target] + term if target in sums else term
                if y > 0:
                    out_ref[
                        (y - 1) * cols : y * cols, sub * LANES : (sub + 1) * LANES
                    ] = gelu_of_half(sums.pop(y - 1)).astype(jnp.bfloat16)

    def project(index, in_ref):
        piece = pl.ds(pl.multiple_of(index * tile, tile), tile)
        total_ref[...] += matmul(in_ref[...], w_project_ref[piece, :])

    total_ref[...] = field_ref[...]
    expand_halo(0, even_halo_ref)
    expand_halo(1, odd_halo_ref)
    convolve(0, even_ref, even_halo_ref)

    def body(index, carry):
        project(2 * index, even_ref)
        convolve(2 * index + 1, odd_ref, odd_halo_ref)
        expand_halo(2 * index + 2, even_halo_ref)
        project(2 * index + 1, odd_ref)
        convolve(2 * index + 2, even_ref, even_halo_ref)
        expand_halo(2 * index + 3, odd_halo_ref)
        return carry

    pairs = width // tile // 2
    lax.fori_loop(0, pairs - 1, body, 0)
    project(2 * pairs - 2, even_ref)
    convolve(2 * pairs - 1, odd_ref, odd_halo_ref)
    project(2 * pairs - 1, odd_ref)

    step = divisor(tokens, 128, 16)
    for start in range(0, tokens, step):
        piece = slice(start, start + step)
        mixed = total_ref[piece, :]
        mixed_ref[piece, :] = mixed
        normed_ref[piece, :] = layer_norm(mixed).astype(jnp.bfloat16)
    grouped_ref[...] = matmul(perm_ref[...], normed_ref[...]).astype(jnp.bfloat16)
    size = slab_refs[0].shape[1]
    for mask, slab_ref in zip(masks, slab_refs):
        for side in range(slab_ref.shape[0]):
            start = pl.multiple_of((own_ref[0] ^ (mask | side)) * size, 16)
            slab_ref[side] = grouped_ref[pl.ds(start, size), :]


def mix(
    own, masks, slab, expanded, field, up, down, left, right, w_expand, depth_kernel, w_project, perm,
    rows, cols,
):
    tokens, channels = field.shape
    width = w_expand.shape[1]
    tile = divisor(width // 2, 256, LANES)
    slot = left.shape[0]
    halo = pltpu.VMEM((tile // LANES, 24 + 2 * cols + 2 * slot, LANES), jnp.float32)
    return pl.pallas_call(
        functools.partial(mix_kernel, rows=rows, cols=cols, masks=masks),
        in_specs=[pl.BlockSpec(memory_space=pltpu.SMEM)] + [vmem()] * 10,
        out_specs=[vmem()] * (1 + len(masks)),
        out_shape=[jax.ShapeDtypeStruct((tokens, channels), jnp.float32)]
        + [jax.ShapeDtypeStruct(slab, jnp.bfloat16)] * len(masks),
        scratch_shapes=[
            pltpu.VMEM((tokens, channels), jnp.float32),
            pltpu.VMEM((tokens, channels), jnp.bfloat16),
            pltpu.VMEM((tokens, channels), jnp.bfloat16),
            pltpu.VMEM((tokens, tile), jnp.bfloat16),
            pltpu.VMEM((tokens, tile), jnp.bfloat16),
            halo,
            halo,
        ],
        compiler_params=pltpu.CompilerParams(vmem_limit_bytes=16 * MIB),
        cost_estimate=pl.CostEstimate(
            flops=2 * tokens * channels * width,
            bytes_accessed=tokens * channels * 10 + 4 * channels * width + tokens * width * 4,
            transcendentals=tokens * width,
        ),
        name="mix",
    )(own, expanded, field, up, down, left, right, w_expand, depth_kernel, w_project, perm)


def identity(size):
    row = lax.broadcasted_iota(jnp.int32, (size, size), 0)
    column = lax.broadcasted_iota(jnp.int32, (size, size), 1)
    return jnp.where(row == column, 1.0, 0.0).astype(jnp.bfloat16)


def attend_kernel(*refs, slabs, sets):
    mine, others, weight_ref = refs[:slabs], refs[slabs : 2 * slabs], refs[2 * slabs]
    out_refs = refs[2 * slabs + 1 : 3 * slabs + 1]
    query_ref, key_ref, value_ref, turned_ref, even_ref, odd_ref = refs[3 * slabs + 1 :]
    sides, size, channels = mine[0].shape
    members = size // sets
    count = slabs * sides * members
    head_width = channels // HEADS
    group_heads = LANES // head_width
    groups = channels // LANES
    factor = math.log2(math.e) / math.sqrt(head_width)
    lane = lax.broadcasted_iota(jnp.int32, (1, LANES), 1)
    masks = [
        jnp.where((lane >= j * head_width) & (lane < (j + 1) * head_width), 1.0, 0.0).astype(
            jnp.bfloat16
        )
        for j in range(group_heads)
    ]
    turn_values = identity(channels)
    for s in range(sets):
        piece = slice(s * members, (s + 1) * members)
        block = jnp.concatenate(
            [
                (mine, others)[side][index][side, piece]
                for index in range(slabs)
                for side in range(sides)
            ],
            axis=0,
        )
        qkv = matmul(block, weight_ref[...]).astype(jnp.bfloat16)
        values = matmul_nt(turn_values, qkv[:, 2 * channels :]).astype(jnp.bfloat16)
        for group in range(groups):
            lanes = slice(group * LANES, (group + 1) * LANES)
            query_ref[s * groups + group] = qkv[:, lanes]
            key_ref[s * groups + group] = qkv[:, channels + group * LANES : channels + (group + 1) * LANES]
            for j in range(group_heads):
                head = (group * group_heads + j) * head_width
                value_ref[s * groups + group, j, :head_width] = values[head : head + head_width]
                value_ref[s * groups + group, j, head_width:] = jnp.ones((16, count), jnp.bfloat16)

    def scores(index, out):
        keys = key_ref[index]
        stacked = jnp.concatenate([keys * mask for mask in masks], axis=0)
        out[...] = matmul_nt(stacked, query_ref[index])

    def weigh(index, scores_ref):
        for j in range(group_heads):
            part = scores_ref[j * count : (j + 1) * count]
            highest = jnp.max(part, axis=0, keepdims=True)
            raised = jnp.exp2((part - highest) * factor).astype(jnp.bfloat16)
            product = matmul(value_ref[index, j], raised)
            scale = 1.0 / product[head_width : head_width + 1]
            turned_ref[index, j * head_width : (j + 1) * head_width] = (
                product[:head_width] * scale
            ).astype(jnp.bfloat16)

    total = sets * groups
    scores(0, even_ref)

    def body(pair, carry):
        scores(2 * pair + 1, odd_ref)
        weigh(2 * pair, even_ref)
        scores(jnp.minimum(2 * pair + 2, total - 1), even_ref)
        weigh(2 * pair + 1, odd_ref)
        return carry

    lax.fori_loop(0, total // 2, body, 0)
    turn_tokens = identity(count)
    for s in range(sets):
        turned = turned_ref[s * groups : (s + 1) * groups].reshape(channels, count)
        attended = matmul_nt(turn_tokens, turned).astype(jnp.bfloat16)
        for index in range(slabs):
            for side in range(sides):
                start = (index * sides + side) * members
                out_refs[index][side, s * members : (s + 1) * members] = attended[
                    start : start + members
                ]


def attend(mine, others, w_qkv, sets):
    slabs = len(mine)
    sides, size, channels = mine[0].shape
    count = slabs * sides * size // sets
    head_width = channels // HEADS
    group_heads = LANES // head_width
    total = sets * channels // LANES
    return pl.pallas_call(
        functools.partial(attend_kernel, slabs=slabs, sets=sets),
        in_specs=[vmem()] * (2 * slabs + 1),
        out_specs=[vmem()] * slabs,
        out_shape=[jax.ShapeDtypeStruct(mine[0].shape, jnp.bfloat16)] * slabs,
        scratch_shapes=[
            pltpu.VMEM((total, count, LANES), jnp.bfloat16),
            pltpu.VMEM((total, count, LANES), jnp.bfloat16),
            pltpu.VMEM((total, group_heads, head_width + 16, count), jnp.bfloat16),
            pltpu.VMEM((total, LANES, count), jnp.bfloat16),
            pltpu.VMEM((group_heads * count, count), jnp.float32),
            pltpu.VMEM((group_heads * count, count), jnp.float32),
        ],
        compiler_params=pltpu.CompilerParams(vmem_limit_bytes=24 * MIB),
        cost_estimate=pl.CostEstimate(
            flops=sets * (2 * count * channels * channels * 3 + 4 * count * count * channels),
            bytes_accessed=4 * sets * count * channels + 6 * channels * channels,
            transcendentals=sets * HEADS * count * count,
        ),
        name="attend",
    )(*mine, *others, w_qkv)


def finish_kernel(own_ref, *refs, masks):
    slabs = len(masks)
    mine, others = refs[:slabs], refs[slabs : 2 * slabs]
    back_ref, weight_ref, mixed_ref, out_ref, attended_ref, made_ref, sent = refs[2 * slabs :]
    tokens = mixed_ref.shape[0]
    sides, size, _ = mine[0].shape
    for index, mask in enumerate(masks):
        for side in range(sides):
            start = pl.multiple_of((own_ref[0] ^ (mask | side)) * size, 16)
            attended_ref[pl.ds(start, size), :] = (mine, others)[side][index][side]
    step = made_ref.shape[1]
    copies = []
    for index, start in enumerate(range(0, tokens, step)):
        rows = slice(start, start + step)
        restored = matmul(back_ref[rows, :], attended_ref[...]).astype(jnp.bfloat16)
        made_ref[index] = mixed_ref[rows, :] + matmul(restored, weight_ref[...])
        copy = pltpu.make_async_copy(
            made_ref.at[index], out_ref.at[pl.ds(start, step)], sent.at[index]
        )
        copy.start()
        copies.append(copy)
    for copy in copies:
        copy.wait()


def finish(own, masks, mine, others, back, w_out, mixed):
    tokens, channels = mixed.shape
    step = divisor(tokens, 128, 16)
    return pl.pallas_call(
        functools.partial(finish_kernel, masks=masks),
        in_specs=[pl.BlockSpec(memory_space=pltpu.SMEM)] + [vmem()] * (2 * len(masks) + 3),
        out_specs=pl.BlockSpec(memory_space=pltpu.HBM),
        out_shape=jax.ShapeDtypeStruct((tokens, channels), jnp.float32),
        scratch_shapes=[
            pltpu.VMEM((tokens, channels), jnp.bfloat16),
            pltpu.VMEM((tokens // step, step, channels), jnp.float32),
            pltpu.SemaphoreType.DMA((tokens // step,)),
        ],
        compiler_params=pltpu.CompilerParams(vmem_limit_bytes=16 * MIB),
        name="finish",
    )(own, *mine, *others, back, w_out, mixed)


def exchange(low_edge, high_edge, axis):
    count = lax.axis_size(axis)
    even = lax.axis_index(axis) % 2 == 0

    def swap(edge, start):
        pairs = [(i, i + 1) for i in range(start, count - 1, 2)]
        return lax.ppermute(edge, axis, pairs + [(b, a) for a, b in pairs])

    one = swap(jnp.where(even, high_edge, low_edge), 0)
    two = swap(jnp.where(even, low_edge, high_edge), 1)
    return jnp.where(even, two, one), jnp.where(even, one, two)


def exchange_plan(row_devices, col_devices):
    return list(range(row_devices * col_devices - 2, -1, -2)), 2


def trade(masks, slabs):
    axes = ("row", "col")
    devices = lax.axis_size("row") * lax.axis_size("col")

    def swap(slab, mask):
        return lax.ppermute(slab, axes, [(i, i ^ mask) for i in range(devices)])

    mine = [swap(slab, mask) if mask else slab for mask, slab in zip(masks, slabs)]
    return mine, [swap(slab, 1) for slab in mine]


def trade_all(slabs, sets, members, outward):
    axes = ("row", "col")
    channels = slabs[0].shape[-1]
    block = slabs[0].reshape(-1, channels)
    devices = block.shape[0] // (sets * members)
    if not outward:
        block = block.reshape(sets, devices, members, channels).transpose(1, 0, 2, 3)
    block = block.reshape(devices, sets * members, channels)
    block = lax.all_to_all(block, axes, 0, 0, tiled=True)
    if outward:
        block = block.reshape(devices, sets, members, channels).transpose(1, 0, 2, 3)
    block = [block.reshape(1, -1, channels)]
    return block, block


def grouping(rows, cols, blocks_rows, blocks_cols):
    order = np.arange(rows * cols).reshape(
        blocks_rows, rows // blocks_rows, blocks_cols, cols // blocks_cols
    )
    order = order.transpose(1, 3, 0, 2).reshape(-1)
    matrix = np.zeros((order.size, order.size), np.float32)
    matrix[np.arange(order.size), order] = 1.0
    return matrix


def shards(field, w_expand, depth_kernel, w_project, w_qkv, w_out):
    rows, cols, channels = field.shape
    tokens = rows * cols
    row_devices = lax.axis_size("row")
    col_devices = lax.axis_size("col")
    devices = row_devices * col_devices
    blocks_rows = GRID // row_devices
    blocks_cols = GRID // col_devices
    members = blocks_rows * blocks_cols
    sets_local = tokens // members // devices
    matrix = grouping(rows, cols, blocks_rows, blocks_cols)
    perm = jnp.asarray(matrix, jnp.bfloat16)
    back = jnp.asarray(matrix.T, jnp.bfloat16)

    flat = field.reshape(tokens, channels)
    edges = half_norm_of(jnp.concatenate([field[0], field[rows - 1]], axis=0), 10**10)
    up, down = exchange(edges[:cols], edges[cols:], "row")
    normed = half_norm_of(flat, 10**9)
    tile = normed.reshape(rows, cols, channels)
    spare = jnp.zeros((round_up(rows + 2, 16) - rows - 2, channels), jnp.bfloat16)
    first = jnp.concatenate([up[:1], tile[:, 0], down[:1], spare], axis=0)
    last = jnp.concatenate([up[cols - 1 :], tile[:, cols - 1], down[cols - 1 :], spare], axis=0)
    normed, first, last = lax.optimization_barrier((normed, first, last))
    expanded = expand(normed, w_expand)
    left, right = exchange(first, last, "col")
    pairwise = devices <= 16 and devices & (devices - 1) == 0 and col_devices % 2 == 0
    if pairwise:
        masks, sides = exchange_plan(row_devices, col_devices)
        own = lax.axis_index(("row", "col")).reshape(1)
    else:
        masks, sides = [0], 1
        own = jnp.zeros(1, jnp.int32)
    slab = (sides, tokens // (sides * len(masks)), channels)
    mixed, *slabs = mix(
        own, masks, slab, expanded, flat, up, down, left, right, w_expand, depth_kernel, w_project,
        perm, rows, cols,
    )

    def route(slabs, outward):
        if pairwise:
            return trade(masks, slabs)
        return trade_all(slabs, sets_local, members, outward)

    mine, others = route(slabs, True)
    slabs = attend(mine, others, w_qkv, sets_local)
    mine, others = route(slabs, False)
    final = finish(own, masks, mine, others, back, w_out, mixed)
    return final.reshape(rows, cols, channels)


def solution(mesh):
    return jax.shard_map(
        shards,
        mesh=mesh,
        in_specs=(P(("field", "row"), "col", None), P(), P(), P(), P(), P()),
        out_specs=P(("field", "row"), "col", None),
        check_vma=False,
    )
```

```python
import functools
import math

import jax
import jax.numpy as jnp
import numpy as np
from jax import lax
from jax.experimental import pallas as pl
from jax.experimental.pallas import tpu as pltpu
from jax.sharding import PartitionSpec as P

HEADS = 16
GRID = 16
LANES = 128
MIB = 1024 * 1024
NT = (((1,), (1,)), ((), ()))


def layer_norm(inputs):
    average = jnp.mean(inputs, axis=-1, keepdims=True)
    centred = inputs - average
    variance = jnp.mean(centred * centred, axis=-1, keepdims=True)
    return centred * lax.rsqrt(variance + 1e-05)


def gelu_of_half(half):
    scale = math.sqrt(2.0 / math.pi)
    inner = half * (2.0 * scale + (8.0 * scale * 0.044715) * (half * half))
    return half + half * jnp.tanh(inner)


def matmul(a, b):
    return jnp.dot(a, b, preferred_element_type=jnp.float32)


def matmul_nt(a, b):
    return lax.dot_general(a, b, NT, preferred_element_type=jnp.float32)


def divisor(size, most, unit):
    best = size
    for piece in range(unit, most + 1, unit):
        if size % piece == 0:
            best = piece
    return best


def round_up(size, unit):
    return -(-size // unit) * unit


def vmem():
    return pl.BlockSpec(memory_space=pltpu.VMEM)


def half_norm(inputs):
    return (layer_norm(inputs) * 0.5).astype(jnp.bfloat16)


def half_norm_kernel(in_ref, out_ref):
    rows = in_ref.shape[0]
    step = divisor(rows, 128, 16)
    for start in range(0, rows, step):
        out_ref[start : start + step, :] = half_norm(in_ref[start : start + step, :])


def half_norm_of(inputs, work):
    return pl.pallas_call(
        half_norm_kernel,
        in_specs=[vmem()],
        out_specs=vmem(),
        out_shape=jax.ShapeDtypeStruct(inputs.shape, jnp.bfloat16),
        compiler_params=pltpu.CompilerParams(vmem_limit_bytes=8 * MIB),
        cost_estimate=pl.CostEstimate(
            flops=work, bytes_accessed=6 * inputs.size, transcendentals=inputs.shape[0]
        ),
        name="half_norm",
    )(inputs)


def padded_rows(tokens):
    return tokens + 16


def expand_kernel(normed_ref, weight_ref, out_ref):
    tokens = normed_ref.shape[0]
    width = weight_ref.shape[1]
    tile = divisor(width, 512, LANES)
    step = divisor(tokens, 128, 16)
    starts = range(0, tokens, step)

    def body(index, carry):
        lanes = pl.ds(pl.multiple_of(index * tile, tile), tile)
        for start in starts:
            made = gelu_of_half(
                matmul(normed_ref[start : start + step, :], weight_ref[:, lanes])
            )
            for sub in range(tile // LANES):
                row = (index * (tile // LANES) + sub) * padded_rows(tokens) + 8 + start
                out_ref[pl.ds(pl.multiple_of(row, 8), step), :] = made[
                    :, sub * LANES : (sub + 1) * LANES
                ]
        return carry

    lax.fori_loop(0, width // tile, body, 0)


def expand(normed, w_expand):
    tokens, channels = normed.shape
    width = w_expand.shape[1]
    return pl.pallas_call(
        expand_kernel,
        in_specs=[vmem()] * 2,
        out_specs=vmem(),
        out_shape=jax.ShapeDtypeStruct((width // LANES * padded_rows(tokens), LANES), jnp.float32),
        compiler_params=pltpu.CompilerParams(vmem_limit_bytes=16 * MIB),
        cost_estimate=pl.CostEstimate(
            flops=10**10,
            bytes_accessed=tokens * channels * 2 + channels * width * 2 + tokens * width * 4,
            transcendentals=tokens * width,
        ),
        name="expand",
    )(normed, w_expand)


def mix_kernel(
    own_ref, expanded_ref, field_ref, up_ref, down_ref, left_ref, right_ref, w_expand_ref, depth_ref,
    w_project_ref, perm_ref, mixed_ref, *refs, rows, cols, masks,
):
    slab_refs = refs[: len(masks)]
    total_ref, normed_ref, grouped_ref, even_ref, odd_ref, even_halo_ref, odd_halo_ref = refs[
        len(masks) :
    ]
    tokens = rows * cols
    width = w_expand_ref.shape[1]
    tile = even_ref.shape[1]
    slot = left_ref.shape[0]
    up_start, down_start, left_start = 8, 16 + cols, 24 + 2 * cols
    right_start = left_start + slot

    edges = jnp.concatenate(
        [up_ref[...], down_ref[...], left_ref[...], right_ref[...]], axis=0
    )

    def expand_halo(index, out_ref):
        lanes = pl.ds(pl.multiple_of(index * tile, tile), tile)
        made = gelu_of_half(matmul(edges, w_expand_ref[:, lanes]))
        for sub in range(tile // LANES):
            part = made[:, sub * LANES : (sub + 1) * LANES]
            out_ref[sub, up_start : up_start + cols] = part[:cols]
            out_ref[sub, down_start : down_start + cols] = part[cols : 2 * cols]
            out_ref[sub, left_start : left_start + 2 * slot] = part[2 * cols :]

    position = lax.broadcasted_iota(jnp.int32, (8, LANES), 0)
    at_first = position == 0
    at_last = position == 7

    def convolve(index, out_ref, halo_ref):
        for sub in range(tile // LANES):
            lanes = pl.ds(pl.multiple_of(index * tile + sub * LANES, LANES), LANES)
            base = (index * (tile // LANES) + sub) * padded_rows(tokens) + 8
            taps = [[0.5 * depth_ref[p, q : q + 1, lanes] for q in range(3)] for p in range(3)]
            sums = {}
            for y in range(-1, rows + 1):
                if y < 0:
                    parts = [halo_ref[sub, up_start + q : up_start + q + cols] for q in (-1, 0, 1)]
                elif y == rows:
                    parts = [
                        halo_ref[sub, down_start + q : down_start + q + cols] for q in (-1, 0, 1)
                    ]
                else:
                    parts = [
                        expanded_ref[pl.ds(base + (y * cols + q), cols), :] for q in (-1, 0, 1)
                    ]
                left = halo_ref[sub, left_start + y + 1 : left_start + y + 2]
                right = halo_ref[sub, right_start + y + 1 : right_start + y + 2]
                parts[0] = jnp.concatenate(
                    [jnp.where(at_first, left, parts[0][:8]), parts[0][8:]], axis=0
                )
                parts[2] = jnp.concatenate(
                    [parts[2][:-8], jnp.where(at_last, right, parts[2][-8:])], axis=0
                )
                for p in range(3):
                    target = y + 1 - p
                    if 0 <= target < rows:
                        for q in range(3):
                            term = taps[p][q] * parts[q]
                            sums[target] = sums[target] + term if target in sums else term
                if y > 0:
                    out_ref[
                        (y - 1) * cols : y * cols, sub * LANES : (sub + 1) * LANES
                    ] = gelu_of_half(sums.pop(y - 1)).astype(jnp.bfloat16)

    def project(index, in_ref):
        piece = pl.ds(pl.multiple_of(index * tile, tile), tile)
        total_ref[...] += matmul(in_ref[...], w_project_ref[piece, :])

    total_ref[...] = field_ref[...]
    expand_halo(0, even_halo_ref)
    expand_halo(1, odd_halo_ref)
    convolve(0, even_ref, even_halo_ref)

    def body(index, carry):
        project(2 * index, even_ref)
        convolve(2 * index + 1, odd_ref, odd_halo_ref)
        expand_halo(2 * index + 2, even_halo_ref)
        project(2 * index + 1, odd_ref)
        convolve(2 * index + 2, even_ref, even_halo_ref)
        expand_halo(2 * index + 3, odd_halo_ref)
        return carry

    pairs = width // tile // 2
    lax.fori_loop(0, pairs - 1, body, 0)
    project(2 * pairs - 2, even_ref)
    convolve(2 * pairs - 1, odd_ref, odd_halo_ref)
    project(2 * pairs - 1, odd_ref)

    step = divisor(tokens, 128, 16)
    for start in range(0, tokens, step):
        piece = slice(start, start + step)
        mixed = total_ref[piece, :]
        mixed_ref[piece, :] = mixed
        normed_ref[piece, :] = layer_norm(mixed).astype(jnp.bfloat16)
    grouped_ref[...] = matmul(perm_ref[...], normed_ref[...]).astype(jnp.bfloat16)
    size = slab_refs[0].shape[1]
    for mask, slab_ref in zip(masks, slab_refs):
        for side in range(slab_ref.shape[0]):
            start = pl.multiple_of((own_ref[0] ^ (mask | side)) * size, 16)
            slab_ref[side] = grouped_ref[pl.ds(start, size), :]


def mix(
    own, masks, slab, expanded, field, up, down, left, right, w_expand, depth_kernel, w_project, perm,
    rows, cols,
):
    tokens, channels = field.shape
    width = w_expand.shape[1]
    tile = divisor(width // 2, 256, LANES)
    slot = left.shape[0]
    halo = pltpu.VMEM((tile // LANES, 24 + 2 * cols + 2 * slot, LANES), jnp.float32)
    return pl.pallas_call(
        functools.partial(mix_kernel, rows=rows, cols=cols, masks=masks),
        in_specs=[pl.BlockSpec(memory_space=pltpu.SMEM)] + [vmem()] * 10,
        out_specs=[vmem()] * (1 + len(masks)),
        out_shape=[jax.ShapeDtypeStruct((tokens, channels), jnp.float32)]
        + [jax.ShapeDtypeStruct(slab, jnp.bfloat16)] * len(masks),
        scratch_shapes=[
            pltpu.VMEM((tokens, channels), jnp.float32),
            pltpu.VMEM((tokens, channels), jnp.bfloat16),
            pltpu.VMEM((tokens, channels), jnp.bfloat16),
            pltpu.VMEM((tokens, tile), jnp.bfloat16),
            pltpu.VMEM((tokens, tile), jnp.bfloat16),
            halo,
            halo,
        ],
        compiler_params=pltpu.CompilerParams(vmem_limit_bytes=16 * MIB),
        cost_estimate=pl.CostEstimate(
            flops=2 * tokens * channels * width,
            bytes_accessed=tokens * channels * 10 + 4 * channels * width + tokens * width * 4,
            transcendentals=tokens * width,
        ),
        name="mix",
    )(own, expanded, field, up, down, left, right, w_expand, depth_kernel, w_project, perm)


def identity(size):
    row = lax.broadcasted_iota(jnp.int32, (size, size), 0)
    column = lax.broadcasted_iota(jnp.int32, (size, size), 1)
    return jnp.where(row == column, 1.0, 0.0).astype(jnp.bfloat16)


def attend_kernel(*refs, slabs, sets):
    mine, others, weight_ref = refs[:slabs], refs[slabs : 2 * slabs], refs[2 * slabs]
    out_refs = refs[2 * slabs + 1 : 3 * slabs + 1]
    query_ref, key_ref, value_ref, turned_ref, even_ref, odd_ref = refs[3 * slabs + 1 :]
    sides, size, channels = mine[0].shape
    members = size // sets
    count = slabs * sides * members
    head_width = channels // HEADS
    group_heads = LANES // head_width
    groups = channels // LANES
    factor = math.log2(math.e) / math.sqrt(head_width)
    lane = lax.broadcasted_iota(jnp.int32, (1, LANES), 1)
    masks = [
        jnp.where((lane >= j * head_width) & (lane < (j + 1) * head_width), 1.0, 0.0).astype(
            jnp.bfloat16
        )
        for j in range(group_heads)
    ]
    turn_values = identity(channels)
    for s in range(sets):
        piece = slice(s * members, (s + 1) * members)
        block = jnp.concatenate(
            [
                (mine, others)[side][index][side, piece]
                for index in range(slabs)
                for side in range(sides)
            ],
            axis=0,
        )
        qkv = matmul(block, weight_ref[...]).astype(jnp.bfloat16)
        values = matmul_nt(turn_values, qkv[:, 2 * channels :]).astype(jnp.bfloat16)
        for group in range(groups):
            lanes = slice(group * LANES, (group + 1) * LANES)
            query_ref[s * groups + group] = qkv[:, lanes]
            key_ref[s * groups + group] = qkv[:, channels + group * LANES : channels + (group + 1) * LANES]
            for j in range(group_heads):
                head = (group * group_heads + j) * head_width
                value_ref[s * groups + group, j, :head_width] = values[head : head + head_width]
                value_ref[s * groups + group, j, head_width:] = jnp.ones((16, count), jnp.bfloat16)

    def scores(index, out):
        keys = key_ref[index]
        stacked = jnp.concatenate([keys * mask for mask in masks], axis=0)
        out[...] = matmul_nt(stacked, query_ref[index])

    def weigh(index, scores_ref):
        for j in range(group_heads):
            part = scores_ref[j * count : (j + 1) * count]
            highest = jnp.max(part, axis=0, keepdims=True)
            raised = jnp.exp2((part - highest) * factor).astype(jnp.bfloat16)
            product = matmul(value_ref[index, j], raised)
            scale = 1.0 / product[head_width : head_width + 1]
            turned_ref[index, j * head_width : (j + 1) * head_width] = (
                product[:head_width] * scale
            ).astype(jnp.bfloat16)

    total = sets * groups
    scores(0, even_ref)

    def body(pair, carry):
        scores(2 * pair + 1, odd_ref)
        weigh(2 * pair, even_ref)
        scores(jnp.minimum(2 * pair + 2, total - 1), even_ref)
        weigh(2 * pair + 1, odd_ref)
        return carry

    lax.fori_loop(0, total // 2, body, 0)
    turn_tokens = identity(count)
    for s in range(sets):
        turned = turned_ref[s * groups : (s + 1) * groups].reshape(channels, count)
        attended = matmul_nt(turn_tokens, turned).astype(jnp.bfloat16)
        for index in range(slabs):
            for side in range(sides):
                start = (index * sides + side) * members
                out_refs[index][side, s * members : (s + 1) * members] = attended[
                    start : start + members
                ]


def attend(mine, others, w_qkv, sets):
    slabs = len(mine)
    sides, size, channels = mine[0].shape
    count = slabs * sides * size // sets
    head_width = channels // HEADS
    group_heads = LANES // head_width
    total = sets * channels // LANES
    return pl.pallas_call(
        functools.partial(attend_kernel, slabs=slabs, sets=sets),
        in_specs=[vmem()] * (2 * slabs + 1),
        out_specs=[vmem()] * slabs,
        out_shape=[jax.ShapeDtypeStruct(mine[0].shape, jnp.bfloat16)] * slabs,
        scratch_shapes=[
            pltpu.VMEM((total, count, LANES), jnp.bfloat16),
            pltpu.VMEM((total, count, LANES), jnp.bfloat16),
            pltpu.VMEM((total, group_heads, head_width + 16, count), jnp.bfloat16),
            pltpu.VMEM((total, LANES, count), jnp.bfloat16),
            pltpu.VMEM((group_heads * count, count), jnp.float32),
            pltpu.VMEM((group_heads * count, count), jnp.float32),
        ],
        compiler_params=pltpu.CompilerParams(vmem_limit_bytes=24 * MIB),
        cost_estimate=pl.CostEstimate(
            flops=sets * (2 * count * channels * channels * 3 + 4 * count * count * channels),
            bytes_accessed=4 * sets * count * channels + 6 * channels * channels,
            transcendentals=sets * HEADS * count * count,
        ),
        name="attend",
    )(*mine, *others, w_qkv)


def finish_kernel(own_ref, *refs, masks):
    slabs = len(masks)
    mine, others = refs[:slabs], refs[slabs : 2 * slabs]
    back_ref, weight_ref, mixed_ref, out_ref, attended_ref, made_ref, sent = refs[2 * slabs :]
    tokens = mixed_ref.shape[0]
    sides, size, _ = mine[0].shape
    for index, mask in enumerate(masks):
        for side in range(sides):
            start = pl.multiple_of((own_ref[0] ^ (mask | side)) * size, 16)
            attended_ref[pl.ds(start, size), :] = (mine, others)[side][index][side]
    step = made_ref.shape[1]
    copies = []
    for index, start in enumerate(range(0, tokens, step)):
        rows = slice(start, start + step)
        restored = matmul(back_ref[rows, :], attended_ref[...]).astype(jnp.bfloat16)
        made_ref[index] = mixed_ref[rows, :] + matmul(restored, weight_ref[...])
        copy = pltpu.make_async_copy(
            made_ref.at[index], out_ref.at[pl.ds(start, step)], sent.at[index]
        )
        copy.start()
        copies.append(copy)
    for copy in copies:
        copy.wait()


def finish(own, masks, mine, others, back, w_out, mixed):
    tokens, channels = mixed.shape
    step = divisor(tokens, 128, 16)
    return pl.pallas_call(
        functools.partial(finish_kernel, masks=masks),
        in_specs=[pl.BlockSpec(memory_space=pltpu.SMEM)] + [vmem()] * (2 * len(masks) + 3),
        out_specs=pl.BlockSpec(memory_space=pltpu.HBM),
        out_shape=jax.ShapeDtypeStruct((tokens, channels), jnp.float32),
        scratch_shapes=[
            pltpu.VMEM((tokens, channels), jnp.bfloat16),
            pltpu.VMEM((tokens // step, step, channels), jnp.float32),
            pltpu.SemaphoreType.DMA((tokens // step,)),
        ],
        compiler_params=pltpu.CompilerParams(vmem_limit_bytes=16 * MIB),
        name="finish",
    )(own, *mine, *others, back, w_out, mixed)


def exchange(low_edge, high_edge, axis):
    count = lax.axis_size(axis)
    even = lax.axis_index(axis) % 2 == 0

    def swap(edge, start):
        pairs = [(i, i + 1) for i in range(start, count - 1, 2)]
        return lax.ppermute(edge, axis, pairs + [(b, a) for a, b in pairs])

    one = swap(jnp.where(even, high_edge, low_edge), 0)
    two = swap(jnp.where(even, low_edge, high_edge), 1)
    return jnp.where(even, two, one), jnp.where(even, one, two)


def exchange_plan(row_devices, col_devices):
    devices = row_devices * col_devices
    crossing = list(range(devices - 2, devices // 2 - 1, -2))
    others = list(range(devices // 2 - 2, 0, -2))
    masks = crossing[:1]
    for index, mask in enumerate(crossing[1:]):
        masks += [mask] + others[index : index + 1]
    return masks + [0], 2


def trade(masks, slabs):
    axes = ("row", "col")
    devices = lax.axis_size("row") * lax.axis_size("col")

    def swap(slab, mask):
        return lax.ppermute(slab, axes, [(i, i ^ mask) for i in range(devices)])

    mine = [swap(slab, mask) if mask else slab for mask, slab in zip(masks, slabs)]
    return mine, [swap(slab, 1) for slab in mine]


def trade_all(slabs, sets, members, outward):
    axes = ("row", "col")
    channels = slabs[0].shape[-1]
    block = slabs[0].reshape(-1, channels)
    devices = block.shape[0] // (sets * members)
    if not outward:
        block = block.reshape(sets, devices, members, channels).transpose(1, 0, 2, 3)
    block = block.reshape(devices, sets * members, channels)
    block = lax.all_to_all(block, axes, 0, 0, tiled=True)
    if outward:
        block = block.reshape(devices, sets, members, channels).transpose(1, 0, 2, 3)
    block = [block.reshape(1, -1, channels)]
    return block, block


def grouping(rows, cols, blocks_rows, blocks_cols):
    order = np.arange(rows * cols).reshape(
        blocks_rows, rows // blocks_rows, blocks_cols, cols // blocks_cols
    )
    order = order.transpose(1, 3, 0, 2).reshape(-1)
    matrix = np.zeros((order.size, order.size), np.float32)
    matrix[np.arange(order.size), order] = 1.0
    return matrix


def shards(field, w_expand, depth_kernel, w_project, w_qkv, w_out):
    rows, cols, channels = field.shape
    tokens = rows * cols
    row_devices = lax.axis_size("row")
    col_devices = lax.axis_size("col")
    devices = row_devices * col_devices
    blocks_rows = GRID // row_devices
    blocks_cols = GRID // col_devices
    members = blocks_rows * blocks_cols
    sets_local = tokens // members // devices
    matrix = grouping(rows, cols, blocks_rows, blocks_cols)
    perm = jnp.asarray(matrix, jnp.bfloat16)
    back = jnp.asarray(matrix.T, jnp.bfloat16)

    flat = field.reshape(tokens, channels)
    edges = half_norm_of(jnp.concatenate([field[0], field[rows - 1]], axis=0), 10**10)
    up, down = exchange(edges[:cols], edges[cols:], "row")
    normed = half_norm_of(flat, 10**9)
    tile = normed.reshape(rows, cols, channels)
    spare = jnp.zeros((round_up(rows + 2, 16) - rows - 2, channels), jnp.bfloat16)
    first = jnp.concatenate([up[:1], tile[:, 0], down[:1], spare], axis=0)
    last = jnp.concatenate([up[cols - 1 :], tile[:, cols - 1], down[cols - 1 :], spare], axis=0)
    normed, first, last = lax.optimization_barrier((normed, first, last))
    expanded = expand(normed, w_expand)
    left, right = exchange(first, last, "col")
    pairwise = devices <= 16 and devices & (devices - 1) == 0 and col_devices % 2 == 0
    if pairwise:
        masks, sides = exchange_plan(row_devices, col_devices)
        own = lax.axis_index(("row", "col")).reshape(1)
    else:
        masks, sides = [0], 1
        own = jnp.zeros(1, jnp.int32)
    slab = (sides, tokens // (sides * len(masks)), channels)
    mixed, *slabs = mix(
        own, masks, slab, expanded, flat, up, down, left, right, w_expand, depth_kernel, w_project,
        perm, rows, cols,
    )

    def route(slabs, outward):
        if pairwise:
            return trade(masks, slabs)
        return trade_all(slabs, sets_local, members, outward)

    mine, others = route(slabs, True)
    slabs = attend(mine, others, w_qkv, sets_local)
    mine, others = route(slabs, False)
    final = finish(own, masks, mine, others, back, w_out, mixed)
    return final.reshape(rows, cols, channels)


def solution(mesh):
    return jax.shard_map(
        shards,
        mesh=mesh,
        in_specs=(P(("field", "row"), "col", None), P(), P(), P(), P(), P()),
        out_specs=P(("field", "row"), "col", None),
        check_vma=False,
    )
```

```python
import functools
import math

import jax
import jax.numpy as jnp
import numpy as np
from jax import lax
from jax.experimental import pallas as pl
from jax.experimental.pallas import tpu as pltpu
from jax.sharding import PartitionSpec as P

HEADS = 16
GRID = 16
LANES = 128
MIB = 1024 * 1024
NT = (((1,), (1,)), ((), ()))


def layer_norm(inputs):
    average = jnp.mean(inputs, axis=-1, keepdims=True)
    centred = inputs - average
    variance = jnp.mean(centred * centred, axis=-1, keepdims=True)
    return centred * lax.rsqrt(variance + 1e-05)


def gelu_of_half(half):
    scale = math.sqrt(2.0 / math.pi)
    inner = half * (2.0 * scale + (8.0 * scale * 0.044715) * (half * half))
    return half + half * jnp.tanh(inner)


def matmul(a, b):
    return jnp.dot(a, b, preferred_element_type=jnp.float32)


def matmul_nt(a, b):
    return lax.dot_general(a, b, NT, preferred_element_type=jnp.float32)


def divisor(size, most, unit):
    best = size
    for piece in range(unit, most + 1, unit):
        if size % piece == 0:
            best = piece
    return best


def round_up(size, unit):
    return -(-size // unit) * unit


def vmem():
    return pl.BlockSpec(memory_space=pltpu.VMEM)


def half_norm(inputs):
    return (layer_norm(inputs) * 0.5).astype(jnp.bfloat16)


def half_norm_kernel(in_ref, out_ref):
    rows = in_ref.shape[0]
    step = divisor(rows, 128, 16)
    for start in range(0, rows, step):
        out_ref[start : start + step, :] = half_norm(in_ref[start : start + step, :])


def half_norm_of(inputs, work):
    return pl.pallas_call(
        half_norm_kernel,
        in_specs=[vmem()],
        out_specs=vmem(),
        out_shape=jax.ShapeDtypeStruct(inputs.shape, jnp.bfloat16),
        compiler_params=pltpu.CompilerParams(vmem_limit_bytes=8 * MIB),
        cost_estimate=pl.CostEstimate(
            flops=work, bytes_accessed=6 * inputs.size, transcendentals=inputs.shape[0]
        ),
        name="half_norm",
    )(inputs)


def padded_rows(tokens):
    return tokens + 16


def expand_kernel(normed_ref, weight_ref, out_ref):
    tokens = normed_ref.shape[0]
    width = weight_ref.shape[1]
    tile = divisor(width, 512, LANES)
    step = divisor(tokens, 128, 16)
    starts = range(0, tokens, step)

    def body(index, carry):
        lanes = pl.ds(pl.multiple_of(index * tile, tile), tile)
        for start in starts:
            made = gelu_of_half(
                matmul(normed_ref[start : start + step, :], weight_ref[:, lanes])
            )
            for sub in range(tile // LANES):
                row = (index * (tile // LANES) + sub) * padded_rows(tokens) + 8 + start
                out_ref[pl.ds(pl.multiple_of(row, 8), step), :] = made[
                    :, sub * LANES : (sub + 1) * LANES
                ]
        return carry

    lax.fori_loop(0, width // tile, body, 0)


def expand(normed, w_expand):
    tokens, channels = normed.shape
    width = w_expand.shape[1]
    return pl.pallas_call(
        expand_kernel,
        in_specs=[vmem()] * 2,
        out_specs=vmem(),
        out_shape=jax.ShapeDtypeStruct((width // LANES * padded_rows(tokens), LANES), jnp.float32),
        compiler_params=pltpu.CompilerParams(vmem_limit_bytes=16 * MIB),
        cost_estimate=pl.CostEstimate(
            flops=10**10,
            bytes_accessed=tokens * channels * 2 + channels * width * 2 + tokens * width * 4,
            transcendentals=tokens * width,
        ),
        name="expand",
    )(normed, w_expand)


def mix_kernel(
    own_ref, expanded_ref, field_ref, up_ref, down_ref, left_ref, right_ref, w_expand_ref, depth_ref,
    w_project_ref, perm_ref, mixed_ref, *refs, rows, cols, plan, size,
):
    masks, _, sides = plan
    sent = len(outgoing_shapes(plan, size, 1))
    slab_refs = refs[:sent]
    total_ref, normed_ref, grouped_ref, even_ref, odd_ref, even_halo_ref, odd_halo_ref = refs[sent:]
    tokens = rows * cols
    width = w_expand_ref.shape[1]
    tile = even_ref.shape[1]
    slot = left_ref.shape[0]
    up_start, down_start, left_start = 8, 16 + cols, 24 + 2 * cols
    right_start = left_start + slot

    edges = jnp.concatenate(
        [up_ref[...], down_ref[...], left_ref[...], right_ref[...]], axis=0
    )

    def expand_halo(index, out_ref):
        lanes = pl.ds(pl.multiple_of(index * tile, tile), tile)
        made = gelu_of_half(matmul(edges, w_expand_ref[:, lanes]))
        for sub in range(tile // LANES):
            part = made[:, sub * LANES : (sub + 1) * LANES]
            out_ref[sub, up_start : up_start + cols] = part[:cols]
            out_ref[sub, down_start : down_start + cols] = part[cols : 2 * cols]
            out_ref[sub, left_start : left_start + 2 * slot] = part[2 * cols :]

    position = lax.broadcasted_iota(jnp.int32, (8, LANES), 0)
    at_first = position == 0
    at_last = position == 7

    def convolve(index, out_ref, halo_ref):
        for sub in range(tile // LANES):
            lanes = pl.ds(pl.multiple_of(index * tile + sub * LANES, LANES), LANES)
            base = (index * (tile // LANES) + sub) * padded_rows(tokens) + 8
            taps = [[0.5 * depth_ref[p, q : q + 1, lanes] for q in range(3)] for p in range(3)]
            sums = {}
            for y in range(-1, rows + 1):
                if y < 0:
                    parts = [halo_ref[sub, up_start + q : up_start + q + cols] for q in (-1, 0, 1)]
                elif y == rows:
                    parts = [
                        halo_ref[sub, down_start + q : down_start + q + cols] for q in (-1, 0, 1)
                    ]
                else:
                    parts = [
                        expanded_ref[pl.ds(base + (y * cols + q), cols), :] for q in (-1, 0, 1)
                    ]
                left = halo_ref[sub, left_start + y + 1 : left_start + y + 2]
                right = halo_ref[sub, right_start + y + 1 : right_start + y + 2]
                parts[0] = jnp.concatenate(
                    [jnp.where(at_first, left, parts[0][:8]), parts[0][8:]], axis=0
                )
                parts[2] = jnp.concatenate(
                    [parts[2][:-8], jnp.where(at_last, right, parts[2][-8:])], axis=0
                )
                for p in range(3):
                    target = y + 1 - p
                    if 0 <= target < rows:
                        for q in range(3):
                            term = taps[p][q] * parts[q]
                            sums[target] = sums[target] + term if target in sums else term
                if y > 0:
                    out_ref[
                        (y - 1) * cols : y * cols, sub * LANES : (sub + 1) * LANES
                    ] = gelu_of_half(sums.pop(y - 1)).astype(jnp.bfloat16)

    def project(index, in_ref):
        piece = pl.ds(pl.multiple_of(index * tile, tile), tile)
        total_ref[...] += matmul(in_ref[...], w_project_ref[piece, :])

    total_ref[...] = field_ref[...]
    expand_halo(0, even_halo_ref)
    expand_halo(1, odd_halo_ref)
    convolve(0, even_ref, even_halo_ref)

    def body(index, carry):
        project(2 * index, even_ref)
        convolve(2 * index + 1, odd_ref, odd_halo_ref)
        expand_halo(2 * index + 2, even_halo_ref)
        project(2 * index + 1, odd_ref)
        convolve(2 * index + 2, even_ref, even_halo_ref)
        expand_halo(2 * index + 3, odd_halo_ref)
        return carry

    pairs = width // tile // 2
    lax.fori_loop(0, pairs - 1, body, 0)
    project(2 * pairs - 2, even_ref)
    convolve(2 * pairs - 1, odd_ref, odd_halo_ref)
    project(2 * pairs - 1, odd_ref)

    step = divisor(tokens, 128, 16)
    for start in range(0, tokens, step):
        piece = slice(start, start + step)
        mixed = total_ref[piece, :]
        mixed_ref[piece, :] = mixed
        normed_ref[piece, :] = layer_norm(mixed).astype(jnp.bfloat16)
    grouped_ref[...] = matmul(perm_ref[...], normed_ref[...]).astype(jnp.bfloat16)
    for index, mask in enumerate(masks):
        for side in range(sides):
            start = pl.multiple_of((own_ref[0] ^ (mask | side)) * size, 16)
            write_block(
                plan, slab_refs, index, side, slice(None), grouped_ref[pl.ds(start, size), :]
            )


def mix(
    own, plan, size, expanded, field, up, down, left, right, w_expand, depth_kernel, w_project, perm,
    rows, cols,
):
    tokens, channels = field.shape
    width = w_expand.shape[1]
    tile = divisor(width // 2, 256, LANES)
    slot = left.shape[0]
    sent = outgoing_shapes(plan, size, channels)
    halo = pltpu.VMEM((tile // LANES, 24 + 2 * cols + 2 * slot, LANES), jnp.float32)
    return pl.pallas_call(
        functools.partial(mix_kernel, rows=rows, cols=cols, plan=plan, size=size),
        in_specs=[pl.BlockSpec(memory_space=pltpu.SMEM)] + [vmem()] * 10,
        out_specs=[vmem()] * (1 + len(sent)),
        out_shape=[jax.ShapeDtypeStruct((tokens, channels), jnp.float32)]
        + [jax.ShapeDtypeStruct(shape, jnp.bfloat16) for shape in sent],
        scratch_shapes=[
            pltpu.VMEM((tokens, channels), jnp.float32),
            pltpu.VMEM((tokens, channels), jnp.bfloat16),
            pltpu.VMEM((tokens, channels), jnp.bfloat16),
            pltpu.VMEM((tokens, tile), jnp.bfloat16),
            pltpu.VMEM((tokens, tile), jnp.bfloat16),
            halo,
            halo,
        ],
        compiler_params=pltpu.CompilerParams(vmem_limit_bytes=16 * MIB),
        cost_estimate=pl.CostEstimate(
            flops=2 * tokens * channels * width,
            bytes_accessed=tokens * channels * 10 + 4 * channels * width + tokens * width * 4,
            transcendentals=tokens * width,
        ),
        name="mix",
    )(own, expanded, field, up, down, left, right, w_expand, depth_kernel, w_project, perm)


def identity(size):
    row = lax.broadcasted_iota(jnp.int32, (size, size), 0)
    column = lax.broadcasted_iota(jnp.int32, (size, size), 1)
    return jnp.where(row == column, 1.0, 0.0).astype(jnp.bfloat16)


def attend_kernel(*refs, plan, sets, came):
    masks, _, sides = plan
    slabs = len(masks)
    _, size, channels = refs[0].shape
    in_refs, weight_ref, out_refs = refs[:came], refs[came], refs[came + 1 : -6]
    query_ref, key_ref, value_ref, turned_ref, even_ref, odd_ref = refs[-6:]
    members = size // sets
    count = slabs * sides * members
    head_width = channels // HEADS
    group_heads = LANES // head_width
    groups = channels // LANES
    factor = math.log2(math.e) / math.sqrt(head_width)
    lane = lax.broadcasted_iota(jnp.int32, (1, LANES), 1)
    masks = [
        jnp.where((lane >= j * head_width) & (lane < (j + 1) * head_width), 1.0, 0.0).astype(
            jnp.bfloat16
        )
        for j in range(group_heads)
    ]
    turn_values = identity(channels)
    for s in range(sets):
        piece = slice(s * members, (s + 1) * members)
        block = jnp.concatenate(
            [
                read_block(plan, in_refs, index, side, piece)
                for index in range(slabs)
                for side in range(sides)
            ],
            axis=0,
        )
        qkv = matmul(block, weight_ref[...]).astype(jnp.bfloat16)
        values = matmul_nt(turn_values, qkv[:, 2 * channels :]).astype(jnp.bfloat16)
        for group in range(groups):
            lanes = slice(group * LANES, (group + 1) * LANES)
            query_ref[s * groups + group] = qkv[:, lanes]
            key_ref[s * groups + group] = qkv[:, channels + group * LANES : channels + (group + 1) * LANES]
            for j in range(group_heads):
                head = (group * group_heads + j) * head_width
                value_ref[s * groups + group, j, :head_width] = values[head : head + head_width]
                value_ref[s * groups + group, j, head_width:] = jnp.ones((16, count), jnp.bfloat16)

    def scores(index, out):
        keys = key_ref[index]
        stacked = jnp.concatenate([keys * mask for mask in masks], axis=0)
        out[...] = matmul_nt(stacked, query_ref[index])

    def weigh(index, scores_ref):
        for j in range(group_heads):
            part = scores_ref[j * count : (j + 1) * count]
            highest = jnp.max(part, axis=0, keepdims=True)
            raised = jnp.exp2((part - highest) * factor).astype(jnp.bfloat16)
            product = matmul(value_ref[index, j], raised)
            scale = 1.0 / product[head_width : head_width + 1]
            turned_ref[index, j * head_width : (j + 1) * head_width] = (
                product[:head_width] * scale
            ).astype(jnp.bfloat16)

    total = sets * groups
    scores(0, even_ref)

    def body(pair, carry):
        scores(2 * pair + 1, odd_ref)
        weigh(2 * pair, even_ref)
        scores(jnp.minimum(2 * pair + 2, total - 1), even_ref)
        weigh(2 * pair + 1, odd_ref)
        return carry

    lax.fori_loop(0, total // 2, body, 0)
    turn_tokens = identity(count)
    for s in range(sets):
        turned = turned_ref[s * groups : (s + 1) * groups].reshape(channels, count)
        attended = matmul_nt(turn_tokens, turned).astype(jnp.bfloat16)
        for index in range(slabs):
            for side in range(sides):
                start = (index * sides + side) * members
                write_block(
                    plan, out_refs, index, side, slice(s * members, (s + 1) * members),
                    attended[start : start + members],
                )


def attend(plan, incoming, w_qkv, sets):
    masks, _, sides = plan
    _, size, channels = incoming[0].shape
    count = len(masks) * sides * size // sets
    sent = outgoing_shapes(plan, size, channels)
    head_width = channels // HEADS
    group_heads = LANES // head_width
    total = sets * channels // LANES
    return pl.pallas_call(
        functools.partial(attend_kernel, plan=plan, sets=sets, came=len(incoming)),
        in_specs=[vmem()] * (len(incoming) + 1),
        out_specs=[vmem()] * len(sent),
        out_shape=[jax.ShapeDtypeStruct(shape, jnp.bfloat16) for shape in sent],
        scratch_shapes=[
            pltpu.VMEM((total, count, LANES), jnp.bfloat16),
            pltpu.VMEM((total, count, LANES), jnp.bfloat16),
            pltpu.VMEM((total, group_heads, head_width + 16, count), jnp.bfloat16),
            pltpu.VMEM((total, LANES, count), jnp.bfloat16),
            pltpu.VMEM((group_heads * count, count), jnp.float32),
            pltpu.VMEM((group_heads * count, count), jnp.float32),
        ],
        compiler_params=pltpu.CompilerParams(vmem_limit_bytes=24 * MIB),
        cost_estimate=pl.CostEstimate(
            flops=sets * (2 * count * channels * channels * 3 + 4 * count * count * channels),
            bytes_accessed=4 * sets * count * channels + 6 * channels * channels,
            transcendentals=sets * HEADS * count * count,
        ),
        name="attend",
    )(*incoming, w_qkv)


def finish_kernel(own_ref, *refs, plan):
    masks, _, sides = plan
    in_refs, rest = refs[:-7], refs[-7:]
    back_ref, weight_ref, mixed_ref, out_ref, attended_ref, made_ref, sent = rest
    tokens = mixed_ref.shape[0]
    size = in_refs[0].shape[1]
    for index, mask in enumerate(masks):
        for side in range(sides):
            start = pl.multiple_of((own_ref[0] ^ (mask | side)) * size, 16)
            attended_ref[pl.ds(start, size), :] = read_block(
                plan, in_refs, index, side, slice(None)
            )
    step = made_ref.shape[1]
    copies = []
    for index, start in enumerate(range(0, tokens, step)):
        rows = slice(start, start + step)
        restored = matmul(back_ref[rows, :], attended_ref[...]).astype(jnp.bfloat16)
        made_ref[index] = mixed_ref[rows, :] + matmul(restored, weight_ref[...])
        copy = pltpu.make_async_copy(
            made_ref.at[index], out_ref.at[pl.ds(start, step)], sent.at[index]
        )
        copy.start()
        copies.append(copy)
    for copy in copies:
        copy.wait()


def finish(own, plan, incoming, back, w_out, mixed):
    tokens, channels = mixed.shape
    step = divisor(tokens, 128, 16)
    return pl.pallas_call(
        functools.partial(finish_kernel, plan=plan),
        in_specs=[pl.BlockSpec(memory_space=pltpu.SMEM)] + [vmem()] * (len(incoming) + 3),
        out_specs=pl.BlockSpec(memory_space=pltpu.HBM),
        out_shape=jax.ShapeDtypeStruct((tokens, channels), jnp.float32),
        scratch_shapes=[
            pltpu.VMEM((tokens, channels), jnp.bfloat16),
            pltpu.VMEM((tokens // step, step, channels), jnp.float32),
            pltpu.SemaphoreType.DMA((tokens // step,)),
        ],
        compiler_params=pltpu.CompilerParams(vmem_limit_bytes=16 * MIB),
        name="finish",
    )(own, *incoming, back, w_out, mixed)


def exchange(low_edge, high_edge, axis):
    count = lax.axis_size(axis)
    even = lax.axis_index(axis) % 2 == 0

    def swap(edge, start):
        pairs = [(i, i + 1) for i in range(start, count - 1, 2)]
        return lax.ppermute(edge, axis, pairs + [(b, a) for a, b in pairs])

    one = swap(jnp.where(even, high_edge, low_edge), 0)
    two = swap(jnp.where(even, low_edge, high_edge), 1)
    return jnp.where(even, two, one), jnp.where(even, one, two)


def exchange_plan(row_devices, col_devices):
    devices = row_devices * col_devices
    crossing = list(range(devices - 2, devices // 2 - 1, -2))
    others = list(range(devices // 2 - 2, 0, -2))
    masks = crossing[:1]
    for index, mask in enumerate(crossing[1:]):
        masks += [mask] + others[index : index + 1]
    return masks + [0], min(2, len(masks)), 2


def outgoing_shapes(plan, size, channels):
    masks, late, sides = plan
    if sides == 1:
        return [(1, size, channels)]
    early = len(masks) - 1 - late
    return [(2, size, channels)] * late + [
        (1, size, channels), (early + 1, size, channels), (early, size, channels)
    ]


def write_block(plan, refs, index, side, rows, value):
    masks, late, sides = plan
    if sides == 1:
        refs[0][0, rows] = value
    elif index < late:
        refs[index][side, rows] = value
    elif index == len(masks) - 1:
        refs[late + side][0, rows] = value
    elif side == 0:
        refs[late + 2][index - late, rows] = value
    else:
        refs[late + 1][index - late + 1, rows] = value


def read_block(plan, refs, index, side, rows):
    masks, late, sides = plan
    if sides == 1:
        return refs[0][0, rows]
    if index < late:
        return refs[index + side * len(masks)][side, rows]
    if index == len(masks) - 1:
        return refs[index + side * (late + 1)][0, rows]
    return refs[index][side, rows]


def join_kernel(own_ref, swapped_ref, *out_refs):
    for index, out_ref in enumerate(out_refs):
        out_ref[0] = own_ref[index]
        out_ref[1] = swapped_ref[index + 1]


def join(own, swapped):
    early, size, channels = own.shape
    return pl.pallas_call(
        join_kernel,
        in_specs=[vmem()] * 2,
        out_specs=[vmem()] * early,
        out_shape=[jax.ShapeDtypeStruct((2, size, channels), own.dtype)] * early,
        compiler_params=pltpu.CompilerParams(vmem_limit_bytes=8 * MIB),
        name="join",
    )(own, swapped)


def trade(plan, outgoing):
    masks, late, _ = plan
    devices = lax.axis_size("row") * lax.axis_size("col")

    def swap(slab, mask):
        return lax.ppermute(slab, ("row", "col"), [(i, i ^ mask) for i in range(devices)])

    slabs, (kept, passed, own) = outgoing[:late], outgoing[late:]
    swapped = swap(passed, 1)
    first = [swap(slab, mask) for slab, mask in zip(slabs, masks)]
    rest = [swap(slab, mask) for slab, mask in zip(join(own, swapped), masks[late:-1])]
    tie = min(1, len(rest) - 1)
    *first, rest[tie] = lax.optimization_barrier((*first, rest[tie]))
    return [*first, *rest, kept, *[swap(slab, 1) for slab in first], swapped]


def trade_all(slabs, sets, members, outward):
    axes = ("row", "col")
    channels = slabs[0].shape[-1]
    block = slabs[0].reshape(-1, channels)
    devices = block.shape[0] // (sets * members)
    if not outward:
        block = block.reshape(sets, devices, members, channels).transpose(1, 0, 2, 3)
    block = block.reshape(devices, sets * members, channels)
    block = lax.all_to_all(block, axes, 0, 0, tiled=True)
    if outward:
        block = block.reshape(devices, sets, members, channels).transpose(1, 0, 2, 3)
    return [block.reshape(1, -1, channels)]


def grouping(rows, cols, blocks_rows, blocks_cols):
    order = np.arange(rows * cols).reshape(
        blocks_rows, rows // blocks_rows, blocks_cols, cols // blocks_cols
    )
    order = order.transpose(1, 3, 0, 2).reshape(-1)
    matrix = np.zeros((order.size, order.size), np.float32)
    matrix[np.arange(order.size), order] = 1.0
    return matrix


def shards(field, w_expand, depth_kernel, w_project, w_qkv, w_out):
    rows, cols, channels = field.shape
    tokens = rows * cols
    row_devices = lax.axis_size("row")
    col_devices = lax.axis_size("col")
    devices = row_devices * col_devices
    blocks_rows = GRID // row_devices
    blocks_cols = GRID // col_devices
    members = blocks_rows * blocks_cols
    sets_local = tokens // members // devices
    matrix = grouping(rows, cols, blocks_rows, blocks_cols)
    perm = jnp.asarray(matrix, jnp.bfloat16)
    back = jnp.asarray(matrix.T, jnp.bfloat16)

    flat = field.reshape(tokens, channels)
    edges = half_norm_of(jnp.concatenate([field[0], field[rows - 1]], axis=0), 10**10)
    up, down = exchange(edges[:cols], edges[cols:], "row")
    normed = half_norm_of(flat, 10**9)
    tile = normed.reshape(rows, cols, channels)
    spare = jnp.zeros((round_up(rows + 2, 16) - rows - 2, channels), jnp.bfloat16)
    first = jnp.concatenate([up[:1], tile[:, 0], down[:1], spare], axis=0)
    last = jnp.concatenate([up[cols - 1 :], tile[:, cols - 1], down[cols - 1 :], spare], axis=0)
    normed, first, last = lax.optimization_barrier((normed, first, last))
    expanded = expand(normed, w_expand)
    left, right = exchange(first, last, "col")
    pairwise = 8 <= devices <= 16 and devices & (devices - 1) == 0 and col_devices % 2 == 0
    if pairwise:
        plan = exchange_plan(row_devices, col_devices)
        own = lax.axis_index(("row", "col")).reshape(1)
    else:
        plan = [0], 0, 1
        own = jnp.zeros(1, jnp.int32)
    size = tokens // (len(plan[0]) * plan[2])
    mixed, *outgoing = mix(
        own, plan, size, expanded, flat, up, down, left, right, w_expand, depth_kernel, w_project,
        perm, rows, cols,
    )

    def route(outgoing, outward):
        if pairwise:
            return trade(plan, outgoing)
        return trade_all(outgoing, sets_local, members, outward)

    outgoing = attend(plan, route(outgoing, True), w_qkv, sets_local)
    final = finish(own, plan, route(outgoing, False), back, w_out, mixed)
    return final.reshape(rows, cols, channels)


def solution(mesh):
    return jax.shard_map(
        shards,
        mesh=mesh,
        in_specs=(P(("field", "row"), "col", None), P(), P(), P(), P(), P()),
        out_specs=P(("field", "row"), "col", None),
        check_vma=False,
    )
```

```python
import functools
import math

import jax
import jax.numpy as jnp
import numpy as np
from jax import lax
from jax.experimental import pallas as pl
from jax.experimental.pallas import tpu as pltpu
from jax.sharding import PartitionSpec as P

HEADS = 16
GRID = 16
LANES = 128
MIB = 1024 * 1024
NT = (((1,), (1,)), ((), ()))


def layer_norm(inputs):
    average = jnp.mean(inputs, axis=-1, keepdims=True)
    centred = inputs - average
    variance = jnp.mean(centred * centred, axis=-1, keepdims=True)
    return centred * lax.rsqrt(variance + 1e-05)


def gelu_of_half(half):
    scale = math.sqrt(2.0 / math.pi)
    inner = half * (2.0 * scale + (8.0 * scale * 0.044715) * (half * half))
    return half + half * jnp.tanh(inner)


def matmul(a, b):
    return jnp.dot(a, b, preferred_element_type=jnp.float32)


def matmul_nt(a, b):
    return lax.dot_general(a, b, NT, preferred_element_type=jnp.float32)


def divisor(size, most, unit):
    best = size
    for piece in range(unit, most + 1, unit):
        if size % piece == 0:
            best = piece
    return best


def round_up(size, unit):
    return -(-size // unit) * unit


def vmem():
    return pl.BlockSpec(memory_space=pltpu.VMEM)


def half_norm(inputs):
    return (layer_norm(inputs) * 0.5).astype(jnp.bfloat16)


def half_norm_kernel(in_ref, out_ref):
    rows = in_ref.shape[0]
    step = divisor(rows, 128, 16)
    for start in range(0, rows, step):
        out_ref[start : start + step, :] = half_norm(in_ref[start : start + step, :])


def half_norm_of(inputs, work):
    return pl.pallas_call(
        half_norm_kernel,
        in_specs=[vmem()],
        out_specs=vmem(),
        out_shape=jax.ShapeDtypeStruct(inputs.shape, jnp.bfloat16),
        compiler_params=pltpu.CompilerParams(vmem_limit_bytes=8 * MIB),
        cost_estimate=pl.CostEstimate(
            flops=work, bytes_accessed=6 * inputs.size, transcendentals=inputs.shape[0]
        ),
        name="half_norm",
    )(inputs)


def padded_rows(tokens):
    return tokens + 16


def expand_kernel(normed_ref, weight_ref, out_ref):
    tokens = normed_ref.shape[0]
    width = weight_ref.shape[1]
    tile = divisor(width, 512, LANES)
    step = divisor(tokens, 128, 16)
    starts = range(0, tokens, step)

    def body(index, carry):
        lanes = pl.ds(pl.multiple_of(index * tile, tile), tile)
        for start in starts:
            made = gelu_of_half(
                matmul(normed_ref[start : start + step, :], weight_ref[:, lanes])
            )
            for sub in range(tile // LANES):
                row = (index * (tile // LANES) + sub) * padded_rows(tokens) + 8 + start
                out_ref[pl.ds(pl.multiple_of(row, 8), step), :] = made[
                    :, sub * LANES : (sub + 1) * LANES
                ]
        return carry

    lax.fori_loop(0, width // tile, body, 0)


def expand(normed, w_expand):
    tokens, channels = normed.shape
    width = w_expand.shape[1]
    return pl.pallas_call(
        expand_kernel,
        in_specs=[vmem()] * 2,
        out_specs=vmem(),
        out_shape=jax.ShapeDtypeStruct((width // LANES * padded_rows(tokens), LANES), jnp.float32),
        compiler_params=pltpu.CompilerParams(vmem_limit_bytes=16 * MIB),
        cost_estimate=pl.CostEstimate(
            flops=10**10,
            bytes_accessed=tokens * channels * 2 + channels * width * 2 + tokens * width * 4,
            transcendentals=tokens * width,
        ),
        name="expand",
    )(normed, w_expand)


def mix_kernel(
    own_ref, expanded_ref, field_ref, up_ref, down_ref, left_ref, right_ref, w_expand_ref, depth_ref,
    w_project_ref, perm_ref, mixed_ref, *refs, rows, cols, plan, size,
):
    masks, _, sides = plan
    sent = len(outgoing_shapes(plan, size, 1))
    slab_refs = refs[:sent]
    total_ref, normed_ref, grouped_ref, even_ref, odd_ref, even_halo_ref, odd_halo_ref = refs[sent:]
    tokens = rows * cols
    width = w_expand_ref.shape[1]
    tile = even_ref.shape[1]
    slot = left_ref.shape[0]
    up_start, down_start, left_start = 8, 16 + cols, 24 + 2 * cols
    right_start = left_start + slot

    edges = jnp.concatenate(
        [up_ref[...], down_ref[...], left_ref[...], right_ref[...]], axis=0
    )

    def expand_halo(index, out_ref):
        lanes = pl.ds(pl.multiple_of(index * tile, tile), tile)
        made = gelu_of_half(matmul(edges, w_expand_ref[:, lanes]))
        for sub in range(tile // LANES):
            part = made[:, sub * LANES : (sub + 1) * LANES]
            out_ref[sub, up_start : up_start + cols] = part[:cols]
            out_ref[sub, down_start : down_start + cols] = part[cols : 2 * cols]
            out_ref[sub, left_start : left_start + 2 * slot] = part[2 * cols :]

    position = lax.broadcasted_iota(jnp.int32, (8, LANES), 0)
    at_first = position == 0
    at_last = position == 7

    def convolve(index, out_ref, halo_ref):
        for sub in range(tile // LANES):
            lanes = pl.ds(pl.multiple_of(index * tile + sub * LANES, LANES), LANES)
            base = (index * (tile // LANES) + sub) * padded_rows(tokens) + 8
            taps = [[0.5 * depth_ref[p, q : q + 1, lanes] for q in range(3)] for p in range(3)]
            sums = {}
            for y in range(-1, rows + 1):
                if y < 0:
                    parts = [halo_ref[sub, up_start + q : up_start + q + cols] for q in (-1, 0, 1)]
                elif y == rows:
                    parts = [
                        halo_ref[sub, down_start + q : down_start + q + cols] for q in (-1, 0, 1)
                    ]
                else:
                    parts = [
                        expanded_ref[pl.ds(base + (y * cols + q), cols), :] for q in (-1, 0, 1)
                    ]
                left = halo_ref[sub, left_start + y + 1 : left_start + y + 2]
                right = halo_ref[sub, right_start + y + 1 : right_start + y + 2]
                parts[0] = jnp.concatenate(
                    [jnp.where(at_first, left, parts[0][:8]), parts[0][8:]], axis=0
                )
                parts[2] = jnp.concatenate(
                    [parts[2][:-8], jnp.where(at_last, right, parts[2][-8:])], axis=0
                )
                for p in range(3):
                    target = y + 1 - p
                    if 0 <= target < rows:
                        for q in range(3):
                            term = taps[p][q] * parts[q]
                            sums[target] = sums[target] + term if target in sums else term
                if y > 0:
                    out_ref[
                        (y - 1) * cols : y * cols, sub * LANES : (sub + 1) * LANES
                    ] = gelu_of_half(sums.pop(y - 1)).astype(jnp.bfloat16)

    def project(index, in_ref):
        piece = pl.ds(pl.multiple_of(index * tile, tile), tile)
        total_ref[...] += matmul(in_ref[...], w_project_ref[piece, :])

    total_ref[...] = field_ref[...]
    expand_halo(0, even_halo_ref)
    expand_halo(1, odd_halo_ref)
    convolve(0, even_ref, even_halo_ref)

    def body(index, carry):
        project(2 * index, even_ref)
        convolve(2 * index + 1, odd_ref, odd_halo_ref)
        expand_halo(2 * index + 2, even_halo_ref)
        project(2 * index + 1, odd_ref)
        convolve(2 * index + 2, even_ref, even_halo_ref)
        expand_halo(2 * index + 3, odd_halo_ref)
        return carry

    pairs = width // tile // 2
    lax.fori_loop(0, pairs - 1, body, 0)
    project(2 * pairs - 2, even_ref)
    convolve(2 * pairs - 1, odd_ref, odd_halo_ref)
    project(2 * pairs - 1, odd_ref)

    step = divisor(tokens, 128, 16)
    for start in range(0, tokens, step):
        piece = slice(start, start + step)
        mixed = total_ref[piece, :]
        mixed_ref[piece, :] = mixed
        normed_ref[piece, :] = layer_norm(mixed).astype(jnp.bfloat16)
    grouped_ref[...] = matmul(perm_ref[...], normed_ref[...]).astype(jnp.bfloat16)
    for index, mask in enumerate(masks):
        for side in range(sides):
            start = pl.multiple_of((own_ref[0] ^ (mask | side)) * size, 16)
            write_block(
                plan, slab_refs, index, side, slice(None), grouped_ref[pl.ds(start, size), :]
            )


def mix(
    own, plan, size, expanded, field, up, down, left, right, w_expand, depth_kernel, w_project, perm,
    rows, cols,
):
    tokens, channels = field.shape
    width = w_expand.shape[1]
    tile = divisor(width // 2, 256, LANES)
    slot = left.shape[0]
    sent = outgoing_shapes(plan, size, channels)
    halo = pltpu.VMEM((tile // LANES, 24 + 2 * cols + 2 * slot, LANES), jnp.float32)
    return pl.pallas_call(
        functools.partial(mix_kernel, rows=rows, cols=cols, plan=plan, size=size),
        in_specs=[pl.BlockSpec(memory_space=pltpu.SMEM)] + [vmem()] * 10,
        out_specs=[vmem()] * (1 + len(sent)),
        out_shape=[jax.ShapeDtypeStruct((tokens, channels), jnp.float32)]
        + [jax.ShapeDtypeStruct(shape, jnp.bfloat16) for shape in sent],
        scratch_shapes=[
            pltpu.VMEM((tokens, channels), jnp.float32),
            pltpu.VMEM((tokens, channels), jnp.bfloat16),
            pltpu.VMEM((tokens, channels), jnp.bfloat16),
            pltpu.VMEM((tokens, tile), jnp.bfloat16),
            pltpu.VMEM((tokens, tile), jnp.bfloat16),
            halo,
            halo,
        ],
        compiler_params=pltpu.CompilerParams(vmem_limit_bytes=16 * MIB),
        cost_estimate=pl.CostEstimate(
            flops=2 * tokens * channels * width,
            bytes_accessed=tokens * channels * 10 + 4 * channels * width + tokens * width * 4,
            transcendentals=tokens * width,
        ),
        name="mix",
    )(own, expanded, field, up, down, left, right, w_expand, depth_kernel, w_project, perm)


def identity(size):
    row = lax.broadcasted_iota(jnp.int32, (size, size), 0)
    column = lax.broadcasted_iota(jnp.int32, (size, size), 1)
    return jnp.where(row == column, 1.0, 0.0).astype(jnp.bfloat16)


def attend_kernel(*refs, plan, sets, came):
    masks, _, sides = plan
    slabs = len(masks)
    _, size, channels = refs[0].shape
    in_refs, weight_ref, out_refs = refs[:came], refs[came], refs[came + 1 : -6]
    query_ref, key_ref, value_ref, turned_ref, even_ref, odd_ref = refs[-6:]
    members = size // sets
    count = slabs * sides * members
    head_width = channels // HEADS
    group_heads = LANES // head_width
    groups = channels // LANES
    factor = math.log2(math.e) / math.sqrt(head_width)
    lane = lax.broadcasted_iota(jnp.int32, (1, LANES), 1)
    masks = [
        jnp.where((lane >= j * head_width) & (lane < (j + 1) * head_width), 1.0, 0.0).astype(
            jnp.bfloat16
        )
        for j in range(group_heads)
    ]
    turn_values = identity(channels)
    for s in range(sets):
        piece = slice(s * members, (s + 1) * members)
        block = jnp.concatenate(
            [
                read_block(plan, in_refs, index, side, piece)
                for index in range(slabs)
                for side in range(sides)
            ],
            axis=0,
        )
        qkv = matmul(block, weight_ref[...]).astype(jnp.bfloat16)
        values = matmul_nt(turn_values, qkv[:, 2 * channels :]).astype(jnp.bfloat16)
        for group in range(groups):
            lanes = slice(group * LANES, (group + 1) * LANES)
            query_ref[s * groups + group] = qkv[:, lanes]
            key_ref[s * groups + group] = qkv[:, channels + group * LANES : channels + (group + 1) * LANES]
            for j in range(group_heads):
                head = (group * group_heads + j) * head_width
                value_ref[s * groups + group, j, :head_width] = values[head : head + head_width]
                value_ref[s * groups + group, j, head_width:] = jnp.ones((16, count), jnp.bfloat16)

    def scores(index, out):
        keys = key_ref[index]
        stacked = jnp.concatenate([keys * mask for mask in masks], axis=0)
        out[...] = matmul_nt(stacked, query_ref[index])

    def weigh(index, scores_ref):
        for j in range(group_heads):
            part = scores_ref[j * count : (j + 1) * count]
            highest = jnp.max(part, axis=0, keepdims=True)
            raised = jnp.exp2((part - highest) * factor).astype(jnp.bfloat16)
            product = matmul(value_ref[index, j], raised)
            scale = 1.0 / product[head_width : head_width + 1]
            turned_ref[index, j * head_width : (j + 1) * head_width] = (
                product[:head_width] * scale
            ).astype(jnp.bfloat16)

    total = sets * groups
    scores(0, even_ref)

    def body(pair, carry):
        scores(2 * pair + 1, odd_ref)
        weigh(2 * pair, even_ref)
        scores(jnp.minimum(2 * pair + 2, total - 1), even_ref)
        weigh(2 * pair + 1, odd_ref)
        return carry

    lax.fori_loop(0, total // 2, body, 0)
    turn_tokens = identity(count)
    for s in range(sets):
        turned = turned_ref[s * groups : (s + 1) * groups].reshape(channels, count)
        attended = matmul_nt(turn_tokens, turned).astype(jnp.bfloat16)
        for index in range(slabs):
            for side in range(sides):
                start = (index * sides + side) * members
                write_block(
                    plan, out_refs, index, side, slice(s * members, (s + 1) * members),
                    attended[start : start + members],
                )


def attend(plan, incoming, w_qkv, sets):
    masks, _, sides = plan
    _, size, channels = incoming[0].shape
    count = len(masks) * sides * size // sets
    sent = outgoing_shapes(plan, size, channels)
    head_width = channels // HEADS
    group_heads = LANES // head_width
    total = sets * channels // LANES
    return pl.pallas_call(
        functools.partial(attend_kernel, plan=plan, sets=sets, came=len(incoming)),
        in_specs=[vmem()] * (len(incoming) + 1),
        out_specs=[vmem()] * len(sent),
        out_shape=[jax.ShapeDtypeStruct(shape, jnp.bfloat16) for shape in sent],
        scratch_shapes=[
            pltpu.VMEM((total, count, LANES), jnp.bfloat16),
            pltpu.VMEM((total, count, LANES), jnp.bfloat16),
            pltpu.VMEM((total, group_heads, head_width + 16, count), jnp.bfloat16),
            pltpu.VMEM((total, LANES, count), jnp.bfloat16),
            pltpu.VMEM((group_heads * count, count), jnp.float32),
            pltpu.VMEM((group_heads * count, count), jnp.float32),
        ],
        compiler_params=pltpu.CompilerParams(vmem_limit_bytes=24 * MIB),
        cost_estimate=pl.CostEstimate(
            flops=sets * (2 * count * channels * channels * 3 + 4 * count * count * channels),
            bytes_accessed=4 * sets * count * channels + 6 * channels * channels,
            transcendentals=sets * HEADS * count * count,
        ),
        name="attend",
    )(*incoming, w_qkv)


def finish_kernel(own_ref, *refs, plan):
    masks, _, sides = plan
    in_refs, rest = refs[:-7], refs[-7:]
    back_ref, weight_ref, mixed_ref, out_ref, attended_ref, made_ref, sent = rest
    tokens = mixed_ref.shape[0]
    size = in_refs[0].shape[1]
    for index, mask in enumerate(masks):
        for side in range(sides):
            start = pl.multiple_of((own_ref[0] ^ (mask | side)) * size, 16)
            attended_ref[pl.ds(start, size), :] = read_block(
                plan, in_refs, index, side, slice(None)
            )
    step = made_ref.shape[1]
    copies = []
    for index, start in enumerate(range(0, tokens, step)):
        rows = slice(start, start + step)
        restored = matmul(back_ref[rows, :], attended_ref[...]).astype(jnp.bfloat16)
        made_ref[index] = mixed_ref[rows, :] + matmul(restored, weight_ref[...])
        copy = pltpu.make_async_copy(
            made_ref.at[index], out_ref.at[pl.ds(start, step)], sent.at[index]
        )
        copy.start()
        copies.append(copy)
    for copy in copies:
        copy.wait()


def finish(own, plan, incoming, back, w_out, mixed):
    tokens, channels = mixed.shape
    step = divisor(tokens, 128, 16)
    return pl.pallas_call(
        functools.partial(finish_kernel, plan=plan),
        in_specs=[pl.BlockSpec(memory_space=pltpu.SMEM)] + [vmem()] * (len(incoming) + 3),
        out_specs=pl.BlockSpec(memory_space=pltpu.HBM),
        out_shape=jax.ShapeDtypeStruct((tokens, channels), jnp.float32),
        scratch_shapes=[
            pltpu.VMEM((tokens, channels), jnp.bfloat16),
            pltpu.VMEM((tokens // step, step, channels), jnp.float32),
            pltpu.SemaphoreType.DMA((tokens // step,)),
        ],
        compiler_params=pltpu.CompilerParams(vmem_limit_bytes=16 * MIB),
        name="finish",
    )(own, *incoming, back, w_out, mixed)


def exchange(low_edge, high_edge, shift):
    counts = lax.axis_size("row"), lax.axis_size("col")
    lead = 0 if shift[0] else 1
    even = lax.axis_index(("row", "col")[lead]) % 2 == 0

    def swap(edge, parity):
        pairs = []
        for row in range(counts[0]):
            for col in range(counts[1]):
                there = row + shift[0], col + shift[1]
                inside = there[0] < counts[0] and 0 <= there[1] < counts[1]
                if (row, col)[lead] % 2 == parity and inside:
                    pairs.append((row * counts[1] + col, there[0] * counts[1] + there[1]))
        return lax.ppermute(edge, ("row", "col"), pairs + [(b, a) for a, b in pairs])

    one = swap(jnp.where(even, high_edge, low_edge), 0)
    two = swap(jnp.where(even, low_edge, high_edge), 1)
    return jnp.where(even, two, one), jnp.where(even, one, two)


def exchange_plan(row_devices, col_devices):
    devices = row_devices * col_devices
    return list(range(devices - 2, -1, -2)), 2, 2


def outgoing_shapes(plan, size, channels):
    masks, late, sides = plan
    if sides == 1:
        return [(1, size, channels)]
    early = len(masks) - 1 - late
    return [(2, size, channels)] * late + [
        (1, size, channels), (early + 1, size, channels), (early, size, channels)
    ]


def write_block(plan, refs, index, side, rows, value):
    masks, late, sides = plan
    if sides == 1:
        refs[0][0, rows] = value
    elif index < late:
        refs[index][side, rows] = value
    elif index == len(masks) - 1:
        refs[late + side][0, rows] = value
    elif side == 0:
        refs[late + 2][index - late, rows] = value
    else:
        refs[late + 1][index - late + 1, rows] = value


def read_block(plan, refs, index, side, rows):
    masks, late, sides = plan
    if sides == 1:
        return refs[0][0, rows]
    if index < late:
        return refs[index + side * len(masks)][side, rows]
    if index == len(masks) - 1:
        return refs[index + side * (late + 1)][0, rows]
    return refs[index][side, rows]


def join_kernel(own_ref, swapped_ref, *out_refs):
    for index, out_ref in enumerate(out_refs):
        out_ref[0] = own_ref[index]
        out_ref[1] = swapped_ref[index + 1]


def join(own, swapped):
    early, size, channels = own.shape
    return pl.pallas_call(
        join_kernel,
        in_specs=[vmem()] * 2,
        out_specs=[vmem()] * early,
        out_shape=[jax.ShapeDtypeStruct((2, size, channels), own.dtype)] * early,
        compiler_params=pltpu.CompilerParams(vmem_limit_bytes=8 * MIB),
        name="join",
    )(own, swapped)


def trade(plan, outgoing):
    masks, late, _ = plan
    devices = lax.axis_size("row") * lax.axis_size("col")

    def swap(slab, mask):
        return lax.ppermute(slab, ("row", "col"), [(i, i ^ mask) for i in range(devices)])

    slabs, (kept, passed, own) = outgoing[:late], outgoing[late:]
    swapped = swap(passed, 1)
    first = [swap(slab, mask) for slab, mask in zip(slabs, masks)]
    rest = [swap(slab, mask) for slab, mask in zip(join(own, swapped), masks[late:-1])]
    *first, rest[0] = lax.optimization_barrier((*first, rest[0]))
    return [*first, *rest, kept, *[swap(slab, 1) for slab in first], swapped]


def trade_all(slabs, sets, members, outward):
    axes = ("row", "col")
    channels = slabs[0].shape[-1]
    block = slabs[0].reshape(-1, channels)
    devices = block.shape[0] // (sets * members)
    if not outward:
        block = block.reshape(sets, devices, members, channels).transpose(1, 0, 2, 3)
    block = block.reshape(devices, sets * members, channels)
    block = lax.all_to_all(block, axes, 0, 0, tiled=True)
    if outward:
        block = block.reshape(devices, sets, members, channels).transpose(1, 0, 2, 3)
    return [block.reshape(1, -1, channels)]


def grouping(rows, cols, blocks_rows, blocks_cols):
    order = np.arange(rows * cols).reshape(
        blocks_rows, rows // blocks_rows, blocks_cols, cols // blocks_cols
    )
    order = order.transpose(1, 3, 0, 2).reshape(-1)
    matrix = np.zeros((order.size, order.size), np.float32)
    matrix[np.arange(order.size), order] = 1.0
    return matrix


def shards(field, w_expand, depth_kernel, w_project, w_qkv, w_out):
    rows, cols, channels = field.shape
    tokens = rows * cols
    row_devices = lax.axis_size("row")
    col_devices = lax.axis_size("col")
    devices = row_devices * col_devices
    blocks_rows = GRID // row_devices
    blocks_cols = GRID // col_devices
    members = blocks_rows * blocks_cols
    sets_local = tokens // members // devices
    matrix = grouping(rows, cols, blocks_rows, blocks_cols)
    perm = jnp.asarray(matrix, jnp.bfloat16)
    back = jnp.asarray(matrix.T, jnp.bfloat16)

    flat = field.reshape(tokens, channels)
    edges = half_norm_of(jnp.concatenate([field[0], field[rows - 1]], axis=0), 10**10)
    top, bottom = edges[:cols], edges[cols:]
    up, down = exchange(top, bottom, (1, 0))
    ready, _ = lax.optimization_barrier((flat, edges))
    normed = half_norm_of(ready, 10**9)
    tile = normed.reshape(rows, cols, channels)
    left_side, right_side = exchange(tile[:, 0], tile[:, cols - 1], (0, 1))
    up_left, down_right = exchange(top[:1], bottom[cols - 1 :], (1, 1))
    up_right, down_left = exchange(top[cols - 1 :], bottom[:1], (1, -1))
    ready, up_right, down_left, up_left, down_right = lax.optimization_barrier((normed, up_right, down_left, up_left, down_right))
    expanded = expand(ready, w_expand)
    spare = jnp.zeros((round_up(rows + 2, 16) - rows - 2, channels), jnp.bfloat16)
    left = jnp.concatenate([up_left, left_side, down_left, spare], axis=0)
    right = jnp.concatenate([up_right, right_side, down_right, spare], axis=0)
    pairwise = 8 <= devices <= 16 and devices & (devices - 1) == 0 and col_devices % 2 == 0
    if pairwise:
        plan = exchange_plan(row_devices, col_devices)
        own = lax.axis_index(("row", "col")).reshape(1)
    else:
        plan = [0], 0, 1
        own = jnp.zeros(1, jnp.int32)
    size = tokens // (len(plan[0]) * plan[2])
    mixed, *outgoing = mix(
        own, plan, size, expanded, flat, up, down, left, right, w_expand, depth_kernel, w_project,
        perm, rows, cols,
    )

    def route(outgoing, outward):
        if pairwise:
            return trade(plan, outgoing)
        return trade_all(outgoing, sets_local, members, outward)

    outgoing = attend(plan, route(outgoing, True), w_qkv, sets_local)
    final = finish(own, plan, route(outgoing, False), back, w_out, mixed)
    return final.reshape(rows, cols, channels)


def solution(mesh):
    return jax.shard_map(
        shards,
        mesh=mesh,
        in_specs=(P(("field", "row"), "col", None), P(), P(), P(), P(), P()),
        out_specs=P(("field", "row"), "col", None),
        check_vma=False,
    )
```

```python
import functools
import math

import jax
import jax.numpy as jnp
import numpy as np
from jax import lax
from jax.experimental import pallas as pl
from jax.experimental.pallas import tpu as pltpu
from jax.sharding import PartitionSpec as P

HEADS = 16
GRID = 16
LANES = 128
MIB = 1024 * 1024
NT = (((1,), (1,)), ((), ()))


def layer_norm(inputs):
    average = jnp.mean(inputs, axis=-1, keepdims=True)
    centred = inputs - average
    variance = jnp.mean(centred * centred, axis=-1, keepdims=True)
    return centred * lax.rsqrt(variance + 1e-05)


def gelu_of_half(half):
    scale = math.sqrt(2.0 / math.pi)
    inner = half * (2.0 * scale + (8.0 * scale * 0.044715) * (half * half))
    return half + half * jnp.tanh(inner)


def matmul(a, b):
    return jnp.dot(a, b, preferred_element_type=jnp.float32)


def matmul_nt(a, b):
    return lax.dot_general(a, b, NT, preferred_element_type=jnp.float32)


def divisor(size, most, unit):
    best = size
    for piece in range(unit, most + 1, unit):
        if size % piece == 0:
            best = piece
    return best


def round_up(size, unit):
    return -(-size // unit) * unit


def vmem():
    return pl.BlockSpec(memory_space=pltpu.VMEM)


def half_norm(inputs):
    return (layer_norm(inputs) * 0.5).astype(jnp.bfloat16)


def half_norm_kernel(in_ref, out_ref):
    rows = in_ref.shape[0]
    step = divisor(rows, 128, 16)
    for start in range(0, rows, step):
        out_ref[start : start + step, :] = half_norm(in_ref[start : start + step, :])


def half_norm_of(inputs, work):
    return pl.pallas_call(
        half_norm_kernel,
        in_specs=[vmem()],
        out_specs=vmem(),
        out_shape=jax.ShapeDtypeStruct(inputs.shape, jnp.bfloat16),
        compiler_params=pltpu.CompilerParams(vmem_limit_bytes=2 * MIB),
        cost_estimate=pl.CostEstimate(
            flops=work, bytes_accessed=6 * inputs.size, transcendentals=inputs.shape[0]
        ),
        name="half_norm",
    )(inputs)


def padded_rows(tokens):
    return tokens + 16


def expand_kernel(normed_ref, weight_ref, out_ref):
    tokens = normed_ref.shape[0]
    width = weight_ref.shape[1]
    tile = divisor(width, 512, LANES)
    step = divisor(tokens, 128, 16)
    starts = range(0, tokens, step)

    def body(index, carry):
        lanes = pl.ds(pl.multiple_of(index * tile, tile), tile)
        for start in starts:
            made = gelu_of_half(
                matmul(normed_ref[start : start + step, :], weight_ref[:, lanes])
            )
            for sub in range(tile // LANES):
                row = (index * (tile // LANES) + sub) * padded_rows(tokens) + 8 + start
                out_ref[pl.ds(pl.multiple_of(row, 8), step), :] = made[
                    :, sub * LANES : (sub + 1) * LANES
                ]
        return carry

    lax.fori_loop(0, width // tile, body, 0)


def expand(normed, w_expand):
    tokens, channels = normed.shape
    width = w_expand.shape[1]
    return pl.pallas_call(
        expand_kernel,
        in_specs=[vmem()] * 2,
        out_specs=vmem(),
        out_shape=jax.ShapeDtypeStruct((width // LANES * padded_rows(tokens), LANES), jnp.float32),
        compiler_params=pltpu.CompilerParams(vmem_limit_bytes=4 * MIB),
        cost_estimate=pl.CostEstimate(
            flops=10**10,
            bytes_accessed=tokens * channels * 2 + channels * width * 2 + tokens * width * 4,
            transcendentals=tokens * width,
        ),
        name="expand",
    )(normed, w_expand)


def mix_kernel(
    own_ref, expanded_ref, field_ref, up_ref, down_ref, left_ref, right_ref, w_expand_ref, depth_ref,
    w_project_ref, perm_ref, mixed_ref, *refs, rows, cols, plan, size,
):
    masks, _, sides = plan
    sent = len(outgoing_shapes(plan, size, 1))
    slab_refs = refs[:sent]
    total_ref, normed_ref, grouped_ref, even_ref, odd_ref, even_halo_ref, odd_halo_ref = refs[sent:]
    tokens = rows * cols
    width = w_expand_ref.shape[1]
    tile = even_ref.shape[1]
    slot = left_ref.shape[0]
    up_start, down_start, left_start = 8, 16 + cols, 24 + 2 * cols
    right_start = left_start + slot

    edges = jnp.concatenate(
        [up_ref[...], down_ref[...], left_ref[...], right_ref[...]], axis=0
    )

    def expand_halo(index, out_ref):
        lanes = pl.ds(pl.multiple_of(index * tile, tile), tile)
        made = gelu_of_half(matmul(edges, w_expand_ref[:, lanes]))
        for sub in range(tile // LANES):
            part = made[:, sub * LANES : (sub + 1) * LANES]
            out_ref[sub, up_start : up_start + cols] = part[:cols]
            out_ref[sub, down_start : down_start + cols] = part[cols : 2 * cols]
            out_ref[sub, left_start : left_start + 2 * slot] = part[2 * cols :]

    position = lax.broadcasted_iota(jnp.int32, (8, LANES), 0)
    at_first = position == 0
    at_last = position == 7

    def convolve(index, out_ref, halo_ref):
        for sub in range(tile // LANES):
            lanes = pl.ds(pl.multiple_of(index * tile + sub * LANES, LANES), LANES)
            base = (index * (tile // LANES) + sub) * padded_rows(tokens) + 8
            taps = [[0.5 * depth_ref[p, q : q + 1, lanes] for q in range(3)] for p in range(3)]
            sums = {}
            for y in range(-1, rows + 1):
                if y < 0:
                    parts = [halo_ref[sub, up_start + q : up_start + q + cols] for q in (-1, 0, 1)]
                elif y == rows:
                    parts = [
                        halo_ref[sub, down_start + q : down_start + q + cols] for q in (-1, 0, 1)
                    ]
                else:
                    parts = [
                        expanded_ref[pl.ds(base + (y * cols + q), cols), :] for q in (-1, 0, 1)
                    ]
                left = halo_ref[sub, left_start + y + 1 : left_start + y + 2]
                right = halo_ref[sub, right_start + y + 1 : right_start + y + 2]
                parts[0] = jnp.concatenate(
                    [jnp.where(at_first, left, parts[0][:8]), parts[0][8:]], axis=0
                )
                parts[2] = jnp.concatenate(
                    [parts[2][:-8], jnp.where(at_last, right, parts[2][-8:])], axis=0
                )
                for p in range(3):
                    target = y + 1 - p
                    if 0 <= target < rows:
                        for q in range(3):
                            term = taps[p][q] * parts[q]
                            sums[target] = sums[target] + term if target in sums else term
                if y > 0:
                    out_ref[
                        (y - 1) * cols : y * cols, sub * LANES : (sub + 1) * LANES
                    ] = gelu_of_half(sums.pop(y - 1)).astype(jnp.bfloat16)

    def project(index, in_ref):
        piece = pl.ds(pl.multiple_of(index * tile, tile), tile)
        total_ref[...] += matmul(in_ref[...], w_project_ref[piece, :])

    total_ref[...] = field_ref[...]
    expand_halo(0, even_halo_ref)
    expand_halo(1, odd_halo_ref)
    convolve(0, even_ref, even_halo_ref)

    def body(index, carry):
        project(2 * index, even_ref)
        convolve(2 * index + 1, odd_ref, odd_halo_ref)
        expand_halo(2 * index + 2, even_halo_ref)
        project(2 * index + 1, odd_ref)
        convolve(2 * index + 2, even_ref, even_halo_ref)
        expand_halo(2 * index + 3, odd_halo_ref)
        return carry

    pairs = width // tile // 2
    lax.fori_loop(0, pairs - 1, body, 0)
    project(2 * pairs - 2, even_ref)
    convolve(2 * pairs - 1, odd_ref, odd_halo_ref)
    project(2 * pairs - 1, odd_ref)

    step = divisor(tokens, 128, 16)
    for start in range(0, tokens, step):
        piece = slice(start, start + step)
        mixed = total_ref[piece, :]
        mixed_ref[piece, :] = mixed
        normed_ref[piece, :] = layer_norm(mixed).astype(jnp.bfloat16)
    grouped_ref[...] = matmul(perm_ref[...], normed_ref[...]).astype(jnp.bfloat16)
    for index, mask in enumerate(masks):
        for side in range(sides):
            start = pl.multiple_of((own_ref[0] ^ (mask | side)) * size, 16)
            write_block(
                plan, slab_refs, index, side, slice(None), grouped_ref[pl.ds(start, size), :]
            )


def mix(
    own, plan, size, expanded, field, up, down, left, right, w_expand, depth_kernel, w_project, perm,
    rows, cols,
):
    tokens, channels = field.shape
    width = w_expand.shape[1]
    tile = divisor(width // 2, 256, LANES)
    slot = left.shape[0]
    sent = outgoing_shapes(plan, size, channels)
    halo = pltpu.VMEM((tile // LANES, 24 + 2 * cols + 2 * slot, LANES), jnp.float32)
    return pl.pallas_call(
        functools.partial(mix_kernel, rows=rows, cols=cols, plan=plan, size=size),
        in_specs=[pl.BlockSpec(memory_space=pltpu.SMEM)] + [vmem()] * 10,
        out_specs=[vmem()] * (1 + len(sent)),
        out_shape=[jax.ShapeDtypeStruct((tokens, channels), jnp.float32)]
        + [jax.ShapeDtypeStruct(shape, jnp.bfloat16) for shape in sent],
        scratch_shapes=[
            pltpu.VMEM((tokens, channels), jnp.float32),
            pltpu.VMEM((tokens, channels), jnp.bfloat16),
            pltpu.VMEM((tokens, channels), jnp.bfloat16),
            pltpu.VMEM((tokens, tile), jnp.bfloat16),
            pltpu.VMEM((tokens, tile), jnp.bfloat16),
            halo,
            halo,
        ],
        compiler_params=pltpu.CompilerParams(vmem_limit_bytes=8 * MIB),
        cost_estimate=pl.CostEstimate(
            flops=2 * tokens * channels * width,
            bytes_accessed=tokens * channels * 10 + 4 * channels * width + tokens * width * 4,
            transcendentals=tokens * width,
        ),
        name="mix",
    )(own, expanded, field, up, down, left, right, w_expand, depth_kernel, w_project, perm)


def identity(size):
    row = lax.broadcasted_iota(jnp.int32, (size, size), 0)
    column = lax.broadcasted_iota(jnp.int32, (size, size), 1)
    return jnp.where(row == column, 1.0, 0.0).astype(jnp.bfloat16)


def attend_kernel(*refs, plan, sets, came):
    masks, _, sides = plan
    slabs = len(masks)
    _, size, channels = refs[0].shape
    in_refs, weight_ref, out_refs = refs[:came], refs[came], refs[came + 1 : -6]
    query_ref, key_ref, value_ref, turned_ref, even_ref, odd_ref = refs[-6:]
    members = size // sets
    count = slabs * sides * members
    head_width = channels // HEADS
    group_heads = LANES // head_width
    groups = channels // LANES
    factor = math.log2(math.e) / math.sqrt(head_width)
    lane = lax.broadcasted_iota(jnp.int32, (1, LANES), 1)
    masks = [
        jnp.where((lane >= j * head_width) & (lane < (j + 1) * head_width), 1.0, 0.0).astype(
            jnp.bfloat16
        )
        for j in range(group_heads)
    ]
    turn_values = identity(channels)
    for s in range(sets):
        piece = slice(s * members, (s + 1) * members)
        block = jnp.concatenate(
            [
                read_block(plan, in_refs, index, side, piece)
                for index in range(slabs)
                for side in range(sides)
            ],
            axis=0,
        )
        qkv = matmul(block, weight_ref[...]).astype(jnp.bfloat16)
        values = matmul_nt(turn_values, qkv[:, 2 * channels :]).astype(jnp.bfloat16)
        for group in range(groups):
            lanes = slice(group * LANES, (group + 1) * LANES)
            query_ref[s * groups + group] = qkv[:, lanes]
            key_ref[s * groups + group] = qkv[:, channels + group * LANES : channels + (group + 1) * LANES]
            for j in range(group_heads):
                head = (group * group_heads + j) * head_width
                value_ref[s * groups + group, j, :head_width] = values[head : head + head_width]
                value_ref[s * groups + group, j, head_width:] = jnp.ones((16, count), jnp.bfloat16)

    def scores(index, out):
        keys = key_ref[index]
        stacked = jnp.concatenate([keys * mask for mask in masks], axis=0)
        out[...] = matmul_nt(stacked, query_ref[index])

    def weigh(index, scores_ref):
        for j in range(group_heads):
            part = scores_ref[j * count : (j + 1) * count]
            highest = jnp.max(part, axis=0, keepdims=True)
            raised = jnp.exp2((part - highest) * factor).astype(jnp.bfloat16)
            product = matmul(value_ref[index, j], raised)
            scale = 1.0 / product[head_width : head_width + 1]
            turned_ref[index, j * head_width : (j + 1) * head_width] = (
                product[:head_width] * scale
            ).astype(jnp.bfloat16)

    total = sets * groups
    scores(0, even_ref)

    def body(pair, carry):
        scores(2 * pair + 1, odd_ref)
        weigh(2 * pair, even_ref)
        scores(jnp.minimum(2 * pair + 2, total - 1), even_ref)
        weigh(2 * pair + 1, odd_ref)
        return carry

    lax.fori_loop(0, total // 2, body, 0)
    turn_tokens = identity(count)
    for s in range(sets):
        turned = turned_ref[s * groups : (s + 1) * groups].reshape(channels, count)
        attended = matmul_nt(turn_tokens, turned).astype(jnp.bfloat16)
        for index in range(slabs):
            for side in range(sides):
                start = (index * sides + side) * members
                write_block(
                    plan, out_refs, index, side, slice(s * members, (s + 1) * members),
                    attended[start : start + members],
                )


def attend(plan, incoming, w_qkv, sets):
    masks, _, sides = plan
    _, size, channels = incoming[0].shape
    count = len(masks) * sides * size // sets
    sent = outgoing_shapes(plan, size, channels)
    head_width = channels // HEADS
    group_heads = LANES // head_width
    total = sets * channels // LANES
    return pl.pallas_call(
        functools.partial(attend_kernel, plan=plan, sets=sets, came=len(incoming)),
        in_specs=[vmem()] * (len(incoming) + 1),
        out_specs=[vmem()] * len(sent),
        out_shape=[jax.ShapeDtypeStruct(shape, jnp.bfloat16) for shape in sent],
        scratch_shapes=[
            pltpu.VMEM((total, count, LANES), jnp.bfloat16),
            pltpu.VMEM((total, count, LANES), jnp.bfloat16),
            pltpu.VMEM((total, group_heads, head_width + 16, count), jnp.bfloat16),
            pltpu.VMEM((total, LANES, count), jnp.bfloat16),
            pltpu.VMEM((group_heads * count, count), jnp.float32),
            pltpu.VMEM((group_heads * count, count), jnp.float32),
        ],
        compiler_params=pltpu.CompilerParams(vmem_limit_bytes=10 * MIB),
        cost_estimate=pl.CostEstimate(
            flops=sets * (2 * count * channels * channels * 3 + 4 * count * count * channels),
            bytes_accessed=4 * sets * count * channels + 6 * channels * channels,
            transcendentals=sets * HEADS * count * count,
        ),
        name="attend",
    )(*incoming, w_qkv)


def finish_kernel(own_ref, *refs, plan):
    masks, _, sides = plan
    in_refs, rest = refs[:-7], refs[-7:]
    back_ref, weight_ref, mixed_ref, out_ref, attended_ref, made_ref, sent = rest
    tokens = mixed_ref.shape[0]
    size = in_refs[0].shape[1]
    for index, mask in enumerate(masks):
        for side in range(sides):
            start = pl.multiple_of((own_ref[0] ^ (mask | side)) * size, 16)
            attended_ref[pl.ds(start, size), :] = read_block(
                plan, in_refs, index, side, slice(None)
            )
    step = made_ref.shape[1]
    copies = []
    for index, start in enumerate(range(0, tokens, step)):
        rows = slice(start, start + step)
        restored = matmul(back_ref[rows, :], attended_ref[...]).astype(jnp.bfloat16)
        made_ref[index] = mixed_ref[rows, :] + matmul(restored, weight_ref[...])
        copy = pltpu.make_async_copy(
            made_ref.at[index], out_ref.at[pl.ds(start, step)], sent.at[index]
        )
        copy.start()
        copies.append(copy)
    for copy in copies:
        copy.wait()


def finish(own, plan, incoming, back, w_out, mixed):
    tokens, channels = mixed.shape
    step = divisor(tokens, 128, 16)
    return pl.pallas_call(
        functools.partial(finish_kernel, plan=plan),
        in_specs=[pl.BlockSpec(memory_space=pltpu.SMEM)] + [vmem()] * (len(incoming) + 3),
        out_specs=pl.BlockSpec(memory_space=pltpu.HBM),
        out_shape=jax.ShapeDtypeStruct((tokens, channels), jnp.float32),
        scratch_shapes=[
            pltpu.VMEM((tokens, channels), jnp.bfloat16),
            pltpu.VMEM((tokens // step, step, channels), jnp.float32),
            pltpu.SemaphoreType.DMA((tokens // step,)),
        ],
        compiler_params=pltpu.CompilerParams(vmem_limit_bytes=6 * MIB),
        name="finish",
    )(own, *incoming, back, w_out, mixed)


def exchange(low_edge, high_edge, axis):
    count = lax.axis_size(axis)
    even = lax.axis_index(axis) % 2 == 0

    def swap(edge, start):
        pairs = [(i, i + 1) for i in range(start, count - 1, 2)]
        return lax.ppermute(edge, axis, pairs + [(b, a) for a, b in pairs])

    one = swap(jnp.where(even, high_edge, low_edge), 0)
    two = swap(jnp.where(even, low_edge, high_edge), 1)
    return jnp.where(even, two, one), jnp.where(even, one, two)


def exchange_plan(row_devices, col_devices):
    devices = row_devices * col_devices
    crossing = list(range(devices - 2, devices // 2 - 1, -2))
    others = list(range(devices // 2 - 2, 0, -2))
    masks = crossing[:1]
    for index, mask in enumerate(crossing[1:]):
        masks += [mask] + others[index : index + 1]
    return masks + [0], min(2, len(masks)), 2


def outgoing_shapes(plan, size, channels):
    masks, late, sides = plan
    if sides == 1:
        return [(1, size, channels)]
    early = len(masks) - 1 - late
    return [(2, size, channels)] * late + [
        (1, size, channels), (early + 1, size, channels), (early, size, channels)
    ]


def write_block(plan, refs, index, side, rows, value):
    masks, late, sides = plan
    if sides == 1:
        refs[0][0, rows] = value
    elif index < late:
        refs[index][side, rows] = value
    elif index == len(masks) - 1:
        refs[late + side][0, rows] = value
    elif side == 0:
        refs[late + 2][index - late, rows] = value
    else:
        refs[late + 1][index - late + 1, rows] = value


def read_block(plan, refs, index, side, rows):
    masks, late, sides = plan
    if sides == 1:
        return refs[0][0, rows]
    if index < late:
        return refs[index + side * len(masks)][side, rows]
    if index == len(masks) - 1:
        return refs[index + side * (late + 1)][0, rows]
    return refs[index][side, rows]


def join_kernel(own_ref, swapped_ref, *out_refs):
    for index, out_ref in enumerate(out_refs):
        out_ref[0] = own_ref[index]
        out_ref[1] = swapped_ref[index + 1]


def join(own, swapped):
    early, size, channels = own.shape
    return pl.pallas_call(
        join_kernel,
        in_specs=[vmem()] * 2,
        out_specs=[vmem()] * early,
        out_shape=[jax.ShapeDtypeStruct((2, size, channels), own.dtype)] * early,
        compiler_params=pltpu.CompilerParams(vmem_limit_bytes=2 * MIB),
        name="join",
    )(own, swapped)


def trade(plan, outgoing):
    masks, late, _ = plan
    devices = lax.axis_size("row") * lax.axis_size("col")

    def swap(slab, mask):
        return lax.ppermute(slab, ("row", "col"), [(i, i ^ mask) for i in range(devices)])

    slabs, (kept, passed, own) = outgoing[:late], outgoing[late:]
    swapped = swap(passed, 1)
    first = [swap(slab, mask) for slab, mask in zip(slabs, masks)]
    rest = [swap(slab, mask) for slab, mask in zip(join(own, swapped), masks[late:-1])]
    tie = min(1, len(rest) - 1)
    *first, rest[tie] = lax.optimization_barrier((*first, rest[tie]))
    return [*first, *rest, kept, *[swap(slab, 1) for slab in first], swapped]


def trade_all(slabs, sets, members, outward):
    axes = ("row", "col")
    channels = slabs[0].shape[-1]
    block = slabs[0].reshape(-1, channels)
    devices = block.shape[0] // (sets * members)
    if not outward:
        block = block.reshape(sets, devices, members, channels).transpose(1, 0, 2, 3)
    block = block.reshape(devices, sets * members, channels)
    block = lax.all_to_all(block, axes, 0, 0, tiled=True)
    if outward:
        block = block.reshape(devices, sets, members, channels).transpose(1, 0, 2, 3)
    return [block.reshape(1, -1, channels)]


def grouping(rows, cols, blocks_rows, blocks_cols):
    order = np.arange(rows * cols).reshape(
        blocks_rows, rows // blocks_rows, blocks_cols, cols // blocks_cols
    )
    order = order.transpose(1, 3, 0, 2).reshape(-1)
    matrix = np.zeros((order.size, order.size), np.float32)
    matrix[np.arange(order.size), order] = 1.0
    return matrix


def shards(field, w_expand, depth_kernel, w_project, w_qkv, w_out):
    rows, cols, channels = field.shape
    tokens = rows * cols
    row_devices = lax.axis_size("row")
    col_devices = lax.axis_size("col")
    devices = row_devices * col_devices
    blocks_rows = GRID // row_devices
    blocks_cols = GRID // col_devices
    members = blocks_rows * blocks_cols
    sets_local = tokens // members // devices
    matrix = grouping(rows, cols, blocks_rows, blocks_cols)
    perm = jnp.asarray(matrix, jnp.bfloat16)
    back = jnp.asarray(matrix.T, jnp.bfloat16)

    flat = field.reshape(tokens, channels)
    edges = half_norm_of(jnp.concatenate([field[0], field[rows - 1]], axis=0), 10**10)
    up, down = exchange(edges[:cols], edges[cols:], "row")
    normed = half_norm_of(flat, 10**9)
    expanded = expand(normed, w_expand)
    up, down, normed, expanded = lax.optimization_barrier((up, down, normed, expanded))
    tile = normed.reshape(rows, cols, channels)
    spare = jnp.zeros((round_up(rows + 2, 16) - rows - 2, channels), jnp.bfloat16)
    first = jnp.concatenate([up[:1], tile[:, 0], down[:1], spare], axis=0)
    last = jnp.concatenate([up[cols - 1 :], tile[:, cols - 1], down[cols - 1 :], spare], axis=0)
    left, right = exchange(first, last, "col")
    pairwise = 8 <= devices <= 16 and devices & (devices - 1) == 0 and col_devices % 2 == 0
    if pairwise:
        plan = exchange_plan(row_devices, col_devices)
        own = lax.axis_index(("row", "col")).reshape(1)
    else:
        plan = [0], 0, 1
        own = jnp.zeros(1, jnp.int32)
    size = tokens // (len(plan[0]) * plan[2])
    mixed, *outgoing = mix(
        own, plan, size, expanded, flat, up, down, left, right, w_expand, depth_kernel, w_project,
        perm, rows, cols,
    )

    def route(outgoing, outward):
        if pairwise:
            return trade(plan, outgoing)
        return trade_all(outgoing, sets_local, members, outward)

    outgoing = attend(plan, route(outgoing, True), w_qkv, sets_local)
    final = finish(own, plan, route(outgoing, False), back, w_out, mixed)
    return final.reshape(rows, cols, channels)


def solution(mesh):
    return jax.shard_map(
        shards,
        mesh=mesh,
        in_specs=(P(("field", "row"), "col", None), P(), P(), P(), P(), P()),
        out_specs=P(("field", "row"), "col", None),
        check_vma=False,
    )
```

```python
import functools
import math

import jax
import jax.numpy as jnp
import numpy as np
from jax import lax
from jax.experimental import pallas as pl
from jax.experimental.pallas import tpu as pltpu
from jax.sharding import PartitionSpec as P

HEADS = 16
GRID = 16
LANES = 128
MIB = 1024 * 1024
NT = (((1,), (1,)), ((), ()))


def layer_norm(inputs):
    average = jnp.mean(inputs, axis=-1, keepdims=True)
    centred = inputs - average
    variance = jnp.mean(centred * centred, axis=-1, keepdims=True)
    return centred * lax.rsqrt(variance + 1e-05)


def gelu_of_half(half):
    scale = math.sqrt(2.0 / math.pi)
    inner = half * (2.0 * scale + (8.0 * scale * 0.044715) * (half * half))
    return half + half * jnp.tanh(inner)


def matmul(a, b):
    return jnp.dot(a, b, preferred_element_type=jnp.float32)


def matmul_nt(a, b):
    return lax.dot_general(a, b, NT, preferred_element_type=jnp.float32)


def divisor(size, most, unit):
    best = size
    for piece in range(unit, most + 1, unit):
        if size % piece == 0:
            best = piece
    return best


def round_up(size, unit):
    return -(-size // unit) * unit


def vmem():
    return pl.BlockSpec(memory_space=pltpu.VMEM)


def half_norm(inputs):
    return (layer_norm(inputs) * 0.5).astype(jnp.bfloat16)


def half_norm_kernel(in_ref, out_ref):
    rows = in_ref.shape[0]
    step = divisor(rows, 128, 16)
    for start in range(0, rows, step):
        out_ref[start : start + step, :] = half_norm(in_ref[start : start + step, :])


def half_norm_of(inputs, work):
    return pl.pallas_call(
        half_norm_kernel,
        in_specs=[pl.BlockSpec(inputs.shape, lambda: (0, 0))],
        out_specs=pl.BlockSpec(inputs.shape, lambda: (0, 0)),
        out_shape=jax.ShapeDtypeStruct(inputs.shape, jnp.bfloat16),
        compiler_params=pltpu.CompilerParams(vmem_limit_bytes=8 * MIB),
        cost_estimate=pl.CostEstimate(
            flops=work, bytes_accessed=6 * inputs.size, transcendentals=inputs.shape[0]
        ),
        name="half_norm",
    )(inputs)


def padded_rows(tokens):
    return tokens + 16


def expand_kernel(normed_ref, weight_ref, out_ref):
    tokens = normed_ref.shape[0]
    tile = weight_ref.shape[1]
    step = divisor(tokens, 128, 16)
    for start in range(0, tokens, step):
        made = gelu_of_half(matmul(normed_ref[start : start + step, :], weight_ref[...]))
        for sub in range(tile // LANES):
            row = sub * padded_rows(tokens) + 8 + start
            out_ref[row : row + step, :] = made[:, sub * LANES : (sub + 1) * LANES]


def expand(normed, w_expand):
    tokens, channels = normed.shape
    width = w_expand.shape[1]
    tile = divisor(width, 512, LANES)
    block = tile // LANES * padded_rows(tokens)
    return pl.pallas_call(
        expand_kernel,
        grid=(width // tile,),
        in_specs=[
            pl.BlockSpec((tokens, channels), lambda j: (0, 0)),
            pl.BlockSpec((channels, tile), lambda j: (0, j)),
        ],
        out_specs=pl.BlockSpec((block, LANES), lambda j: (j, 0)),
        out_shape=jax.ShapeDtypeStruct((width // LANES * padded_rows(tokens), LANES), jnp.float32),
        compiler_params=pltpu.CompilerParams(vmem_limit_bytes=12 * MIB),
        cost_estimate=pl.CostEstimate(
            flops=10**10,
            bytes_accessed=tokens * channels * 2 + channels * width * 2 + tokens * width * 4,
            transcendentals=tokens * width,
        ),
        name="expand",
    )(normed, w_expand)


def mix_kernel(
    own_ref, expanded_ref, field_ref, up_ref, down_ref, left_ref, right_ref, w_expand_ref, depth_ref,
    w_project_ref, perm_ref, mixed_ref, *refs, rows, cols, plan, size,
):
    masks, _, sides = plan
    sent = len(outgoing_shapes(plan, size, 1))
    slab_refs = refs[:sent]
    total_ref, normed_ref, grouped_ref, even_ref, odd_ref, even_halo_ref, odd_halo_ref = refs[sent:]
    tokens = rows * cols
    width = w_expand_ref.shape[1]
    tile = even_ref.shape[1]
    slot = left_ref.shape[0]
    up_start, down_start, left_start = 8, 16 + cols, 24 + 2 * cols
    right_start = left_start + slot

    edges = jnp.concatenate(
        [up_ref[...], down_ref[...], left_ref[...], right_ref[...]], axis=0
    )

    def expand_halo(index, out_ref):
        lanes = pl.ds(pl.multiple_of(index * tile, tile), tile)
        made = gelu_of_half(matmul(edges, w_expand_ref[:, lanes]))
        for sub in range(tile // LANES):
            part = made[:, sub * LANES : (sub + 1) * LANES]
            out_ref[sub, up_start : up_start + cols] = part[:cols]
            out_ref[sub, down_start : down_start + cols] = part[cols : 2 * cols]
            out_ref[sub, left_start : left_start + 2 * slot] = part[2 * cols :]

    position = lax.broadcasted_iota(jnp.int32, (8, LANES), 0)
    at_first = position == 0
    at_last = position == 7

    def convolve(index, out_ref, halo_ref):
        for sub in range(tile // LANES):
            lanes = pl.ds(pl.multiple_of(index * tile + sub * LANES, LANES), LANES)
            base = (index * (tile // LANES) + sub) * padded_rows(tokens) + 8
            taps = [[0.5 * depth_ref[p, q : q + 1, lanes] for q in range(3)] for p in range(3)]
            sums = {}
            for y in range(-1, rows + 1):
                if y < 0:
                    parts = [halo_ref[sub, up_start + q : up_start + q + cols] for q in (-1, 0, 1)]
                elif y == rows:
                    parts = [
                        halo_ref[sub, down_start + q : down_start + q + cols] for q in (-1, 0, 1)
                    ]
                else:
                    parts = [
                        expanded_ref[pl.ds(base + (y * cols + q), cols), :] for q in (-1, 0, 1)
                    ]
                left = halo_ref[sub, left_start + y + 1 : left_start + y + 2]
                right = halo_ref[sub, right_start + y + 1 : right_start + y + 2]
                parts[0] = jnp.concatenate(
                    [jnp.where(at_first, left, parts[0][:8]), parts[0][8:]], axis=0
                )
                parts[2] = jnp.concatenate(
                    [parts[2][:-8], jnp.where(at_last, right, parts[2][-8:])], axis=0
                )
                for p in range(3):
                    target = y + 1 - p
                    if 0 <= target < rows:
                        for q in range(3):
                            term = taps[p][q] * parts[q]
                            sums[target] = sums[target] + term if target in sums else term
                if y > 0:
                    out_ref[
                        (y - 1) * cols : y * cols, sub * LANES : (sub + 1) * LANES
                    ] = gelu_of_half(sums.pop(y - 1)).astype(jnp.bfloat16)

    def project(index, in_ref):
        piece = pl.ds(pl.multiple_of(index * tile, tile), tile)
        total_ref[...] += matmul(in_ref[...], w_project_ref[piece, :])

    total_ref[...] = field_ref[...]
    expand_halo(0, even_halo_ref)
    expand_halo(1, odd_halo_ref)
    convolve(0, even_ref, even_halo_ref)

    def body(index, carry):
        project(2 * index, even_ref)
        convolve(2 * index + 1, odd_ref, odd_halo_ref)
        expand_halo(2 * index + 2, even_halo_ref)
        project(2 * index + 1, odd_ref)
        convolve(2 * index + 2, even_ref, even_halo_ref)
        expand_halo(2 * index + 3, odd_halo_ref)
        return carry

    pairs = width // tile // 2
    lax.fori_loop(0, pairs - 1, body, 0)
    project(2 * pairs - 2, even_ref)
    convolve(2 * pairs - 1, odd_ref, odd_halo_ref)
    project(2 * pairs - 1, odd_ref)

    step = divisor(tokens, 128, 16)
    for start in range(0, tokens, step):
        piece = slice(start, start + step)
        mixed = total_ref[piece, :]
        mixed_ref[piece, :] = mixed
        normed_ref[piece, :] = layer_norm(mixed).astype(jnp.bfloat16)
    grouped_ref[...] = matmul(perm_ref[...], normed_ref[...]).astype(jnp.bfloat16)
    for index, mask in enumerate(masks):
        for side in range(sides):
            start = pl.multiple_of((own_ref[0] ^ (mask | side)) * size, 16)
            write_block(
                plan, slab_refs, index, side, slice(None), grouped_ref[pl.ds(start, size), :]
            )


def mix(
    own, plan, size, expanded, field, up, down, left, right, w_expand, depth_kernel, w_project, perm,
    rows, cols,
):
    tokens, channels = field.shape
    width = w_expand.shape[1]
    tile = divisor(width // 2, 256, LANES)
    slot = left.shape[0]
    sent = outgoing_shapes(plan, size, channels)
    halo = pltpu.VMEM((tile // LANES, 24 + 2 * cols + 2 * slot, LANES), jnp.float32)
    return pl.pallas_call(
        functools.partial(mix_kernel, rows=rows, cols=cols, plan=plan, size=size),
        in_specs=[pl.BlockSpec(memory_space=pltpu.SMEM)] + [vmem()] * 10,
        out_specs=[vmem()] * (1 + len(sent)),
        out_shape=[jax.ShapeDtypeStruct((tokens, channels), jnp.float32)]
        + [jax.ShapeDtypeStruct(shape, jnp.bfloat16) for shape in sent],
        scratch_shapes=[
            pltpu.VMEM((tokens, channels), jnp.float32),
            pltpu.VMEM((tokens, channels), jnp.bfloat16),
            pltpu.VMEM((tokens, channels), jnp.bfloat16),
            pltpu.VMEM((tokens, tile), jnp.bfloat16),
            pltpu.VMEM((tokens, tile), jnp.bfloat16),
            halo,
            halo,
        ],
        compiler_params=pltpu.CompilerParams(vmem_limit_bytes=8 * MIB),
        cost_estimate=pl.CostEstimate(
            flops=2 * tokens * channels * width,
            bytes_accessed=tokens * channels * 10 + 4 * channels * width + tokens * width * 4,
            transcendentals=tokens * width,
        ),
        name="mix",
    )(own, expanded, field, up, down, left, right, w_expand, depth_kernel, w_project, perm)


def identity(size):
    row = lax.broadcasted_iota(jnp.int32, (size, size), 0)
    column = lax.broadcasted_iota(jnp.int32, (size, size), 1)
    return jnp.where(row == column, 1.0, 0.0).astype(jnp.bfloat16)


def attend_kernel(*refs, plan, sets, came):
    masks, _, sides = plan
    slabs = len(masks)
    _, size, channels = refs[0].shape
    in_refs, weight_ref, out_refs = refs[:came], refs[came], refs[came + 1 : -6]
    query_ref, key_ref, value_ref, turned_ref, even_ref, odd_ref = refs[-6:]
    members = size // sets
    count = slabs * sides * members
    head_width = channels // HEADS
    group_heads = LANES // head_width
    groups = channels // LANES
    factor = math.log2(math.e) / math.sqrt(head_width)
    lane = lax.broadcasted_iota(jnp.int32, (1, LANES), 1)
    masks = [
        jnp.where((lane >= j * head_width) & (lane < (j + 1) * head_width), 1.0, 0.0).astype(
            jnp.bfloat16
        )
        for j in range(group_heads)
    ]
    turn_values = identity(channels)
    for s in range(sets):
        piece = slice(s * members, (s + 1) * members)
        block = jnp.concatenate(
            [
                read_block(plan, in_refs, index, side, piece)
                for index in range(slabs)
                for side in range(sides)
            ],
            axis=0,
        )
        qkv = matmul(block, weight_ref[...]).astype(jnp.bfloat16)
        values = matmul_nt(turn_values, qkv[:, 2 * channels :]).astype(jnp.bfloat16)
        for group in range(groups):
            lanes = slice(group * LANES, (group + 1) * LANES)
            query_ref[s * groups + group] = qkv[:, lanes]
            key_ref[s * groups + group] = qkv[:, channels + group * LANES : channels + (group + 1) * LANES]
            for j in range(group_heads):
                head = (group * group_heads + j) * head_width
                value_ref[s * groups + group, j, :head_width] = values[head : head + head_width]
                value_ref[s * groups + group, j, head_width:] = jnp.ones((16, count), jnp.bfloat16)

    def scores(index, out):
        keys = key_ref[index]
        stacked = jnp.concatenate([keys * mask for mask in masks], axis=0)
        out[...] = matmul_nt(stacked, query_ref[index])

    def weigh(index, scores_ref):
        for j in range(group_heads):
            part = scores_ref[j * count : (j + 1) * count]
            highest = jnp.max(part, axis=0, keepdims=True)
            raised = jnp.exp2((part - highest) * factor).astype(jnp.bfloat16)
            product = matmul(value_ref[index, j], raised)
            scale = 1.0 / product[head_width : head_width + 1]
            turned_ref[index, j * head_width : (j + 1) * head_width] = (
                product[:head_width] * scale
            ).astype(jnp.bfloat16)

    total = sets * groups
    scores(0, even_ref)

    def body(pair, carry):
        scores(2 * pair + 1, odd_ref)
        weigh(2 * pair, even_ref)
        scores(jnp.minimum(2 * pair + 2, total - 1), even_ref)
        weigh(2 * pair + 1, odd_ref)
        return carry

    lax.fori_loop(0, total // 2, body, 0)
    turn_tokens = identity(count)
    for s in range(sets):
        turned = turned_ref[s * groups : (s + 1) * groups].reshape(channels, count)
        attended = matmul_nt(turn_tokens, turned).astype(jnp.bfloat16)
        for index in range(slabs):
            for side in range(sides):
                start = (index * sides + side) * members
                write_block(
                    plan, out_refs, index, side, slice(s * members, (s + 1) * members),
                    attended[start : start + members],
                )


def attend(plan, incoming, w_qkv, sets):
    masks, _, sides = plan
    _, size, channels = incoming[0].shape
    count = len(masks) * sides * size // sets
    sent = outgoing_shapes(plan, size, channels)
    head_width = channels // HEADS
    group_heads = LANES // head_width
    total = sets * channels // LANES
    return pl.pallas_call(
        functools.partial(attend_kernel, plan=plan, sets=sets, came=len(incoming)),
        in_specs=[vmem()] * (len(incoming) + 1),
        out_specs=[vmem()] * len(sent),
        out_shape=[jax.ShapeDtypeStruct(shape, jnp.bfloat16) for shape in sent],
        scratch_shapes=[
            pltpu.VMEM((total, count, LANES), jnp.bfloat16),
            pltpu.VMEM((total, count, LANES), jnp.bfloat16),
            pltpu.VMEM((total, group_heads, head_width + 16, count), jnp.bfloat16),
            pltpu.VMEM((total, LANES, count), jnp.bfloat16),
            pltpu.VMEM((group_heads * count, count), jnp.float32),
            pltpu.VMEM((group_heads * count, count), jnp.float32),
        ],
        compiler_params=pltpu.CompilerParams(vmem_limit_bytes=10 * MIB),
        cost_estimate=pl.CostEstimate(
            flops=sets * (2 * count * channels * channels * 3 + 4 * count * count * channels),
            bytes_accessed=4 * sets * count * channels + 6 * channels * channels,
            transcendentals=sets * HEADS * count * count,
        ),
        name="attend",
    )(*incoming, w_qkv)


def finish_kernel(own_ref, *refs, plan):
    masks, _, sides = plan
    in_refs, rest = refs[:-7], refs[-7:]
    back_ref, weight_ref, mixed_ref, out_ref, attended_ref, made_ref, sent = rest
    tokens = mixed_ref.shape[0]
    size = in_refs[0].shape[1]
    for index, mask in enumerate(masks):
        for side in range(sides):
            start = pl.multiple_of((own_ref[0] ^ (mask | side)) * size, 16)
            attended_ref[pl.ds(start, size), :] = read_block(
                plan, in_refs, index, side, slice(None)
            )
    step = made_ref.shape[1]
    copies = []
    for index, start in enumerate(range(0, tokens, step)):
        rows = slice(start, start + step)
        restored = matmul(back_ref[rows, :], attended_ref[...]).astype(jnp.bfloat16)
        made_ref[index] = mixed_ref[rows, :] + matmul(restored, weight_ref[...])
        copy = pltpu.make_async_copy(
            made_ref.at[index], out_ref.at[pl.ds(start, step)], sent.at[index]
        )
        copy.start()
        copies.append(copy)
    for copy in copies:
        copy.wait()


def finish(own, plan, incoming, back, w_out, mixed):
    tokens, channels = mixed.shape
    step = divisor(tokens, 128, 16)
    return pl.pallas_call(
        functools.partial(finish_kernel, plan=plan),
        in_specs=[pl.BlockSpec(memory_space=pltpu.SMEM)] + [vmem()] * (len(incoming) + 3),
        out_specs=pl.BlockSpec(memory_space=pltpu.HBM),
        out_shape=jax.ShapeDtypeStruct((tokens, channels), jnp.float32),
        scratch_shapes=[
            pltpu.VMEM((tokens, channels), jnp.bfloat16),
            pltpu.VMEM((tokens // step, step, channels), jnp.float32),
            pltpu.SemaphoreType.DMA((tokens // step,)),
        ],
        compiler_params=pltpu.CompilerParams(vmem_limit_bytes=6 * MIB),
        name="finish",
    )(own, *incoming, back, w_out, mixed)


def exchange(low_edge, high_edge, axis):
    count = lax.axis_size(axis)
    even = lax.axis_index(axis) % 2 == 0

    def swap(edge, start):
        pairs = [(i, i + 1) for i in range(start, count - 1, 2)]
        return lax.ppermute(edge, axis, pairs + [(b, a) for a, b in pairs])

    one = swap(jnp.where(even, high_edge, low_edge), 0)
    two = swap(jnp.where(even, low_edge, high_edge), 1)
    return jnp.where(even, two, one), jnp.where(even, one, two)


def exchange_plan(row_devices, col_devices):
    devices = row_devices * col_devices
    crossing = list(range(devices - 2, devices // 2 - 1, -2))
    others = list(range(devices // 2 - 2, 0, -2))
    masks = crossing[:1]
    for index, mask in enumerate(crossing[1:]):
        masks += [mask] + others[index : index + 1]
    return masks + [0], min(2, len(masks)), 2


def outgoing_shapes(plan, size, channels):
    masks, late, sides = plan
    if sides == 1:
        return [(1, size, channels)]
    early = len(masks) - 1 - late
    return [(2, size, channels)] * late + [
        (1, size, channels), (early + 1, size, channels), (early, size, channels)
    ]


def write_block(plan, refs, index, side, rows, value):
    masks, late, sides = plan
    if sides == 1:
        refs[0][0, rows] = value
    elif index < late:
        refs[index][side, rows] = value
    elif index == len(masks) - 1:
        refs[late + side][0, rows] = value
    elif side == 0:
        refs[late + 2][index - late, rows] = value
    else:
        refs[late + 1][index - late + 1, rows] = value


def read_block(plan, refs, index, side, rows):
    masks, late, sides = plan
    if sides == 1:
        return refs[0][0, rows]
    if index < late:
        return refs[index + side * len(masks)][side, rows]
    if index == len(masks) - 1:
        return refs[index + side * (late + 1)][0, rows]
    return refs[index][side, rows]


def join_kernel(own_ref, swapped_ref, *out_refs):
    for index, out_ref in enumerate(out_refs):
        out_ref[0] = own_ref[index]
        out_ref[1] = swapped_ref[index + 1]


def join(own, swapped):
    early, size, channels = own.shape
    return pl.pallas_call(
        join_kernel,
        in_specs=[vmem()] * 2,
        out_specs=[vmem()] * early,
        out_shape=[jax.ShapeDtypeStruct((2, size, channels), own.dtype)] * early,
        compiler_params=pltpu.CompilerParams(vmem_limit_bytes=2 * MIB),
        name="join",
    )(own, swapped)


def trade(plan, outgoing):
    masks, late, _ = plan
    devices = lax.axis_size("row") * lax.axis_size("col")

    def swap(slab, mask):
        return lax.ppermute(slab, ("row", "col"), [(i, i ^ mask) for i in range(devices)])

    slabs, (kept, passed, own) = outgoing[:late], outgoing[late:]
    swapped = swap(passed, 1)
    first = [swap(slab, mask) for slab, mask in zip(slabs, masks)]
    rest = [swap(slab, mask) for slab, mask in zip(join(own, swapped), masks[late:-1])]
    tie = min(1, len(rest) - 1)
    *first, rest[tie] = lax.optimization_barrier((*first, rest[tie]))
    return [*first, *rest, kept, *[swap(slab, 1) for slab in first], swapped]


def trade_all(slabs, sets, members, outward):
    axes = ("row", "col")
    channels = slabs[0].shape[-1]
    block = slabs[0].reshape(-1, channels)
    devices = block.shape[0] // (sets * members)
    if not outward:
        block = block.reshape(sets, devices, members, channels).transpose(1, 0, 2, 3)
    block = block.reshape(devices, sets * members, channels)
    block = lax.all_to_all(block, axes, 0, 0, tiled=True)
    if outward:
        block = block.reshape(devices, sets, members, channels).transpose(1, 0, 2, 3)
    return [block.reshape(1, -1, channels)]


def grouping(rows, cols, blocks_rows, blocks_cols):
    order = np.arange(rows * cols).reshape(
        blocks_rows, rows // blocks_rows, blocks_cols, cols // blocks_cols
    )
    order = order.transpose(1, 3, 0, 2).reshape(-1)
    matrix = np.zeros((order.size, order.size), np.float32)
    matrix[np.arange(order.size), order] = 1.0
    return matrix


def shards(field, w_expand, depth_kernel, w_project, w_qkv, w_out):
    rows, cols, channels = field.shape
    tokens = rows * cols
    row_devices = lax.axis_size("row")
    col_devices = lax.axis_size("col")
    devices = row_devices * col_devices
    blocks_rows = GRID // row_devices
    blocks_cols = GRID // col_devices
    members = blocks_rows * blocks_cols
    sets_local = tokens // members // devices
    matrix = grouping(rows, cols, blocks_rows, blocks_cols)
    perm = jnp.asarray(matrix, jnp.bfloat16)
    back = jnp.asarray(matrix.T, jnp.bfloat16)

    flat = field.reshape(tokens, channels)
    edges = half_norm_of(jnp.concatenate([field[0], field[rows - 1]], axis=0), 10**10)
    up, down = exchange(edges[:cols], edges[cols:], "row")
    normed = half_norm_of(flat, 10**9)
    expanded = expand(normed, w_expand)
    up, down, normed, expanded = lax.optimization_barrier((up, down, normed, expanded))
    tile = normed.reshape(rows, cols, channels)
    spare = jnp.zeros((round_up(rows + 2, 16) - rows - 2, channels), jnp.bfloat16)
    first = jnp.concatenate([up[:1], tile[:, 0], down[:1], spare], axis=0)
    last = jnp.concatenate([up[cols - 1 :], tile[:, cols - 1], down[cols - 1 :], spare], axis=0)
    left, right = exchange(first, last, "col")
    pairwise = 8 <= devices <= 16 and devices & (devices - 1) == 0 and col_devices % 2 == 0
    if pairwise:
        plan = exchange_plan(row_devices, col_devices)
        own = lax.axis_index(("row", "col")).reshape(1)
    else:
        plan = [0], 0, 1
        own = jnp.zeros(1, jnp.int32)
    size = tokens // (len(plan[0]) * plan[2])
    mixed, *outgoing = mix(
        own, plan, size, expanded, flat, up, down, left, right, w_expand, depth_kernel, w_project,
        perm, rows, cols,
    )

    def route(outgoing, outward):
        if pairwise:
            return trade(plan, outgoing)
        return trade_all(outgoing, sets_local, members, outward)

    outgoing = attend(plan, route(outgoing, True), w_qkv, sets_local)
    final = finish(own, plan, route(outgoing, False), back, w_out, mixed)
    return final.reshape(rows, cols, channels)


def solution(mesh):
    return jax.shard_map(
        shards,
        mesh=mesh,
        in_specs=(P(("field", "row"), "col", None), P(), P(), P(), P(), P()),
        out_specs=P(("field", "row"), "col", None),
        check_vma=False,
    )
```

```python
import functools
import math

import jax
import jax.numpy as jnp
import numpy as np
from jax import lax
from jax.experimental import pallas as pl
from jax.experimental.pallas import tpu as pltpu
from jax.sharding import PartitionSpec as P

HEADS = 16
GRID = 16
LANES = 128
MIB = 1024 * 1024
NT = (((1,), (1,)), ((), ()))


def layer_norm(inputs):
    average = jnp.mean(inputs, axis=-1, keepdims=True)
    centred = inputs - average
    variance = jnp.mean(centred * centred, axis=-1, keepdims=True)
    return centred * lax.rsqrt(variance + 1e-05)


def gelu_of_half(half):
    scale = math.sqrt(2.0 / math.pi)
    inner = half * (2.0 * scale + (8.0 * scale * 0.044715) * (half * half))
    return half + half * jnp.tanh(inner)


def matmul(a, b):
    return jnp.dot(a, b, preferred_element_type=jnp.float32)


def matmul_nt(a, b):
    return lax.dot_general(a, b, NT, preferred_element_type=jnp.float32)


def divisor(size, most, unit):
    best = size
    for piece in range(unit, most + 1, unit):
        if size % piece == 0:
            best = piece
    return best


def round_up(size, unit):
    return -(-size // unit) * unit


def vmem():
    return pl.BlockSpec(memory_space=pltpu.VMEM)


def half_norm(inputs):
    return (layer_norm(inputs) * 0.5).astype(jnp.bfloat16)


def half_norm_kernel(in_ref, out_ref):
    rows = in_ref.shape[0]
    step = divisor(rows, 128, 16)
    for start in range(0, rows, step):
        out_ref[start : start + step, :] = half_norm(in_ref[start : start + step, :])


def half_norm_of(inputs, work):
    return pl.pallas_call(
        half_norm_kernel,
        in_specs=[vmem()],
        out_specs=vmem(),
        out_shape=jax.ShapeDtypeStruct(inputs.shape, jnp.bfloat16),
        compiler_params=pltpu.CompilerParams(vmem_limit_bytes=2 * MIB),
        cost_estimate=pl.CostEstimate(
            flops=work, bytes_accessed=6 * inputs.size, transcendentals=inputs.shape[0]
        ),
        name="half_norm",
    )(inputs)


def padded_rows(tokens):
    return tokens + 16


def expand_kernel(normed_ref, weight_ref, out_ref):
    tokens = normed_ref.shape[0]
    width = weight_ref.shape[1]
    tile = divisor(width, 512, LANES)
    step = divisor(tokens, 128, 16)
    starts = range(0, tokens, step)

    def body(index, carry):
        lanes = pl.ds(pl.multiple_of(index * tile, tile), tile)
        for start in starts:
            made = gelu_of_half(
                matmul(normed_ref[start : start + step, :], weight_ref[:, lanes])
            )
            for sub in range(tile // LANES):
                row = (index * (tile // LANES) + sub) * padded_rows(tokens) + 8 + start
                out_ref[pl.ds(pl.multiple_of(row, 8), step), :] = made[
                    :, sub * LANES : (sub + 1) * LANES
                ]
        return carry

    lax.fori_loop(0, width // tile, body, 0)


def expand(normed, w_expand):
    tokens, channels = normed.shape
    width = w_expand.shape[1]
    return pl.pallas_call(
        expand_kernel,
        in_specs=[vmem()] * 2,
        out_specs=vmem(),
        out_shape=jax.ShapeDtypeStruct((width // LANES * padded_rows(tokens), LANES), jnp.float32),
        compiler_params=pltpu.CompilerParams(vmem_limit_bytes=4 * MIB),
        cost_estimate=pl.CostEstimate(
            flops=10**10,
            bytes_accessed=tokens * channels * 2 + channels * width * 2 + tokens * width * 4,
            transcendentals=tokens * width,
        ),
        name="expand",
    )(normed, w_expand)


def mix_kernel(
    own_ref, expanded_ref, field_ref, up_ref, down_ref, left_ref, right_ref, w_expand_ref, depth_ref,
    w_project_ref, perm_ref, mixed_ref, *refs, rows, cols, plan, size,
):
    masks, _, sides = plan
    sent = len(outgoing_shapes(plan, size, 1))
    slab_refs = refs[:sent]
    total_ref, normed_ref, grouped_ref, even_ref, odd_ref, even_halo_ref, odd_halo_ref = refs[sent:]
    tokens = rows * cols
    width = w_expand_ref.shape[1]
    tile = even_ref.shape[1]
    slot = left_ref.shape[0]
    up_start, down_start, left_start = 8, 16 + cols, 24 + 2 * cols
    right_start = left_start + slot

    edges = jnp.concatenate(
        [up_ref[...], down_ref[...], left_ref[...], right_ref[...]], axis=0
    )

    def expand_halo(index, out_ref):
        lanes = pl.ds(pl.multiple_of(index * tile, tile), tile)
        made = gelu_of_half(matmul(edges, w_expand_ref[:, lanes]))
        for sub in range(tile // LANES):
            part = made[:, sub * LANES : (sub + 1) * LANES]
            out_ref[sub, up_start : up_start + cols] = part[:cols]
            out_ref[sub, down_start : down_start + cols] = part[cols : 2 * cols]
            out_ref[sub, left_start : left_start + 2 * slot] = part[2 * cols :]

    position = lax.broadcasted_iota(jnp.int32, (8, LANES), 0)
    at_first = position == 0
    at_last = position == 7

    def convolve(index, out_ref, halo_ref):
        for sub in range(tile // LANES):
            lanes = pl.ds(pl.multiple_of(index * tile + sub * LANES, LANES), LANES)
            base = (index * (tile // LANES) + sub) * padded_rows(tokens) + 8
            taps = [[0.5 * depth_ref[p, q : q + 1, lanes] for q in range(3)] for p in range(3)]
            sums = {}
            for y in range(-1, rows + 1):
                if y < 0:
                    parts = [halo_ref[sub, up_start + q : up_start + q + cols] for q in (-1, 0, 1)]
                elif y == rows:
                    parts = [
                        halo_ref[sub, down_start + q : down_start + q + cols] for q in (-1, 0, 1)
                    ]
                else:
                    parts = [
                        expanded_ref[pl.ds(base + (y * cols + q), cols), :] for q in (-1, 0, 1)
                    ]
                left = halo_ref[sub, left_start + y + 1 : left_start + y + 2]
                right = halo_ref[sub, right_start + y + 1 : right_start + y + 2]
                parts[0] = jnp.concatenate(
                    [jnp.where(at_first, left, parts[0][:8]), parts[0][8:]], axis=0
                )
                parts[2] = jnp.concatenate(
                    [parts[2][:-8], jnp.where(at_last, right, parts[2][-8:])], axis=0
                )
                for p in range(3):
                    target = y + 1 - p
                    if 0 <= target < rows:
                        for q in range(3):
                            term = taps[p][q] * parts[q]
                            sums[target] = sums[target] + term if target in sums else term
                if y > 0:
                    out_ref[
                        (y - 1) * cols : y * cols, sub * LANES : (sub + 1) * LANES
                    ] = gelu_of_half(sums.pop(y - 1)).astype(jnp.bfloat16)

    def project(index, in_ref):
        piece = pl.ds(pl.multiple_of(index * tile, tile), tile)
        total_ref[...] += matmul(in_ref[...], w_project_ref[piece, :])

    total_ref[...] = field_ref[...]
    expand_halo(0, even_halo_ref)
    expand_halo(1, odd_halo_ref)
    convolve(0, even_ref, even_halo_ref)

    def body(index, carry):
        project(2 * index, even_ref)
        convolve(2 * index + 1, odd_ref, odd_halo_ref)
        expand_halo(2 * index + 2, even_halo_ref)
        project(2 * index + 1, odd_ref)
        convolve(2 * index + 2, even_ref, even_halo_ref)
        expand_halo(2 * index + 3, odd_halo_ref)
        return carry

    pairs = width // tile // 2
    lax.fori_loop(0, pairs - 1, body, 0)
    project(2 * pairs - 2, even_ref)
    convolve(2 * pairs - 1, odd_ref, odd_halo_ref)
    project(2 * pairs - 1, odd_ref)

    step = divisor(tokens, 128, 16)
    for start in range(0, tokens, step):
        piece = slice(start, start + step)
        mixed = total_ref[piece, :]
        mixed_ref[piece, :] = mixed
        normed_ref[piece, :] = layer_norm(mixed).astype(jnp.bfloat16)
    grouped_ref[...] = matmul(perm_ref[...], normed_ref[...]).astype(jnp.bfloat16)
    for index, mask in enumerate(masks):
        for side in range(sides):
            start = pl.multiple_of((own_ref[0] ^ (mask | side)) * size, 16)
            write_block(
                plan, slab_refs, index, side, slice(None), grouped_ref[pl.ds(start, size), :]
            )


def mix(
    own, plan, size, expanded, field, up, down, left, right, w_expand, depth_kernel, w_project, perm,
    rows, cols,
):
    tokens, channels = field.shape
    width = w_expand.shape[1]
    tile = divisor(width // 2, 256, LANES)
    slot = left.shape[0]
    sent = outgoing_shapes(plan, size, channels)
    halo = pltpu.VMEM((tile // LANES, 24 + 2 * cols + 2 * slot, LANES), jnp.float32)
    return pl.pallas_call(
        functools.partial(mix_kernel, rows=rows, cols=cols, plan=plan, size=size),
        in_specs=[pl.BlockSpec(memory_space=pltpu.SMEM)] + [vmem()] * 10,
        out_specs=[vmem()] * (1 + len(sent)),
        out_shape=[jax.ShapeDtypeStruct((tokens, channels), jnp.float32)]
        + [jax.ShapeDtypeStruct(shape, jnp.bfloat16) for shape in sent],
        scratch_shapes=[
            pltpu.VMEM((tokens, channels), jnp.float32),
            pltpu.VMEM((tokens, channels), jnp.bfloat16),
            pltpu.VMEM((tokens, channels), jnp.bfloat16),
            pltpu.VMEM((tokens, tile), jnp.bfloat16),
            pltpu.VMEM((tokens, tile), jnp.bfloat16),
            halo,
            halo,
        ],
        compiler_params=pltpu.CompilerParams(vmem_limit_bytes=8 * MIB),
        cost_estimate=pl.CostEstimate(
            flops=2 * tokens * channels * width,
            bytes_accessed=tokens * channels * 10 + 4 * channels * width + tokens * width * 4,
            transcendentals=tokens * width,
        ),
        name="mix",
    )(own, expanded, field, up, down, left, right, w_expand, depth_kernel, w_project, perm)


def identity(size):
    row = lax.broadcasted_iota(jnp.int32, (size, size), 0)
    column = lax.broadcasted_iota(jnp.int32, (size, size), 1)
    return jnp.where(row == column, 1.0, 0.0).astype(jnp.bfloat16)


def attend_kernel(*refs, plan, sets, came):
    masks, _, sides = plan
    slabs = len(masks)
    _, size, channels = refs[0].shape
    in_refs, weight_ref, out_refs = refs[:came], refs[came], refs[came + 1 : -6]
    query_ref, key_ref, value_ref, turned_ref, even_ref, odd_ref = refs[-6:]
    members = size // sets
    count = slabs * sides * members
    head_width = channels // HEADS
    group_heads = LANES // head_width
    groups = channels // LANES
    factor = math.log2(math.e) / math.sqrt(head_width)
    lane = lax.broadcasted_iota(jnp.int32, (1, LANES), 1)
    masks = [
        jnp.where((lane >= j * head_width) & (lane < (j + 1) * head_width), 1.0, 0.0).astype(
            jnp.bfloat16
        )
        for j in range(group_heads)
    ]
    turn_values = identity(channels)
    for s in range(sets):
        piece = slice(s * members, (s + 1) * members)
        block = jnp.concatenate(
            [
                read_block(plan, in_refs, index, side, piece)
                for index in range(slabs)
                for side in range(sides)
            ],
            axis=0,
        )
        qkv = matmul(block, weight_ref[...]).astype(jnp.bfloat16)
        values = matmul_nt(turn_values, qkv[:, 2 * channels :]).astype(jnp.bfloat16)
        for group in range(groups):
            lanes = slice(group * LANES, (group + 1) * LANES)
            query_ref[s * groups + group] = qkv[:, lanes]
            key_ref[s * groups + group] = qkv[:, channels + group * LANES : channels + (group + 1) * LANES]
            for j in range(group_heads):
                head = (group * group_heads + j) * head_width
                value_ref[s * groups + group, j, :head_width] = values[head : head + head_width]
                value_ref[s * groups + group, j, head_width:] = jnp.ones((16, count), jnp.bfloat16)

    def scores(index, out):
        keys = key_ref[index]
        stacked = jnp.concatenate([keys * mask for mask in masks], axis=0)
        out[...] = matmul_nt(stacked, query_ref[index])

    def weigh(index, scores_ref):
        for j in range(group_heads):
            part = scores_ref[j * count : (j + 1) * count]
            highest = jnp.max(part, axis=0, keepdims=True)
            raised = jnp.exp2((part - highest) * factor).astype(jnp.bfloat16)
            product = matmul(value_ref[index, j], raised)
            scale = 1.0 / product[head_width : head_width + 1]
            turned_ref[index, j * head_width : (j + 1) * head_width] = (
                product[:head_width] * scale
            ).astype(jnp.bfloat16)

    total = sets * groups
    scores(0, even_ref)

    def body(pair, carry):
        scores(2 * pair + 1, odd_ref)
        weigh(2 * pair, even_ref)
        scores(jnp.minimum(2 * pair + 2, total - 1), even_ref)
        weigh(2 * pair + 1, odd_ref)
        return carry

    lax.fori_loop(0, total // 2, body, 0)
    turn_tokens = identity(count)
    for s in range(sets):
        turned = turned_ref[s * groups : (s + 1) * groups].reshape(channels, count)
        attended = matmul_nt(turn_tokens, turned).astype(jnp.bfloat16)
        for index in range(slabs):
            for side in range(sides):
                start = (index * sides + side) * members
                write_block(
                    plan, out_refs, index, side, slice(s * members, (s + 1) * members),
                    attended[start : start + members],
                )


def attend(plan, incoming, w_qkv, sets):
    masks, _, sides = plan
    _, size, channels = incoming[0].shape
    count = len(masks) * sides * size // sets
    sent = outgoing_shapes(plan, size, channels)
    head_width = channels // HEADS
    group_heads = LANES // head_width
    total = sets * channels // LANES
    return pl.pallas_call(
        functools.partial(attend_kernel, plan=plan, sets=sets, came=len(incoming)),
        in_specs=[vmem()] * (len(incoming) + 1),
        out_specs=[vmem()] * len(sent),
        out_shape=[jax.ShapeDtypeStruct(shape, jnp.bfloat16) for shape in sent],
        scratch_shapes=[
            pltpu.VMEM((total, count, LANES), jnp.bfloat16),
            pltpu.VMEM((total, count, LANES), jnp.bfloat16),
            pltpu.VMEM((total, group_heads, head_width + 16, count), jnp.bfloat16),
            pltpu.VMEM((total, LANES, count), jnp.bfloat16),
            pltpu.VMEM((group_heads * count, count), jnp.float32),
            pltpu.VMEM((group_heads * count, count), jnp.float32),
        ],
        compiler_params=pltpu.CompilerParams(vmem_limit_bytes=10 * MIB),
        cost_estimate=pl.CostEstimate(
            flops=sets * (2 * count * channels * channels * 3 + 4 * count * count * channels),
            bytes_accessed=4 * sets * count * channels + 6 * channels * channels,
            transcendentals=sets * HEADS * count * count,
        ),
        name="attend",
    )(*incoming, w_qkv)


def finish_kernel(own_ref, *refs, plan):
    masks, _, sides = plan
    in_refs, rest = refs[:-7], refs[-7:]
    back_ref, weight_ref, mixed_ref, out_ref, attended_ref, made_ref, sent = rest
    tokens = mixed_ref.shape[0]
    size = in_refs[0].shape[1]
    for index, mask in enumerate(masks):
        for side in range(sides):
            start = pl.multiple_of((own_ref[0] ^ (mask | side)) * size, 16)
            attended_ref[pl.ds(start, size), :] = read_block(
                plan, in_refs, index, side, slice(None)
            )
    step = made_ref.shape[1]
    copies = []
    for index, start in enumerate(range(0, tokens, step)):
        rows = slice(start, start + step)
        restored = matmul(back_ref[rows, :], attended_ref[...]).astype(jnp.bfloat16)
        made_ref[index] = mixed_ref[rows, :] + matmul(restored, weight_ref[...])
        copy = pltpu.make_async_copy(
            made_ref.at[index], out_ref.at[pl.ds(start, step)], sent.at[index]
        )
        copy.start()
        copies.append(copy)
    for copy in copies:
        copy.wait()


def finish(own, plan, incoming, back, w_out, mixed):
    tokens, channels = mixed.shape
    step = divisor(tokens, 128, 16)
    return pl.pallas_call(
        functools.partial(finish_kernel, plan=plan),
        in_specs=[pl.BlockSpec(memory_space=pltpu.SMEM)] + [vmem()] * (len(incoming) + 3),
        out_specs=pl.BlockSpec(memory_space=pltpu.HBM),
        out_shape=jax.ShapeDtypeStruct((tokens, channels), jnp.float32),
        scratch_shapes=[
            pltpu.VMEM((tokens, channels), jnp.bfloat16),
            pltpu.VMEM((tokens // step, step, channels), jnp.float32),
            pltpu.SemaphoreType.DMA((tokens // step,)),
        ],
        compiler_params=pltpu.CompilerParams(vmem_limit_bytes=6 * MIB),
        name="finish",
    )(own, *incoming, back, w_out, mixed)


def exchange(low_edge, high_edge, axis):
    count = lax.axis_size(axis)
    even = lax.axis_index(axis) % 2 == 0

    def swap(edge, start):
        pairs = [(i, i + 1) for i in range(start, count - 1, 2)]
        return lax.ppermute(edge, axis, pairs + [(b, a) for a, b in pairs])

    one = swap(jnp.where(even, high_edge, low_edge), 0)
    two = swap(jnp.where(even, low_edge, high_edge), 1)
    return jnp.where(even, two, one), jnp.where(even, one, two)


def exchange_plan(row_devices, col_devices):
    devices = row_devices * col_devices
    crossing = list(range(devices - 2, devices // 2 - 1, -2))
    others = list(range(devices // 2 - 2, 0, -2))
    masks = crossing[:1]
    for index, mask in enumerate(crossing[1:]):
        masks += [mask] + others[index : index + 1]
    return masks + [0], min(2, len(masks)), 2


def outgoing_shapes(plan, size, channels):
    masks, late, sides = plan
    if sides == 1:
        return [(1, size, channels)]
    early = len(masks) - 1 - late
    return [(2, size, channels)] * late + [
        (1, size, channels), (early + 1, size, channels), (early, size, channels)
    ]


def write_block(plan, refs, index, side, rows, value):
    masks, late, sides = plan
    if sides == 1:
        refs[0][0, rows] = value
    elif index < late:
        refs[index][side, rows] = value
    elif index == len(masks) - 1:
        refs[late + side][0, rows] = value
    elif side == 0:
        refs[late + 2][index - late, rows] = value
    else:
        refs[late + 1][index - late + 1, rows] = value


def read_block(plan, refs, index, side, rows):
    masks, late, sides = plan
    if sides == 1:
        return refs[0][0, rows]
    if index < late:
        return refs[index + side * len(masks)][side, rows]
    if index == len(masks) - 1:
        return refs[index + side * (late + 1)][0, rows]
    return refs[index][side, rows]


def join_kernel(own_ref, swapped_ref, *out_refs):
    for index, out_ref in enumerate(out_refs):
        out_ref[0] = own_ref[index]
        out_ref[1] = swapped_ref[index + 1]


def join(own, swapped):
    early, size, channels = own.shape
    return pl.pallas_call(
        join_kernel,
        in_specs=[vmem()] * 2,
        out_specs=[vmem()] * early,
        out_shape=[jax.ShapeDtypeStruct((2, size, channels), own.dtype)] * early,
        compiler_params=pltpu.CompilerParams(vmem_limit_bytes=2 * MIB),
        name="join",
    )(own, swapped)


def trade(plan, outgoing):
    masks, late, _ = plan
    devices = lax.axis_size("row") * lax.axis_size("col")

    def swap(slab, mask):
        return lax.ppermute(slab, ("row", "col"), [(i, i ^ mask) for i in range(devices)])

    slabs, (kept, passed, own) = outgoing[:late], outgoing[late:]
    swapped = swap(passed, 1)
    first = [swap(slab, mask) for slab, mask in zip(slabs, masks)]
    rest = [swap(slab, mask) for slab, mask in zip(join(own, swapped), masks[late:-1])]
    tie = min(1, len(rest) - 1)
    *first, rest[tie] = lax.optimization_barrier((*first, rest[tie]))
    return [*first, *rest, kept, *[swap(slab, 1) for slab in first], swapped]


def trade_all(slabs, sets, members, outward):
    axes = ("row", "col")
    channels = slabs[0].shape[-1]
    block = slabs[0].reshape(-1, channels)
    devices = block.shape[0] // (sets * members)
    if not outward:
        block = block.reshape(sets, devices, members, channels).transpose(1, 0, 2, 3)
    block = block.reshape(devices, sets * members, channels)
    block = lax.all_to_all(block, axes, 0, 0, tiled=True)
    if outward:
        block = block.reshape(devices, sets, members, channels).transpose(1, 0, 2, 3)
    return [block.reshape(1, -1, channels)]


def grouping(rows, cols, blocks_rows, blocks_cols):
    order = np.arange(rows * cols).reshape(
        blocks_rows, rows // blocks_rows, blocks_cols, cols // blocks_cols
    )
    order = order.transpose(1, 3, 0, 2).reshape(-1)
    matrix = np.zeros((order.size, order.size), np.float32)
    matrix[np.arange(order.size), order] = 1.0
    return matrix


def shards(field, w_expand, depth_kernel, w_project, w_qkv, w_out):
    rows, cols, channels = field.shape
    tokens = rows * cols
    row_devices = lax.axis_size("row")
    col_devices = lax.axis_size("col")
    devices = row_devices * col_devices
    blocks_rows = GRID // row_devices
    blocks_cols = GRID // col_devices
    members = blocks_rows * blocks_cols
    sets_local = tokens // members // devices
    matrix = grouping(rows, cols, blocks_rows, blocks_cols)
    perm = jnp.asarray(matrix, jnp.bfloat16)
    back = jnp.asarray(matrix.T, jnp.bfloat16)

    flat = field.reshape(tokens, channels)
    edges = half_norm_of(jnp.concatenate([field[0], field[rows - 1]], axis=0), 10**10)
    up, down = exchange(edges[:cols], edges[cols:], "row")
    normed = half_norm_of(flat, 10**9)
    expanded = expand(normed, w_expand)
    up, down, normed, expanded = lax.optimization_barrier((up, down, normed, expanded))
    tile = normed.reshape(rows, cols, channels)
    spare = round_up(rows + 2, 16) - rows - 2
    first = jnp.concatenate([up[:1], tile[:, 0], down[:1], up[:spare]], axis=0)
    last = jnp.concatenate([up[cols - 1 :], tile[:, cols - 1], down[cols - 1 :], up[:spare]], axis=0)
    left, right = exchange(first, last, "col")
    pairwise = 8 <= devices <= 16 and devices & (devices - 1) == 0 and col_devices % 2 == 0
    if pairwise:
        plan = exchange_plan(row_devices, col_devices)
        own = lax.axis_index(("row", "col")).reshape(1)
    else:
        plan = [0], 0, 1
        own = jnp.zeros(1, jnp.int32)
    size = tokens // (len(plan[0]) * plan[2])
    mixed, *outgoing = mix(
        own, plan, size, expanded, flat, up, down, left, right, w_expand, depth_kernel, w_project,
        perm, rows, cols,
    )

    def route(outgoing, outward):
        if pairwise:
            return trade(plan, outgoing)
        return trade_all(outgoing, sets_local, members, outward)

    outgoing = attend(plan, route(outgoing, True), w_qkv, sets_local)
    final = finish(own, plan, route(outgoing, False), back, w_out, mixed)
    return final.reshape(rows, cols, channels)


def solution(mesh):
    return jax.shard_map(
        shards,
        mesh=mesh,
        in_specs=(P(("field", "row"), "col", None), P(), P(), P(), P(), P()),
        out_specs=P(("field", "row"), "col", None),
        check_vma=False,
    )
```

```python
import functools
import math

import jax
import jax.numpy as jnp
import numpy as np
from jax import lax
from jax.experimental import pallas as pl
from jax.experimental.pallas import tpu as pltpu
from jax.sharding import PartitionSpec as P

HEADS = 16
GRID = 16
LANES = 128
MIB = 1024 * 1024
NT = (((1,), (1,)), ((), ()))


def layer_norm(inputs):
    average = jnp.mean(inputs, axis=-1, keepdims=True)
    centred = inputs - average
    variance = jnp.mean(centred * centred, axis=-1, keepdims=True)
    return centred * lax.rsqrt(variance + 1e-05)


def gelu_of_half(half):
    scale = math.sqrt(2.0 / math.pi)
    inner = half * (2.0 * scale + (8.0 * scale * 0.044715) * (half * half))
    return half + half * jnp.tanh(inner)


def matmul(a, b):
    return jnp.dot(a, b, preferred_element_type=jnp.float32)


def matmul_nt(a, b):
    return lax.dot_general(a, b, NT, preferred_element_type=jnp.float32)


def divisor(size, most, unit):
    best = size
    for piece in range(unit, most + 1, unit):
        if size % piece == 0:
            best = piece
    return best


def round_up(size, unit):
    return -(-size // unit) * unit


def vmem():
    return pl.BlockSpec(memory_space=pltpu.VMEM)


def half_norm(inputs):
    return (layer_norm(inputs) * 0.5).astype(jnp.bfloat16)


def half_norm_kernel(in_ref, out_ref):
    rows = in_ref.shape[0]
    step = divisor(rows, 128, 16)
    for start in range(0, rows, step):
        out_ref[start : start + step, :] = half_norm(in_ref[start : start + step, :])


def half_norm_of(inputs):
    return pl.pallas_call(
        half_norm_kernel,
        in_specs=[vmem()],
        out_specs=vmem(),
        out_shape=jax.ShapeDtypeStruct(inputs.shape, jnp.bfloat16),
        compiler_params=pltpu.CompilerParams(vmem_limit_bytes=4 * MIB),
        cost_estimate=pl.CostEstimate(
            flops=10**9, bytes_accessed=6 * inputs.size, transcendentals=inputs.shape[0]
        ),
        name="half_norm",
    )(inputs)


def choose(condition, one, two):
    flags = jnp.full((one.shape[0], 1), condition, jnp.int32) == 1
    return jnp.where(flags, one.astype(jnp.float32), two.astype(jnp.float32)).astype(one.dtype)


def edges_kernel(place_ref, top_ref, bottom_ref, one_ref, two_ref):
    odd = place_ref[1]
    top, bottom = half_norm(top_ref[...]), half_norm(bottom_ref[...])
    one_ref[...] = choose(odd, top, bottom)
    two_ref[...] = choose(odd, bottom, top)


def row_edges(place, top, bottom):
    return pl.pallas_call(
        edges_kernel,
        in_specs=[pl.BlockSpec(memory_space=pltpu.SMEM)] + [vmem()] * 2,
        out_specs=[vmem()] * 2,
        out_shape=[jax.ShapeDtypeStruct(top.shape, jnp.bfloat16)] * 2,
        compiler_params=pltpu.CompilerParams(vmem_limit_bytes=4 * MIB),
        cost_estimate=pl.CostEstimate(
            flops=10**10, bytes_accessed=12 * top.size, transcendentals=2 * top.shape[0]
        ),
        name="row_edges",
    )(place, top, bottom)


def picker(shape, pick):
    row = lax.broadcasted_iota(jnp.int32, shape, 0)
    column = lax.broadcasted_iota(jnp.int32, shape, 1)
    return jnp.where(pick(row, column), 1.0, 0.0).astype(jnp.bfloat16)


def strips_kernel(place_ref, normed_ref, row_one_ref, row_two_ref, up_ref, down_ref, one_ref, two_ref):
    tokens = normed_ref.shape[0]
    cols = up_ref.shape[0]
    rows = tokens // cols
    slot = one_ref.shape[0]
    odd_row, odd_col = place_ref[1], place_ref[2]
    up = choose(odd_row, row_one_ref[...], row_two_ref[...])
    down = choose(odd_row, row_two_ref[...], row_one_ref[...])
    up_ref[...] = up
    down_ref[...] = down
    strips = []
    for x in (0, cols - 1):
        body = picker(
            (slot, tokens), lambda i, j: (i >= 1) & (i <= rows) & (j == (i - 1) * cols + x)
        )
        head = picker((slot, cols), lambda i, j: (i == 0) & (j == x))
        foot = picker((slot, cols), lambda i, j: (i == rows + 1) & (j == x))
        strip = matmul(body, normed_ref[...]) + matmul(head, up) + matmul(foot, down)
        strips.append(strip.astype(jnp.bfloat16))
    one_ref[...] = choose(odd_col, strips[0], strips[1])
    two_ref[...] = choose(odd_col, strips[1], strips[0])


def column_strips(place, normed, row_one, row_two, slot):
    cols, channels = row_one.shape
    shapes = [(cols, channels)] * 2 + [(slot, channels)] * 2
    return pl.pallas_call(
        strips_kernel,
        in_specs=[pl.BlockSpec(memory_space=pltpu.SMEM)] + [vmem()] * 3,
        out_specs=[vmem()] * 4,
        out_shape=[jax.ShapeDtypeStruct(shape, jnp.bfloat16) for shape in shapes],
        compiler_params=pltpu.CompilerParams(vmem_limit_bytes=4 * MIB),
        name="column_strips",
    )(place, normed, row_one, row_two)


def padded_rows(tokens):
    return tokens + 16


def expand_kernel(normed_ref, weight_ref, out_ref):
    tokens = normed_ref.shape[0]
    width = weight_ref.shape[1]
    tile = divisor(width, 512, LANES)
    step = divisor(tokens, 128, 16)
    starts = range(0, tokens, step)

    def body(index, carry):
        lanes = pl.ds(pl.multiple_of(index * tile, tile), tile)
        for start in starts:
            made = gelu_of_half(
                matmul(normed_ref[start : start + step, :], weight_ref[:, lanes])
            )
            for sub in range(tile // LANES):
                row = (index * (tile // LANES) + sub) * padded_rows(tokens) + 8 + start
                out_ref[pl.ds(pl.multiple_of(row, 8), step), :] = made[
                    :, sub * LANES : (sub + 1) * LANES
                ]
        return carry

    lax.fori_loop(0, width // tile, body, 0)


def expand(normed, w_expand):
    tokens, channels = normed.shape
    width = w_expand.shape[1]
    return pl.pallas_call(
        expand_kernel,
        in_specs=[vmem()] * 2,
        out_specs=vmem(),
        out_shape=jax.ShapeDtypeStruct((width // LANES * padded_rows(tokens), LANES), jnp.float32),
        compiler_params=pltpu.CompilerParams(vmem_limit_bytes=4 * MIB),
        cost_estimate=pl.CostEstimate(
            flops=10**10,
            bytes_accessed=tokens * channels * 2 + channels * width * 2 + tokens * width * 4,
            transcendentals=tokens * width,
        ),
        name="expand",
    )(normed, w_expand)


def mix_kernel(
    place_ref, expanded_ref, field_ref, up_ref, down_ref, one_ref, two_ref, w_expand_ref, depth_ref,
    w_project_ref, perm_ref, mixed_ref, *refs, rows, cols, plan, size,
):
    masks, _, sides = plan
    sent = len(outgoing_shapes(plan, size, 1))
    slab_refs = refs[:sent]
    total_ref, normed_ref, grouped_ref, even_ref, odd_ref, even_halo_ref, odd_halo_ref = refs[sent:]
    tokens = rows * cols
    width = w_expand_ref.shape[1]
    tile = even_ref.shape[1]
    slot = one_ref.shape[0]
    up_start, down_start, left_start = 8, 16 + cols, 24 + 2 * cols
    right_start = left_start + slot

    odd_col = place_ref[2]
    left = choose(odd_col, one_ref[...], two_ref[...])
    right = choose(odd_col, two_ref[...], one_ref[...])
    edges = jnp.concatenate([up_ref[...], down_ref[...], left, right], axis=0)

    def expand_halo(index, out_ref):
        lanes = pl.ds(pl.multiple_of(index * tile, tile), tile)
        made = gelu_of_half(matmul(edges, w_expand_ref[:, lanes]))
        for sub in range(tile // LANES):
            part = made[:, sub * LANES : (sub + 1) * LANES]
            out_ref[sub, up_start : up_start + cols] = part[:cols]
            out_ref[sub, down_start : down_start + cols] = part[cols : 2 * cols]
            out_ref[sub, left_start : left_start + 2 * slot] = part[2 * cols :]

    position = lax.broadcasted_iota(jnp.int32, (8, LANES), 0)
    at_first = position == 0
    at_last = position == 7

    def convolve(index, out_ref, halo_ref):
        for sub in range(tile // LANES):
            lanes = pl.ds(pl.multiple_of(index * tile + sub * LANES, LANES), LANES)
            base = (index * (tile // LANES) + sub) * padded_rows(tokens) + 8
            taps = [[0.5 * depth_ref[p, q : q + 1, lanes] for q in range(3)] for p in range(3)]
            sums = {}
            for y in range(-1, rows + 1):
                if y < 0:
                    parts = [halo_ref[sub, up_start + q : up_start + q + cols] for q in (-1, 0, 1)]
                elif y == rows:
                    parts = [
                        halo_ref[sub, down_start + q : down_start + q + cols] for q in (-1, 0, 1)
                    ]
                else:
                    parts = [
                        expanded_ref[pl.ds(base + (y * cols + q), cols), :] for q in (-1, 0, 1)
                    ]
                left = halo_ref[sub, left_start + y + 1 : left_start + y + 2]
                right = halo_ref[sub, right_start + y + 1 : right_start + y + 2]
                parts[0] = jnp.concatenate(
                    [jnp.where(at_first, left, parts[0][:8]), parts[0][8:]], axis=0
                )
                parts[2] = jnp.concatenate(
                    [parts[2][:-8], jnp.where(at_last, right, parts[2][-8:])], axis=0
                )
                for p in range(3):
                    target = y + 1 - p
                    if 0 <= target < rows:
                        for q in range(3):
                            term = taps[p][q] * parts[q]
                            sums[target] = sums[target] + term if target in sums else term
                if y > 0:
                    out_ref[
                        (y - 1) * cols : y * cols, sub * LANES : (sub + 1) * LANES
                    ] = gelu_of_half(sums.pop(y - 1)).astype(jnp.bfloat16)

    def project(index, in_ref):
        piece = pl.ds(pl.multiple_of(index * tile, tile), tile)
        total_ref[...] += matmul(in_ref[...], w_project_ref[piece, :])

    total_ref[...] = field_ref[...]
    expand_halo(0, even_halo_ref)
    expand_halo(1, odd_halo_ref)
    convolve(0, even_ref, even_halo_ref)

    def body(index, carry):
        project(2 * index, even_ref)
        convolve(2 * index + 1, odd_ref, odd_halo_ref)
        expand_halo(2 * index + 2, even_halo_ref)
        project(2 * index + 1, odd_ref)
        convolve(2 * index + 2, even_ref, even_halo_ref)
        expand_halo(2 * index + 3, odd_halo_ref)
        return carry

    pairs = width // tile // 2
    lax.fori_loop(0, pairs - 1, body, 0)
    project(2 * pairs - 2, even_ref)
    convolve(2 * pairs - 1, odd_ref, odd_halo_ref)
    project(2 * pairs - 1, odd_ref)

    step = divisor(tokens, 128, 16)
    for start in range(0, tokens, step):
        piece = slice(start, start + step)
        mixed = total_ref[piece, :]
        mixed_ref[piece, :] = mixed
        normed_ref[piece, :] = layer_norm(mixed).astype(jnp.bfloat16)
    grouped_ref[...] = matmul(perm_ref[...], normed_ref[...]).astype(jnp.bfloat16)
    for index, mask in enumerate(masks):
        for side in range(sides):
            start = pl.multiple_of((place_ref[0] ^ (mask | side)) * size, 16)
            write_block(
                plan, slab_refs, index, side, slice(None), grouped_ref[pl.ds(start, size), :]
            )


def mix(
    place, plan, size, expanded, field, up, down, one, two, w_expand, depth_kernel, w_project, perm,
    rows, cols,
):
    tokens, channels = field.shape
    width = w_expand.shape[1]
    tile = divisor(width // 2, 256, LANES)
    slot = one.shape[0]
    sent = outgoing_shapes(plan, size, channels)
    halo = pltpu.VMEM((tile // LANES, 24 + 2 * cols + 2 * slot, LANES), jnp.float32)
    return pl.pallas_call(
        functools.partial(mix_kernel, rows=rows, cols=cols, plan=plan, size=size),
        in_specs=[pl.BlockSpec(memory_space=pltpu.SMEM)] + [vmem()] * 10,
        out_specs=[vmem()] * (1 + len(sent)),
        out_shape=[jax.ShapeDtypeStruct((tokens, channels), jnp.float32)]
        + [jax.ShapeDtypeStruct(shape, jnp.bfloat16) for shape in sent],
        scratch_shapes=[
            pltpu.VMEM((tokens, channels), jnp.float32),
            pltpu.VMEM((tokens, channels), jnp.bfloat16),
            pltpu.VMEM((tokens, channels), jnp.bfloat16),
            pltpu.VMEM((tokens, tile), jnp.bfloat16),
            pltpu.VMEM((tokens, tile), jnp.bfloat16),
            halo,
            halo,
        ],
        compiler_params=pltpu.CompilerParams(vmem_limit_bytes=8 * MIB),
        cost_estimate=pl.CostEstimate(
            flops=2 * tokens * channels * width,
            bytes_accessed=tokens * channels * 10 + 4 * channels * width + tokens * width * 4,
            transcendentals=tokens * width,
        ),
        name="mix",
    )(place, expanded, field, up, down, one, two, w_expand, depth_kernel, w_project, perm)


def identity(size):
    row = lax.broadcasted_iota(jnp.int32, (size, size), 0)
    column = lax.broadcasted_iota(jnp.int32, (size, size), 1)
    return jnp.where(row == column, 1.0, 0.0).astype(jnp.bfloat16)


def attend_kernel(*refs, plan, sets, came):
    masks, _, sides = plan
    slabs = len(masks)
    _, size, channels = refs[0].shape
    in_refs, weight_ref, out_refs = refs[:came], refs[came], refs[came + 1 : -6]
    query_ref, key_ref, value_ref, turned_ref, even_ref, odd_ref = refs[-6:]
    members = size // sets
    count = slabs * sides * members
    head_width = channels // HEADS
    group_heads = LANES // head_width
    groups = channels // LANES
    factor = math.log2(math.e) / math.sqrt(head_width)
    lane = lax.broadcasted_iota(jnp.int32, (1, LANES), 1)
    masks = [
        jnp.where((lane >= j * head_width) & (lane < (j + 1) * head_width), 1.0, 0.0).astype(
            jnp.bfloat16
        )
        for j in range(group_heads)
    ]
    turn_values = identity(channels)
    for s in range(sets):
        piece = slice(s * members, (s + 1) * members)
        block = jnp.concatenate(
            [
                read_block(plan, in_refs, index, side, piece)
                for index in range(slabs)
                for side in range(sides)
            ],
            axis=0,
        )
        qkv = matmul(block, weight_ref[...]).astype(jnp.bfloat16)
        values = matmul_nt(turn_values, qkv[:, 2 * channels :]).astype(jnp.bfloat16)
        for group in range(groups):
            lanes = slice(group * LANES, (group + 1) * LANES)
            query_ref[s * groups + group] = qkv[:, lanes]
            key_ref[s * groups + group] = qkv[:, channels + group * LANES : channels + (group + 1) * LANES]
            for j in range(group_heads):
                head = (group * group_heads + j) * head_width
                value_ref[s * groups + group, j, :head_width] = values[head : head + head_width]
                value_ref[s * groups + group, j, head_width:] = jnp.ones((16, count), jnp.bfloat16)

    def scores(index, out):
        keys = key_ref[index]
        stacked = jnp.concatenate([keys * mask for mask in masks], axis=0)
        out[...] = matmul_nt(stacked, query_ref[index])

    def weigh(index, scores_ref):
        for j in range(group_heads):
            part = scores_ref[j * count : (j + 1) * count]
            highest = jnp.max(part, axis=0, keepdims=True)
            raised = jnp.exp2((part - highest) * factor).astype(jnp.bfloat16)
            product = matmul(value_ref[index, j], raised)
            scale = 1.0 / product[head_width : head_width + 1]
            turned_ref[index, j * head_width : (j + 1) * head_width] = (
                product[:head_width] * scale
            ).astype(jnp.bfloat16)

    total = sets * groups
    scores(0, even_ref)

    def body(pair, carry):
        scores(2 * pair + 1, odd_ref)
        weigh(2 * pair, even_ref)
        scores(jnp.minimum(2 * pair + 2, total - 1), even_ref)
        weigh(2 * pair + 1, odd_ref)
        return carry

    lax.fori_loop(0, total // 2, body, 0)
    turn_tokens = identity(count)
    for s in range(sets):
        turned = turned_ref[s * groups : (s + 1) * groups].reshape(channels, count)
        attended = matmul_nt(turn_tokens, turned).astype(jnp.bfloat16)
        for index in range(slabs):
            for side in range(sides):
                start = (index * sides + side) * members
                write_block(
                    plan, out_refs, index, side, slice(s * members, (s + 1) * members),
                    attended[start : start + members],
                )


def attend(plan, incoming, w_qkv, sets):
    masks, _, sides = plan
    _, size, channels = incoming[0].shape
    count = len(masks) * sides * size // sets
    sent = outgoing_shapes(plan, size, channels)
    head_width = channels // HEADS
    group_heads = LANES // head_width
    total = sets * channels // LANES
    return pl.pallas_call(
        functools.partial(attend_kernel, plan=plan, sets=sets, came=len(incoming)),
        in_specs=[vmem()] * (len(incoming) + 1),
        out_specs=[vmem()] * len(sent),
        out_shape=[jax.ShapeDtypeStruct(shape, jnp.bfloat16) for shape in sent],
        scratch_shapes=[
            pltpu.VMEM((total, count, LANES), jnp.bfloat16),
            pltpu.VMEM((total, count, LANES), jnp.bfloat16),
            pltpu.VMEM((total, group_heads, head_width + 16, count), jnp.bfloat16),
            pltpu.VMEM((total, LANES, count), jnp.bfloat16),
            pltpu.VMEM((group_heads * count, count), jnp.float32),
            pltpu.VMEM((group_heads * count, count), jnp.float32),
        ],
        compiler_params=pltpu.CompilerParams(vmem_limit_bytes=10 * MIB),
        cost_estimate=pl.CostEstimate(
            flops=sets * (2 * count * channels * channels * 3 + 4 * count * count * channels),
            bytes_accessed=4 * sets * count * channels + 6 * channels * channels,
            transcendentals=sets * HEADS * count * count,
        ),
        name="attend",
    )(*incoming, w_qkv)


def finish_kernel(place_ref, *refs, plan):
    masks, _, sides = plan
    in_refs, rest = refs[:-7], refs[-7:]
    back_ref, weight_ref, mixed_ref, out_ref, attended_ref, made_ref, sent = rest
    tokens = mixed_ref.shape[0]
    size = in_refs[0].shape[1]
    for index, mask in enumerate(masks):
        for side in range(sides):
            start = pl.multiple_of((place_ref[0] ^ (mask | side)) * size, 16)
            attended_ref[pl.ds(start, size), :] = read_block(
                plan, in_refs, index, side, slice(None)
            )
    step = made_ref.shape[1]
    copies = []
    for index, start in enumerate(range(0, tokens, step)):
        rows = slice(start, start + step)
        restored = matmul(back_ref[rows, :], attended_ref[...]).astype(jnp.bfloat16)
        made_ref[index] = mixed_ref[rows, :] + matmul(restored, weight_ref[...])
        copy = pltpu.make_async_copy(
            made_ref.at[index], out_ref.at[pl.ds(start, step)], sent.at[index]
        )
        copy.start()
        copies.append(copy)
    for copy in copies:
        copy.wait()


def finish(place, plan, incoming, back, w_out, mixed):
    tokens, channels = mixed.shape
    step = divisor(tokens, 128, 16)
    return pl.pallas_call(
        functools.partial(finish_kernel, plan=plan),
        in_specs=[pl.BlockSpec(memory_space=pltpu.SMEM)] + [vmem()] * (len(incoming) + 3),
        out_specs=pl.BlockSpec(memory_space=pltpu.HBM),
        out_shape=jax.ShapeDtypeStruct((tokens, channels), jnp.float32),
        scratch_shapes=[
            pltpu.VMEM((tokens, channels), jnp.bfloat16),
            pltpu.VMEM((tokens // step, step, channels), jnp.float32),
            pltpu.SemaphoreType.DMA((tokens // step,)),
        ],
        compiler_params=pltpu.CompilerParams(vmem_limit_bytes=6 * MIB),
        name="finish",
    )(place, *incoming, back, w_out, mixed)


def swap_pairs(edge, axis, start):
    pairs = [(i, i + 1) for i in range(start, lax.axis_size(axis) - 1, 2)]
    return lax.ppermute(edge, axis, pairs + [(b, a) for a, b in pairs])


def exchange_plan(row_devices, col_devices):
    devices = row_devices * col_devices
    crossing = list(range(devices - 2, devices // 2 - 1, -2))
    others = list(range(devices // 2 - 2, 0, -2))
    masks = crossing[:1]
    for index, mask in enumerate(crossing[1:]):
        masks += [mask] + others[index : index + 1]
    return masks + [0], min(2, len(masks)), 2


def outgoing_shapes(plan, size, channels):
    masks, late, sides = plan
    if sides == 1:
        return [(1, size, channels)]
    early = len(masks) - 1 - late
    return [(2, size, channels)] * late + [
        (1, size, channels), (early + 1, size, channels), (early, size, channels)
    ]


def write_block(plan, refs, index, side, rows, value):
    masks, late, sides = plan
    if sides == 1:
        refs[0][0, rows] = value
    elif index < late:
        refs[index][side, rows] = value
    elif index == len(masks) - 1:
        refs[late + side][0, rows] = value
    elif side == 0:
        refs[late + 2][index - late, rows] = value
    else:
        refs[late + 1][index - late + 1, rows] = value


def read_block(plan, refs, index, side, rows):
    masks, late, sides = plan
    if sides == 1:
        return refs[0][0, rows]
    if index < late:
        return refs[index + side * len(masks)][side, rows]
    if index == len(masks) - 1:
        return refs[index + side * (late + 1)][0, rows]
    return refs[index][side, rows]


def join_kernel(own_ref, swapped_ref, *out_refs):
    for index, out_ref in enumerate(out_refs):
        out_ref[0] = own_ref[index]
        out_ref[1] = swapped_ref[index + 1]


def join(own, swapped):
    early, size, channels = own.shape
    return pl.pallas_call(
        join_kernel,
        in_specs=[vmem()] * 2,
        out_specs=[vmem()] * early,
        out_shape=[jax.ShapeDtypeStruct((2, size, channels), own.dtype)] * early,
        compiler_params=pltpu.CompilerParams(vmem_limit_bytes=2 * MIB),
        name="join",
    )(own, swapped)


def trade(plan, outgoing):
    masks, late, _ = plan
    devices = lax.axis_size("row") * lax.axis_size("col")

    def swap(slab, mask):
        return lax.ppermute(slab, ("row", "col"), [(i, i ^ mask) for i in range(devices)])

    slabs, (kept, passed, own) = outgoing[:late], outgoing[late:]
    swapped = swap(passed, 1)
    first = [swap(slab, mask) for slab, mask in zip(slabs, masks)]
    rest = [swap(slab, mask) for slab, mask in zip(join(own, swapped), masks[late:-1])]
    tie = min(1, len(rest) - 1)
    *first, rest[tie] = lax.optimization_barrier((*first, rest[tie]))
    return [*first, *rest, kept, *[swap(slab, 1) for slab in first], swapped]


def trade_all(slabs, sets, members, outward):
    axes = ("row", "col")
    channels = slabs[0].shape[-1]
    block = slabs[0].reshape(-1, channels)
    devices = block.shape[0] // (sets * members)
    if not outward:
        block = block.reshape(sets, devices, members, channels).transpose(1, 0, 2, 3)
    block = block.reshape(devices, sets * members, channels)
    block = lax.all_to_all(block, axes, 0, 0, tiled=True)
    if outward:
        block = block.reshape(devices, sets, members, channels).transpose(1, 0, 2, 3)
    return [block.reshape(1, -1, channels)]


def grouping(rows, cols, blocks_rows, blocks_cols):
    order = np.arange(rows * cols).reshape(
        blocks_rows, rows // blocks_rows, blocks_cols, cols // blocks_cols
    )
    order = order.transpose(1, 3, 0, 2).reshape(-1)
    matrix = np.zeros((order.size, order.size), np.float32)
    matrix[np.arange(order.size), order] = 1.0
    return matrix


def shards(field, w_expand, depth_kernel, w_project, w_qkv, w_out):
    rows, cols, channels = field.shape
    tokens = rows * cols
    row_devices = lax.axis_size("row")
    col_devices = lax.axis_size("col")
    devices = row_devices * col_devices
    blocks_rows = GRID // row_devices
    blocks_cols = GRID // col_devices
    members = blocks_rows * blocks_cols
    sets_local = tokens // members // devices
    matrix = grouping(rows, cols, blocks_rows, blocks_cols)
    perm = jnp.asarray(matrix, jnp.bfloat16)
    back = jnp.asarray(matrix.T, jnp.bfloat16)

    flat = field.reshape(tokens, channels)
    pairwise = 8 <= devices <= 16 and devices & (devices - 1) == 0 and col_devices % 2 == 0
    plan = exchange_plan(row_devices, col_devices) if pairwise else ([0], 0, 1)
    row, col = lax.axis_index("row"), lax.axis_index("col")
    own = row * col_devices + col if pairwise else row * 0
    place = jnp.stack([own, row % 2, col % 2]).astype(jnp.int32)

    one, two = row_edges(place, field[0], field[rows - 1])
    one, two = swap_pairs(one, "row", 0), swap_pairs(two, "row", 1)
    normed = half_norm_of(flat)
    expanded = expand(normed, w_expand)
    one, two, normed, expanded = lax.optimization_barrier((one, two, normed, expanded))
    up, down, one, two = column_strips(place, normed, one, two, round_up(rows + 2, 16))
    one, two = swap_pairs(one, "col", 0), swap_pairs(two, "col", 1)

    size = tokens // (len(plan[0]) * plan[2])
    mixed, *outgoing = mix(
        place, plan, size, expanded, flat, up, down, one, two, w_expand, depth_kernel, w_project,
        perm, rows, cols,
    )

    def route(outgoing, outward):
        if pairwise:
            return trade(plan, outgoing)
        return trade_all(outgoing, sets_local, members, outward)

    outgoing = attend(plan, route(outgoing, True), w_qkv, sets_local)
    final = finish(place, plan, route(outgoing, False), back, w_out, mixed)
    return final.reshape(rows, cols, channels)


def solution(mesh):
    return jax.shard_map(
        shards,
        mesh=mesh,
        in_specs=(P(("field", "row"), "col", None), P(), P(), P(), P(), P()),
        out_specs=P(("field", "row"), "col", None),
        check_vma=False,
    )
```

```python
import functools
import math

import jax
import jax.numpy as jnp
import numpy as np
from jax import lax
from jax.experimental import pallas as pl
from jax.experimental.pallas import tpu as pltpu
from jax.sharding import PartitionSpec as P

HEADS = 16
GRID = 16
LANES = 128
MIB = 1024 * 1024
NT = (((1,), (1,)), ((), ()))


def layer_norm(inputs):
    average = jnp.mean(inputs, axis=-1, keepdims=True)
    centred = inputs - average
    variance = jnp.mean(centred * centred, axis=-1, keepdims=True)
    return centred * lax.rsqrt(variance + 1e-05)


def gelu_of_half(half):
    scale = math.sqrt(2.0 / math.pi)
    inner = half * (2.0 * scale + (8.0 * scale * 0.044715) * (half * half))
    return half + half * jnp.tanh(inner)


def matmul(a, b):
    return jnp.dot(a, b, preferred_element_type=jnp.float32)


def matmul_nt(a, b):
    return lax.dot_general(a, b, NT, preferred_element_type=jnp.float32)


def divisor(size, most, unit):
    best = size
    for piece in range(unit, most + 1, unit):
        if size % piece == 0:
            best = piece
    return best


def round_up(size, unit):
    return -(-size // unit) * unit


def vmem():
    return pl.BlockSpec(memory_space=pltpu.VMEM)


def half_norm(inputs):
    return (layer_norm(inputs) * 0.5).astype(jnp.bfloat16)


def half_norm_kernel(in_ref, out_ref):
    rows = in_ref.shape[0]
    step = divisor(rows, 128, 16)
    for start in range(0, rows, step):
        out_ref[start : start + step, :] = half_norm(in_ref[start : start + step, :])


def half_norm_of(inputs):
    return pl.pallas_call(
        half_norm_kernel,
        in_specs=[vmem()],
        out_specs=vmem(),
        out_shape=jax.ShapeDtypeStruct(inputs.shape, jnp.bfloat16),
        compiler_params=pltpu.CompilerParams(vmem_limit_bytes=4 * MIB),
        cost_estimate=pl.CostEstimate(
            flops=10**9, bytes_accessed=6 * inputs.size, transcendentals=inputs.shape[0]
        ),
        name="half_norm",
    )(inputs)


def choose(condition, one, two):
    flags = jnp.full((one.shape[0], 1), condition, jnp.int32) == 1
    return jnp.where(flags, one.astype(jnp.float32), two.astype(jnp.float32)).astype(one.dtype)


def edges_kernel(odd_row_ref, top_ref, bottom_ref, one_ref, two_ref):
    odd = odd_row_ref[0]
    top, bottom = half_norm(top_ref[...]), half_norm(bottom_ref[...])
    one_ref[...] = choose(odd, top, bottom)
    two_ref[...] = choose(odd, bottom, top)


def row_edges(odd_row, top, bottom):
    return pl.pallas_call(
        edges_kernel,
        in_specs=[pl.BlockSpec(memory_space=pltpu.SMEM)] + [vmem()] * 2,
        out_specs=[vmem()] * 2,
        out_shape=[jax.ShapeDtypeStruct(top.shape, jnp.bfloat16)] * 2,
        compiler_params=pltpu.CompilerParams(vmem_limit_bytes=4 * MIB),
        cost_estimate=pl.CostEstimate(
            flops=10**10, bytes_accessed=12 * top.size, transcendentals=2 * top.shape[0]
        ),
        name="row_edges",
    )(odd_row, top, bottom)


def picker(shape, pick):
    row = lax.broadcasted_iota(jnp.int32, shape, 0)
    column = lax.broadcasted_iota(jnp.int32, shape, 1)
    return jnp.where(pick(row, column), 1.0, 0.0).astype(jnp.bfloat16)


def strips_kernel(
    odd_row_ref, odd_col_ref, normed_ref, row_one_ref, row_two_ref, up_ref, down_ref, one_ref, two_ref
):
    tokens = normed_ref.shape[0]
    cols = up_ref.shape[0]
    rows = tokens // cols
    slot = one_ref.shape[0]
    odd_row, odd_col = odd_row_ref[0], odd_col_ref[0]
    up = choose(odd_row, row_one_ref[...], row_two_ref[...])
    down = choose(odd_row, row_two_ref[...], row_one_ref[...])
    up_ref[...] = up
    down_ref[...] = down
    strips = []
    for x in (0, cols - 1):
        body = picker(
            (slot, tokens), lambda i, j: (i >= 1) & (i <= rows) & (j == (i - 1) * cols + x)
        )
        head = picker((slot, cols), lambda i, j: (i == 0) & (j == x))
        foot = picker((slot, cols), lambda i, j: (i == rows + 1) & (j == x))
        strip = matmul(body, normed_ref[...]) + matmul(head, up) + matmul(foot, down)
        strips.append(strip.astype(jnp.bfloat16))
    one_ref[...] = choose(odd_col, strips[0], strips[1])
    two_ref[...] = choose(odd_col, strips[1], strips[0])


def column_strips(odd_row, odd_col, normed, row_one, row_two, slot):
    cols, channels = row_one.shape
    shapes = [(cols, channels)] * 2 + [(slot, channels)] * 2
    return pl.pallas_call(
        strips_kernel,
        in_specs=[pl.BlockSpec(memory_space=pltpu.SMEM)] * 2 + [vmem()] * 3,
        out_specs=[vmem()] * 4,
        out_shape=[jax.ShapeDtypeStruct(shape, jnp.bfloat16) for shape in shapes],
        compiler_params=pltpu.CompilerParams(vmem_limit_bytes=4 * MIB),
        name="column_strips",
    )(odd_row, odd_col, normed, row_one, row_two)


def padded_rows(tokens):
    return tokens + 16


def expand_kernel(normed_ref, weight_ref, out_ref):
    tokens = normed_ref.shape[0]
    width = weight_ref.shape[1]
    tile = divisor(width, 512, LANES)
    step = divisor(tokens, 128, 16)
    starts = range(0, tokens, step)

    def body(index, carry):
        lanes = pl.ds(pl.multiple_of(index * tile, tile), tile)
        for start in starts:
            made = gelu_of_half(
                matmul(normed_ref[start : start + step, :], weight_ref[:, lanes])
            )
            for sub in range(tile // LANES):
                row = (index * (tile // LANES) + sub) * padded_rows(tokens) + 8 + start
                out_ref[pl.ds(pl.multiple_of(row, 8), step), :] = made[
                    :, sub * LANES : (sub + 1) * LANES
                ]
        return carry

    lax.fori_loop(0, width // tile, body, 0)


def expand(normed, w_expand):
    tokens, channels = normed.shape
    width = w_expand.shape[1]
    return pl.pallas_call(
        expand_kernel,
        in_specs=[vmem()] * 2,
        out_specs=vmem(),
        out_shape=jax.ShapeDtypeStruct((width // LANES * padded_rows(tokens), LANES), jnp.float32),
        compiler_params=pltpu.CompilerParams(vmem_limit_bytes=4 * MIB),
        cost_estimate=pl.CostEstimate(
            flops=10**10,
            bytes_accessed=tokens * channels * 2 + channels * width * 2 + tokens * width * 4,
            transcendentals=tokens * width,
        ),
        name="expand",
    )(normed, w_expand)


def mix_kernel(
    own_ref, odd_col_ref, expanded_ref, field_ref, up_ref, down_ref, one_ref, two_ref, w_expand_ref, depth_ref,
    w_project_ref, perm_ref, mixed_ref, *refs, rows, cols, plan, size,
):
    masks, _, sides = plan
    sent = len(outgoing_shapes(plan, size, 1))
    slab_refs = refs[:sent]
    total_ref, normed_ref, grouped_ref, even_ref, odd_ref, even_halo_ref, odd_halo_ref = refs[sent:]
    tokens = rows * cols
    width = w_expand_ref.shape[1]
    tile = even_ref.shape[1]
    slot = one_ref.shape[0]
    up_start, down_start, left_start = 8, 16 + cols, 24 + 2 * cols
    right_start = left_start + slot

    odd_col = odd_col_ref[0]
    left = choose(odd_col, one_ref[...], two_ref[...])
    right = choose(odd_col, two_ref[...], one_ref[...])
    edges = jnp.concatenate([up_ref[...], down_ref[...], left, right], axis=0)

    def expand_halo(index, out_ref):
        lanes = pl.ds(pl.multiple_of(index * tile, tile), tile)
        made = gelu_of_half(matmul(edges, w_expand_ref[:, lanes]))
        for sub in range(tile // LANES):
            part = made[:, sub * LANES : (sub + 1) * LANES]
            out_ref[sub, up_start : up_start + cols] = part[:cols]
            out_ref[sub, down_start : down_start + cols] = part[cols : 2 * cols]
            out_ref[sub, left_start : left_start + 2 * slot] = part[2 * cols :]

    position = lax.broadcasted_iota(jnp.int32, (8, LANES), 0)
    at_first = position == 0
    at_last = position == 7

    def convolve(index, out_ref, halo_ref):
        for sub in range(tile // LANES):
            lanes = pl.ds(pl.multiple_of(index * tile + sub * LANES, LANES), LANES)
            base = (index * (tile // LANES) + sub) * padded_rows(tokens) + 8
            taps = [[0.5 * depth_ref[p, q : q + 1, lanes] for q in range(3)] for p in range(3)]
            sums = {}
            for y in range(-1, rows + 1):
                if y < 0:
                    parts = [halo_ref[sub, up_start + q : up_start + q + cols] for q in (-1, 0, 1)]
                elif y == rows:
                    parts = [
                        halo_ref[sub, down_start + q : down_start + q + cols] for q in (-1, 0, 1)
                    ]
                else:
                    parts = [
                        expanded_ref[pl.ds(base + (y * cols + q), cols), :] for q in (-1, 0, 1)
                    ]
                left = halo_ref[sub, left_start + y + 1 : left_start + y + 2]
                right = halo_ref[sub, right_start + y + 1 : right_start + y + 2]
                parts[0] = jnp.concatenate(
                    [jnp.where(at_first, left, parts[0][:8]), parts[0][8:]], axis=0
                )
                parts[2] = jnp.concatenate(
                    [parts[2][:-8], jnp.where(at_last, right, parts[2][-8:])], axis=0
                )
                for p in range(3):
                    target = y + 1 - p
                    if 0 <= target < rows:
                        for q in range(3):
                            term = taps[p][q] * parts[q]
                            sums[target] = sums[target] + term if target in sums else term
                if y > 0:
                    out_ref[
                        (y - 1) * cols : y * cols, sub * LANES : (sub + 1) * LANES
                    ] = gelu_of_half(sums.pop(y - 1)).astype(jnp.bfloat16)

    def project(index, in_ref):
        piece = pl.ds(pl.multiple_of(index * tile, tile), tile)
        total_ref[...] += matmul(in_ref[...], w_project_ref[piece, :])

    total_ref[...] = field_ref[...]
    expand_halo(0, even_halo_ref)
    expand_halo(1, odd_halo_ref)
    convolve(0, even_ref, even_halo_ref)

    def body(index, carry):
        project(2 * index, even_ref)
        convolve(2 * index + 1, odd_ref, odd_halo_ref)
        expand_halo(2 * index + 2, even_halo_ref)
        project(2 * index + 1, odd_ref)
        convolve(2 * index + 2, even_ref, even_halo_ref)
        expand_halo(2 * index + 3, odd_halo_ref)
        return carry

    pairs = width // tile // 2
    lax.fori_loop(0, pairs - 1, body, 0)
    project(2 * pairs - 2, even_ref)
    convolve(2 * pairs - 1, odd_ref, odd_halo_ref)
    project(2 * pairs - 1, odd_ref)

    step = divisor(tokens, 128, 16)
    for start in range(0, tokens, step):
        piece = slice(start, start + step)
        mixed = total_ref[piece, :]
        mixed_ref[piece, :] = mixed
        normed_ref[piece, :] = layer_norm(mixed).astype(jnp.bfloat16)
    grouped_ref[...] = matmul(perm_ref[...], normed_ref[...]).astype(jnp.bfloat16)
    for index, mask in enumerate(masks):
        for side in range(sides):
            start = pl.multiple_of((own_ref[0] ^ (mask | side)) * size, 16)
            write_block(
                plan, slab_refs, index, side, slice(None), grouped_ref[pl.ds(start, size), :]
            )


def mix(
    own, odd_col, plan, size, expanded, field, up, down, one, two, w_expand, depth_kernel, w_project,
    perm, rows, cols,
):
    tokens, channels = field.shape
    width = w_expand.shape[1]
    tile = divisor(width // 2, 256, LANES)
    slot = one.shape[0]
    sent = outgoing_shapes(plan, size, channels)
    halo = pltpu.VMEM((tile // LANES, 24 + 2 * cols + 2 * slot, LANES), jnp.float32)
    return pl.pallas_call(
        functools.partial(mix_kernel, rows=rows, cols=cols, plan=plan, size=size),
        in_specs=[pl.BlockSpec(memory_space=pltpu.SMEM)] * 2 + [vmem()] * 10,
        out_specs=[vmem()] * (1 + len(sent)),
        out_shape=[jax.ShapeDtypeStruct((tokens, channels), jnp.float32)]
        + [jax.ShapeDtypeStruct(shape, jnp.bfloat16) for shape in sent],
        scratch_shapes=[
            pltpu.VMEM((tokens, channels), jnp.float32),
            pltpu.VMEM((tokens, channels), jnp.bfloat16),
            pltpu.VMEM((tokens, channels), jnp.bfloat16),
            pltpu.VMEM((tokens, tile), jnp.bfloat16),
            pltpu.VMEM((tokens, tile), jnp.bfloat16),
            halo,
            halo,
        ],
        compiler_params=pltpu.CompilerParams(vmem_limit_bytes=8 * MIB),
        cost_estimate=pl.CostEstimate(
            flops=2 * tokens * channels * width,
            bytes_accessed=tokens * channels * 10 + 4 * channels * width + tokens * width * 4,
            transcendentals=tokens * width,
        ),
        name="mix",
    )(own, odd_col, expanded, field, up, down, one, two, w_expand, depth_kernel, w_project, perm)


def identity(size):
    row = lax.broadcasted_iota(jnp.int32, (size, size), 0)
    column = lax.broadcasted_iota(jnp.int32, (size, size), 1)
    return jnp.where(row == column, 1.0, 0.0).astype(jnp.bfloat16)


def attend_kernel(*refs, plan, sets, came):
    masks, _, sides = plan
    slabs = len(masks)
    _, size, channels = refs[0].shape
    in_refs, weight_ref, out_refs = refs[:came], refs[came], refs[came + 1 : -6]
    query_ref, key_ref, value_ref, turned_ref, even_ref, odd_ref = refs[-6:]
    members = size // sets
    count = slabs * sides * members
    head_width = channels // HEADS
    group_heads = LANES // head_width
    groups = channels // LANES
    factor = math.log2(math.e) / math.sqrt(head_width)
    lane = lax.broadcasted_iota(jnp.int32, (1, LANES), 1)
    masks = [
        jnp.where((lane >= j * head_width) & (lane < (j + 1) * head_width), 1.0, 0.0).astype(
            jnp.bfloat16
        )
        for j in range(group_heads)
    ]
    turn_values = identity(channels)
    for s in range(sets):
        piece = slice(s * members, (s + 1) * members)
        block = jnp.concatenate(
            [
                read_block(plan, in_refs, index, side, piece)
                for index in range(slabs)
                for side in range(sides)
            ],
            axis=0,
        )
        qkv = matmul(block, weight_ref[...]).astype(jnp.bfloat16)
        values = matmul_nt(turn_values, qkv[:, 2 * channels :]).astype(jnp.bfloat16)
        for group in range(groups):
            lanes = slice(group * LANES, (group + 1) * LANES)
            query_ref[s * groups + group] = qkv[:, lanes]
            key_ref[s * groups + group] = qkv[:, channels + group * LANES : channels + (group + 1) * LANES]
            for j in range(group_heads):
                head = (group * group_heads + j) * head_width
                value_ref[s * groups + group, j, :head_width] = values[head : head + head_width]
                value_ref[s * groups + group, j, head_width:] = jnp.ones((16, count), jnp.bfloat16)

    def scores(index, out):
        keys = key_ref[index]
        stacked = jnp.concatenate([keys * mask for mask in masks], axis=0)
        out[...] = matmul_nt(stacked, query_ref[index])

    def weigh(index, scores_ref):
        for j in range(group_heads):
            part = scores_ref[j * count : (j + 1) * count]
            highest = jnp.max(part, axis=0, keepdims=True)
            raised = jnp.exp2((part - highest) * factor).astype(jnp.bfloat16)
            product = matmul(value_ref[index, j], raised)
            scale = 1.0 / product[head_width : head_width + 1]
            turned_ref[index, j * head_width : (j + 1) * head_width] = (
                product[:head_width] * scale
            ).astype(jnp.bfloat16)

    total = sets * groups
    scores(0, even_ref)

    def body(pair, carry):
        scores(2 * pair + 1, odd_ref)
        weigh(2 * pair, even_ref)
        scores(jnp.minimum(2 * pair + 2, total - 1), even_ref)
        weigh(2 * pair + 1, odd_ref)
        return carry

    lax.fori_loop(0, total // 2, body, 0)
    turn_tokens = identity(count)
    for s in range(sets):
        turned = turned_ref[s * groups : (s + 1) * groups].reshape(channels, count)
        attended = matmul_nt(turn_tokens, turned).astype(jnp.bfloat16)
        for index in range(slabs):
            for side in range(sides):
                start = (index * sides + side) * members
                write_block(
                    plan, out_refs, index, side, slice(s * members, (s + 1) * members),
                    attended[start : start + members],
                )


def attend(plan, incoming, w_qkv, sets):
    masks, _, sides = plan
    _, size, channels = incoming[0].shape
    count = len(masks) * sides * size // sets
    sent = outgoing_shapes(plan, size, channels)
    head_width = channels // HEADS
    group_heads = LANES // head_width
    total = sets * channels // LANES
    return pl.pallas_call(
        functools.partial(attend_kernel, plan=plan, sets=sets, came=len(incoming)),
        in_specs=[vmem()] * (len(incoming) + 1),
        out_specs=[vmem()] * len(sent),
        out_shape=[jax.ShapeDtypeStruct(shape, jnp.bfloat16) for shape in sent],
        scratch_shapes=[
            pltpu.VMEM((total, count, LANES), jnp.bfloat16),
            pltpu.VMEM((total, count, LANES), jnp.bfloat16),
            pltpu.VMEM((total, group_heads, head_width + 16, count), jnp.bfloat16),
            pltpu.VMEM((total, LANES, count), jnp.bfloat16),
            pltpu.VMEM((group_heads * count, count), jnp.float32),
            pltpu.VMEM((group_heads * count, count), jnp.float32),
        ],
        compiler_params=pltpu.CompilerParams(vmem_limit_bytes=10 * MIB),
        cost_estimate=pl.CostEstimate(
            flops=sets * (2 * count * channels * channels * 3 + 4 * count * count * channels),
            bytes_accessed=4 * sets * count * channels + 6 * channels * channels,
            transcendentals=sets * HEADS * count * count,
        ),
        name="attend",
    )(*incoming, w_qkv)


def finish_kernel(own_ref, *refs, plan):
    masks, _, sides = plan
    in_refs, rest = refs[:-7], refs[-7:]
    back_ref, weight_ref, mixed_ref, out_ref, attended_ref, made_ref, sent = rest
    tokens = mixed_ref.shape[0]
    size = in_refs[0].shape[1]
    for index, mask in enumerate(masks):
        for side in range(sides):
            start = pl.multiple_of((own_ref[0] ^ (mask | side)) * size, 16)
            attended_ref[pl.ds(start, size), :] = read_block(
                plan, in_refs, index, side, slice(None)
            )
    step = made_ref.shape[1]
    copies = []
    for index, start in enumerate(range(0, tokens, step)):
        rows = slice(start, start + step)
        restored = matmul(back_ref[rows, :], attended_ref[...]).astype(jnp.bfloat16)
        made_ref[index] = mixed_ref[rows, :] + matmul(restored, weight_ref[...])
        copy = pltpu.make_async_copy(
            made_ref.at[index], out_ref.at[pl.ds(start, step)], sent.at[index]
        )
        copy.start()
        copies.append(copy)
    for copy in copies:
        copy.wait()


def finish(own, plan, incoming, back, w_out, mixed):
    tokens, channels = mixed.shape
    step = divisor(tokens, 128, 16)
    return pl.pallas_call(
        functools.partial(finish_kernel, plan=plan),
        in_specs=[pl.BlockSpec(memory_space=pltpu.SMEM)] + [vmem()] * (len(incoming) + 3),
        out_specs=pl.BlockSpec(memory_space=pltpu.HBM),
        out_shape=jax.ShapeDtypeStruct((tokens, channels), jnp.float32),
        scratch_shapes=[
            pltpu.VMEM((tokens, channels), jnp.bfloat16),
            pltpu.VMEM((tokens // step, step, channels), jnp.float32),
            pltpu.SemaphoreType.DMA((tokens // step,)),
        ],
        compiler_params=pltpu.CompilerParams(vmem_limit_bytes=6 * MIB),
        name="finish",
    )(own, *incoming, back, w_out, mixed)


def swap_pairs(edge, axis, start):
    pairs = [(i, i + 1) for i in range(start, lax.axis_size(axis) - 1, 2)]
    return lax.ppermute(edge, axis, pairs + [(b, a) for a, b in pairs])


def exchange_plan(row_devices, col_devices):
    devices = row_devices * col_devices
    crossing = list(range(devices - 2, devices // 2 - 1, -2))
    others = list(range(devices // 2 - 2, 0, -2))
    masks = crossing[:1]
    for index, mask in enumerate(crossing[1:]):
        masks += [mask] + others[index : index + 1]
    return masks + [0], min(2, len(masks)), 2


def outgoing_shapes(plan, size, channels):
    masks, late, sides = plan
    if sides == 1:
        return [(1, size, channels)]
    early = len(masks) - 1 - late
    return [(2, size, channels)] * late + [
        (1, size, channels), (early + 1, size, channels), (early, size, channels)
    ]


def write_block(plan, refs, index, side, rows, value):
    masks, late, sides = plan
    if sides == 1:
        refs[0][0, rows] = value
    elif index < late:
        refs[index][side, rows] = value
    elif index == len(masks) - 1:
        refs[late + side][0, rows] = value
    elif side == 0:
        refs[late + 2][index - late, rows] = value
    else:
        refs[late + 1][index - late + 1, rows] = value


def read_block(plan, refs, index, side, rows):
    masks, late, sides = plan
    if sides == 1:
        return refs[0][0, rows]
    if index < late:
        return refs[index + side * len(masks)][side, rows]
    if index == len(masks) - 1:
        return refs[index + side * (late + 1)][0, rows]
    return refs[index][side, rows]


def join_kernel(own_ref, swapped_ref, *out_refs):
    for index, out_ref in enumerate(out_refs):
        out_ref[0] = own_ref[index]
        out_ref[1] = swapped_ref[index + 1]


def join(own, swapped):
    early, size, channels = own.shape
    return pl.pallas_call(
        join_kernel,
        in_specs=[vmem()] * 2,
        out_specs=[vmem()] * early,
        out_shape=[jax.ShapeDtypeStruct((2, size, channels), own.dtype)] * early,
        compiler_params=pltpu.CompilerParams(vmem_limit_bytes=2 * MIB),
        name="join",
    )(own, swapped)


def trade(plan, outgoing):
    masks, late, _ = plan
    devices = lax.axis_size("row") * lax.axis_size("col")

    def swap(slab, mask):
        return lax.ppermute(slab, ("row", "col"), [(i, i ^ mask) for i in range(devices)])

    slabs, (kept, passed, own) = outgoing[:late], outgoing[late:]
    swapped = swap(passed, 1)
    first = [swap(slab, mask) for slab, mask in zip(slabs, masks)]
    rest = [swap(slab, mask) for slab, mask in zip(join(own, swapped), masks[late:-1])]
    tie = min(1, len(rest) - 1)
    *first, rest[tie] = lax.optimization_barrier((*first, rest[tie]))
    return [*first, *rest, kept, *[swap(slab, 1) for slab in first], swapped]


def trade_all(slabs, sets, members, outward):
    axes = ("row", "col")
    channels = slabs[0].shape[-1]
    block = slabs[0].reshape(-1, channels)
    devices = block.shape[0] // (sets * members)
    if not outward:
        block = block.reshape(sets, devices, members, channels).transpose(1, 0, 2, 3)
    block = block.reshape(devices, sets * members, channels)
    block = lax.all_to_all(block, axes, 0, 0, tiled=True)
    if outward:
        block = block.reshape(devices, sets, members, channels).transpose(1, 0, 2, 3)
    return [block.reshape(1, -1, channels)]


def grouping(rows, cols, blocks_rows, blocks_cols):
    order = np.arange(rows * cols).reshape(
        blocks_rows, rows // blocks_rows, blocks_cols, cols // blocks_cols
    )
    order = order.transpose(1, 3, 0, 2).reshape(-1)
    matrix = np.zeros((order.size, order.size), np.float32)
    matrix[np.arange(order.size), order] = 1.0
    return matrix


def shards(field, w_expand, depth_kernel, w_project, w_qkv, w_out):
    rows, cols, channels = field.shape
    tokens = rows * cols
    row_devices = lax.axis_size("row")
    col_devices = lax.axis_size("col")
    devices = row_devices * col_devices
    blocks_rows = GRID // row_devices
    blocks_cols = GRID // col_devices
    members = blocks_rows * blocks_cols
    sets_local = tokens // members // devices
    matrix = grouping(rows, cols, blocks_rows, blocks_cols)
    perm = jnp.asarray(matrix, jnp.bfloat16)
    back = jnp.asarray(matrix.T, jnp.bfloat16)

    flat = field.reshape(tokens, channels)
    pairwise = 8 <= devices <= 16 and devices & (devices - 1) == 0 and col_devices % 2 == 0
    plan = exchange_plan(row_devices, col_devices) if pairwise else ([0], 0, 1)
    row, col = lax.axis_index("row"), lax.axis_index("col")
    own = (row * col_devices + col if pairwise else row * 0).reshape(1)
    odd_row, odd_col = (row % 2).reshape(1), (col % 2).reshape(1)

    one, two = row_edges(odd_row, field[0], field[rows - 1])
    one, two = swap_pairs(one, "row", 0), swap_pairs(two, "row", 1)
    normed = half_norm_of(flat)
    expanded = expand(normed, w_expand)
    one, two, normed, expanded = lax.optimization_barrier((one, two, normed, expanded))
    up, down, one, two = column_strips(odd_row, odd_col, normed, one, two, round_up(rows + 2, 16))
    one, two = swap_pairs(one, "col", 0), swap_pairs(two, "col", 1)

    size = tokens // (len(plan[0]) * plan[2])
    mixed, *outgoing = mix(
        own, odd_col, plan, size, expanded, flat, up, down, one, two, w_expand, depth_kernel, w_project,
        perm, rows, cols,
    )

    def route(outgoing, outward):
        if pairwise:
            return trade(plan, outgoing)
        return trade_all(outgoing, sets_local, members, outward)

    outgoing = attend(plan, route(outgoing, True), w_qkv, sets_local)
    final = finish(own, plan, route(outgoing, False), back, w_out, mixed)
    return final.reshape(rows, cols, channels)


def solution(mesh):
    return jax.shard_map(
        shards,
        mesh=mesh,
        in_specs=(P(("field", "row"), "col", None), P(), P(), P(), P(), P()),
        out_specs=P(("field", "row"), "col", None),
        check_vma=False,
    )
```

```python
import functools
import math

import jax
import jax.numpy as jnp
import numpy as np
from jax import lax
from jax.experimental import pallas as pl
from jax.experimental.pallas import tpu as pltpu
from jax.sharding import PartitionSpec as P

HEADS = 16
GRID = 16
LANES = 128
MIB = 1024 * 1024
NT = (((1,), (1,)), ((), ()))


def layer_norm(inputs):
    average = jnp.mean(inputs, axis=-1, keepdims=True)
    centred = inputs - average
    variance = jnp.mean(centred * centred, axis=-1, keepdims=True)
    return centred * lax.rsqrt(variance + 1e-05)


def gelu_of_half(half):
    scale = math.sqrt(2.0 / math.pi)
    inner = half * (2.0 * scale + (8.0 * scale * 0.044715) * (half * half))
    return half + half * jnp.tanh(inner)


def matmul(a, b):
    return jnp.dot(a, b, preferred_element_type=jnp.float32)


def matmul_nt(a, b):
    return lax.dot_general(a, b, NT, preferred_element_type=jnp.float32)


def divisor(size, most, unit):
    best = size
    for piece in range(unit, most + 1, unit):
        if size % piece == 0:
            best = piece
    return best


def round_up(size, unit):
    return -(-size // unit) * unit


def vmem():
    return pl.BlockSpec(memory_space=pltpu.VMEM)


def half_norm(inputs):
    return (layer_norm(inputs) * 0.5).astype(jnp.bfloat16)


def half_norm_kernel(in_ref, out_ref):
    rows = in_ref.shape[0]
    step = divisor(rows, 128, 16)
    for start in range(0, rows, step):
        out_ref[start : start + step, :] = half_norm(in_ref[start : start + step, :])


def half_norm_of(inputs):
    return pl.pallas_call(
        half_norm_kernel,
        in_specs=[vmem()],
        out_specs=vmem(),
        out_shape=jax.ShapeDtypeStruct(inputs.shape, jnp.bfloat16),
        compiler_params=pltpu.CompilerParams(vmem_limit_bytes=4 * MIB),
        cost_estimate=pl.CostEstimate(
            flops=10**9, bytes_accessed=6 * inputs.size, transcendentals=inputs.shape[0]
        ),
        name="half_norm",
    )(inputs)


def choose(condition, one, two):
    flags = jnp.full((one.shape[0], 1), condition, jnp.int32) == 1
    return jnp.where(flags, one.astype(jnp.float32), two.astype(jnp.float32)).astype(one.dtype)


def edges_kernel(odd_row_ref, top_ref, bottom_ref, one_ref, two_ref):
    odd = odd_row_ref[0]
    top, bottom = half_norm(top_ref[...]), half_norm(bottom_ref[...])
    one_ref[...] = choose(odd, top, bottom)
    two_ref[...] = choose(odd, bottom, top)


def row_edges(odd_row, top, bottom):
    return pl.pallas_call(
        edges_kernel,
        in_specs=[pl.BlockSpec(memory_space=pltpu.SMEM)] + [vmem()] * 2,
        out_specs=[vmem()] * 2,
        out_shape=[jax.ShapeDtypeStruct(top.shape, jnp.bfloat16)] * 2,
        compiler_params=pltpu.CompilerParams(vmem_limit_bytes=4 * MIB),
        cost_estimate=pl.CostEstimate(
            flops=10**10, bytes_accessed=12 * top.size, transcendentals=2 * top.shape[0]
        ),
        name="row_edges",
    )(odd_row, top, bottom)


def picker(shape, pick):
    row = lax.broadcasted_iota(jnp.int32, shape, 0)
    column = lax.broadcasted_iota(jnp.int32, shape, 1)
    return jnp.where(pick(row, column), 1.0, 0.0).astype(jnp.bfloat16)


def strips_kernel(
    odd_row_ref, odd_col_ref, normed_ref, row_one_ref, row_two_ref, up_ref, down_ref, one_ref, two_ref
):
    tokens = normed_ref.shape[0]
    cols = up_ref.shape[0]
    rows = tokens // cols
    slot = one_ref.shape[0]
    odd_row, odd_col = odd_row_ref[0], odd_col_ref[0]
    up = choose(odd_row, row_one_ref[...], row_two_ref[...])
    down = choose(odd_row, row_two_ref[...], row_one_ref[...])
    up_ref[...] = up
    down_ref[...] = down
    strips = []
    for x in (0, cols - 1):
        body = picker(
            (slot, tokens), lambda i, j: (i >= 1) & (i <= rows) & (j == (i - 1) * cols + x)
        )
        head = picker((slot, cols), lambda i, j: (i == 0) & (j == x))
        foot = picker((slot, cols), lambda i, j: (i == rows + 1) & (j == x))
        strip = matmul(body, normed_ref[...]) + matmul(head, up) + matmul(foot, down)
        strips.append(strip.astype(jnp.bfloat16))
    one_ref[...] = choose(odd_col, strips[0], strips[1])
    two_ref[...] = choose(odd_col, strips[1], strips[0])


def column_strips(odd_row, odd_col, normed, row_one, row_two, slot):
    cols, channels = row_one.shape
    shapes = [(cols, channels)] * 2 + [(slot, channels)] * 2
    return pl.pallas_call(
        strips_kernel,
        in_specs=[pl.BlockSpec(memory_space=pltpu.SMEM)] * 2 + [vmem()] * 3,
        out_specs=[vmem()] * 4,
        out_shape=[jax.ShapeDtypeStruct(shape, jnp.bfloat16) for shape in shapes],
        compiler_params=pltpu.CompilerParams(vmem_limit_bytes=4 * MIB),
        name="column_strips",
    )(odd_row, odd_col, normed, row_one, row_two)


def padded_rows(tokens):
    return tokens + 16


def expand_kernel(normed_ref, weight_ref, out_ref):
    tokens = normed_ref.shape[0]
    width = weight_ref.shape[1]
    tile = divisor(width, 512, LANES)
    step = divisor(tokens, 128, 16)
    starts = range(0, tokens, step)

    def body(index, carry):
        lanes = pl.ds(pl.multiple_of(index * tile, tile), tile)
        for start in starts:
            made = gelu_of_half(
                matmul(normed_ref[start : start + step, :], weight_ref[:, lanes])
            )
            for sub in range(tile // LANES):
                row = (index * (tile // LANES) + sub) * padded_rows(tokens) + 8 + start
                out_ref[pl.ds(pl.multiple_of(row, 8), step), :] = made[
                    :, sub * LANES : (sub + 1) * LANES
                ]
        return carry

    lax.fori_loop(0, width // tile, body, 0)


def expand(normed, w_expand):
    tokens, channels = normed.shape
    width = w_expand.shape[1]
    return pl.pallas_call(
        expand_kernel,
        in_specs=[vmem()] * 2,
        out_specs=vmem(),
        out_shape=jax.ShapeDtypeStruct((width // LANES * padded_rows(tokens), LANES), jnp.float32),
        compiler_params=pltpu.CompilerParams(vmem_limit_bytes=4 * MIB),
        cost_estimate=pl.CostEstimate(
            flops=10**10,
            bytes_accessed=tokens * channels * 2 + channels * width * 2 + tokens * width * 4,
            transcendentals=tokens * width,
        ),
        name="expand",
    )(normed, w_expand)


def mix_kernel(
    own_ref, odd_col_ref, expanded_ref, field_ref, up_ref, down_ref, one_ref, two_ref, w_expand_ref, depth_ref,
    w_project_ref, perm_ref, mixed_ref, *refs, rows, cols, plan, size,
):
    masks, _, sides = plan
    sent = len(outgoing_shapes(plan, size, 1))
    slab_refs = refs[:sent]
    total_ref, normed_ref, grouped_ref, even_ref, odd_ref, even_halo_ref, odd_halo_ref = refs[sent:]
    tokens = rows * cols
    width = w_expand_ref.shape[1]
    tile = even_ref.shape[1]
    slot = one_ref.shape[0]
    up_start, down_start, left_start = 8, 16 + cols, 24 + 2 * cols
    right_start = left_start + slot

    odd_col = odd_col_ref[0]
    left = choose(odd_col, one_ref[...], two_ref[...])
    right = choose(odd_col, two_ref[...], one_ref[...])
    edges = jnp.concatenate([up_ref[...], down_ref[...], left, right], axis=0)

    def expand_halo(index, out_ref):
        lanes = pl.ds(pl.multiple_of(index * tile, tile), tile)
        made = gelu_of_half(matmul(edges, w_expand_ref[:, lanes]))
        for sub in range(tile // LANES):
            part = made[:, sub * LANES : (sub + 1) * LANES]
            out_ref[sub, up_start : up_start + cols] = part[:cols]
            out_ref[sub, down_start : down_start + cols] = part[cols : 2 * cols]
            out_ref[sub, left_start : left_start + 2 * slot] = part[2 * cols :]

    position = lax.broadcasted_iota(jnp.int32, (8, LANES), 0)
    at_first = position == 0
    at_last = position == 7

    def convolve(index, out_ref, halo_ref):
        for sub in range(tile // LANES):
            lanes = pl.ds(pl.multiple_of(index * tile + sub * LANES, LANES), LANES)
            base = (index * (tile // LANES) + sub) * padded_rows(tokens) + 8
            taps = [[0.5 * depth_ref[p, q : q + 1, lanes] for q in range(3)] for p in range(3)]
            sums = {}
            for y in range(-1, rows + 1):
                if y < 0:
                    parts = [halo_ref[sub, up_start + q : up_start + q + cols] for q in (-1, 0, 1)]
                elif y == rows:
                    parts = [
                        halo_ref[sub, down_start + q : down_start + q + cols] for q in (-1, 0, 1)
                    ]
                else:
                    parts = [
                        expanded_ref[pl.ds(base + (y * cols + q), cols), :] for q in (-1, 0, 1)
                    ]
                left = halo_ref[sub, left_start + y + 1 : left_start + y + 2]
                right = halo_ref[sub, right_start + y + 1 : right_start + y + 2]
                parts[0] = jnp.concatenate(
                    [jnp.where(at_first, left, parts[0][:8]), parts[0][8:]], axis=0
                )
                parts[2] = jnp.concatenate(
                    [parts[2][:-8], jnp.where(at_last, right, parts[2][-8:])], axis=0
                )
                for p in range(3):
                    target = y + 1 - p
                    if 0 <= target < rows:
                        for q in range(3):
                            term = taps[p][q] * parts[q]
                            sums[target] = sums[target] + term if target in sums else term
                if y > 0:
                    out_ref[
                        (y - 1) * cols : y * cols, sub * LANES : (sub + 1) * LANES
                    ] = gelu_of_half(sums.pop(y - 1)).astype(jnp.bfloat16)

    def project(index, in_ref):
        piece = pl.ds(pl.multiple_of(index * tile, tile), tile)
        total_ref[...] += matmul(in_ref[...], w_project_ref[piece, :])

    total_ref[...] = field_ref[...]
    expand_halo(0, even_halo_ref)
    expand_halo(1, odd_halo_ref)
    convolve(0, even_ref, even_halo_ref)

    def body(index, carry):
        project(2 * index, even_ref)
        convolve(2 * index + 1, odd_ref, odd_halo_ref)
        expand_halo(2 * index + 2, even_halo_ref)
        project(2 * index + 1, odd_ref)
        convolve(2 * index + 2, even_ref, even_halo_ref)
        expand_halo(2 * index + 3, odd_halo_ref)
        return carry

    pairs = width // tile // 2
    lax.fori_loop(0, pairs - 1, body, 0)
    project(2 * pairs - 2, even_ref)
    convolve(2 * pairs - 1, odd_ref, odd_halo_ref)
    project(2 * pairs - 1, odd_ref)

    step = divisor(tokens, 128, 16)
    for start in range(0, tokens, step):
        piece = slice(start, start + step)
        mixed = total_ref[piece, :]
        mixed_ref[piece, :] = mixed
        normed_ref[piece, :] = layer_norm(mixed).astype(jnp.bfloat16)
    grouped_ref[...] = matmul(perm_ref[...], normed_ref[...]).astype(jnp.bfloat16)
    for index, mask in enumerate(masks):
        for side in range(sides):
            start = pl.multiple_of((own_ref[0] ^ (mask | side)) * size, 16)
            write_block(
                plan, slab_refs, index, side, slice(None), grouped_ref[pl.ds(start, size), :]
            )


def mix(
    own, odd_col, plan, size, expanded, field, up, down, one, two, w_expand, depth_kernel, w_project,
    perm, rows, cols,
):
    tokens, channels = field.shape
    width = w_expand.shape[1]
    tile = divisor(width // 2, 256, LANES)
    slot = one.shape[0]
    sent = outgoing_shapes(plan, size, channels)
    halo = pltpu.VMEM((tile // LANES, 24 + 2 * cols + 2 * slot, LANES), jnp.float32)
    return pl.pallas_call(
        functools.partial(mix_kernel, rows=rows, cols=cols, plan=plan, size=size),
        in_specs=[pl.BlockSpec(memory_space=pltpu.SMEM)] * 2 + [vmem()] * 10,
        out_specs=[vmem()] * (1 + len(sent)),
        out_shape=[jax.ShapeDtypeStruct((tokens, channels), jnp.float32)]
        + [jax.ShapeDtypeStruct(shape, jnp.bfloat16) for shape in sent],
        scratch_shapes=[
            pltpu.VMEM((tokens, channels), jnp.float32),
            pltpu.VMEM((tokens, channels), jnp.bfloat16),
            pltpu.VMEM((tokens, channels), jnp.bfloat16),
            pltpu.VMEM((tokens, tile), jnp.bfloat16),
            pltpu.VMEM((tokens, tile), jnp.bfloat16),
            halo,
            halo,
        ],
        compiler_params=pltpu.CompilerParams(vmem_limit_bytes=8 * MIB),
        cost_estimate=pl.CostEstimate(
            flops=2 * tokens * channels * width,
            bytes_accessed=tokens * channels * 10 + 4 * channels * width + tokens * width * 4,
            transcendentals=tokens * width,
        ),
        name="mix",
    )(own, odd_col, expanded, field, up, down, one, two, w_expand, depth_kernel, w_project, perm)


def identity(size):
    row = lax.broadcasted_iota(jnp.int32, (size, size), 0)
    column = lax.broadcasted_iota(jnp.int32, (size, size), 1)
    return jnp.where(row == column, 1.0, 0.0).astype(jnp.bfloat16)


def attend_kernel(*refs, plan, sets, came):
    masks, _, sides = plan
    slabs = len(masks)
    _, size, channels = refs[0].shape
    in_refs, weight_ref, out_refs = refs[:came], refs[came], refs[came + 1 : -6]
    query_ref, key_ref, value_ref, turned_ref, even_ref, odd_ref = refs[-6:]
    members = size // sets
    count = slabs * sides * members
    head_width = channels // HEADS
    group_heads = LANES // head_width
    groups = channels // LANES
    factor = math.log2(math.e) / math.sqrt(head_width)
    lane = lax.broadcasted_iota(jnp.int32, (1, LANES), 1)
    masks = [
        jnp.where((lane >= j * head_width) & (lane < (j + 1) * head_width), 1.0, 0.0).astype(
            jnp.bfloat16
        )
        for j in range(group_heads)
    ]
    turn_values = identity(channels)
    for s in range(sets):
        piece = slice(s * members, (s + 1) * members)
        block = jnp.concatenate(
            [
                read_block(plan, in_refs, index, side, piece)
                for index in range(slabs)
                for side in range(sides)
            ],
            axis=0,
        )
        qkv = matmul(block, weight_ref[...]).astype(jnp.bfloat16)
        values = matmul_nt(turn_values, qkv[:, 2 * channels :]).astype(jnp.bfloat16)
        for group in range(groups):
            lanes = slice(group * LANES, (group + 1) * LANES)
            query_ref[s * groups + group] = qkv[:, lanes]
            key_ref[s * groups + group] = qkv[:, channels + group * LANES : channels + (group + 1) * LANES]
            for j in range(group_heads):
                head = (group * group_heads + j) * head_width
                value_ref[s * groups + group, j, :head_width] = values[head : head + head_width]
                value_ref[s * groups + group, j, head_width:] = jnp.ones((16, count), jnp.bfloat16)

    def scores(index, out):
        keys = key_ref[index]
        stacked = jnp.concatenate([keys * mask for mask in masks], axis=0)
        out[...] = matmul_nt(stacked, query_ref[index])

    def weigh(index, scores_ref):
        for j in range(group_heads):
            part = scores_ref[j * count : (j + 1) * count]
            highest = jnp.max(part, axis=0, keepdims=True)
            raised = jnp.exp2((part - highest) * factor).astype(jnp.bfloat16)
            product = matmul(value_ref[index, j], raised)
            scale = 1.0 / product[head_width : head_width + 1]
            turned_ref[index, j * head_width : (j + 1) * head_width] = (
                product[:head_width] * scale
            ).astype(jnp.bfloat16)

    total = sets * groups
    scores(0, even_ref)

    def body(pair, carry):
        scores(2 * pair + 1, odd_ref)
        weigh(2 * pair, even_ref)
        scores(jnp.minimum(2 * pair + 2, total - 1), even_ref)
        weigh(2 * pair + 1, odd_ref)
        return carry

    lax.fori_loop(0, total // 2, body, 0)
    turn_tokens = identity(count)
    for s in range(sets):
        turned = turned_ref[s * groups : (s + 1) * groups].reshape(channels, count)
        attended = matmul_nt(turn_tokens, turned).astype(jnp.bfloat16)
        for index in range(slabs):
            for side in range(sides):
                start = (index * sides + side) * members
                write_block(
                    plan, out_refs, index, side, slice(s * members, (s + 1) * members),
                    attended[start : start + members],
                )


def attend(plan, incoming, w_qkv, sets):
    masks, _, sides = plan
    _, size, channels = incoming[0].shape
    count = len(masks) * sides * size // sets
    sent = outgoing_shapes(plan, size, channels)
    head_width = channels // HEADS
    group_heads = LANES // head_width
    total = sets * channels // LANES
    return pl.pallas_call(
        functools.partial(attend_kernel, plan=plan, sets=sets, came=len(incoming)),
        in_specs=[vmem()] * (len(incoming) + 1),
        out_specs=[vmem()] * len(sent),
        out_shape=[jax.ShapeDtypeStruct(shape, jnp.bfloat16) for shape in sent],
        scratch_shapes=[
            pltpu.VMEM((total, count, LANES), jnp.bfloat16),
            pltpu.VMEM((total, count, LANES), jnp.bfloat16),
            pltpu.VMEM((total, group_heads, head_width + 16, count), jnp.bfloat16),
            pltpu.VMEM((total, LANES, count), jnp.bfloat16),
            pltpu.VMEM((group_heads * count, count), jnp.float32),
            pltpu.VMEM((group_heads * count, count), jnp.float32),
        ],
        compiler_params=pltpu.CompilerParams(vmem_limit_bytes=10 * MIB),
        cost_estimate=pl.CostEstimate(
            flops=sets * (2 * count * channels * channels * 3 + 4 * count * count * channels),
            bytes_accessed=4 * sets * count * channels + 6 * channels * channels,
            transcendentals=sets * HEADS * count * count,
        ),
        name="attend",
    )(*incoming, w_qkv)


def finish_kernel(own_ref, *refs, plan):
    masks, _, sides = plan
    in_refs, rest = refs[:-7], refs[-7:]
    back_ref, weight_ref, mixed_ref, out_ref, attended_ref, made_ref, sent = rest
    tokens = mixed_ref.shape[0]
    size = in_refs[0].shape[1]
    for index, mask in enumerate(masks):
        for side in range(sides):
            start = pl.multiple_of((own_ref[0] ^ (mask | side)) * size, 16)
            attended_ref[pl.ds(start, size), :] = read_block(
                plan, in_refs, index, side, slice(None)
            )
    step = made_ref.shape[1]
    copies = []
    for index, start in enumerate(range(0, tokens, step)):
        rows = slice(start, start + step)
        restored = matmul(back_ref[rows, :], attended_ref[...]).astype(jnp.bfloat16)
        made_ref[index] = mixed_ref[rows, :] + matmul(restored, weight_ref[...])
        copy = pltpu.make_async_copy(
            made_ref.at[index], out_ref.at[pl.ds(start, step)], sent.at[index]
        )
        copy.start()
        copies.append(copy)
    for copy in copies:
        copy.wait()


def finish(own, plan, incoming, back, w_out, mixed):
    tokens, channels = mixed.shape
    step = divisor(tokens, 128, 16)
    return pl.pallas_call(
        functools.partial(finish_kernel, plan=plan),
        in_specs=[pl.BlockSpec(memory_space=pltpu.SMEM)] + [vmem()] * (len(incoming) + 3),
        out_specs=pl.BlockSpec(memory_space=pltpu.HBM),
        out_shape=jax.ShapeDtypeStruct((tokens, channels), jnp.float32),
        scratch_shapes=[
            pltpu.VMEM((tokens, channels), jnp.bfloat16),
            pltpu.VMEM((tokens // step, step, channels), jnp.float32),
            pltpu.SemaphoreType.DMA((tokens // step,)),
        ],
        compiler_params=pltpu.CompilerParams(vmem_limit_bytes=6 * MIB),
        name="finish",
    )(own, *incoming, back, w_out, mixed)


def swap_pairs(edge, axis, start):
    pairs = [(i, i + 1) for i in range(start, lax.axis_size(axis) - 1, 2)]
    return lax.ppermute(edge, axis, pairs + [(b, a) for a, b in pairs])


def exchange_plan(row_devices, col_devices):
    devices = row_devices * col_devices
    crossing = list(range(devices - 2, devices // 2 - 1, -2))
    others = list(range(devices // 2 - 2, 0, -2))
    masks = crossing[:1]
    for index, mask in enumerate(crossing[1:]):
        masks += [mask] + others[index : index + 1]
    return masks + [0], min(2, len(masks)), 2


def outgoing_shapes(plan, size, channels):
    masks, late, sides = plan
    if sides == 1:
        return [(1, size, channels)]
    early = len(masks) - 1 - late
    return [(2, size, channels)] * late + [
        (1, size, channels), (early + 1, size, channels), (early, size, channels)
    ]


def write_block(plan, refs, index, side, rows, value):
    masks, late, sides = plan
    if sides == 1:
        refs[0][0, rows] = value
    elif index < late:
        refs[index][side, rows] = value
    elif index == len(masks) - 1:
        refs[late + side][0, rows] = value
    elif side == 0:
        refs[late + 2][index - late, rows] = value
    else:
        refs[late + 1][index - late + 1, rows] = value


def read_block(plan, refs, index, side, rows):
    masks, late, sides = plan
    if sides == 1:
        return refs[0][0, rows]
    if index < late:
        return refs[index + side * len(masks)][side, rows]
    if index == len(masks) - 1:
        return refs[index + side * (late + 1)][0, rows]
    return refs[index][side, rows]


def join_kernel(own_ref, swapped_ref, *out_refs):
    for index, out_ref in enumerate(out_refs):
        out_ref[0] = own_ref[index]
        out_ref[1] = swapped_ref[index + 1]


def join(own, swapped):
    early, size, channels = own.shape
    return pl.pallas_call(
        join_kernel,
        in_specs=[vmem()] * 2,
        out_specs=[vmem()] * early,
        out_shape=[jax.ShapeDtypeStruct((2, size, channels), own.dtype)] * early,
        compiler_params=pltpu.CompilerParams(vmem_limit_bytes=2 * MIB),
        name="join",
    )(own, swapped)


def trade(plan, outgoing):
    masks, late, _ = plan
    devices = lax.axis_size("row") * lax.axis_size("col")

    def swap(slab, mask):
        return lax.ppermute(slab, ("row", "col"), [(i, i ^ mask) for i in range(devices)])

    slabs, (kept, passed, own) = outgoing[:late], outgoing[late:]
    swapped = swap(passed, 1)
    first = [swap(slab, mask) for slab, mask in zip(slabs, masks)]
    rest = [swap(slab, mask) for slab, mask in zip(join(own, swapped), masks[late:-1])]
    tie = min(1, len(rest) - 1)
    *first, rest[tie] = lax.optimization_barrier((*first, rest[tie]))
    return [*first, *rest, kept, *[swap(slab, 1) for slab in first], swapped]


def trade_all(slabs, sets, members, outward):
    axes = ("row", "col")
    channels = slabs[0].shape[-1]
    block = slabs[0].reshape(-1, channels)
    devices = block.shape[0] // (sets * members)
    if not outward:
        block = block.reshape(sets, devices, members, channels).transpose(1, 0, 2, 3)
    block = block.reshape(devices, sets * members, channels)
    block = lax.all_to_all(block, axes, 0, 0, tiled=True)
    if outward:
        block = block.reshape(devices, sets, members, channels).transpose(1, 0, 2, 3)
    return [block.reshape(1, -1, channels)]


def grouping(rows, cols, blocks_rows, blocks_cols):
    order = np.arange(rows * cols).reshape(
        blocks_rows, rows // blocks_rows, blocks_cols, cols // blocks_cols
    )
    order = order.transpose(1, 3, 0, 2).reshape(-1)
    matrix = np.zeros((order.size, order.size), np.float32)
    matrix[np.arange(order.size), order] = 1.0
    return matrix


def shards(field, w_expand, depth_kernel, w_project, w_qkv, w_out):
    rows, cols, channels = field.shape
    tokens = rows * cols
    row_devices = lax.axis_size("row")
    col_devices = lax.axis_size("col")
    devices = row_devices * col_devices
    blocks_rows = GRID // row_devices
    blocks_cols = GRID // col_devices
    members = blocks_rows * blocks_cols
    sets_local = tokens // members // devices
    matrix = grouping(rows, cols, blocks_rows, blocks_cols)
    perm = jnp.asarray(matrix, jnp.bfloat16)
    back = jnp.asarray(matrix.T, jnp.bfloat16)

    flat = field.reshape(tokens, channels)
    pairwise = 8 <= devices <= 16 and devices & (devices - 1) == 0 and col_devices % 2 == 0
    plan = exchange_plan(row_devices, col_devices) if pairwise else ([0], 0, 1)
    row, col = lax.axis_index("row"), lax.axis_index("col")
    own = (row * col_devices + col if pairwise else row * 0).reshape(1)
    odd_row, odd_col = (row % 2).reshape(1), (col % 2).reshape(1)

    own, odd_row, odd_col, top, bottom = lax.optimization_barrier(
        (own, odd_row, odd_col, field[0], field[rows - 1])
    )
    one, two = row_edges(odd_row, top, bottom)
    one, two = swap_pairs(one, "row", 0), swap_pairs(two, "row", 1)
    normed = half_norm_of(flat)
    expanded = expand(normed, w_expand)
    one, two, normed, expanded = lax.optimization_barrier((one, two, normed, expanded))
    up, down, one, two = column_strips(odd_row, odd_col, normed, one, two, round_up(rows + 2, 16))
    one, two = swap_pairs(one, "col", 0), swap_pairs(two, "col", 1)

    size = tokens // (len(plan[0]) * plan[2])
    mixed, *outgoing = mix(
        own, odd_col, plan, size, expanded, flat, up, down, one, two, w_expand, depth_kernel, w_project,
        perm, rows, cols,
    )

    def route(outgoing, outward):
        if pairwise:
            return trade(plan, outgoing)
        return trade_all(outgoing, sets_local, members, outward)

    outgoing = attend(plan, route(outgoing, True), w_qkv, sets_local)
    final = finish(own, plan, route(outgoing, False), back, w_out, mixed)
    return final.reshape(rows, cols, channels)


def solution(mesh):
    return jax.shard_map(
        shards,
        mesh=mesh,
        in_specs=(P(("field", "row"), "col", None), P(), P(), P(), P(), P()),
        out_specs=P(("field", "row"), "col", None),
        check_vma=False,
    )
```

```python
import functools
import math

import jax
import jax.numpy as jnp
import numpy as np
from jax import lax
from jax.experimental import pallas as pl
from jax.experimental.pallas import tpu as pltpu
from jax.sharding import PartitionSpec as P

HEADS = 16
GRID = 16
LANES = 128
MIB = 1024 * 1024
NT = (((1,), (1,)), ((), ()))


def layer_norm(inputs):
    average = jnp.mean(inputs, axis=-1, keepdims=True)
    centred = inputs - average
    variance = jnp.mean(centred * centred, axis=-1, keepdims=True)
    return centred * lax.rsqrt(variance + 1e-05)


def gelu_of_half(half):
    scale = math.sqrt(2.0 / math.pi)
    inner = half * (2.0 * scale + (8.0 * scale * 0.044715) * (half * half))
    return half + half * jnp.tanh(inner)


def matmul(a, b):
    return jnp.dot(a, b, preferred_element_type=jnp.float32)


def matmul_nt(a, b):
    return lax.dot_general(a, b, NT, preferred_element_type=jnp.float32)


def divisor(size, most, unit):
    best = size
    for piece in range(unit, most + 1, unit):
        if size % piece == 0:
            best = piece
    return best


def round_up(size, unit):
    return -(-size // unit) * unit


def vmem():
    return pl.BlockSpec(memory_space=pltpu.VMEM)


def half_norm(inputs):
    return (layer_norm(inputs) * 0.5).astype(jnp.bfloat16)


def half_norm_kernel(in_ref, out_ref):
    rows = in_ref.shape[0]
    step = divisor(rows, 128, 16)
    for start in range(0, rows, step):
        out_ref[start : start + step, :] = half_norm(in_ref[start : start + step, :])


def half_norm_of(inputs):
    return pl.pallas_call(
        half_norm_kernel,
        in_specs=[vmem()],
        out_specs=vmem(),
        out_shape=jax.ShapeDtypeStruct(inputs.shape, jnp.bfloat16),
        compiler_params=pltpu.CompilerParams(vmem_limit_bytes=4 * MIB),
        cost_estimate=pl.CostEstimate(
            flops=10**9, bytes_accessed=6 * inputs.size, transcendentals=inputs.shape[0]
        ),
        name="half_norm",
    )(inputs)


def choose(condition, one, two):
    flags = jnp.full((one.shape[0], 1), condition, jnp.int32) == 1
    return jnp.where(flags, one.astype(jnp.float32), two.astype(jnp.float32)).astype(one.dtype)


def edges_kernel(odd_row_ref, top_ref, bottom_ref, one_ref, two_ref):
    odd = odd_row_ref[0]
    top, bottom = half_norm(top_ref[...]), half_norm(bottom_ref[...])
    one_ref[...] = choose(odd, top, bottom)
    two_ref[...] = choose(odd, bottom, top)


def row_edges(odd_row, top, bottom):
    return pl.pallas_call(
        edges_kernel,
        in_specs=[pl.BlockSpec(memory_space=pltpu.SMEM)] + [vmem()] * 2,
        out_specs=[vmem()] * 2,
        out_shape=[jax.ShapeDtypeStruct(top.shape, jnp.bfloat16)] * 2,
        compiler_params=pltpu.CompilerParams(vmem_limit_bytes=4 * MIB),
        cost_estimate=pl.CostEstimate(
            flops=10**10, bytes_accessed=12 * top.size, transcendentals=2 * top.shape[0]
        ),
        name="row_edges",
    )(odd_row, top, bottom)


def picker(shape, pick):
    row = lax.broadcasted_iota(jnp.int32, shape, 0)
    column = lax.broadcasted_iota(jnp.int32, shape, 1)
    return jnp.where(pick(row, column), 1.0, 0.0).astype(jnp.bfloat16)


def strips_kernel(
    odd_row_ref, odd_col_ref, normed_ref, row_one_ref, row_two_ref, up_ref, down_ref, one_ref, two_ref
):
    tokens = normed_ref.shape[0]
    cols = up_ref.shape[0]
    rows = tokens // cols
    slot = one_ref.shape[0]
    odd_row, odd_col = odd_row_ref[0], odd_col_ref[0]
    up = choose(odd_row, row_one_ref[...], row_two_ref[...])
    down = choose(odd_row, row_two_ref[...], row_one_ref[...])
    up_ref[...] = up
    down_ref[...] = down
    strips = []
    for x in (0, cols - 1):
        body = picker(
            (slot, tokens), lambda i, j: (i >= 1) & (i <= rows) & (j == (i - 1) * cols + x)
        )
        head = picker((slot, cols), lambda i, j: (i == 0) & (j == x))
        foot = picker((slot, cols), lambda i, j: (i == rows + 1) & (j == x))
        strip = matmul(body, normed_ref[...]) + matmul(head, up) + matmul(foot, down)
        strips.append(strip.astype(jnp.bfloat16))
    one_ref[...] = choose(odd_col, strips[0], strips[1])
    two_ref[...] = choose(odd_col, strips[1], strips[0])


def column_strips(odd_row, odd_col, normed, row_one, row_two, slot):
    cols, channels = row_one.shape
    shapes = [(cols, channels)] * 2 + [(slot, channels)] * 2
    return pl.pallas_call(
        strips_kernel,
        in_specs=[pl.BlockSpec(memory_space=pltpu.SMEM)] * 2 + [vmem()] * 3,
        out_specs=[vmem()] * 4,
        out_shape=[jax.ShapeDtypeStruct(shape, jnp.bfloat16) for shape in shapes],
        compiler_params=pltpu.CompilerParams(vmem_limit_bytes=4 * MIB),
        name="column_strips",
    )(odd_row, odd_col, normed, row_one, row_two)


def padded_rows(tokens):
    return tokens + 16


def expand_kernel(normed_ref, weight_ref, out_ref):
    tokens = normed_ref.shape[0]
    width = weight_ref.shape[1]
    tile = divisor(width, 512, LANES)
    step = divisor(tokens, 128, 16)
    starts = range(0, tokens, step)

    def body(index, carry):
        lanes = pl.ds(pl.multiple_of(index * tile, tile), tile)
        for start in starts:
            made = gelu_of_half(
                matmul(normed_ref[start : start + step, :], weight_ref[:, lanes])
            )
            for sub in range(tile // LANES):
                row = (index * (tile // LANES) + sub) * padded_rows(tokens) + 8 + start
                out_ref[pl.ds(pl.multiple_of(row, 8), step), :] = made[
                    :, sub * LANES : (sub + 1) * LANES
                ]
        return carry

    lax.fori_loop(0, width // tile, body, 0)


def expand(normed, w_expand):
    tokens, channels = normed.shape
    width = w_expand.shape[1]
    return pl.pallas_call(
        expand_kernel,
        in_specs=[vmem()] * 2,
        out_specs=vmem(),
        out_shape=jax.ShapeDtypeStruct((width // LANES * padded_rows(tokens), LANES), jnp.float32),
        compiler_params=pltpu.CompilerParams(vmem_limit_bytes=4 * MIB),
        cost_estimate=pl.CostEstimate(
            flops=10**10,
            bytes_accessed=tokens * channels * 2 + channels * width * 2 + tokens * width * 4,
            transcendentals=tokens * width,
        ),
        name="expand",
    )(normed, w_expand)


def inner_kernel(
    expanded_ref, start_ref, depth_ref, w_project_ref, total_ref, rim_ref, even_ref, odd_ref,
    *, rows, cols, first, count,
):
    tokens = rows * cols
    tile = even_ref.shape[1]
    subs = tile // LANES
    position = lax.broadcasted_iota(jnp.int32, (8, LANES), 0)
    at_first = position == 0
    at_last = position == 7

    def clear_ends(value, low, high):
        head = jnp.where(at_first, 0.0, value[:8]) if low else value[:8]
        foot = jnp.where(at_last, 0.0, value[-8:]) if high else value[-8:]
        return jnp.concatenate([head, value[8:-8], foot], axis=0)

    def convolve(index, out_ref):
        for sub in range(subs):
            chunk = (first + index) * subs + sub
            lanes = pl.ds(pl.multiple_of(chunk * LANES, LANES), LANES)
            base = chunk * padded_rows(tokens) + 8
            here = index * subs + sub
            taps = [[0.5 * depth_ref[p, q : q + 1, lanes] for q in range(3)] for p in range(3)]
            spot = slice(sub * LANES, (sub + 1) * LANES)
            sums = {}
            for y in range(rows + 1):
                if y < rows:
                    parts = [
                        expanded_ref[pl.ds(base + (y * cols + q), cols), :] for q in (-1, 0, 1)
                    ]
                    parts[0] = clear_ends(parts[0], True, False)
                    parts[2] = clear_ends(parts[2], False, True)
                    for p in range(3):
                        target = y + 1 - p
                        if 0 <= target < rows:
                            for q in range(3):
                                term = taps[p][q] * parts[q]
                                sums[target] = sums[target] + term if target in sums else term
                if y > 0:
                    done = sums.pop(y - 1)
                    rim_ref[here, 2 * cols + y - 1 : 2 * cols + y] = done[:1]
                    rim_ref[here, 2 * cols + rows + y - 1 : 2 * cols + rows + y] = done[-1:]
                    if y in (1, rows):
                        start = 0 if y == 1 else cols
                        rim_ref[here, start : start + cols] = done
                        made = jnp.zeros_like(done)
                    else:
                        made = clear_ends(gelu_of_half(done), True, True)
                    out_ref[(y - 1) * cols : y * cols, spot] = made.astype(jnp.bfloat16)

    def project(index, in_ref, from_ref):
        piece = pl.ds(pl.multiple_of((first + index) * tile, tile), tile)
        total_ref[...] = from_ref[...] + matmul(in_ref[...], w_project_ref[piece, :])

    convolve(0, even_ref)
    project(0, even_ref, start_ref)
    convolve(1, odd_ref)

    def body(index, carry):
        convolve(2 * index, even_ref)
        project(2 * index - 1, odd_ref, total_ref)
        convolve(2 * index + 1, odd_ref)
        project(2 * index, even_ref, total_ref)
        return carry

    lax.fori_loop(1, count // 2, body, 0)
    project(count - 1, odd_ref, total_ref)


def inner(expanded, start, depth_kernel, w_project, rows, cols, first, count, tile):
    tokens, channels = start.shape
    rim = (count * tile // LANES, 2 * cols + 2 * rows, LANES)
    return pl.pallas_call(
        functools.partial(inner_kernel, rows=rows, cols=cols, first=first, count=count),
        in_specs=[vmem()] * 4,
        out_specs=[vmem()] * 2,
        out_shape=[
            jax.ShapeDtypeStruct((tokens, channels), jnp.float32),
            jax.ShapeDtypeStruct(rim, jnp.float32),
        ],
        scratch_shapes=[pltpu.VMEM((tokens, tile), jnp.bfloat16)] * 2,
        compiler_params=pltpu.CompilerParams(vmem_limit_bytes=6 * MIB),
        cost_estimate=pl.CostEstimate(
            flops=2 * 10**9 * count,
            bytes_accessed=tokens * channels * 8 + tokens * count * tile * 4,
            transcendentals=tokens * count * tile,
        ),
        name="inner",
    )(expanded, start, depth_kernel, w_project)


def rim_kernel(
    own_ref, odd_col_ref, inner_ref, *refs, rows, cols, plan, size, pieces,
):
    masks, _, sides = plan
    sent = len(outgoing_shapes(plan, size, 1))
    rim_refs, refs = refs[:pieces], refs[pieces:]
    up_ref, down_ref, one_ref, two_ref, w_expand_ref, depth_ref, w_project_ref, perm_ref = refs[:8]
    mixed_ref, slab_refs = refs[8], refs[9 : 9 + sent]
    halo_ref, active_ref, normed_ref, grouped_ref = refs[9 + sent :]
    tokens = rows * cols
    width = w_expand_ref.shape[1]
    tile = divisor(width, 512, LANES)
    subs = tile // LANES
    slot = one_ref.shape[0]
    left_start, right_start = 2 * cols, 2 * cols + slot

    odd_col = odd_col_ref[0]
    left = choose(odd_col, one_ref[...], two_ref[...])
    right = choose(odd_col, two_ref[...], one_ref[...])
    edges = jnp.concatenate([up_ref[...], down_ref[...], left, right], axis=0)

    def expand_halo(index, carry):
        lanes = pl.ds(pl.multiple_of(index * tile, tile), tile)
        made = gelu_of_half(matmul(edges, w_expand_ref[:, lanes]))
        for sub in range(subs):
            halo_ref[index * subs + sub] = made[:, sub * LANES : (sub + 1) * LANES]
        return carry

    lax.fori_loop(0, width // tile, expand_halo, 0)
    mixed_ref[...] = inner_ref[...]
    position = lax.broadcasted_iota(jnp.int32, (cols, LANES), 0)
    at_first = position == 0
    at_last = position == cols - 1

    def activate(chunk, here, sums_ref):
        lanes = pl.ds(pl.multiple_of(chunk * LANES, LANES), LANES)
        taps = [[0.5 * depth_ref[p, q : q + 1, lanes] for q in range(3)] for p in range(3)]
        beside = []
        for q, start in ((0, left_start), (2, right_start)):
            beside.append(
                sum(taps[p][q] * halo_ref[chunk, start + p : start + p + rows] for p in range(3))
            )
        made = []
        for p, start, y in ((0, 0, 0), (2, cols, rows - 1)):
            row = halo_ref[chunk, start : start + cols]
            before = jnp.where(at_first, beside[0][y : y + 1], taps[p][0] * pltpu.roll(row, 1, 0))
            after = jnp.where(
                at_last, beside[1][y : y + 1], taps[p][2] * pltpu.roll(row, cols - 1, 0)
            )
            made.append(sums_ref[here, start : start + cols] + before + taps[p][1] * row + after)
        for index in range(2):
            start = 2 * cols + index * rows
            made.append(sums_ref[here, start : start + rows] + beside[index])
        active_ref[:, lanes] = gelu_of_half(jnp.concatenate(made, axis=0)).astype(jnp.bfloat16)

    chunk = 0
    for sums_ref in rim_refs:
        offset = chunk

        def body(index, carry, sums_ref=sums_ref, offset=offset):
            activate(offset + 2 * index, 2 * index, sums_ref)
            activate(offset + 2 * index + 1, 2 * index + 1, sums_ref)
            return carry

        lax.fori_loop(0, sums_ref.shape[0] // 2, body, 0)
        chunk += sums_ref.shape[0]

    branch = matmul(active_ref[...], w_project_ref[...])
    mixed_ref[:cols, :] += branch[:cols]
    mixed_ref[tokens - cols :, :] += branch[cols : 2 * cols]
    for y in range(1, rows - 1):
        for index, x in ((0, 0), (1, cols - 1)):
            spot = y * cols + x
            start = 2 * cols + index * rows + y
            mixed_ref[spot : spot + 1, :] += branch[start : start + 1]

    step = divisor(tokens, 128, 16)
    for start in range(0, tokens, step):
        piece = slice(start, start + step)
        normed_ref[piece, :] = layer_norm(mixed_ref[piece, :]).astype(jnp.bfloat16)
    grouped_ref[...] = matmul(perm_ref[...], normed_ref[...]).astype(jnp.bfloat16)
    for index, mask in enumerate(masks):
        for side in range(sides):
            start = pl.multiple_of((own_ref[0] ^ (mask | side)) * size, 16)
            write_block(
                plan, slab_refs, index, side, slice(None), grouped_ref[pl.ds(start, size), :]
            )


def rim(
    own, odd_col, plan, size, total, rims, up, down, one, two, w_expand, depth_kernel, w_project, perm,
    rows, cols,
):
    tokens, channels = total.shape
    width = w_expand.shape[1]
    halo_rows = 2 * cols + 2 * one.shape[0]
    sent = outgoing_shapes(plan, size, channels)
    return pl.pallas_call(
        functools.partial(
            rim_kernel, rows=rows, cols=cols, plan=plan, size=size, pieces=len(rims)
        ),
        in_specs=[pl.BlockSpec(memory_space=pltpu.SMEM)] * 2 + [vmem()] * (9 + len(rims)),
        out_specs=[vmem()] * (1 + len(sent)),
        out_shape=[jax.ShapeDtypeStruct((tokens, channels), jnp.float32)]
        + [jax.ShapeDtypeStruct(shape, jnp.bfloat16) for shape in sent],
        scratch_shapes=[
            pltpu.VMEM((width // LANES, halo_rows, LANES), jnp.float32),
            pltpu.VMEM((2 * cols + 2 * rows, width), jnp.bfloat16),
            pltpu.VMEM((tokens, channels), jnp.bfloat16),
            pltpu.VMEM((tokens, channels), jnp.bfloat16),
        ],
        compiler_params=pltpu.CompilerParams(vmem_limit_bytes=8 * MIB),
        cost_estimate=pl.CostEstimate(
            flops=2 * halo_rows * channels * width * 2 + 2 * tokens * tokens * channels,
            bytes_accessed=tokens * channels * 10 + 4 * channels * width,
            transcendentals=2 * halo_rows * width,
        ),
        name="rim",
    )(own, odd_col, total, *rims, up, down, one, two, w_expand, depth_kernel, w_project, perm)


def identity(size):
    row = lax.broadcasted_iota(jnp.int32, (size, size), 0)
    column = lax.broadcasted_iota(jnp.int32, (size, size), 1)
    return jnp.where(row == column, 1.0, 0.0).astype(jnp.bfloat16)


def attend_kernel(*refs, plan, sets, came):
    masks, _, sides = plan
    slabs = len(masks)
    _, size, channels = refs[0].shape
    in_refs, weight_ref, out_refs = refs[:came], refs[came], refs[came + 1 : -6]
    query_ref, key_ref, value_ref, turned_ref, even_ref, odd_ref = refs[-6:]
    members = size // sets
    count = slabs * sides * members
    head_width = channels // HEADS
    group_heads = LANES // head_width
    groups = channels // LANES
    factor = math.log2(math.e) / math.sqrt(head_width)
    lane = lax.broadcasted_iota(jnp.int32, (1, LANES), 1)
    masks = [
        jnp.where((lane >= j * head_width) & (lane < (j + 1) * head_width), 1.0, 0.0).astype(
            jnp.bfloat16
        )
        for j in range(group_heads)
    ]
    turn_values = identity(channels)
    for s in range(sets):
        piece = slice(s * members, (s + 1) * members)
        block = jnp.concatenate(
            [
                read_block(plan, in_refs, index, side, piece)
                for index in range(slabs)
                for side in range(sides)
            ],
            axis=0,
        )
        qkv = matmul(block, weight_ref[...]).astype(jnp.bfloat16)
        values = matmul_nt(turn_values, qkv[:, 2 * channels :]).astype(jnp.bfloat16)
        for group in range(groups):
            lanes = slice(group * LANES, (group + 1) * LANES)
            query_ref[s * groups + group] = qkv[:, lanes]
            key_ref[s * groups + group] = qkv[:, channels + group * LANES : channels + (group + 1) * LANES]
            for j in range(group_heads):
                head = (group * group_heads + j) * head_width
                value_ref[s * groups + group, j, :head_width] = values[head : head + head_width]
                value_ref[s * groups + group, j, head_width:] = jnp.ones((16, count), jnp.bfloat16)

    def scores(index, out):
        keys = key_ref[index]
        stacked = jnp.concatenate([keys * mask for mask in masks], axis=0)
        out[...] = matmul_nt(stacked, query_ref[index])

    def weigh(index, scores_ref):
        for j in range(group_heads):
            part = scores_ref[j * count : (j + 1) * count]
            highest = jnp.max(part, axis=0, keepdims=True)
            raised = jnp.exp2((part - highest) * factor).astype(jnp.bfloat16)
            product = matmul(value_ref[index, j], raised)
            scale = 1.0 / product[head_width : head_width + 1]
            turned_ref[index, j * head_width : (j + 1) * head_width] = (
                product[:head_width] * scale
            ).astype(jnp.bfloat16)

    total = sets * groups
    scores(0, even_ref)

    def body(pair, carry):
        scores(2 * pair + 1, odd_ref)
        weigh(2 * pair, even_ref)
        scores(jnp.minimum(2 * pair + 2, total - 1), even_ref)
        weigh(2 * pair + 1, odd_ref)
        return carry

    lax.fori_loop(0, total // 2, body, 0)
    turn_tokens = identity(count)
    for s in range(sets):
        turned = turned_ref[s * groups : (s + 1) * groups].reshape(channels, count)
        attended = matmul_nt(turn_tokens, turned).astype(jnp.bfloat16)
        for index in range(slabs):
            for side in range(sides):
                start = (index * sides + side) * members
                write_block(
                    plan, out_refs, index, side, slice(s * members, (s + 1) * members),
                    attended[start : start + members],
                )


def attend(plan, incoming, w_qkv, sets):
    masks, _, sides = plan
    _, size, channels = incoming[0].shape
    count = len(masks) * sides * size // sets
    sent = outgoing_shapes(plan, size, channels)
    head_width = channels // HEADS
    group_heads = LANES // head_width
    total = sets * channels // LANES
    return pl.pallas_call(
        functools.partial(attend_kernel, plan=plan, sets=sets, came=len(incoming)),
        in_specs=[vmem()] * (len(incoming) + 1),
        out_specs=[vmem()] * len(sent),
        out_shape=[jax.ShapeDtypeStruct(shape, jnp.bfloat16) for shape in sent],
        scratch_shapes=[
            pltpu.VMEM((total, count, LANES), jnp.bfloat16),
            pltpu.VMEM((total, count, LANES), jnp.bfloat16),
            pltpu.VMEM((total, group_heads, head_width + 16, count), jnp.bfloat16),
            pltpu.VMEM((total, LANES, count), jnp.bfloat16),
            pltpu.VMEM((group_heads * count, count), jnp.float32),
            pltpu.VMEM((group_heads * count, count), jnp.float32),
        ],
        compiler_params=pltpu.CompilerParams(vmem_limit_bytes=10 * MIB),
        cost_estimate=pl.CostEstimate(
            flops=sets * (2 * count * channels * channels * 3 + 4 * count * count * channels),
            bytes_accessed=4 * sets * count * channels + 6 * channels * channels,
            transcendentals=sets * HEADS * count * count,
        ),
        name="attend",
    )(*incoming, w_qkv)


def finish_kernel(own_ref, *refs, plan):
    masks, _, sides = plan
    in_refs, rest = refs[:-7], refs[-7:]
    back_ref, weight_ref, mixed_ref, out_ref, attended_ref, made_ref, sent = rest
    tokens = mixed_ref.shape[0]
    size = in_refs[0].shape[1]
    for index, mask in enumerate(masks):
        for side in range(sides):
            start = pl.multiple_of((own_ref[0] ^ (mask | side)) * size, 16)
            attended_ref[pl.ds(start, size), :] = read_block(
                plan, in_refs, index, side, slice(None)
            )
    step = made_ref.shape[1]
    copies = []
    for index, start in enumerate(range(0, tokens, step)):
        rows = slice(start, start + step)
        restored = matmul(back_ref[rows, :], attended_ref[...]).astype(jnp.bfloat16)
        made_ref[index] = mixed_ref[rows, :] + matmul(restored, weight_ref[...])
        copy = pltpu.make_async_copy(
            made_ref.at[index], out_ref.at[pl.ds(start, step)], sent.at[index]
        )
        copy.start()
        copies.append(copy)
    for copy in copies:
        copy.wait()


def finish(own, plan, incoming, back, w_out, mixed):
    tokens, channels = mixed.shape
    step = divisor(tokens, 128, 16)
    return pl.pallas_call(
        functools.partial(finish_kernel, plan=plan),
        in_specs=[pl.BlockSpec(memory_space=pltpu.SMEM)] + [vmem()] * (len(incoming) + 3),
        out_specs=pl.BlockSpec(memory_space=pltpu.HBM),
        out_shape=jax.ShapeDtypeStruct((tokens, channels), jnp.float32),
        scratch_shapes=[
            pltpu.VMEM((tokens, channels), jnp.bfloat16),
            pltpu.VMEM((tokens // step, step, channels), jnp.float32),
            pltpu.SemaphoreType.DMA((tokens // step,)),
        ],
        compiler_params=pltpu.CompilerParams(vmem_limit_bytes=6 * MIB),
        name="finish",
    )(own, *incoming, back, w_out, mixed)


def swap_pairs(edge, axis, start):
    pairs = [(i, i + 1) for i in range(start, lax.axis_size(axis) - 1, 2)]
    return lax.ppermute(edge, axis, pairs + [(b, a) for a, b in pairs])


def exchange_plan(row_devices, col_devices):
    devices = row_devices * col_devices
    crossing = list(range(devices - 2, devices // 2 - 1, -2))
    others = list(range(devices // 2 - 2, 0, -2))
    masks = crossing[:1]
    for index, mask in enumerate(crossing[1:]):
        masks += [mask] + others[index : index + 1]
    return masks + [0], min(2, len(masks)), 2


def outgoing_shapes(plan, size, channels):
    masks, late, sides = plan
    if sides == 1:
        return [(1, size, channels)]
    early = len(masks) - 1 - late
    return [(2, size, channels)] * late + [
        (1, size, channels), (early + 1, size, channels), (early, size, channels)
    ]


def write_block(plan, refs, index, side, rows, value):
    masks, late, sides = plan
    if sides == 1:
        refs[0][0, rows] = value
    elif index < late:
        refs[index][side, rows] = value
    elif index == len(masks) - 1:
        refs[late + side][0, rows] = value
    elif side == 0:
        refs[late + 2][index - late, rows] = value
    else:
        refs[late + 1][index - late + 1, rows] = value


def read_block(plan, refs, index, side, rows):
    masks, late, sides = plan
    if sides == 1:
        return refs[0][0, rows]
    if index < late:
        return refs[index + side * len(masks)][side, rows]
    if index == len(masks) - 1:
        return refs[index + side * (late + 1)][0, rows]
    return refs[index][side, rows]


def join_kernel(own_ref, swapped_ref, *out_refs):
    for index, out_ref in enumerate(out_refs):
        out_ref[0] = own_ref[index]
        out_ref[1] = swapped_ref[index + 1]


def join(own, swapped):
    early, size, channels = own.shape
    return pl.pallas_call(
        join_kernel,
        in_specs=[vmem()] * 2,
        out_specs=[vmem()] * early,
        out_shape=[jax.ShapeDtypeStruct((2, size, channels), own.dtype)] * early,
        compiler_params=pltpu.CompilerParams(vmem_limit_bytes=2 * MIB),
        name="join",
    )(own, swapped)


def trade(plan, outgoing):
    masks, late, _ = plan
    devices = lax.axis_size("row") * lax.axis_size("col")

    def swap(slab, mask):
        return lax.ppermute(slab, ("row", "col"), [(i, i ^ mask) for i in range(devices)])

    slabs, (kept, passed, own) = outgoing[:late], outgoing[late:]
    swapped = swap(passed, 1)
    first = [swap(slab, mask) for slab, mask in zip(slabs, masks)]
    rest = [swap(slab, mask) for slab, mask in zip(join(own, swapped), masks[late:-1])]
    tie = min(1, len(rest) - 1)
    *first, rest[tie] = lax.optimization_barrier((*first, rest[tie]))
    return [*first, *rest, kept, *[swap(slab, 1) for slab in first], swapped]


def trade_all(slabs, sets, members, outward):
    axes = ("row", "col")
    channels = slabs[0].shape[-1]
    block = slabs[0].reshape(-1, channels)
    devices = block.shape[0] // (sets * members)
    if not outward:
        block = block.reshape(sets, devices, members, channels).transpose(1, 0, 2, 3)
    block = block.reshape(devices, sets * members, channels)
    block = lax.all_to_all(block, axes, 0, 0, tiled=True)
    if outward:
        block = block.reshape(devices, sets, members, channels).transpose(1, 0, 2, 3)
    return [block.reshape(1, -1, channels)]


def grouping(rows, cols, blocks_rows, blocks_cols):
    order = np.arange(rows * cols).reshape(
        blocks_rows, rows // blocks_rows, blocks_cols, cols // blocks_cols
    )
    order = order.transpose(1, 3, 0, 2).reshape(-1)
    matrix = np.zeros((order.size, order.size), np.float32)
    matrix[np.arange(order.size), order] = 1.0
    return matrix


def shards(field, w_expand, depth_kernel, w_project, w_qkv, w_out):
    rows, cols, channels = field.shape
    tokens = rows * cols
    row_devices = lax.axis_size("row")
    col_devices = lax.axis_size("col")
    devices = row_devices * col_devices
    blocks_rows = GRID // row_devices
    blocks_cols = GRID // col_devices
    members = blocks_rows * blocks_cols
    sets_local = tokens // members // devices
    matrix = grouping(rows, cols, blocks_rows, blocks_cols)
    perm = jnp.asarray(matrix, jnp.bfloat16)
    back = jnp.asarray(matrix.T, jnp.bfloat16)

    flat = field.reshape(tokens, channels)
    pairwise = 8 <= devices <= 16 and devices & (devices - 1) == 0 and col_devices % 2 == 0
    plan = exchange_plan(row_devices, col_devices) if pairwise else ([0], 0, 1)
    row, col = lax.axis_index("row"), lax.axis_index("col")
    own = (row * col_devices + col if pairwise else row * 0).reshape(1)
    odd_row, odd_col = (row % 2).reshape(1), (col % 2).reshape(1)

    own, odd_row, odd_col, top, bottom = lax.optimization_barrier(
        (own, odd_row, odd_col, field[0], field[rows - 1])
    )
    one, two = row_edges(odd_row, top, bottom)
    one, two = swap_pairs(one, "row", 0), swap_pairs(two, "row", 1)
    normed = half_norm_of(flat)
    expanded = expand(normed, w_expand)
    tile = divisor(w_expand.shape[1] // 2, 256, LANES)
    count = w_expand.shape[1] // tile
    early = 2
    total, rim_one = inner(
        expanded, flat, depth_kernel, w_project, rows, cols, 0, early, tile
    )
    one, two, normed, expanded, total, rim_one = lax.optimization_barrier(
        (one, two, normed, expanded, total, rim_one)
    )
    up, down, one, two = column_strips(odd_row, odd_col, normed, one, two, round_up(rows + 2, 16))
    one, two = swap_pairs(one, "col", 0), swap_pairs(two, "col", 1)
    total, rim_two = inner(
        expanded, total, depth_kernel, w_project, rows, cols, early, count - early, tile
    )

    size = tokens // (len(plan[0]) * plan[2])
    mixed, *outgoing = rim(
        own, odd_col, plan, size, total, [rim_one, rim_two], up, down, one, two, w_expand,
        depth_kernel, w_project, perm, rows, cols,
    )

    def route(outgoing, outward):
        if pairwise:
            return trade(plan, outgoing)
        return trade_all(outgoing, sets_local, members, outward)

    outgoing = attend(plan, route(outgoing, True), w_qkv, sets_local)
    final = finish(own, plan, route(outgoing, False), back, w_out, mixed)
    return final.reshape(rows, cols, channels)


def solution(mesh):
    return jax.shard_map(
        shards,
        mesh=mesh,
        in_specs=(P(("field", "row"), "col", None), P(), P(), P(), P(), P()),
        out_specs=P(("field", "row"), "col", None),
        check_vma=False,
    )
```

```python
import functools
import math

import jax
import jax.numpy as jnp
import numpy as np
from jax import lax
from jax.experimental import pallas as pl
from jax.experimental.pallas import tpu as pltpu
from jax.sharding import PartitionSpec as P

HEADS = 16
GRID = 16
LANES = 128
MIB = 1024 * 1024
NT = (((1,), (1,)), ((), ()))


def layer_norm(inputs):
    average = jnp.mean(inputs, axis=-1, keepdims=True)
    centred = inputs - average
    variance = jnp.mean(centred * centred, axis=-1, keepdims=True)
    return centred * lax.rsqrt(variance + 1e-05)


def gelu_of_half(half):
    scale = math.sqrt(2.0 / math.pi)
    inner = half * (2.0 * scale + (8.0 * scale * 0.044715) * (half * half))
    return half + half * jnp.tanh(inner)


def matmul(a, b):
    return jnp.dot(a, b, preferred_element_type=jnp.float32)


def matmul_nt(a, b):
    return lax.dot_general(a, b, NT, preferred_element_type=jnp.float32)


def divisor(size, most, unit):
    best = size
    for piece in range(unit, most + 1, unit):
        if size % piece == 0:
            best = piece
    return best


def round_up(size, unit):
    return -(-size // unit) * unit


def vmem():
    return pl.BlockSpec(memory_space=pltpu.VMEM)


def half_norm(inputs):
    return (layer_norm(inputs) * 0.5).astype(jnp.bfloat16)


def half_norm_kernel(in_ref, out_ref):
    rows = in_ref.shape[0]
    step = divisor(rows, 128, 16)
    for start in range(0, rows, step):
        out_ref[start : start + step, :] = half_norm(in_ref[start : start + step, :])


def half_norm_of(inputs):
    return pl.pallas_call(
        half_norm_kernel,
        in_specs=[vmem()],
        out_specs=vmem(),
        out_shape=jax.ShapeDtypeStruct(inputs.shape, jnp.bfloat16),
        compiler_params=pltpu.CompilerParams(vmem_limit_bytes=4 * MIB),
        cost_estimate=pl.CostEstimate(
            flops=10**9, bytes_accessed=6 * inputs.size, transcendentals=inputs.shape[0]
        ),
        name="half_norm",
    )(inputs)


def choose(condition, one, two):
    flags = jnp.full((one.shape[0], 1), condition, jnp.int32) == 1
    return jnp.where(flags, one.astype(jnp.float32), two.astype(jnp.float32)).astype(one.dtype)


def edges_kernel(odd_row_ref, top_ref, bottom_ref, one_ref, two_ref):
    odd = odd_row_ref[0]
    top, bottom = half_norm(top_ref[...]), half_norm(bottom_ref[...])
    one_ref[...] = choose(odd, top, bottom)
    two_ref[...] = choose(odd, bottom, top)


def row_edges(odd_row, top, bottom):
    return pl.pallas_call(
        edges_kernel,
        in_specs=[pl.BlockSpec(memory_space=pltpu.SMEM)] + [vmem()] * 2,
        out_specs=[vmem()] * 2,
        out_shape=[jax.ShapeDtypeStruct(top.shape, jnp.bfloat16)] * 2,
        compiler_params=pltpu.CompilerParams(vmem_limit_bytes=4 * MIB),
        cost_estimate=pl.CostEstimate(
            flops=10**10, bytes_accessed=12 * top.size, transcendentals=2 * top.shape[0]
        ),
        name="row_edges",
    )(odd_row, top, bottom)


def picker(shape, pick):
    row = lax.broadcasted_iota(jnp.int32, shape, 0)
    column = lax.broadcasted_iota(jnp.int32, shape, 1)
    return jnp.where(pick(row, column), 1.0, 0.0).astype(jnp.bfloat16)


def strips_kernel(
    odd_row_ref, odd_col_ref, normed_ref, row_one_ref, row_two_ref, up_ref, down_ref, one_ref, two_ref
):
    tokens = normed_ref.shape[0]
    cols = up_ref.shape[0]
    rows = tokens // cols
    slot = one_ref.shape[0]
    odd_row, odd_col = odd_row_ref[0], odd_col_ref[0]
    up = choose(odd_row, row_one_ref[...], row_two_ref[...])
    down = choose(odd_row, row_two_ref[...], row_one_ref[...])
    up_ref[...] = up
    down_ref[...] = down
    strips = []
    for x in (0, cols - 1):
        body = picker(
            (slot, tokens), lambda i, j: (i >= 1) & (i <= rows) & (j == (i - 1) * cols + x)
        )
        head = picker((slot, cols), lambda i, j: (i == 0) & (j == x))
        foot = picker((slot, cols), lambda i, j: (i == rows + 1) & (j == x))
        strip = matmul(body, normed_ref[...]) + matmul(head, up) + matmul(foot, down)
        strips.append(strip.astype(jnp.bfloat16))
    one_ref[...] = choose(odd_col, strips[0], strips[1])
    two_ref[...] = choose(odd_col, strips[1], strips[0])


def column_strips(odd_row, odd_col, normed, row_one, row_two, slot):
    cols, channels = row_one.shape
    shapes = [(cols, channels)] * 2 + [(slot, channels)] * 2
    return pl.pallas_call(
        strips_kernel,
        in_specs=[pl.BlockSpec(memory_space=pltpu.SMEM)] * 2 + [vmem()] * 3,
        out_specs=[vmem()] * 4,
        out_shape=[jax.ShapeDtypeStruct(shape, jnp.bfloat16) for shape in shapes],
        compiler_params=pltpu.CompilerParams(vmem_limit_bytes=4 * MIB),
        name="column_strips",
    )(odd_row, odd_col, normed, row_one, row_two)


def padded_rows(tokens):
    return tokens + 16


def expand_kernel(normed_ref, weight_ref, out_ref):
    tokens = normed_ref.shape[0]
    width = weight_ref.shape[1]
    tile = divisor(width, 512, LANES)
    step = divisor(tokens, 128, 16)
    starts = range(0, tokens, step)

    def body(index, carry):
        lanes = pl.ds(pl.multiple_of(index * tile, tile), tile)
        for start in starts:
            made = gelu_of_half(
                matmul(normed_ref[start : start + step, :], weight_ref[:, lanes])
            )
            for sub in range(tile // LANES):
                row = (index * (tile // LANES) + sub) * padded_rows(tokens) + 8 + start
                out_ref[pl.ds(pl.multiple_of(row, 8), step), :] = made[
                    :, sub * LANES : (sub + 1) * LANES
                ]
        return carry

    lax.fori_loop(0, width // tile, body, 0)


def expand(normed, w_expand):
    tokens, channels = normed.shape
    width = w_expand.shape[1]
    return pl.pallas_call(
        expand_kernel,
        in_specs=[vmem()] * 2,
        out_specs=vmem(),
        out_shape=jax.ShapeDtypeStruct((width // LANES * padded_rows(tokens), LANES), jnp.float32),
        compiler_params=pltpu.CompilerParams(vmem_limit_bytes=4 * MIB),
        cost_estimate=pl.CostEstimate(
            flops=10**10,
            bytes_accessed=tokens * channels * 2 + channels * width * 2 + tokens * width * 4,
            transcendentals=tokens * width,
        ),
        name="expand",
    )(normed, w_expand)


def inner_kernel(
    expanded_ref, start_ref, depth_ref, w_project_ref, total_ref, rim_ref, even_ref, odd_ref,
    *, rows, cols, first, count,
):
    tokens = rows * cols
    tile = even_ref.shape[1]
    subs = tile // LANES
    position = lax.broadcasted_iota(jnp.int32, (8, LANES), 0)
    at_first = position == 0
    at_last = position == 7

    def clear_ends(value, low, high):
        head = jnp.where(at_first, 0.0, value[:8]) if low else value[:8]
        foot = jnp.where(at_last, 0.0, value[-8:]) if high else value[-8:]
        return jnp.concatenate([head, value[8:-8], foot], axis=0)

    def convolve(index, out_ref):
        for sub in range(subs):
            chunk = (first + index) * subs + sub
            lanes = pl.ds(pl.multiple_of(chunk * LANES, LANES), LANES)
            base = chunk * padded_rows(tokens) + 8
            here = index * subs + sub
            taps = [[0.5 * depth_ref[p, q : q + 1, lanes] for q in range(3)] for p in range(3)]
            spot = slice(sub * LANES, (sub + 1) * LANES)
            sums = {}
            for y in range(rows + 1):
                if y < rows:
                    parts = [
                        expanded_ref[pl.ds(base + (y * cols + q), cols), :] for q in (-1, 0, 1)
                    ]
                    parts[0] = clear_ends(parts[0], True, False)
                    parts[2] = clear_ends(parts[2], False, True)
                    for p in range(3):
                        target = y + 1 - p
                        if 0 <= target < rows:
                            for q in range(3):
                                term = taps[p][q] * parts[q]
                                sums[target] = sums[target] + term if target in sums else term
                if y > 0:
                    done = sums.pop(y - 1)
                    rim_ref[here, 2 * cols + y - 1 : 2 * cols + y] = done[:1]
                    rim_ref[here, 2 * cols + rows + y - 1 : 2 * cols + rows + y] = done[-1:]
                    if y in (1, rows):
                        start = 0 if y == 1 else cols
                        rim_ref[here, start : start + cols] = done
                        made = jnp.zeros_like(done)
                    else:
                        made = clear_ends(gelu_of_half(done), True, True)
                    out_ref[(y - 1) * cols : y * cols, spot] = made.astype(jnp.bfloat16)

    def project(index, in_ref, from_ref):
        piece = pl.ds(pl.multiple_of((first + index) * tile, tile), tile)
        total_ref[...] = from_ref[...] + matmul(in_ref[...], w_project_ref[piece, :])

    convolve(0, even_ref)
    project(0, even_ref, start_ref)
    convolve(1, odd_ref)

    def body(index, carry):
        convolve(2 * index, even_ref)
        project(2 * index - 1, odd_ref, total_ref)
        convolve(2 * index + 1, odd_ref)
        project(2 * index, even_ref, total_ref)
        return carry

    lax.fori_loop(1, count // 2, body, 0)
    project(count - 1, odd_ref, total_ref)


def inner(expanded, start, depth_kernel, w_project, rows, cols, first, count, tile):
    tokens, channels = start.shape
    rim = (count * tile // LANES, 2 * cols + 2 * rows, LANES)
    return pl.pallas_call(
        functools.partial(inner_kernel, rows=rows, cols=cols, first=first, count=count),
        in_specs=[vmem()] * 4,
        out_specs=[vmem()] * 2,
        out_shape=[
            jax.ShapeDtypeStruct((tokens, channels), jnp.float32),
            jax.ShapeDtypeStruct(rim, jnp.float32),
        ],
        scratch_shapes=[pltpu.VMEM((tokens, tile), jnp.bfloat16)] * 2,
        compiler_params=pltpu.CompilerParams(vmem_limit_bytes=6 * MIB),
        cost_estimate=pl.CostEstimate(
            flops=2 * 10**9 * count,
            bytes_accessed=tokens * channels * 8 + tokens * count * tile * 4,
            transcendentals=tokens * count * tile,
        ),
        name="inner",
    )(expanded, start, depth_kernel, w_project)


def rim_kernel(
    own_ref, odd_col_ref, inner_ref, *refs, rows, cols, plan, size, pieces,
):
    masks, _, sides = plan
    sent = len(outgoing_shapes(plan, size, 1))
    rim_refs, refs = refs[:pieces], refs[pieces:]
    up_ref, down_ref, one_ref, two_ref, w_expand_ref, depth_ref, w_project_ref, perm_ref = refs[:8]
    mixed_ref, slab_refs = refs[8], refs[9 : 9 + sent]
    halo_ref, active_ref, normed_ref, grouped_ref = refs[9 + sent :]
    tokens = rows * cols
    width = w_expand_ref.shape[1]
    tile = divisor(width, 512, LANES)
    subs = tile // LANES
    slot = one_ref.shape[0]
    left_start, right_start = 2 * cols, 2 * cols + slot

    odd_col = odd_col_ref[0]
    left = choose(odd_col, one_ref[...], two_ref[...])
    right = choose(odd_col, two_ref[...], one_ref[...])
    edges = jnp.concatenate([up_ref[...], down_ref[...], left, right], axis=0)

    def expand_halo(index, carry):
        lanes = pl.ds(pl.multiple_of(index * tile, tile), tile)
        made = gelu_of_half(matmul(edges, w_expand_ref[:, lanes]))
        for sub in range(subs):
            halo_ref[index * subs + sub] = made[:, sub * LANES : (sub + 1) * LANES]
        return carry

    lax.fori_loop(0, width // tile, expand_halo, 0)
    mixed_ref[...] = inner_ref[...]
    position = lax.broadcasted_iota(jnp.int32, (cols, LANES), 0)
    at_first = position == 0
    at_last = position == cols - 1

    def activate(chunk, here, sums_ref):
        lanes = pl.ds(pl.multiple_of(chunk * LANES, LANES), LANES)
        taps = [[0.5 * depth_ref[p, q : q + 1, lanes] for q in range(3)] for p in range(3)]
        beside = []
        for q, start in ((0, left_start), (2, right_start)):
            beside.append(
                sum(taps[p][q] * halo_ref[chunk, start + p : start + p + rows] for p in range(3))
            )
        made = []
        for p, start, y in ((0, 0, 0), (2, cols, rows - 1)):
            row = halo_ref[chunk, start : start + cols]
            before = jnp.where(at_first, beside[0][y : y + 1], taps[p][0] * pltpu.roll(row, 1, 0))
            after = jnp.where(
                at_last, beside[1][y : y + 1], taps[p][2] * pltpu.roll(row, cols - 1, 0)
            )
            made.append(sums_ref[here, start : start + cols] + before + taps[p][1] * row + after)
        for index in range(2):
            start = 2 * cols + index * rows
            made.append(sums_ref[here, start : start + rows] + beside[index])
        active_ref[:, lanes] = gelu_of_half(jnp.concatenate(made, axis=0)).astype(jnp.bfloat16)

    chunk = 0
    for sums_ref in rim_refs:
        offset = chunk

        def body(index, carry, sums_ref=sums_ref, offset=offset):
            activate(offset + 2 * index, 2 * index, sums_ref)
            activate(offset + 2 * index + 1, 2 * index + 1, sums_ref)
            return carry

        lax.fori_loop(0, sums_ref.shape[0] // 2, body, 0)
        chunk += sums_ref.shape[0]

    branch = matmul(active_ref[...], w_project_ref[...])
    mixed_ref[:cols, :] += branch[:cols]
    mixed_ref[tokens - cols :, :] += branch[cols : 2 * cols]
    for y in range(1, rows - 1):
        for index, x in ((0, 0), (1, cols - 1)):
            spot = y * cols + x
            start = 2 * cols + index * rows + y
            mixed_ref[spot : spot + 1, :] += branch[start : start + 1]

    step = divisor(tokens, 128, 16)
    for start in range(0, tokens, step):
        piece = slice(start, start + step)
        normed_ref[piece, :] = layer_norm(mixed_ref[piece, :]).astype(jnp.bfloat16)
    grouped_ref[...] = matmul(perm_ref[...], normed_ref[...]).astype(jnp.bfloat16)
    for index, mask in enumerate(masks):
        for side in range(sides):
            start = pl.multiple_of((own_ref[0] ^ (mask | side)) * size, 16)
            write_block(
                plan, slab_refs, index, side, slice(None), grouped_ref[pl.ds(start, size), :]
            )


def rim(
    own, odd_col, plan, size, total, rims, up, down, one, two, w_expand, depth_kernel, w_project, perm,
    rows, cols,
):
    tokens, channels = total.shape
    width = w_expand.shape[1]
    halo_rows = 2 * cols + 2 * one.shape[0]
    sent = outgoing_shapes(plan, size, channels)
    return pl.pallas_call(
        functools.partial(
            rim_kernel, rows=rows, cols=cols, plan=plan, size=size, pieces=len(rims)
        ),
        in_specs=[pl.BlockSpec(memory_space=pltpu.SMEM)] * 2 + [vmem()] * (9 + len(rims)),
        out_specs=[vmem()] * (1 + len(sent)),
        out_shape=[jax.ShapeDtypeStruct((tokens, channels), jnp.float32)]
        + [jax.ShapeDtypeStruct(shape, jnp.bfloat16) for shape in sent],
        scratch_shapes=[
            pltpu.VMEM((width // LANES, halo_rows, LANES), jnp.float32),
            pltpu.VMEM((2 * cols + 2 * rows, width), jnp.bfloat16),
            pltpu.VMEM((tokens, channels), jnp.bfloat16),
            pltpu.VMEM((tokens, channels), jnp.bfloat16),
        ],
        compiler_params=pltpu.CompilerParams(vmem_limit_bytes=8 * MIB),
        cost_estimate=pl.CostEstimate(
            flops=2 * halo_rows * channels * width * 2 + 2 * tokens * tokens * channels,
            bytes_accessed=tokens * channels * 10 + 4 * channels * width,
            transcendentals=2 * halo_rows * width,
        ),
        name="rim",
    )(own, odd_col, total, *rims, up, down, one, two, w_expand, depth_kernel, w_project, perm)


def identity(size):
    row = lax.broadcasted_iota(jnp.int32, (size, size), 0)
    column = lax.broadcasted_iota(jnp.int32, (size, size), 1)
    return jnp.where(row == column, 1.0, 0.0).astype(jnp.bfloat16)


def attend_kernel(*refs, plan, sets, came):
    masks, _, sides = plan
    slabs = len(masks)
    _, size, channels = refs[0].shape
    in_refs, weight_ref, out_refs = refs[:came], refs[came], refs[came + 1 : -6]
    query_ref, key_ref, value_ref, turned_ref, even_ref, odd_ref = refs[-6:]
    members = size // sets
    count = slabs * sides * members
    head_width = channels // HEADS
    group_heads = LANES // head_width
    groups = channels // LANES
    factor = math.log2(math.e) / math.sqrt(head_width)
    lane = lax.broadcasted_iota(jnp.int32, (1, LANES), 1)
    masks = [
        jnp.where((lane >= j * head_width) & (lane < (j + 1) * head_width), 1.0, 0.0).astype(
            jnp.bfloat16
        )
        for j in range(group_heads)
    ]
    turn_values = identity(channels)
    for s in range(sets):
        piece = slice(s * members, (s + 1) * members)
        block = jnp.concatenate(
            [
                read_block(plan, in_refs, index, side, piece)
                for index in range(slabs)
                for side in range(sides)
            ],
            axis=0,
        )
        qkv = matmul(block, weight_ref[...]).astype(jnp.bfloat16)
        values = matmul_nt(turn_values, qkv[:, 2 * channels :]).astype(jnp.bfloat16)
        for group in range(groups):
            lanes = slice(group * LANES, (group + 1) * LANES)
            query_ref[s * groups + group] = qkv[:, lanes]
            key_ref[s * groups + group] = qkv[:, channels + group * LANES : channels + (group + 1) * LANES]
            for j in range(group_heads):
                head = (group * group_heads + j) * head_width
                value_ref[s * groups + group, j, :head_width] = values[head : head + head_width]
                value_ref[s * groups + group, j, head_width:] = jnp.ones((16, count), jnp.bfloat16)

    def scores(index, out):
        keys = key_ref[index]
        stacked = jnp.concatenate([keys * mask for mask in masks], axis=0)
        out[...] = matmul_nt(stacked, query_ref[index])

    def weigh(index, scores_ref):
        for j in range(group_heads):
            part = scores_ref[j * count : (j + 1) * count]
            highest = jnp.max(part, axis=0, keepdims=True)
            raised = jnp.exp2((part - highest) * factor).astype(jnp.bfloat16)
            product = matmul(value_ref[index, j], raised)
            scale = 1.0 / product[head_width : head_width + 1]
            turned_ref[index, j * head_width : (j + 1) * head_width] = (
                product[:head_width] * scale
            ).astype(jnp.bfloat16)

    total = sets * groups
    scores(0, even_ref)

    def body(pair, carry):
        scores(2 * pair + 1, odd_ref)
        weigh(2 * pair, even_ref)
        scores(jnp.minimum(2 * pair + 2, total - 1), even_ref)
        weigh(2 * pair + 1, odd_ref)
        return carry

    lax.fori_loop(0, total // 2, body, 0)
    turn_tokens = identity(count)
    for s in range(sets):
        turned = turned_ref[s * groups : (s + 1) * groups].reshape(channels, count)
        attended = matmul_nt(turn_tokens, turned).astype(jnp.bfloat16)
        for index in range(slabs):
            for side in range(sides):
                start = (index * sides + side) * members
                write_block(
                    plan, out_refs, index, side, slice(s * members, (s + 1) * members),
                    attended[start : start + members],
                )


def attend(plan, incoming, w_qkv, sets):
    masks, _, sides = plan
    _, size, channels = incoming[0].shape
    count = len(masks) * sides * size // sets
    sent = outgoing_shapes(plan, size, channels)
    head_width = channels // HEADS
    group_heads = LANES // head_width
    total = sets * channels // LANES
    return pl.pallas_call(
        functools.partial(attend_kernel, plan=plan, sets=sets, came=len(incoming)),
        in_specs=[vmem()] * (len(incoming) + 1),
        out_specs=[vmem()] * len(sent),
        out_shape=[jax.ShapeDtypeStruct(shape, jnp.bfloat16) for shape in sent],
        scratch_shapes=[
            pltpu.VMEM((total, count, LANES), jnp.bfloat16),
            pltpu.VMEM((total, count, LANES), jnp.bfloat16),
            pltpu.VMEM((total, group_heads, head_width + 16, count), jnp.bfloat16),
            pltpu.VMEM((total, LANES, count), jnp.bfloat16),
            pltpu.VMEM((group_heads * count, count), jnp.float32),
            pltpu.VMEM((group_heads * count, count), jnp.float32),
        ],
        compiler_params=pltpu.CompilerParams(vmem_limit_bytes=10 * MIB),
        cost_estimate=pl.CostEstimate(
            flops=sets * (2 * count * channels * channels * 3 + 4 * count * count * channels),
            bytes_accessed=4 * sets * count * channels + 6 * channels * channels,
            transcendentals=sets * HEADS * count * count,
        ),
        name="attend",
    )(*incoming, w_qkv)


def finish_kernel(own_ref, *refs, plan):
    masks, _, sides = plan
    in_refs, rest = refs[:-7], refs[-7:]
    back_ref, weight_ref, mixed_ref, out_ref, attended_ref, made_ref, sent = rest
    tokens = mixed_ref.shape[0]
    size = in_refs[0].shape[1]
    for index, mask in enumerate(masks):
        for side in range(sides):
            start = pl.multiple_of((own_ref[0] ^ (mask | side)) * size, 16)
            attended_ref[pl.ds(start, size), :] = read_block(
                plan, in_refs, index, side, slice(None)
            )
    step = made_ref.shape[1]
    copies = []
    for index, start in enumerate(range(0, tokens, step)):
        rows = slice(start, start + step)
        restored = matmul(back_ref[rows, :], attended_ref[...]).astype(jnp.bfloat16)
        made_ref[index] = mixed_ref[rows, :] + matmul(restored, weight_ref[...])
        copy = pltpu.make_async_copy(
            made_ref.at[index], out_ref.at[pl.ds(start, step)], sent.at[index]
        )
        copy.start()
        copies.append(copy)
    for copy in copies:
        copy.wait()


def finish(own, plan, incoming, back, w_out, mixed):
    tokens, channels = mixed.shape
    step = divisor(tokens, 128, 16)
    return pl.pallas_call(
        functools.partial(finish_kernel, plan=plan),
        in_specs=[pl.BlockSpec(memory_space=pltpu.SMEM)] + [vmem()] * (len(incoming) + 3),
        out_specs=pl.BlockSpec(memory_space=pltpu.HBM),
        out_shape=jax.ShapeDtypeStruct((tokens, channels), jnp.float32),
        scratch_shapes=[
            pltpu.VMEM((tokens, channels), jnp.bfloat16),
            pltpu.VMEM((tokens // step, step, channels), jnp.float32),
            pltpu.SemaphoreType.DMA((tokens // step,)),
        ],
        compiler_params=pltpu.CompilerParams(vmem_limit_bytes=6 * MIB),
        name="finish",
    )(own, *incoming, back, w_out, mixed)


def swap_pairs(edge, axis, start):
    pairs = [(i, i + 1) for i in range(start, lax.axis_size(axis) - 1, 2)]
    return lax.ppermute(edge, axis, pairs + [(b, a) for a, b in pairs])


def exchange_plan(row_devices, col_devices):
    devices = row_devices * col_devices
    crossing = list(range(devices - 2, devices // 2 - 1, -2))
    others = list(range(devices // 2 - 2, 0, -2))
    masks = crossing[:-1] + others[:-1] + crossing[-1:] + others[-1:] + [0]
    return masks, 2, 2


def outgoing_shapes(plan, size, channels):
    masks, late, sides = plan
    if sides == 1:
        return [(1, size, channels)]
    early = len(masks) - 1 - late
    return [(2, size, channels)] * late + [
        (1, size, channels), (early + 1, size, channels), (early, size, channels)
    ]


def write_block(plan, refs, index, side, rows, value):
    masks, late, sides = plan
    if sides == 1:
        refs[0][0, rows] = value
    elif index < late:
        refs[index][side, rows] = value
    elif index == len(masks) - 1:
        refs[late + side][0, rows] = value
    elif side == 0:
        refs[late + 2][index - late, rows] = value
    else:
        refs[late + 1][index - late + 1, rows] = value


def read_block(plan, refs, index, side, rows):
    masks, late, sides = plan
    if sides == 1:
        return refs[0][0, rows]
    if index < late:
        return refs[index + side * len(masks)][side, rows]
    if index == len(masks) - 1:
        return refs[index + side * (late + 1)][0, rows]
    return refs[index][side, rows]


def join_kernel(own_ref, swapped_ref, *out_refs):
    for index, out_ref in enumerate(out_refs):
        out_ref[0] = own_ref[index]
        out_ref[1] = swapped_ref[index + 1]


def join(own, swapped):
    early, size, channels = own.shape
    return pl.pallas_call(
        join_kernel,
        in_specs=[vmem()] * 2,
        out_specs=[vmem()] * early,
        out_shape=[jax.ShapeDtypeStruct((2, size, channels), own.dtype)] * early,
        compiler_params=pltpu.CompilerParams(vmem_limit_bytes=2 * MIB),
        name="join",
    )(own, swapped)


def trade(plan, outgoing):
    masks, late, _ = plan
    devices = lax.axis_size("row") * lax.axis_size("col")

    def swap(slab, mask):
        return lax.ppermute(slab, ("row", "col"), [(i, i ^ mask) for i in range(devices)])

    slabs, (kept, passed, own) = outgoing[:late], outgoing[late:]
    swapped = swap(passed, 1)
    first = [swap(slab, mask) for slab, mask in zip(slabs, masks)]
    rest = [swap(slab, mask) for slab, mask in zip(join(own, swapped), masks[late:-1])]
    tied = lax.optimization_barrier((*first, *rest[:-late]))
    first, rest = tied[:late], [*tied[late:], *rest[-late:]]
    return [*first, *rest, kept, *[swap(slab, 1) for slab in first], swapped]


def trade_all(slabs, sets, members, outward):
    axes = ("row", "col")
    channels = slabs[0].shape[-1]
    block = slabs[0].reshape(-1, channels)
    devices = block.shape[0] // (sets * members)
    if not outward:
        block = block.reshape(sets, devices, members, channels).transpose(1, 0, 2, 3)
    block = block.reshape(devices, sets * members, channels)
    block = lax.all_to_all(block, axes, 0, 0, tiled=True)
    if outward:
        block = block.reshape(devices, sets, members, channels).transpose(1, 0, 2, 3)
    return [block.reshape(1, -1, channels)]


def grouping(rows, cols, blocks_rows, blocks_cols):
    order = np.arange(rows * cols).reshape(
        blocks_rows, rows // blocks_rows, blocks_cols, cols // blocks_cols
    )
    order = order.transpose(1, 3, 0, 2).reshape(-1)
    matrix = np.zeros((order.size, order.size), np.float32)
    matrix[np.arange(order.size), order] = 1.0
    return matrix


def shards(field, w_expand, depth_kernel, w_project, w_qkv, w_out):
    rows, cols, channels = field.shape
    tokens = rows * cols
    row_devices = lax.axis_size("row")
    col_devices = lax.axis_size("col")
    devices = row_devices * col_devices
    blocks_rows = GRID // row_devices
    blocks_cols = GRID // col_devices
    members = blocks_rows * blocks_cols
    sets_local = tokens // members // devices
    matrix = grouping(rows, cols, blocks_rows, blocks_cols)
    perm = jnp.asarray(matrix, jnp.bfloat16)
    back = jnp.asarray(matrix.T, jnp.bfloat16)

    flat = field.reshape(tokens, channels)
    pairwise = 8 <= devices <= 16 and devices & (devices - 1) == 0 and col_devices % 2 == 0
    plan = exchange_plan(row_devices, col_devices) if pairwise else ([0], 0, 1)
    row, col = lax.axis_index("row"), lax.axis_index("col")
    own = (row * col_devices + col if pairwise else row * 0).reshape(1)
    odd_row, odd_col = (row % 2).reshape(1), (col % 2).reshape(1)

    own, odd_row, odd_col, top, bottom = lax.optimization_barrier(
        (own, odd_row, odd_col, field[0], field[rows - 1])
    )
    one, two = row_edges(odd_row, top, bottom)
    one, two = swap_pairs(one, "row", 0), swap_pairs(two, "row", 1)
    normed = half_norm_of(flat)
    expanded = expand(normed, w_expand)
    tile = divisor(w_expand.shape[1] // 2, 256, LANES)
    count = w_expand.shape[1] // tile
    early = 2
    total, rim_one = inner(
        expanded, flat, depth_kernel, w_project, rows, cols, 0, early, tile
    )
    one, two, normed, expanded, total, rim_one = lax.optimization_barrier(
        (one, two, normed, expanded, total, rim_one)
    )
    up, down, one, two = column_strips(odd_row, odd_col, normed, one, two, round_up(rows + 2, 16))
    one, two = swap_pairs(one, "col", 0), swap_pairs(two, "col", 1)
    total, rim_two = inner(
        expanded, total, depth_kernel, w_project, rows, cols, early, count - early, tile
    )

    size = tokens // (len(plan[0]) * plan[2])
    mixed, *outgoing = rim(
        own, odd_col, plan, size, total, [rim_one, rim_two], up, down, one, two, w_expand,
        depth_kernel, w_project, perm, rows, cols,
    )

    def route(outgoing, outward):
        if pairwise:
            return trade(plan, outgoing)
        return trade_all(outgoing, sets_local, members, outward)

    outgoing = attend(plan, route(outgoing, True), w_qkv, sets_local)
    final = finish(own, plan, route(outgoing, False), back, w_out, mixed)
    return final.reshape(rows, cols, channels)


def solution(mesh):
    return jax.shard_map(
        shards,
        mesh=mesh,
        in_specs=(P(("field", "row"), "col", None), P(), P(), P(), P(), P()),
        out_specs=P(("field", "row"), "col", None),
        check_vma=False,
    )
```

```python
import functools
import math

import jax
import jax.numpy as jnp
import numpy as np
from jax import lax
from jax.experimental import pallas as pl
from jax.experimental.pallas import tpu as pltpu
from jax.sharding import PartitionSpec as P

HEADS = 16
GRID = 16
LANES = 128
MIB = 1024 * 1024
NT = (((1,), (1,)), ((), ()))


def layer_norm(inputs):
    average = jnp.mean(inputs, axis=-1, keepdims=True)
    centred = inputs - average
    variance = jnp.mean(centred * centred, axis=-1, keepdims=True)
    return centred * lax.rsqrt(variance + 1e-05)


def gelu_of_half(half):
    scale = math.sqrt(2.0 / math.pi)
    inner = half * (2.0 * scale + (8.0 * scale * 0.044715) * (half * half))
    return half + half * jnp.tanh(inner)


def matmul(a, b):
    return jnp.dot(a, b, preferred_element_type=jnp.float32)


def matmul_nt(a, b):
    return lax.dot_general(a, b, NT, preferred_element_type=jnp.float32)


def divisor(size, most, unit):
    best = size
    for piece in range(unit, most + 1, unit):
        if size % piece == 0:
            best = piece
    return best


def round_up(size, unit):
    return -(-size // unit) * unit


def vmem():
    return pl.BlockSpec(memory_space=pltpu.VMEM)


def half_norm(inputs):
    return (layer_norm(inputs) * 0.5).astype(jnp.bfloat16)


def half_norm_kernel(in_ref, out_ref):
    rows = in_ref.shape[0]
    step = divisor(rows, 128, 16)
    for start in range(0, rows, step):
        out_ref[start : start + step, :] = half_norm(in_ref[start : start + step, :])


def half_norm_of(inputs):
    return pl.pallas_call(
        half_norm_kernel,
        in_specs=[vmem()],
        out_specs=vmem(),
        out_shape=jax.ShapeDtypeStruct(inputs.shape, jnp.bfloat16),
        compiler_params=pltpu.CompilerParams(vmem_limit_bytes=4 * MIB),
        cost_estimate=pl.CostEstimate(
            flops=10**9, bytes_accessed=6 * inputs.size, transcendentals=inputs.shape[0]
        ),
        name="half_norm",
    )(inputs)


def choose(condition, one, two):
    flags = jnp.full((one.shape[0], 1), condition, jnp.int32) == 1
    return jnp.where(flags, one.astype(jnp.float32), two.astype(jnp.float32)).astype(one.dtype)


def edges_kernel(odd_row_ref, top_ref, bottom_ref, one_ref, two_ref):
    odd = odd_row_ref[0]
    top, bottom = half_norm(top_ref[...]), half_norm(bottom_ref[...])
    one_ref[...] = choose(odd, top, bottom)
    two_ref[...] = choose(odd, bottom, top)


def row_edges(odd_row, top, bottom):
    return pl.pallas_call(
        edges_kernel,
        in_specs=[pl.BlockSpec(memory_space=pltpu.SMEM)] + [vmem()] * 2,
        out_specs=[vmem()] * 2,
        out_shape=[jax.ShapeDtypeStruct(top.shape, jnp.bfloat16)] * 2,
        compiler_params=pltpu.CompilerParams(vmem_limit_bytes=4 * MIB),
        cost_estimate=pl.CostEstimate(
            flops=10**10, bytes_accessed=12 * top.size, transcendentals=2 * top.shape[0]
        ),
        name="row_edges",
    )(odd_row, top, bottom)


def picker(shape, pick):
    row = lax.broadcasted_iota(jnp.int32, shape, 0)
    column = lax.broadcasted_iota(jnp.int32, shape, 1)
    return jnp.where(pick(row, column), 1.0, 0.0).astype(jnp.bfloat16)


def strips_kernel(
    odd_row_ref, odd_col_ref, normed_ref, row_one_ref, row_two_ref, up_ref, down_ref, one_ref, two_ref
):
    tokens = normed_ref.shape[0]
    cols = up_ref.shape[0]
    rows = tokens // cols
    slot = one_ref.shape[0]
    odd_row, odd_col = odd_row_ref[0], odd_col_ref[0]
    up = choose(odd_row, row_one_ref[...], row_two_ref[...])
    down = choose(odd_row, row_two_ref[...], row_one_ref[...])
    up_ref[...] = up
    down_ref[...] = down
    strips = []
    for x in (0, cols - 1):
        body = picker(
            (slot, tokens), lambda i, j: (i >= 1) & (i <= rows) & (j == (i - 1) * cols + x)
        )
        head = picker((slot, cols), lambda i, j: (i == 0) & (j == x))
        foot = picker((slot, cols), lambda i, j: (i == rows + 1) & (j == x))
        strip = matmul(body, normed_ref[...]) + matmul(head, up) + matmul(foot, down)
        strips.append(strip.astype(jnp.bfloat16))
    one_ref[...] = choose(odd_col, strips[0], strips[1])
    two_ref[...] = choose(odd_col, strips[1], strips[0])


def column_strips(odd_row, odd_col, normed, row_one, row_two, slot):
    cols, channels = row_one.shape
    shapes = [(cols, channels)] * 2 + [(slot, channels)] * 2
    return pl.pallas_call(
        strips_kernel,
        in_specs=[pl.BlockSpec(memory_space=pltpu.SMEM)] * 2 + [vmem()] * 3,
        out_specs=[vmem()] * 4,
        out_shape=[jax.ShapeDtypeStruct(shape, jnp.bfloat16) for shape in shapes],
        compiler_params=pltpu.CompilerParams(vmem_limit_bytes=4 * MIB),
        name="column_strips",
    )(odd_row, odd_col, normed, row_one, row_two)


def padded_rows(tokens):
    return tokens + 16


def expand_kernel(normed_ref, weight_ref, out_ref):
    tokens = normed_ref.shape[0]
    width = weight_ref.shape[1]
    tile = divisor(width, 512, LANES)
    step = divisor(tokens, 128, 16)
    starts = range(0, tokens, step)

    def body(index, carry):
        lanes = pl.ds(pl.multiple_of(index * tile, tile), tile)
        for start in starts:
            made = gelu_of_half(
                matmul(normed_ref[start : start + step, :], weight_ref[:, lanes])
            )
            for sub in range(tile // LANES):
                row = (index * (tile // LANES) + sub) * padded_rows(tokens) + 8 + start
                out_ref[pl.ds(pl.multiple_of(row, 8), step), :] = made[
                    :, sub * LANES : (sub + 1) * LANES
                ]
        return carry

    lax.fori_loop(0, width // tile, body, 0)


def expand(normed, w_expand):
    tokens, channels = normed.shape
    width = w_expand.shape[1]
    return pl.pallas_call(
        expand_kernel,
        in_specs=[vmem()] * 2,
        out_specs=vmem(),
        out_shape=jax.ShapeDtypeStruct((width // LANES * padded_rows(tokens), LANES), jnp.float32),
        compiler_params=pltpu.CompilerParams(vmem_limit_bytes=4 * MIB),
        cost_estimate=pl.CostEstimate(
            flops=10**10,
            bytes_accessed=tokens * channels * 2 + channels * width * 2 + tokens * width * 4,
            transcendentals=tokens * width,
        ),
        name="expand",
    )(normed, w_expand)


def inner_kernel(
    expanded_ref, start_ref, depth_ref, w_project_ref, total_ref, rim_ref, even_ref, odd_ref,
    *, rows, cols, first, count,
):
    tokens = rows * cols
    tile = even_ref.shape[1]
    subs = tile // LANES
    position = lax.broadcasted_iota(jnp.int32, (8, LANES), 0)
    at_first = position == 0
    at_last = position == 7

    def clear_ends(value, low, high):
        head = jnp.where(at_first, 0.0, value[:8]) if low else value[:8]
        foot = jnp.where(at_last, 0.0, value[-8:]) if high else value[-8:]
        return jnp.concatenate([head, value[8:-8], foot], axis=0)

    def convolve(index, out_ref, between):
        for sub in range(subs):
            chunk = (first + index) * subs + sub
            lanes = pl.ds(pl.multiple_of(chunk * LANES, LANES), LANES)
            base = chunk * padded_rows(tokens) + 8
            here = index * subs + sub
            taps = [[0.5 * depth_ref[p, q : q + 1, lanes] for q in range(3)] for p in range(3)]
            spot = slice(sub * LANES, (sub + 1) * LANES)
            sums = {}
            for y in range(rows + 1):
                if y < rows:
                    parts = [
                        expanded_ref[pl.ds(base + (y * cols + q), cols), :] for q in (-1, 0, 1)
                    ]
                    parts[0] = clear_ends(parts[0], True, False)
                    parts[2] = clear_ends(parts[2], False, True)
                    for p in range(3):
                        target = y + 1 - p
                        if 0 <= target < rows:
                            for q in range(3):
                                term = taps[p][q] * parts[q]
                                sums[target] = sums[target] + term if target in sums else term
                if y > 0:
                    done = sums.pop(y - 1)
                    rim_ref[here, 2 * cols + y - 1 : 2 * cols + y] = done[:1]
                    rim_ref[here, 2 * cols + rows + y - 1 : 2 * cols + rows + y] = done[-1:]
                    if y in (1, rows):
                        start = 0 if y == 1 else cols
                        rim_ref[here, start : start + cols] = done
                        made = jnp.zeros_like(done)
                    else:
                        made = clear_ends(gelu_of_half(done), True, True)
                    out_ref[(y - 1) * cols : y * cols, spot] = made.astype(jnp.bfloat16)
                    between(sub * rows + y - 1)

    def project(index, in_ref, from_ref):
        piece = pl.ds(pl.multiple_of((first + index) * tile, tile), tile)
        step = divisor(tokens, tokens // rows * 2, 16)

        def between(turn):
            if turn % subs == 0 and turn // subs * step < tokens:
                part = slice(turn // subs * step, (turn // subs + 1) * step)
                total_ref[part, :] = from_ref[part, :] + matmul(
                    in_ref[part, :], w_project_ref[piece, :]
                )

        return between

    def nothing(turn):
        return None

    convolve(0, even_ref, nothing)
    convolve(1, odd_ref, project(0, even_ref, start_ref))

    def body(index, carry):
        convolve(2 * index, even_ref, project(2 * index - 1, odd_ref, total_ref))
        convolve(2 * index + 1, odd_ref, project(2 * index, even_ref, total_ref))
        return carry

    lax.fori_loop(1, count // 2, body, 0)
    last = project(count - 1, odd_ref, total_ref)
    for turn in range(subs * rows):
        last(turn)


def inner(expanded, start, depth_kernel, w_project, rows, cols, first, count, tile):
    tokens, channels = start.shape
    rim = (count * tile // LANES, 2 * cols + 2 * rows, LANES)
    return pl.pallas_call(
        functools.partial(inner_kernel, rows=rows, cols=cols, first=first, count=count),
        in_specs=[vmem()] * 4,
        out_specs=[vmem()] * 2,
        out_shape=[
            jax.ShapeDtypeStruct((tokens, channels), jnp.float32),
            jax.ShapeDtypeStruct(rim, jnp.float32),
        ],
        scratch_shapes=[pltpu.VMEM((tokens, tile), jnp.bfloat16)] * 2,
        compiler_params=pltpu.CompilerParams(vmem_limit_bytes=6 * MIB),
        cost_estimate=pl.CostEstimate(
            flops=2 * 10**9 * count,
            bytes_accessed=tokens * channels * 8 + tokens * count * tile * 4,
            transcendentals=tokens * count * tile,
        ),
        name="inner",
    )(expanded, start, depth_kernel, w_project)


def rim_kernel(
    own_ref, odd_col_ref, inner_ref, *refs, rows, cols, plan, size, pieces,
):
    masks, _, sides = plan
    sent = len(outgoing_shapes(plan, size, 1))
    rim_refs, refs = refs[:pieces], refs[pieces:]
    up_ref, down_ref, one_ref, two_ref, w_expand_ref, depth_ref, w_project_ref, perm_ref = refs[:8]
    mixed_ref, slab_refs = refs[8], refs[9 : 9 + sent]
    halo_ref, active_ref, normed_ref, grouped_ref = refs[9 + sent :]
    tokens = rows * cols
    width = w_expand_ref.shape[1]
    tile = divisor(width, 512, LANES)
    subs = tile // LANES
    slot = one_ref.shape[0]
    left_start, right_start = 2 * cols, 2 * cols + slot

    odd_col = odd_col_ref[0]
    left = choose(odd_col, one_ref[...], two_ref[...])
    right = choose(odd_col, two_ref[...], one_ref[...])
    edges = jnp.concatenate([up_ref[...], down_ref[...], left, right], axis=0)

    def expand_halo(index, carry):
        lanes = pl.ds(pl.multiple_of(index * tile, tile), tile)
        made = gelu_of_half(matmul(edges, w_expand_ref[:, lanes]))
        for sub in range(subs):
            halo_ref[index * subs + sub] = made[:, sub * LANES : (sub + 1) * LANES]
        return carry

    lax.fori_loop(0, width // tile, expand_halo, 0)
    mixed_ref[...] = inner_ref[...]
    position = lax.broadcasted_iota(jnp.int32, (cols, LANES), 0)
    at_first = position == 0
    at_last = position == cols - 1

    def activate(chunk, here, sums_ref):
        lanes = pl.ds(pl.multiple_of(chunk * LANES, LANES), LANES)
        taps = [[0.5 * depth_ref[p, q : q + 1, lanes] for q in range(3)] for p in range(3)]
        beside = []
        for q, start in ((0, left_start), (2, right_start)):
            beside.append(
                sum(taps[p][q] * halo_ref[chunk, start + p : start + p + rows] for p in range(3))
            )
        made = []
        for p, start, y in ((0, 0, 0), (2, cols, rows - 1)):
            row = halo_ref[chunk, start : start + cols]
            before = jnp.where(at_first, beside[0][y : y + 1], taps[p][0] * pltpu.roll(row, 1, 0))
            after = jnp.where(
                at_last, beside[1][y : y + 1], taps[p][2] * pltpu.roll(row, cols - 1, 0)
            )
            made.append(sums_ref[here, start : start + cols] + before + taps[p][1] * row + after)
        for index in range(2):
            start = 2 * cols + index * rows
            made.append(sums_ref[here, start : start + rows] + beside[index])
        active_ref[:, lanes] = gelu_of_half(jnp.concatenate(made, axis=0)).astype(jnp.bfloat16)

    chunk = 0
    for sums_ref in rim_refs:
        offset = chunk

        def body(index, carry, sums_ref=sums_ref, offset=offset):
            activate(offset + 2 * index, 2 * index, sums_ref)
            activate(offset + 2 * index + 1, 2 * index + 1, sums_ref)
            return carry

        lax.fori_loop(0, sums_ref.shape[0] // 2, body, 0)
        chunk += sums_ref.shape[0]

    branch = matmul(active_ref[...], w_project_ref[...])
    mixed_ref[:cols, :] += branch[:cols]
    mixed_ref[tokens - cols :, :] += branch[cols : 2 * cols]
    for y in range(1, rows - 1):
        for index, x in ((0, 0), (1, cols - 1)):
            spot = y * cols + x
            start = 2 * cols + index * rows + y
            mixed_ref[spot : spot + 1, :] += branch[start : start + 1]

    step = divisor(tokens, 128, 16)
    for start in range(0, tokens, step):
        piece = slice(start, start + step)
        normed_ref[piece, :] = layer_norm(mixed_ref[piece, :]).astype(jnp.bfloat16)
    grouped_ref[...] = matmul(perm_ref[...], normed_ref[...]).astype(jnp.bfloat16)
    for index, mask in enumerate(masks):
        for side in range(sides):
            start = pl.multiple_of((own_ref[0] ^ (mask | side)) * size, 16)
            write_block(
                plan, slab_refs, index, side, slice(None), grouped_ref[pl.ds(start, size), :]
            )


def rim(
    own, odd_col, plan, size, total, rims, up, down, one, two, w_expand, depth_kernel, w_project, perm,
    rows, cols,
):
    tokens, channels = total.shape
    width = w_expand.shape[1]
    halo_rows = 2 * cols + 2 * one.shape[0]
    sent = outgoing_shapes(plan, size, channels)
    return pl.pallas_call(
        functools.partial(
            rim_kernel, rows=rows, cols=cols, plan=plan, size=size, pieces=len(rims)
        ),
        in_specs=[pl.BlockSpec(memory_space=pltpu.SMEM)] * 2 + [vmem()] * (9 + len(rims)),
        out_specs=[vmem()] * (1 + len(sent)),
        out_shape=[jax.ShapeDtypeStruct((tokens, channels), jnp.float32)]
        + [jax.ShapeDtypeStruct(shape, jnp.bfloat16) for shape in sent],
        scratch_shapes=[
            pltpu.VMEM((width // LANES, halo_rows, LANES), jnp.float32),
            pltpu.VMEM((2 * cols + 2 * rows, width), jnp.bfloat16),
            pltpu.VMEM((tokens, channels), jnp.bfloat16),
            pltpu.VMEM((tokens, channels), jnp.bfloat16),
        ],
        compiler_params=pltpu.CompilerParams(vmem_limit_bytes=8 * MIB),
        cost_estimate=pl.CostEstimate(
            flops=2 * halo_rows * channels * width * 2 + 2 * tokens * tokens * channels,
            bytes_accessed=tokens * channels * 10 + 4 * channels * width,
            transcendentals=2 * halo_rows * width,
        ),
        name="rim",
    )(own, odd_col, total, *rims, up, down, one, two, w_expand, depth_kernel, w_project, perm)


def identity(size):
    row = lax.broadcasted_iota(jnp.int32, (size, size), 0)
    column = lax.broadcasted_iota(jnp.int32, (size, size), 1)
    return jnp.where(row == column, 1.0, 0.0).astype(jnp.bfloat16)


def attend_kernel(*refs, plan, sets, came):
    masks, _, sides = plan
    slabs = len(masks)
    _, size, channels = refs[0].shape
    in_refs, weight_ref, out_refs = refs[:came], refs[came], refs[came + 1 : -6]
    query_ref, key_ref, value_ref, turned_ref, even_ref, odd_ref = refs[-6:]
    members = size // sets
    count = slabs * sides * members
    head_width = channels // HEADS
    group_heads = LANES // head_width
    groups = channels // LANES
    factor = math.log2(math.e) / math.sqrt(head_width)
    lane = lax.broadcasted_iota(jnp.int32, (1, LANES), 1)
    masks = [
        jnp.where((lane >= j * head_width) & (lane < (j + 1) * head_width), 1.0, 0.0).astype(
            jnp.bfloat16
        )
        for j in range(group_heads)
    ]
    turn_values = identity(channels)
    block = jnp.concatenate(
        [
            read_block(plan, in_refs, index, side, slice(s * members, (s + 1) * members))
            for s in range(sets)
            for index in range(slabs)
            for side in range(sides)
        ],
        axis=0,
    )
    qkv = matmul(block, weight_ref[...]).astype(jnp.bfloat16)
    for s in range(sets):
        own_rows = slice(s * count, (s + 1) * count)
        values = matmul_nt(turn_values, qkv[own_rows, 2 * channels :]).astype(jnp.bfloat16)
        for group in range(groups):
            spot = group * LANES
            query_ref[s * groups + group] = qkv[own_rows, spot : spot + LANES]
            key_ref[s * groups + group] = qkv[own_rows, channels + spot : channels + spot + LANES]
            for j in range(group_heads):
                head = (group * group_heads + j) * head_width
                value_ref[s * groups + group, j, :head_width] = values[head : head + head_width]
                value_ref[s * groups + group, j, head_width:] = jnp.ones((16, count), jnp.bfloat16)

    def scores(index, out):
        keys = key_ref[index]
        stacked = jnp.concatenate([keys * mask for mask in masks], axis=0)
        out[...] = matmul_nt(stacked, query_ref[index])

    def weigh(index, scores_ref):
        for j in range(group_heads):
            part = scores_ref[j * count : (j + 1) * count]
            highest = jnp.max(part, axis=0, keepdims=True)
            raised = jnp.exp2((part - highest) * factor).astype(jnp.bfloat16)
            product = matmul(value_ref[index, j], raised)
            scale = 1.0 / product[head_width : head_width + 1]
            turned_ref[index, j * head_width : (j + 1) * head_width] = (
                product[:head_width] * scale
            ).astype(jnp.bfloat16)

    total = sets * groups
    scores(0, even_ref)

    def body(pair, carry):
        scores(2 * pair + 1, odd_ref)
        weigh(2 * pair, even_ref)
        scores(jnp.minimum(2 * pair + 2, total - 1), even_ref)
        weigh(2 * pair + 1, odd_ref)
        return carry

    lax.fori_loop(0, total // 2, body, 0)
    turn_tokens = identity(count)
    for s in range(sets):
        turned = turned_ref[s * groups : (s + 1) * groups].reshape(channels, count)
        attended = matmul_nt(turn_tokens, turned).astype(jnp.bfloat16)
        for index in range(slabs):
            for side in range(sides):
                start = (index * sides + side) * members
                write_block(
                    plan, out_refs, index, side, slice(s * members, (s + 1) * members),
                    attended[start : start + members],
                )


def attend(plan, incoming, w_qkv, sets):
    masks, _, sides = plan
    _, size, channels = incoming[0].shape
    count = len(masks) * sides * size // sets
    sent = outgoing_shapes(plan, size, channels)
    head_width = channels // HEADS
    group_heads = LANES // head_width
    total = sets * channels // LANES
    return pl.pallas_call(
        functools.partial(attend_kernel, plan=plan, sets=sets, came=len(incoming)),
        in_specs=[vmem()] * (len(incoming) + 1),
        out_specs=[vmem()] * len(sent),
        out_shape=[jax.ShapeDtypeStruct(shape, jnp.bfloat16) for shape in sent],
        scratch_shapes=[
            pltpu.VMEM((total, count, LANES), jnp.bfloat16),
            pltpu.VMEM((total, count, LANES), jnp.bfloat16),
            pltpu.VMEM((total, group_heads, head_width + 16, count), jnp.bfloat16),
            pltpu.VMEM((total, LANES, count), jnp.bfloat16),
            pltpu.VMEM((group_heads * count, count), jnp.float32),
            pltpu.VMEM((group_heads * count, count), jnp.float32),
        ],
        compiler_params=pltpu.CompilerParams(vmem_limit_bytes=10 * MIB),
        cost_estimate=pl.CostEstimate(
            flops=sets * (2 * count * channels * channels * 3 + 4 * count * count * channels),
            bytes_accessed=4 * sets * count * channels + 6 * channels * channels,
            transcendentals=sets * HEADS * count * count,
        ),
        name="attend",
    )(*incoming, w_qkv)


def finish_kernel(own_ref, *refs, plan):
    masks, _, sides = plan
    in_refs, rest = refs[:-7], refs[-7:]
    back_ref, weight_ref, mixed_ref, out_ref, attended_ref, made_ref, sent = rest
    tokens = mixed_ref.shape[0]
    size = in_refs[0].shape[1]
    for index, mask in enumerate(masks):
        for side in range(sides):
            start = pl.multiple_of((own_ref[0] ^ (mask | side)) * size, 16)
            attended_ref[pl.ds(start, size), :] = read_block(
                plan, in_refs, index, side, slice(None)
            )
    step = made_ref.shape[1]
    copies = []
    for index, start in enumerate(range(0, tokens, step)):
        rows = slice(start, start + step)
        restored = matmul(back_ref[rows, :], attended_ref[...]).astype(jnp.bfloat16)
        made_ref[index] = mixed_ref[rows, :] + matmul(restored, weight_ref[...])
        copy = pltpu.make_async_copy(
            made_ref.at[index], out_ref.at[pl.ds(start, step)], sent.at[index]
        )
        copy.start()
        copies.append(copy)
    for copy in copies:
        copy.wait()


def finish(own, plan, incoming, back, w_out, mixed):
    tokens, channels = mixed.shape
    step = divisor(tokens, 128, 16)
    return pl.pallas_call(
        functools.partial(finish_kernel, plan=plan),
        in_specs=[pl.BlockSpec(memory_space=pltpu.SMEM)] + [vmem()] * (len(incoming) + 3),
        out_specs=pl.BlockSpec(memory_space=pltpu.HBM),
        out_shape=jax.ShapeDtypeStruct((tokens, channels), jnp.float32),
        scratch_shapes=[
            pltpu.VMEM((tokens, channels), jnp.bfloat16),
            pltpu.VMEM((tokens // step, step, channels), jnp.float32),
            pltpu.SemaphoreType.DMA((tokens // step,)),
        ],
        compiler_params=pltpu.CompilerParams(vmem_limit_bytes=6 * MIB),
        name="finish",
    )(own, *incoming, back, w_out, mixed)


def swap_pairs(edge, axis, start):
    pairs = [(i, i + 1) for i in range(start, lax.axis_size(axis) - 1, 2)]
    return lax.ppermute(edge, axis, pairs + [(b, a) for a, b in pairs])


def exchange_plan(row_devices, col_devices):
    devices = row_devices * col_devices
    crossing = list(range(devices - 2, devices // 2 - 1, -2))
    others = list(range(devices // 2 - 2, 0, -2))
    masks = crossing[:-1] + others[:-1] + crossing[-1:] + others[-1:] + [0]
    return masks, 2, 2


def outgoing_shapes(plan, size, channels):
    masks, late, sides = plan
    if sides == 1:
        return [(1, size, channels)]
    early = len(masks) - 1 - late
    return [(2, size, channels)] * late + [
        (1, size, channels), (early + 1, size, channels), (early, size, channels)
    ]


def write_block(plan, refs, index, side, rows, value):
    masks, late, sides = plan
    if sides == 1:
        refs[0][0, rows] = value
    elif index < late:
        refs[index][side, rows] = value
    elif index == len(masks) - 1:
        refs[late + side][0, rows] = value
    elif side == 0:
        refs[late + 2][index - late, rows] = value
    else:
        refs[late + 1][index - late + 1, rows] = value


def read_block(plan, refs, index, side, rows):
    masks, late, sides = plan
    if sides == 1:
        return refs[0][0, rows]
    if index < late:
        return refs[index + side * len(masks)][side, rows]
    if index == len(masks) - 1:
        return refs[index + side * (late + 1)][0, rows]
    return refs[index][side, rows]


def join_kernel(own_ref, swapped_ref, *out_refs):
    for index, out_ref in enumerate(out_refs):
        out_ref[0] = own_ref[index]
        out_ref[1] = swapped_ref[index + 1]


def join(own, swapped):
    early, size, channels = own.shape
    return pl.pallas_call(
        join_kernel,
        in_specs=[vmem()] * 2,
        out_specs=[vmem()] * early,
        out_shape=[jax.ShapeDtypeStruct((2, size, channels), own.dtype)] * early,
        compiler_params=pltpu.CompilerParams(vmem_limit_bytes=2 * MIB),
        name="join",
    )(own, swapped)


def trade(plan, outgoing):
    masks, late, _ = plan
    devices = lax.axis_size("row") * lax.axis_size("col")

    def swap(slab, mask):
        return lax.ppermute(slab, ("row", "col"), [(i, i ^ mask) for i in range(devices)])

    slabs, (kept, passed, own) = outgoing[:late], outgoing[late:]
    swapped = swap(passed, 1)
    first = [swap(slab, mask) for slab, mask in zip(slabs, masks)]
    rest = [swap(slab, mask) for slab, mask in zip(join(own, swapped), masks[late:-1])]
    tied = lax.optimization_barrier((*first, *rest[:-late]))
    first, rest = tied[:late], [*tied[late:], *rest[-late:]]
    return [*first, *rest, kept, *[swap(slab, 1) for slab in first], swapped]


def trade_all(slabs, sets, members, outward):
    axes = ("row", "col")
    channels = slabs[0].shape[-1]
    block = slabs[0].reshape(-1, channels)
    devices = block.shape[0] // (sets * members)
    if not outward:
        block = block.reshape(sets, devices, members, channels).transpose(1, 0, 2, 3)
    block = block.reshape(devices, sets * members, channels)
    block = lax.all_to_all(block, axes, 0, 0, tiled=True)
    if outward:
        block = block.reshape(devices, sets, members, channels).transpose(1, 0, 2, 3)
    return [block.reshape(1, -1, channels)]


def grouping(rows, cols, blocks_rows, blocks_cols):
    order = np.arange(rows * cols).reshape(
        blocks_rows, rows // blocks_rows, blocks_cols, cols // blocks_cols
    )
    order = order.transpose(1, 3, 0, 2).reshape(-1)
    matrix = np.zeros((order.size, order.size), np.float32)
    matrix[np.arange(order.size), order] = 1.0
    return matrix


def shards(field, w_expand, depth_kernel, w_project, w_qkv, w_out):
    rows, cols, channels = field.shape
    tokens = rows * cols
    row_devices = lax.axis_size("row")
    col_devices = lax.axis_size("col")
    devices = row_devices * col_devices
    blocks_rows = GRID // row_devices
    blocks_cols = GRID // col_devices
    members = blocks_rows * blocks_cols
    sets_local = tokens // members // devices
    matrix = grouping(rows, cols, blocks_rows, blocks_cols)
    perm = jnp.asarray(matrix, jnp.bfloat16)
    back = jnp.asarray(matrix.T, jnp.bfloat16)

    flat = field.reshape(tokens, channels)
    pairwise = 8 <= devices <= 16 and devices & (devices - 1) == 0 and col_devices % 2 == 0
    plan = exchange_plan(row_devices, col_devices) if pairwise else ([0], 0, 1)
    row, col = lax.axis_index("row"), lax.axis_index("col")
    own = (row * col_devices + col if pairwise else row * 0).reshape(1)
    odd_row, odd_col = (row % 2).reshape(1), (col % 2).reshape(1)

    own, odd_row, odd_col, top, bottom = lax.optimization_barrier(
        (own, odd_row, odd_col, field[0], field[rows - 1])
    )
    one, two = row_edges(odd_row, top, bottom)
    one, two = swap_pairs(one, "row", 0), swap_pairs(two, "row", 1)
    normed = half_norm_of(flat)
    expanded = expand(normed, w_expand)
    tile = divisor(w_expand.shape[1] // 2, 256, LANES)
    count = w_expand.shape[1] // tile
    early = 2
    total, rim_one = inner(
        expanded, flat, depth_kernel, w_project, rows, cols, 0, early, tile
    )
    one, two, normed, expanded, total, rim_one = lax.optimization_barrier(
        (one, two, normed, expanded, total, rim_one)
    )
    up, down, one, two = column_strips(odd_row, odd_col, normed, one, two, round_up(rows + 2, 16))
    one, two = swap_pairs(one, "col", 0), swap_pairs(two, "col", 1)
    total, rim_two = inner(
        expanded, total, depth_kernel, w_project, rows, cols, early, count - early, tile
    )

    size = tokens // (len(plan[0]) * plan[2])
    mixed, *outgoing = rim(
        own, odd_col, plan, size, total, [rim_one, rim_two], up, down, one, two, w_expand,
        depth_kernel, w_project, perm, rows, cols,
    )

    def route(outgoing, outward):
        if pairwise:
            return trade(plan, outgoing)
        return trade_all(outgoing, sets_local, members, outward)

    outgoing = attend(plan, route(outgoing, True), w_qkv, sets_local)
    final = finish(own, plan, route(outgoing, False), back, w_out, mixed)
    return final.reshape(rows, cols, channels)


def solution(mesh):
    return jax.shard_map(
        shards,
        mesh=mesh,
        in_specs=(P(("field", "row"), "col", None), P(), P(), P(), P(), P()),
        out_specs=P(("field", "row"), "col", None),
        check_vma=False,
    )
```

```python
import functools
import math

import jax
import jax.numpy as jnp
import numpy as np
from jax import lax
from jax.experimental import pallas as pl
from jax.experimental.pallas import tpu as pltpu
from jax.sharding import PartitionSpec as P

HEADS = 16
GRID = 16
LANES = 128
MIB = 1024 * 1024
NT = (((1,), (1,)), ((), ()))


def layer_norm(inputs):
    average = jnp.mean(inputs, axis=-1, keepdims=True)
    centred = inputs - average
    variance = jnp.mean(centred * centred, axis=-1, keepdims=True)
    return centred * lax.rsqrt(variance + 1e-05)


def gelu_of_half(half):
    scale = math.sqrt(2.0 / math.pi)
    inner = half * (2.0 * scale + (8.0 * scale * 0.044715) * (half * half))
    return half + half * jnp.tanh(inner)


def matmul(a, b):
    return jnp.dot(a, b, preferred_element_type=jnp.float32)


def matmul_nt(a, b):
    return lax.dot_general(a, b, NT, preferred_element_type=jnp.float32)


def divisor(size, most, unit):
    best = size
    for piece in range(unit, most + 1, unit):
        if size % piece == 0:
            best = piece
    return best


def round_up(size, unit):
    return -(-size // unit) * unit


def vmem():
    return pl.BlockSpec(memory_space=pltpu.VMEM)


def half_norm(inputs):
    return (layer_norm(inputs) * 0.5).astype(jnp.bfloat16)


def half_norm_kernel(in_ref, out_ref):
    rows = in_ref.shape[0]
    step = divisor(rows, 128, 16)
    for start in range(0, rows, step):
        out_ref[start : start + step, :] = half_norm(in_ref[start : start + step, :])


def half_norm_of(inputs):
    return pl.pallas_call(
        half_norm_kernel,
        in_specs=[vmem()],
        out_specs=vmem(),
        out_shape=jax.ShapeDtypeStruct(inputs.shape, jnp.bfloat16),
        compiler_params=pltpu.CompilerParams(vmem_limit_bytes=4 * MIB),
        cost_estimate=pl.CostEstimate(
            flops=10**9, bytes_accessed=6 * inputs.size, transcendentals=inputs.shape[0]
        ),
        name="half_norm",
    )(inputs)


def choose(condition, one, two):
    flags = jnp.full((one.shape[0], 1), condition, jnp.int32) == 1
    return jnp.where(flags, one.astype(jnp.float32), two.astype(jnp.float32)).astype(one.dtype)


def edges_kernel(odd_row_ref, top_ref, bottom_ref, one_ref, two_ref):
    odd = odd_row_ref[0]
    top, bottom = half_norm(top_ref[...]), half_norm(bottom_ref[...])
    one_ref[...] = choose(odd, top, bottom)
    two_ref[...] = choose(odd, bottom, top)


def row_edges(odd_row, top, bottom):
    return pl.pallas_call(
        edges_kernel,
        in_specs=[pl.BlockSpec(memory_space=pltpu.SMEM)] + [vmem()] * 2,
        out_specs=[vmem()] * 2,
        out_shape=[jax.ShapeDtypeStruct(top.shape, jnp.bfloat16)] * 2,
        compiler_params=pltpu.CompilerParams(vmem_limit_bytes=4 * MIB),
        cost_estimate=pl.CostEstimate(
            flops=10**10, bytes_accessed=12 * top.size, transcendentals=2 * top.shape[0]
        ),
        name="row_edges",
    )(odd_row, top, bottom)


def picker(shape, pick):
    row = lax.broadcasted_iota(jnp.int32, shape, 0)
    column = lax.broadcasted_iota(jnp.int32, shape, 1)
    return jnp.where(pick(row, column), 1.0, 0.0).astype(jnp.bfloat16)


def strips_kernel(
    odd_row_ref, odd_col_ref, normed_ref, row_one_ref, row_two_ref, up_ref, down_ref, one_ref, two_ref
):
    tokens = normed_ref.shape[0]
    cols = up_ref.shape[0]
    rows = tokens // cols
    slot = one_ref.shape[0]
    odd_row, odd_col = odd_row_ref[0], odd_col_ref[0]
    up = choose(odd_row, row_one_ref[...], row_two_ref[...])
    down = choose(odd_row, row_two_ref[...], row_one_ref[...])
    up_ref[...] = up
    down_ref[...] = down
    strips = []
    for x in (0, cols - 1):
        body = picker(
            (slot, tokens), lambda i, j: (i >= 1) & (i <= rows) & (j == (i - 1) * cols + x)
        )
        head = picker((slot, cols), lambda i, j: (i == 0) & (j == x))
        foot = picker((slot, cols), lambda i, j: (i == rows + 1) & (j == x))
        strip = matmul(body, normed_ref[...]) + matmul(head, up) + matmul(foot, down)
        strips.append(strip.astype(jnp.bfloat16))
    one_ref[...] = choose(odd_col, strips[0], strips[1])
    two_ref[...] = choose(odd_col, strips[1], strips[0])


def column_strips(odd_row, odd_col, normed, row_one, row_two, slot):
    cols, channels = row_one.shape
    shapes = [(cols, channels)] * 2 + [(slot, channels)] * 2
    return pl.pallas_call(
        strips_kernel,
        in_specs=[pl.BlockSpec(memory_space=pltpu.SMEM)] * 2 + [vmem()] * 3,
        out_specs=[vmem()] * 4,
        out_shape=[jax.ShapeDtypeStruct(shape, jnp.bfloat16) for shape in shapes],
        compiler_params=pltpu.CompilerParams(vmem_limit_bytes=4 * MIB),
        name="column_strips",
    )(odd_row, odd_col, normed, row_one, row_two)


def padded_rows(tokens):
    return tokens + 16


def expand_kernel(normed_ref, weight_ref, out_ref):
    tokens = normed_ref.shape[0]
    width = weight_ref.shape[1]
    tile = divisor(width, 512, LANES)

    def body(index, carry):
        lanes = pl.ds(pl.multiple_of(index * tile, tile), tile)
        made = gelu_of_half(matmul(normed_ref[...], weight_ref[:, lanes]))
        for sub in range(tile // LANES):
            row = (index * (tile // LANES) + sub) * padded_rows(tokens) + 8
            out_ref[pl.ds(pl.multiple_of(row, 8), tokens), :] = made[
                :, sub * LANES : (sub + 1) * LANES
            ]
        return carry

    lax.fori_loop(0, width // tile, body, 0)


def expand(normed, w_expand):
    tokens, channels = normed.shape
    width = w_expand.shape[1]
    return pl.pallas_call(
        expand_kernel,
        in_specs=[vmem()] * 2,
        out_specs=vmem(),
        out_shape=jax.ShapeDtypeStruct((width // LANES * padded_rows(tokens), LANES), jnp.float32),
        compiler_params=pltpu.CompilerParams(vmem_limit_bytes=4 * MIB),
        cost_estimate=pl.CostEstimate(
            flops=10**10,
            bytes_accessed=tokens * channels * 2 + channels * width * 2 + tokens * width * 4,
            transcendentals=tokens * width,
        ),
        name="expand",
    )(normed, w_expand)


def inner_kernel(
    expanded_ref, start_ref, depth_ref, w_project_ref, total_ref, rim_ref, even_ref, odd_ref,
    *, rows, cols, first, count,
):
    tokens = rows * cols
    tile = even_ref.shape[1]
    subs = tile // LANES
    position = lax.broadcasted_iota(jnp.int32, (8, LANES), 0)
    at_first = position == 0
    at_last = position == 7

    def clear_ends(value, low, high):
        head = jnp.where(at_first, 0.0, value[:8]) if low else value[:8]
        foot = jnp.where(at_last, 0.0, value[-8:]) if high else value[-8:]
        return jnp.concatenate([head, value[8:-8], foot], axis=0)

    def convolve(index, out_ref):
        for sub in range(subs):
            chunk = (first + index) * subs + sub
            lanes = pl.ds(pl.multiple_of(chunk * LANES, LANES), LANES)
            base = chunk * padded_rows(tokens) + 8
            here = index * subs + sub
            taps = [[0.5 * depth_ref[p, q : q + 1, lanes] for q in range(3)] for p in range(3)]
            spot = slice(sub * LANES, (sub + 1) * LANES)
            sums = {}
            for y in range(rows + 1):
                if y < rows:
                    parts = [
                        expanded_ref[pl.ds(base + (y * cols + q), cols), :] for q in (-1, 0, 1)
                    ]
                    parts[0] = clear_ends(parts[0], True, False)
                    parts[2] = clear_ends(parts[2], False, True)
                    for p in range(3):
                        target = y + 1 - p
                        if 0 <= target < rows:
                            for q in range(3):
                                term = taps[p][q] * parts[q]
                                sums[target] = sums[target] + term if target in sums else term
                if y > 0:
                    done = sums.pop(y - 1)
                    rim_ref[here, 2 * cols + y - 1 : 2 * cols + y] = done[:1]
                    rim_ref[here, 2 * cols + rows + y - 1 : 2 * cols + rows + y] = done[-1:]
                    if y in (1, rows):
                        start = 0 if y == 1 else cols
                        rim_ref[here, start : start + cols] = done
                        made = jnp.zeros_like(done)
                    else:
                        made = clear_ends(gelu_of_half(done), True, True)
                    out_ref[(y - 1) * cols : y * cols, spot] = made.astype(jnp.bfloat16)

    def project(index, in_ref, from_ref):
        piece = pl.ds(pl.multiple_of((first + index) * tile, tile), tile)
        total_ref[...] = from_ref[...] + matmul(in_ref[...], w_project_ref[piece, :])

    convolve(0, even_ref)
    project(0, even_ref, start_ref)
    convolve(1, odd_ref)

    def body(index, carry):
        convolve(2 * index, even_ref)
        project(2 * index - 1, odd_ref, total_ref)
        convolve(2 * index + 1, odd_ref)
        project(2 * index, even_ref, total_ref)
        return carry

    lax.fori_loop(1, count // 2, body, 0)
    project(count - 1, odd_ref, total_ref)


def inner(expanded, start, depth_kernel, w_project, rows, cols, first, count, tile):
    tokens, channels = start.shape
    rim = (count * tile // LANES, 2 * cols + 2 * rows, LANES)
    return pl.pallas_call(
        functools.partial(inner_kernel, rows=rows, cols=cols, first=first, count=count),
        in_specs=[vmem()] * 4,
        out_specs=[vmem()] * 2,
        out_shape=[
            jax.ShapeDtypeStruct((tokens, channels), jnp.float32),
            jax.ShapeDtypeStruct(rim, jnp.float32),
        ],
        scratch_shapes=[pltpu.VMEM((tokens, tile), jnp.bfloat16)] * 2,
        compiler_params=pltpu.CompilerParams(vmem_limit_bytes=6 * MIB),
        cost_estimate=pl.CostEstimate(
            flops=2 * 10**9 * count,
            bytes_accessed=tokens * channels * 8 + tokens * count * tile * 4,
            transcendentals=tokens * count * tile,
        ),
        name="inner",
    )(expanded, start, depth_kernel, w_project)


def rim_kernel(
    own_ref, odd_col_ref, inner_ref, *refs, rows, cols, plan, size, pieces,
):
    masks, _, sides = plan
    sent = len(outgoing_shapes(plan, size, 1))
    rim_refs, refs = refs[:pieces], refs[pieces:]
    up_ref, down_ref, one_ref, two_ref, w_expand_ref, depth_ref, w_project_ref, perm_ref = refs[:8]
    mixed_ref, slab_refs = refs[8], refs[9 : 9 + sent]
    halo_ref, active_ref, normed_ref, grouped_ref = refs[9 + sent :]
    tokens = rows * cols
    width = w_expand_ref.shape[1]
    tile = divisor(width, 512, LANES)
    subs = tile // LANES
    slot = one_ref.shape[0]
    left_start, right_start = 2 * cols, 2 * cols + slot

    odd_col = odd_col_ref[0]
    left = choose(odd_col, one_ref[...], two_ref[...])
    right = choose(odd_col, two_ref[...], one_ref[...])
    edges = jnp.concatenate([up_ref[...], down_ref[...], left, right], axis=0)

    def expand_halo(index, carry):
        lanes = pl.ds(pl.multiple_of(index * tile, tile), tile)
        made = gelu_of_half(matmul(edges, w_expand_ref[:, lanes]))
        for sub in range(subs):
            halo_ref[index * subs + sub] = made[:, sub * LANES : (sub + 1) * LANES]
        return carry

    lax.fori_loop(0, width // tile, expand_halo, 0)
    mixed_ref[...] = inner_ref[...]
    position = lax.broadcasted_iota(jnp.int32, (cols, LANES), 0)
    at_first = position == 0
    at_last = position == cols - 1

    def activate(chunk, here, sums_ref):
        lanes = pl.ds(pl.multiple_of(chunk * LANES, LANES), LANES)
        taps = [[0.5 * depth_ref[p, q : q + 1, lanes] for q in range(3)] for p in range(3)]
        beside = []
        for q, start in ((0, left_start), (2, right_start)):
            beside.append(
                sum(taps[p][q] * halo_ref[chunk, start + p : start + p + rows] for p in range(3))
            )
        made = []
        for p, start, y in ((0, 0, 0), (2, cols, rows - 1)):
            row = halo_ref[chunk, start : start + cols]
            before = jnp.where(at_first, beside[0][y : y + 1], taps[p][0] * pltpu.roll(row, 1, 0))
            after = jnp.where(
                at_last, beside[1][y : y + 1], taps[p][2] * pltpu.roll(row, cols - 1, 0)
            )
            made.append(sums_ref[here, start : start + cols] + before + taps[p][1] * row + after)
        for index in range(2):
            start = 2 * cols + index * rows
            made.append(sums_ref[here, start : start + rows] + beside[index])
        active_ref[:, lanes] = gelu_of_half(jnp.concatenate(made, axis=0)).astype(jnp.bfloat16)

    chunk = 0
    for sums_ref in rim_refs:
        offset = chunk

        def body(index, carry, sums_ref=sums_ref, offset=offset):
            activate(offset + 2 * index, 2 * index, sums_ref)
            activate(offset + 2 * index + 1, 2 * index + 1, sums_ref)
            return carry

        lax.fori_loop(0, sums_ref.shape[0] // 2, body, 0)
        chunk += sums_ref.shape[0]

    branch = matmul(active_ref[...], w_project_ref[...])
    mixed_ref[:cols, :] += branch[:cols]
    mixed_ref[tokens - cols :, :] += branch[cols : 2 * cols]
    for y in range(1, rows - 1):
        for index, x in ((0, 0), (1, cols - 1)):
            spot = y * cols + x
            start = 2 * cols + index * rows + y
            mixed_ref[spot : spot + 1, :] += branch[start : start + 1]

    step = divisor(tokens, 128, 16)
    for start in range(0, tokens, step):
        piece = slice(start, start + step)
        normed_ref[piece, :] = layer_norm(mixed_ref[piece, :]).astype(jnp.bfloat16)
    grouped_ref[...] = matmul(perm_ref[...], normed_ref[...]).astype(jnp.bfloat16)
    for index, mask in enumerate(masks):
        for side in range(sides):
            start = pl.multiple_of((own_ref[0] ^ (mask | side)) * size, 16)
            write_block(
                plan, slab_refs, index, side, slice(None), grouped_ref[pl.ds(start, size), :]
            )


def rim(
    own, odd_col, plan, size, total, rims, up, down, one, two, w_expand, depth_kernel, w_project, perm,
    rows, cols,
):
    tokens, channels = total.shape
    width = w_expand.shape[1]
    halo_rows = 2 * cols + 2 * one.shape[0]
    sent = outgoing_shapes(plan, size, channels)
    return pl.pallas_call(
        functools.partial(
            rim_kernel, rows=rows, cols=cols, plan=plan, size=size, pieces=len(rims)
        ),
        in_specs=[pl.BlockSpec(memory_space=pltpu.SMEM)] * 2 + [vmem()] * (9 + len(rims)),
        out_specs=[vmem()] * (1 + len(sent)),
        out_shape=[jax.ShapeDtypeStruct((tokens, channels), jnp.float32)]
        + [jax.ShapeDtypeStruct(shape, jnp.bfloat16) for shape in sent],
        scratch_shapes=[
            pltpu.VMEM((width // LANES, halo_rows, LANES), jnp.float32),
            pltpu.VMEM((2 * cols + 2 * rows, width), jnp.bfloat16),
            pltpu.VMEM((tokens, channels), jnp.bfloat16),
            pltpu.VMEM((tokens, channels), jnp.bfloat16),
        ],
        compiler_params=pltpu.CompilerParams(vmem_limit_bytes=8 * MIB),
        cost_estimate=pl.CostEstimate(
            flops=2 * halo_rows * channels * width * 2 + 2 * tokens * tokens * channels,
            bytes_accessed=tokens * channels * 10 + 4 * channels * width,
            transcendentals=2 * halo_rows * width,
        ),
        name="rim",
    )(own, odd_col, total, *rims, up, down, one, two, w_expand, depth_kernel, w_project, perm)


def identity(size):
    row = lax.broadcasted_iota(jnp.int32, (size, size), 0)
    column = lax.broadcasted_iota(jnp.int32, (size, size), 1)
    return jnp.where(row == column, 1.0, 0.0).astype(jnp.bfloat16)


def attend_kernel(*refs, plan, sets, came):
    masks, _, sides = plan
    slabs = len(masks)
    _, size, channels = refs[0].shape
    in_refs, weight_ref, out_refs = refs[:came], refs[came], refs[came + 1 : -6]
    query_ref, key_ref, value_ref, turned_ref, even_ref, odd_ref = refs[-6:]
    members = size // sets
    count = slabs * sides * members
    head_width = channels // HEADS
    group_heads = LANES // head_width
    groups = channels // LANES
    factor = math.log2(math.e) / math.sqrt(head_width)
    lane = lax.broadcasted_iota(jnp.int32, (1, LANES), 1)
    masks = [
        jnp.where((lane >= j * head_width) & (lane < (j + 1) * head_width), 1.0, 0.0).astype(
            jnp.bfloat16
        )
        for j in range(group_heads)
    ]
    turn_values = identity(channels)
    block = jnp.concatenate(
        [
            read_block(plan, in_refs, index, side, slice(s * members, (s + 1) * members))
            for s in range(sets)
            for index in range(slabs)
            for side in range(sides)
        ],
        axis=0,
    )
    qkv = matmul(block, weight_ref[...]).astype(jnp.bfloat16)
    for s in range(sets):
        own_rows = slice(s * count, (s + 1) * count)
        values = matmul_nt(turn_values, qkv[own_rows, 2 * channels :]).astype(jnp.bfloat16)
        for group in range(groups):
            spot = group * LANES
            query_ref[s * groups + group] = qkv[own_rows, spot : spot + LANES]
            key_ref[s * groups + group] = qkv[own_rows, channels + spot : channels + spot + LANES]
            for j in range(group_heads):
                head = (group * group_heads + j) * head_width
                value_ref[s * groups + group, j, :head_width] = values[head : head + head_width]
                value_ref[s * groups + group, j, head_width:] = jnp.ones((16, count), jnp.bfloat16)

    def scores(index, out):
        keys = key_ref[index]
        stacked = jnp.concatenate([keys * mask for mask in masks], axis=0)
        out[...] = matmul_nt(stacked, query_ref[index])

    def weigh(index, scores_ref):
        for j in range(group_heads):
            part = scores_ref[j * count : (j + 1) * count]
            highest = jnp.max(part, axis=0, keepdims=True)
            raised = jnp.exp2((part - highest) * factor).astype(jnp.bfloat16)
            product = matmul(value_ref[index, j], raised)
            scale = 1.0 / product[head_width : head_width + 1]
            turned_ref[index, j * head_width : (j + 1) * head_width] = (
                product[:head_width] * scale
            ).astype(jnp.bfloat16)

    total = sets * groups
    scores(0, even_ref)

    def body(pair, carry):
        scores(2 * pair + 1, odd_ref)
        weigh(2 * pair, even_ref)
        scores(jnp.minimum(2 * pair + 2, total - 1), even_ref)
        weigh(2 * pair + 1, odd_ref)
        return carry

    lax.fori_loop(0, total // 2, body, 0)
    turn_tokens = identity(count)
    for s in range(sets):
        turned = turned_ref[s * groups : (s + 1) * groups].reshape(channels, count)
        attended = matmul_nt(turn_tokens, turned).astype(jnp.bfloat16)
        for index in range(slabs):
            for side in range(sides):
                start = (index * sides + side) * members
                write_block(
                    plan, out_refs, index, side, slice(s * members, (s + 1) * members),
                    attended[start : start + members],
                )


def attend(plan, incoming, w_qkv, sets):
    masks, _, sides = plan
    _, size, channels = incoming[0].shape
    count = len(masks) * sides * size // sets
    sent = outgoing_shapes(plan, size, channels)
    head_width = channels // HEADS
    group_heads = LANES // head_width
    total = sets * channels // LANES
    return pl.pallas_call(
        functools.partial(attend_kernel, plan=plan, sets=sets, came=len(incoming)),
        in_specs=[vmem()] * (len(incoming) + 1),
        out_specs=[vmem()] * len(sent),
        out_shape=[jax.ShapeDtypeStruct(shape, jnp.bfloat16) for shape in sent],
        scratch_shapes=[
            pltpu.VMEM((total, count, LANES), jnp.bfloat16),
            pltpu.VMEM((total, count, LANES), jnp.bfloat16),
            pltpu.VMEM((total, group_heads, head_width + 16, count), jnp.bfloat16),
            pltpu.VMEM((total, LANES, count), jnp.bfloat16),
            pltpu.VMEM((group_heads * count, count), jnp.float32),
            pltpu.VMEM((group_heads * count, count), jnp.float32),
        ],
        compiler_params=pltpu.CompilerParams(vmem_limit_bytes=10 * MIB),
        cost_estimate=pl.CostEstimate(
            flops=sets * (2 * count * channels * channels * 3 + 4 * count * count * channels),
            bytes_accessed=4 * sets * count * channels + 6 * channels * channels,
            transcendentals=sets * HEADS * count * count,
        ),
        name="attend",
    )(*incoming, w_qkv)


def finish_kernel(own_ref, *refs, plan):
    masks, _, sides = plan
    in_refs, rest = refs[:-7], refs[-7:]
    back_ref, weight_ref, mixed_ref, out_ref, attended_ref, made_ref, sent = rest
    tokens = mixed_ref.shape[0]
    size = in_refs[0].shape[1]
    for index, mask in enumerate(masks):
        for side in range(sides):
            start = pl.multiple_of((own_ref[0] ^ (mask | side)) * size, 16)
            attended_ref[pl.ds(start, size), :] = read_block(
                plan, in_refs, index, side, slice(None)
            )
    step = made_ref.shape[1]
    copies = []
    for index, start in enumerate(range(0, tokens, step)):
        rows = slice(start, start + step)
        restored = matmul(back_ref[rows, :], attended_ref[...]).astype(jnp.bfloat16)
        made_ref[index] = mixed_ref[rows, :] + matmul(restored, weight_ref[...])
        copy = pltpu.make_async_copy(
            made_ref.at[index], out_ref.at[pl.ds(start, step)], sent.at[index]
        )
        copy.start()
        copies.append(copy)
    for copy in copies:
        copy.wait()


def finish(own, plan, incoming, back, w_out, mixed):
    tokens, channels = mixed.shape
    step = divisor(tokens, 256, 16)
    return pl.pallas_call(
        functools.partial(finish_kernel, plan=plan),
        in_specs=[pl.BlockSpec(memory_space=pltpu.SMEM)] + [vmem()] * (len(incoming) + 3),
        out_specs=pl.BlockSpec(memory_space=pltpu.HBM),
        out_shape=jax.ShapeDtypeStruct((tokens, channels), jnp.float32),
        scratch_shapes=[
            pltpu.VMEM((tokens, channels), jnp.bfloat16),
            pltpu.VMEM((tokens // step, step, channels), jnp.float32),
            pltpu.SemaphoreType.DMA((tokens // step,)),
        ],
        compiler_params=pltpu.CompilerParams(vmem_limit_bytes=6 * MIB),
        name="finish",
    )(own, *incoming, back, w_out, mixed)


def swap_pairs(edge, axis, start):
    pairs = [(i, i + 1) for i in range(start, lax.axis_size(axis) - 1, 2)]
    return lax.ppermute(edge, axis, pairs + [(b, a) for a, b in pairs])


def exchange_plan(row_devices, col_devices):
    devices = row_devices * col_devices
    crossing = list(range(devices - 2, devices // 2 - 1, -2))
    others = list(range(devices // 2 - 2, 0, -2))
    masks = crossing[:-1] + others[:-1] + crossing[-1:] + others[-1:] + [0]
    return masks, 2, 2


def outgoing_shapes(plan, size, channels):
    masks, late, sides = plan
    if sides == 1:
        return [(1, size, channels)]
    early = len(masks) - 1 - late
    return [(2, size, channels)] * late + [
        (1, size, channels), (early + 1, size, channels), (early, size, channels)
    ]


def write_block(plan, refs, index, side, rows, value):
    masks, late, sides = plan
    if sides == 1:
        refs[0][0, rows] = value
    elif index < late:
        refs[index][side, rows] = value
    elif index == len(masks) - 1:
        refs[late + side][0, rows] = value
    elif side == 0:
        refs[late + 2][index - late, rows] = value
    else:
        refs[late + 1][index - late + 1, rows] = value


def read_block(plan, refs, index, side, rows):
    masks, late, sides = plan
    if sides == 1:
        return refs[0][0, rows]
    if index < late:
        return refs[index + side * len(masks)][side, rows]
    if index == len(masks) - 1:
        return refs[index + side * (late + 1)][0, rows]
    return refs[index][side, rows]


def join_kernel(own_ref, swapped_ref, *out_refs):
    for index, out_ref in enumerate(out_refs):
        out_ref[0] = own_ref[index]
        out_ref[1] = swapped_ref[index + 1]


def join(own, swapped):
    early, size, channels = own.shape
    return pl.pallas_call(
        join_kernel,
        in_specs=[vmem()] * 2,
        out_specs=[vmem()] * early,
        out_shape=[jax.ShapeDtypeStruct((2, size, channels), own.dtype)] * early,
        compiler_params=pltpu.CompilerParams(vmem_limit_bytes=2 * MIB),
        name="join",
    )(own, swapped)


def trade(plan, outgoing):
    masks, late, _ = plan
    devices = lax.axis_size("row") * lax.axis_size("col")

    def swap(slab, mask):
        return lax.ppermute(slab, ("row", "col"), [(i, i ^ mask) for i in range(devices)])

    slabs, (kept, passed, own) = outgoing[:late], outgoing[late:]
    swapped = swap(passed, 1)
    first = [swap(slab, mask) for slab, mask in zip(slabs, masks)]
    rest = [swap(slab, mask) for slab, mask in zip(join(own, swapped), masks[late:-1])]
    tied = lax.optimization_barrier((*first, *rest[:-late]))
    first, rest = tied[:late], [*tied[late:], *rest[-late:]]
    return [*first, *rest, kept, *[swap(slab, 1) for slab in first], swapped]


def trade_all(slabs, sets, members, outward):
    axes = ("row", "col")
    channels = slabs[0].shape[-1]
    block = slabs[0].reshape(-1, channels)
    devices = block.shape[0] // (sets * members)
    if not outward:
        block = block.reshape(sets, devices, members, channels).transpose(1, 0, 2, 3)
    block = block.reshape(devices, sets * members, channels)
    block = lax.all_to_all(block, axes, 0, 0, tiled=True)
    if outward:
        block = block.reshape(devices, sets, members, channels).transpose(1, 0, 2, 3)
    return [block.reshape(1, -1, channels)]


def grouping(rows, cols, blocks_rows, blocks_cols):
    order = np.arange(rows * cols).reshape(
        blocks_rows, rows // blocks_rows, blocks_cols, cols // blocks_cols
    )
    order = order.transpose(1, 3, 0, 2).reshape(-1)
    matrix = np.zeros((order.size, order.size), np.float32)
    matrix[np.arange(order.size), order] = 1.0
    return matrix


def shards(field, w_expand, depth_kernel, w_project, w_qkv, w_out):
    rows, cols, channels = field.shape
    tokens = rows * cols
    row_devices = lax.axis_size("row")
    col_devices = lax.axis_size("col")
    devices = row_devices * col_devices
    blocks_rows = GRID // row_devices
    blocks_cols = GRID // col_devices
    members = blocks_rows * blocks_cols
    sets_local = tokens // members // devices
    matrix = grouping(rows, cols, blocks_rows, blocks_cols)
    perm = jnp.asarray(matrix, jnp.bfloat16)
    back = jnp.asarray(matrix.T, jnp.bfloat16)

    flat = field.reshape(tokens, channels)
    pairwise = 8 <= devices <= 16 and devices & (devices - 1) == 0 and col_devices % 2 == 0
    plan = exchange_plan(row_devices, col_devices) if pairwise else ([0], 0, 1)
    row, col = lax.axis_index("row"), lax.axis_index("col")
    own = (row * col_devices + col if pairwise else row * 0).reshape(1)
    odd_row, odd_col = (row % 2).reshape(1), (col % 2).reshape(1)

    own, odd_row, odd_col, top, bottom = lax.optimization_barrier(
        (own, odd_row, odd_col, field[0], field[rows - 1])
    )
    one, two = row_edges(odd_row, top, bottom)
    one, two = swap_pairs(one, "row", 0), swap_pairs(two, "row", 1)
    normed = half_norm_of(flat)
    expanded = expand(normed, w_expand)
    tile = divisor(w_expand.shape[1] // 2, 256, LANES)
    count = w_expand.shape[1] // tile
    early = 2
    total, rim_one = inner(
        expanded, flat, depth_kernel, w_project, rows, cols, 0, early, tile
    )
    one, two, normed, expanded, total, rim_one = lax.optimization_barrier(
        (one, two, normed, expanded, total, rim_one)
    )
    up, down, one, two = column_strips(odd_row, odd_col, normed, one, two, round_up(rows + 2, 16))
    one, two = swap_pairs(one, "col", 0), swap_pairs(two, "col", 1)
    total, rim_two = inner(
        expanded, total, depth_kernel, w_project, rows, cols, early, count - early, tile
    )

    size = tokens // (len(plan[0]) * plan[2])
    mixed, *outgoing = rim(
        own, odd_col, plan, size, total, [rim_one, rim_two], up, down, one, two, w_expand,
        depth_kernel, w_project, perm, rows, cols,
    )

    def route(outgoing, outward):
        if pairwise:
            return trade(plan, outgoing)
        return trade_all(outgoing, sets_local, members, outward)

    outgoing = attend(plan, route(outgoing, True), w_qkv, sets_local)
    final = finish(own, plan, route(outgoing, False), back, w_out, mixed)
    return final.reshape(rows, cols, channels)


def solution(mesh):
    return jax.shard_map(
        shards,
        mesh=mesh,
        in_specs=(P(("field", "row"), "col", None), P(), P(), P(), P(), P()),
        out_specs=P(("field", "row"), "col", None),
        check_vma=False,
    )
```

```python
import functools
import math

import jax
import jax.numpy as jnp
import numpy as np
from jax import lax
from jax.experimental import pallas as pl
from jax.experimental.pallas import tpu as pltpu
from jax.sharding import PartitionSpec as P

HEADS = 16
GRID = 16
LANES = 128
MIB = 1024 * 1024
NT = (((1,), (1,)), ((), ()))


def layer_norm(inputs):
    average = jnp.mean(inputs, axis=-1, keepdims=True)
    centred = inputs - average
    variance = jnp.mean(centred * centred, axis=-1, keepdims=True)
    return centred * lax.rsqrt(variance + 1e-05)


def gelu_of_half(half):
    scale = math.sqrt(2.0 / math.pi)
    inner = half * (2.0 * scale + (8.0 * scale * 0.044715) * (half * half))
    return half + half * jnp.tanh(inner)


def matmul(a, b):
    return jnp.dot(a, b, preferred_element_type=jnp.float32)


def matmul_nt(a, b):
    return lax.dot_general(a, b, NT, preferred_element_type=jnp.float32)


def divisor(size, most, unit):
    best = size
    for piece in range(unit, most + 1, unit):
        if size % piece == 0:
            best = piece
    return best


def round_up(size, unit):
    return -(-size // unit) * unit


def vmem():
    return pl.BlockSpec(memory_space=pltpu.VMEM)


def half_norm(inputs):
    return (layer_norm(inputs) * 0.5).astype(jnp.bfloat16)


def half_norm_kernel(in_ref, out_ref):
    rows = in_ref.shape[0]
    step = divisor(rows, 128, 16)
    for start in range(0, rows, step):
        out_ref[start : start + step, :] = half_norm(in_ref[start : start + step, :])


def half_norm_of(inputs):
    return pl.pallas_call(
        half_norm_kernel,
        in_specs=[vmem()],
        out_specs=vmem(),
        out_shape=jax.ShapeDtypeStruct(inputs.shape, jnp.bfloat16),
        compiler_params=pltpu.CompilerParams(vmem_limit_bytes=4 * MIB),
        cost_estimate=pl.CostEstimate(
            flops=10**9, bytes_accessed=6 * inputs.size, transcendentals=inputs.shape[0]
        ),
        name="half_norm",
    )(inputs)


def choose(condition, one, two):
    flags = jnp.full((one.shape[0], 1), condition, jnp.int32) == 1
    return jnp.where(flags, one.astype(jnp.float32), two.astype(jnp.float32)).astype(one.dtype)


def edges_kernel(odd_row_ref, top_ref, bottom_ref, one_ref, two_ref):
    odd = odd_row_ref[0]
    top, bottom = half_norm(top_ref[...]), half_norm(bottom_ref[...])
    one_ref[...] = choose(odd, top, bottom)
    two_ref[...] = choose(odd, bottom, top)


def row_edges(odd_row, top, bottom):
    return pl.pallas_call(
        edges_kernel,
        in_specs=[pl.BlockSpec(memory_space=pltpu.SMEM)] + [vmem()] * 2,
        out_specs=[vmem()] * 2,
        out_shape=[jax.ShapeDtypeStruct(top.shape, jnp.bfloat16)] * 2,
        compiler_params=pltpu.CompilerParams(vmem_limit_bytes=4 * MIB),
        cost_estimate=pl.CostEstimate(
            flops=10**10, bytes_accessed=12 * top.size, transcendentals=2 * top.shape[0]
        ),
        name="row_edges",
    )(odd_row, top, bottom)


def picker(shape, pick):
    row = lax.broadcasted_iota(jnp.int32, shape, 0)
    column = lax.broadcasted_iota(jnp.int32, shape, 1)
    return jnp.where(pick(row, column), 1.0, 0.0).astype(jnp.bfloat16)


def strips_kernel(
    odd_row_ref, odd_col_ref, normed_ref, row_one_ref, row_two_ref, up_ref, down_ref, one_ref, two_ref
):
    tokens = normed_ref.shape[0]
    cols = up_ref.shape[0]
    rows = tokens // cols
    slot = one_ref.shape[0]
    odd_row, odd_col = odd_row_ref[0], odd_col_ref[0]
    up = choose(odd_row, row_one_ref[...], row_two_ref[...])
    down = choose(odd_row, row_two_ref[...], row_one_ref[...])
    up_ref[...] = up
    down_ref[...] = down
    strips = []
    for x in (0, cols - 1):
        body = picker(
            (slot, tokens), lambda i, j: (i >= 1) & (i <= rows) & (j == (i - 1) * cols + x)
        )
        head = picker((slot, cols), lambda i, j: (i == 0) & (j == x))
        foot = picker((slot, cols), lambda i, j: (i == rows + 1) & (j == x))
        strip = matmul(body, normed_ref[...]) + matmul(head, up) + matmul(foot, down)
        strips.append(strip.astype(jnp.bfloat16))
    one_ref[...] = choose(odd_col, strips[0], strips[1])
    two_ref[...] = choose(odd_col, strips[1], strips[0])


def column_strips(odd_row, odd_col, normed, row_one, row_two, slot):
    cols, channels = row_one.shape
    shapes = [(cols, channels)] * 2 + [(slot, channels)] * 2
    return pl.pallas_call(
        strips_kernel,
        in_specs=[pl.BlockSpec(memory_space=pltpu.SMEM)] * 2 + [vmem()] * 3,
        out_specs=[vmem()] * 4,
        out_shape=[jax.ShapeDtypeStruct(shape, jnp.bfloat16) for shape in shapes],
        compiler_params=pltpu.CompilerParams(vmem_limit_bytes=4 * MIB),
        name="column_strips",
    )(odd_row, odd_col, normed, row_one, row_two)


def padded_rows(tokens):
    return tokens + 16


def expand_kernel(normed_ref, weight_ref, out_ref, even_ref, odd_ref):
    tokens, tile = even_ref.shape
    width = weight_ref.shape[1]
    subs = tile // LANES

    def multiply(index, made_ref):
        lanes = pl.ds(pl.multiple_of(index * tile, tile), tile)
        made_ref[...] = matmul(normed_ref[...], weight_ref[:, lanes])

    def activate(index, made_ref):
        for sub in range(subs):
            row = (index * subs + sub) * padded_rows(tokens) + 8
            out_ref[pl.ds(pl.multiple_of(row, 8), tokens), :] = gelu_of_half(
                made_ref[:, sub * LANES : (sub + 1) * LANES]
            )

    def body(index, carry):
        multiply(2 * index + 1, odd_ref)
        activate(2 * index, even_ref)
        multiply(2 * index + 2, even_ref)
        activate(2 * index + 1, odd_ref)
        return carry

    count = width // tile
    multiply(0, even_ref)
    lax.fori_loop(0, count // 2 - 1, body, 0)
    multiply(count - 1, odd_ref)
    activate(count - 2, even_ref)
    activate(count - 1, odd_ref)


def expand(normed, w_expand):
    tokens, channels = normed.shape
    width = w_expand.shape[1]
    return pl.pallas_call(
        expand_kernel,
        in_specs=[vmem()] * 2,
        out_specs=vmem(),
        out_shape=jax.ShapeDtypeStruct((width // LANES * padded_rows(tokens), LANES), jnp.float32),
        scratch_shapes=[
            pltpu.VMEM((tokens, divisor(width // 2, 256, LANES)), jnp.float32)
        ] * 2,
        compiler_params=pltpu.CompilerParams(vmem_limit_bytes=6 * MIB),
        cost_estimate=pl.CostEstimate(
            flops=10**10,
            bytes_accessed=tokens * channels * 2 + channels * width * 2 + tokens * width * 4,
            transcendentals=tokens * width,
        ),
        name="expand",
    )(normed, w_expand)


def inner_kernel(
    expanded_ref, start_ref, depth_ref, w_project_ref, total_ref, rim_ref, even_ref, odd_ref,
    *, rows, cols, first, count,
):
    tokens = rows * cols
    tile = even_ref.shape[1]
    subs = tile // LANES
    position = lax.broadcasted_iota(jnp.int32, (8, LANES), 0)
    at_first = position == 0
    at_last = position == 7

    def clear_ends(value, low, high):
        head = jnp.where(at_first, 0.0, value[:8]) if low else value[:8]
        foot = jnp.where(at_last, 0.0, value[-8:]) if high else value[-8:]
        return jnp.concatenate([head, value[8:-8], foot], axis=0)

    def convolve(index, out_ref):
        for sub in range(subs):
            chunk = (first + index) * subs + sub
            lanes = pl.ds(pl.multiple_of(chunk * LANES, LANES), LANES)
            base = chunk * padded_rows(tokens) + 8
            here = index * subs + sub
            taps = [[0.5 * depth_ref[p, q : q + 1, lanes] for q in range(3)] for p in range(3)]
            spot = slice(sub * LANES, (sub + 1) * LANES)
            sums = {}
            for y in range(rows + 1):
                if y < rows:
                    parts = [
                        expanded_ref[pl.ds(base + (y * cols + q), cols), :] for q in (-1, 0, 1)
                    ]
                    parts[0] = clear_ends(parts[0], True, False)
                    parts[2] = clear_ends(parts[2], False, True)
                    for p in range(3):
                        target = y + 1 - p
                        if 0 <= target < rows:
                            for q in range(3):
                                term = taps[p][q] * parts[q]
                                sums[target] = sums[target] + term if target in sums else term
                if y > 0:
                    done = sums.pop(y - 1)
                    rim_ref[here, 2 * cols + y - 1 : 2 * cols + y] = done[:1]
                    rim_ref[here, 2 * cols + rows + y - 1 : 2 * cols + rows + y] = done[-1:]
                    if y in (1, rows):
                        start = 0 if y == 1 else cols
                        rim_ref[here, start : start + cols] = done
                        made = jnp.zeros_like(done)
                    else:
                        made = clear_ends(gelu_of_half(done), True, True)
                    out_ref[(y - 1) * cols : y * cols, spot] = made.astype(jnp.bfloat16)

    def project(index, in_ref, from_ref):
        piece = pl.ds(pl.multiple_of((first + index) * tile, tile), tile)
        total_ref[...] = from_ref[...] + matmul(in_ref[...], w_project_ref[piece, :])

    convolve(0, even_ref)
    project(0, even_ref, start_ref)
    convolve(1, odd_ref)

    def body(index, carry):
        convolve(2 * index, even_ref)
        project(2 * index - 1, odd_ref, total_ref)
        convolve(2 * index + 1, odd_ref)
        project(2 * index, even_ref, total_ref)
        return carry

    lax.fori_loop(1, count // 2, body, 0)
    project(count - 1, odd_ref, total_ref)


def inner(expanded, start, depth_kernel, w_project, rows, cols, first, count, tile):
    tokens, channels = start.shape
    rim = (count * tile // LANES, 2 * cols + 2 * rows, LANES)
    return pl.pallas_call(
        functools.partial(inner_kernel, rows=rows, cols=cols, first=first, count=count),
        in_specs=[vmem()] * 4,
        out_specs=[vmem()] * 2,
        out_shape=[
            jax.ShapeDtypeStruct((tokens, channels), jnp.float32),
            jax.ShapeDtypeStruct(rim, jnp.float32),
        ],
        scratch_shapes=[pltpu.VMEM((tokens, tile), jnp.bfloat16)] * 2,
        compiler_params=pltpu.CompilerParams(vmem_limit_bytes=6 * MIB),
        cost_estimate=pl.CostEstimate(
            flops=2 * 10**9 * count,
            bytes_accessed=tokens * channels * 8 + tokens * count * tile * 4,
            transcendentals=tokens * count * tile,
        ),
        name="inner",
    )(expanded, start, depth_kernel, w_project)


def rim_kernel(
    own_ref, odd_col_ref, inner_ref, *refs, rows, cols, plan, size, pieces,
):
    masks, _, sides = plan
    sent = len(outgoing_shapes(plan, size, 1))
    rim_refs, refs = refs[:pieces], refs[pieces:]
    up_ref, down_ref, one_ref, two_ref, w_expand_ref, depth_ref, w_project_ref, perm_ref = refs[:8]
    mixed_ref, slab_refs = refs[8], refs[9 : 9 + sent]
    halo_ref, active_ref, normed_ref, grouped_ref = refs[9 + sent :]
    tokens = rows * cols
    width = w_expand_ref.shape[1]
    tile = divisor(width, 512, LANES)
    subs = tile // LANES
    slot = one_ref.shape[0]
    left_start, right_start = 2 * cols, 2 * cols + slot

    odd_col = odd_col_ref[0]
    left = choose(odd_col, one_ref[...], two_ref[...])
    right = choose(odd_col, two_ref[...], one_ref[...])
    edges = jnp.concatenate([up_ref[...], down_ref[...], left, right], axis=0)

    def expand_halo(index):
        made = gelu_of_half(matmul(edges, w_expand_ref[:, index * tile : (index + 1) * tile]))
        for sub in range(subs):
            halo_ref[index * subs + sub] = made[:, sub * LANES : (sub + 1) * LANES]

    position = lax.broadcasted_iota(jnp.int32, (cols, LANES), 0)
    at_first = position == 0
    at_last = position == cols - 1

    def activate(chunk, here, sums_ref):
        lanes = slice(chunk * LANES, (chunk + 1) * LANES)
        taps = [[0.5 * depth_ref[p, q : q + 1, lanes] for q in range(3)] for p in range(3)]
        beside = []
        for q, start in ((0, left_start), (2, right_start)):
            beside.append(
                sum(taps[p][q] * halo_ref[chunk, start + p : start + p + rows] for p in range(3))
            )
        made = []
        for p, start, y in ((0, 0, 0), (2, cols, rows - 1)):
            row = halo_ref[chunk, start : start + cols]
            before = jnp.where(at_first, beside[0][y : y + 1], taps[p][0] * pltpu.roll(row, 1, 0))
            after = jnp.where(
                at_last, beside[1][y : y + 1], taps[p][2] * pltpu.roll(row, cols - 1, 0)
            )
            made.append(sums_ref[here, start : start + cols] + before + taps[p][1] * row + after)
        for index in range(2):
            start = 2 * cols + index * rows
            made.append(sums_ref[here, start : start + rows] + beside[index])
        active_ref[:, lanes] = gelu_of_half(jnp.concatenate(made, axis=0)).astype(jnp.bfloat16)

    spots = [(ref, here) for ref in rim_refs for here in range(ref.shape[0])]
    expand_halo(0)
    for index in range(width // tile):
        if (index + 1) * tile < width:
            expand_halo(index + 1)
        for chunk in range(index * subs, (index + 1) * subs):
            activate(chunk, spots[chunk][1], spots[chunk][0])

    mixed_ref[...] = inner_ref[...]
    branch = matmul(active_ref[...], w_project_ref[...])
    mixed_ref[:cols, :] += branch[:cols]
    mixed_ref[tokens - cols :, :] += branch[cols : 2 * cols]
    for y in range(1, rows - 1):
        for index, x in ((0, 0), (1, cols - 1)):
            spot = y * cols + x
            start = 2 * cols + index * rows + y
            mixed_ref[spot : spot + 1, :] += branch[start : start + 1]

    step = divisor(tokens, 128, 16)
    for start in range(0, tokens, step):
        piece = slice(start, start + step)
        normed_ref[piece, :] = layer_norm(mixed_ref[piece, :]).astype(jnp.bfloat16)
    grouped_ref[...] = matmul(perm_ref[...], normed_ref[...]).astype(jnp.bfloat16)
    for index, mask in enumerate(masks):
        for side in range(sides):
            start = pl.multiple_of((own_ref[0] ^ (mask | side)) * size, 16)
            write_block(
                plan, slab_refs, index, side, slice(None), grouped_ref[pl.ds(start, size), :]
            )


def rim(
    own, odd_col, plan, size, total, rims, up, down, one, two, w_expand, depth_kernel, w_project, perm,
    rows, cols,
):
    tokens, channels = total.shape
    width = w_expand.shape[1]
    halo_rows = 2 * cols + 2 * one.shape[0]
    sent = outgoing_shapes(plan, size, channels)
    return pl.pallas_call(
        functools.partial(
            rim_kernel, rows=rows, cols=cols, plan=plan, size=size, pieces=len(rims)
        ),
        in_specs=[pl.BlockSpec(memory_space=pltpu.SMEM)] * 2 + [vmem()] * (9 + len(rims)),
        out_specs=[vmem()] * (1 + len(sent)),
        out_shape=[jax.ShapeDtypeStruct((tokens, channels), jnp.float32)]
        + [jax.ShapeDtypeStruct(shape, jnp.bfloat16) for shape in sent],
        scratch_shapes=[
            pltpu.VMEM((width // LANES, halo_rows, LANES), jnp.float32),
            pltpu.VMEM((2 * cols + 2 * rows, width), jnp.bfloat16),
            pltpu.VMEM((tokens, channels), jnp.bfloat16),
            pltpu.VMEM((tokens, channels), jnp.bfloat16),
        ],
        compiler_params=pltpu.CompilerParams(vmem_limit_bytes=8 * MIB),
        cost_estimate=pl.CostEstimate(
            flops=2 * halo_rows * channels * width * 2 + 2 * tokens * tokens * channels,
            bytes_accessed=tokens * channels * 10 + 4 * channels * width,
            transcendentals=2 * halo_rows * width,
        ),
        name="rim",
    )(own, odd_col, total, *rims, up, down, one, two, w_expand, depth_kernel, w_project, perm)


def identity(size):
    row = lax.broadcasted_iota(jnp.int32, (size, size), 0)
    column = lax.broadcasted_iota(jnp.int32, (size, size), 1)
    return jnp.where(row == column, 1.0, 0.0).astype(jnp.bfloat16)


def attend_kernel(*refs, plan, sets, came):
    masks, _, sides = plan
    slabs = len(masks)
    _, size, channels = refs[0].shape
    in_refs, weight_ref, out_refs = refs[:came], refs[came], refs[came + 1 : -6]
    query_ref, key_ref, value_ref, turned_ref, even_ref, odd_ref = refs[-6:]
    members = size // sets
    count = slabs * sides * members
    head_width = channels // HEADS
    group_heads = LANES // head_width
    groups = channels // LANES
    factor = math.log2(math.e) / math.sqrt(head_width)
    lane = lax.broadcasted_iota(jnp.int32, (1, LANES), 1)
    masks = [
        jnp.where((lane >= j * head_width) & (lane < (j + 1) * head_width), 1.0, 0.0).astype(
            jnp.bfloat16
        )
        for j in range(group_heads)
    ]
    turn_values = identity(channels)
    block = jnp.concatenate(
        [
            read_block(plan, in_refs, index, side, slice(s * members, (s + 1) * members))
            for s in range(sets)
            for index in range(slabs)
            for side in range(sides)
        ],
        axis=0,
    )
    qkv = matmul(block, weight_ref[...]).astype(jnp.bfloat16)
    for s in range(sets):
        own_rows = slice(s * count, (s + 1) * count)
        values = matmul_nt(turn_values, qkv[own_rows, 2 * channels :]).astype(jnp.bfloat16)
        for group in range(groups):
            spot = group * LANES
            query_ref[s * groups + group] = qkv[own_rows, spot : spot + LANES]
            key_ref[s * groups + group] = qkv[own_rows, channels + spot : channels + spot + LANES]
            for j in range(group_heads):
                head = (group * group_heads + j) * head_width
                value_ref[s * groups + group, j, :head_width] = values[head : head + head_width]
                value_ref[s * groups + group, j, head_width:] = jnp.ones((16, count), jnp.bfloat16)

    def scores(index, out):
        keys = key_ref[index]
        stacked = jnp.concatenate([keys * mask for mask in masks], axis=0)
        out[...] = matmul_nt(stacked, query_ref[index])

    def weigh(index, scores_ref):
        for j in range(group_heads):
            part = scores_ref[j * count : (j + 1) * count]
            highest = jnp.max(part, axis=0, keepdims=True)
            raised = jnp.exp2((part - highest) * factor).astype(jnp.bfloat16)
            product = matmul(value_ref[index, j], raised)
            scale = 1.0 / product[head_width : head_width + 1]
            turned_ref[index, j * head_width : (j + 1) * head_width] = (
                product[:head_width] * scale
            ).astype(jnp.bfloat16)

    total = sets * groups
    scores(0, even_ref)

    def body(pair, carry):
        scores(2 * pair + 1, odd_ref)
        weigh(2 * pair, even_ref)
        scores(jnp.minimum(2 * pair + 2, total - 1), even_ref)
        weigh(2 * pair + 1, odd_ref)
        return carry

    lax.fori_loop(0, total // 2, body, 0)
    turn_tokens = identity(count)
    for s in range(sets):
        turned = turned_ref[s * groups : (s + 1) * groups].reshape(channels, count)
        attended = matmul_nt(turn_tokens, turned).astype(jnp.bfloat16)
        for index in range(slabs):
            for side in range(sides):
                start = (index * sides + side) * members
                write_block(
                    plan, out_refs, index, side, slice(s * members, (s + 1) * members),
                    attended[start : start + members],
                )


def attend(plan, incoming, w_qkv, sets):
    masks, _, sides = plan
    _, size, channels = incoming[0].shape
    count = len(masks) * sides * size // sets
    sent = outgoing_shapes(plan, size, channels)
    head_width = channels // HEADS
    group_heads = LANES // head_width
    total = sets * channels // LANES
    return pl.pallas_call(
        functools.partial(attend_kernel, plan=plan, sets=sets, came=len(incoming)),
        in_specs=[vmem()] * (len(incoming) + 1),
        out_specs=[vmem()] * len(sent),
        out_shape=[jax.ShapeDtypeStruct(shape, jnp.bfloat16) for shape in sent],
        scratch_shapes=[
            pltpu.VMEM((total, count, LANES), jnp.bfloat16),
            pltpu.VMEM((total, count, LANES), jnp.bfloat16),
            pltpu.VMEM((total, group_heads, head_width + 16, count), jnp.bfloat16),
            pltpu.VMEM((total, LANES, count), jnp.bfloat16),
            pltpu.VMEM((group_heads * count, count), jnp.float32),
            pltpu.VMEM((group_heads * count, count), jnp.float32),
        ],
        compiler_params=pltpu.CompilerParams(vmem_limit_bytes=10 * MIB),
        cost_estimate=pl.CostEstimate(
            flops=sets * (2 * count * channels * channels * 3 + 4 * count * count * channels),
            bytes_accessed=4 * sets * count * channels + 6 * channels * channels,
            transcendentals=sets * HEADS * count * count,
        ),
        name="attend",
    )(*incoming, w_qkv)


def finish_kernel(own_ref, *refs, plan):
    masks, _, sides = plan
    in_refs, rest = refs[:-7], refs[-7:]
    back_ref, weight_ref, mixed_ref, out_ref, attended_ref, made_ref, sent = rest
    tokens = mixed_ref.shape[0]
    size = in_refs[0].shape[1]
    for index, mask in enumerate(masks):
        for side in range(sides):
            start = pl.multiple_of((own_ref[0] ^ (mask | side)) * size, 16)
            attended_ref[pl.ds(start, size), :] = read_block(
                plan, in_refs, index, side, slice(None)
            )
    step = made_ref.shape[1]
    copies = []
    for index, start in enumerate(range(0, tokens, step)):
        rows = slice(start, start + step)
        restored = matmul(back_ref[rows, :], attended_ref[...]).astype(jnp.bfloat16)
        made_ref[index] = mixed_ref[rows, :] + matmul(restored, weight_ref[...])
        copy = pltpu.make_async_copy(
            made_ref.at[index], out_ref.at[pl.ds(start, step)], sent.at[index]
        )
        copy.start()
        copies.append(copy)
    for copy in copies:
        copy.wait()


def finish(own, plan, incoming, back, w_out, mixed):
    tokens, channels = mixed.shape
    step = divisor(tokens, 256, 16)
    return pl.pallas_call(
        functools.partial(finish_kernel, plan=plan),
        in_specs=[pl.BlockSpec(memory_space=pltpu.SMEM)] + [vmem()] * (len(incoming) + 3),
        out_specs=pl.BlockSpec(memory_space=pltpu.HBM),
        out_shape=jax.ShapeDtypeStruct((tokens, channels), jnp.float32),
        scratch_shapes=[
            pltpu.VMEM((tokens, channels), jnp.bfloat16),
            pltpu.VMEM((tokens // step, step, channels), jnp.float32),
            pltpu.SemaphoreType.DMA((tokens // step,)),
        ],
        compiler_params=pltpu.CompilerParams(vmem_limit_bytes=6 * MIB),
        name="finish",
    )(own, *incoming, back, w_out, mixed)


def swap_pairs(edge, axis, start):
    pairs = [(i, i + 1) for i in range(start, lax.axis_size(axis) - 1, 2)]
    return lax.ppermute(edge, axis, pairs + [(b, a) for a, b in pairs])


def exchange_plan(row_devices, col_devices):
    devices = row_devices * col_devices
    crossing = list(range(devices - 2, devices // 2 - 1, -2))
    others = list(range(devices // 2 - 2, 0, -2))
    masks = crossing[:-1] + others[:-1] + crossing[-1:] + others[-1:] + [0]
    return masks, 2, 2


def outgoing_shapes(plan, size, channels):
    masks, late, sides = plan
    if sides == 1:
        return [(1, size, channels)]
    early = len(masks) - 1 - late
    return [(2, size, channels)] * late + [
        (1, size, channels), (early + 1, size, channels), (early, size, channels)
    ]


def write_block(plan, refs, index, side, rows, value):
    masks, late, sides = plan
    if sides == 1:
        refs[0][0, rows] = value
    elif index < late:
        refs[index][side, rows] = value
    elif index == len(masks) - 1:
        refs[late + side][0, rows] = value
    elif side == 0:
        refs[late + 2][index - late, rows] = value
    else:
        refs[late + 1][index - late + 1, rows] = value


def read_block(plan, refs, index, side, rows):
    masks, late, sides = plan
    if sides == 1:
        return refs[0][0, rows]
    if index < late:
        return refs[index + side * len(masks)][side, rows]
    if index == len(masks) - 1:
        return refs[index + side * (late + 1)][0, rows]
    return refs[index][side, rows]


def join_kernel(own_ref, swapped_ref, *out_refs):
    for index, out_ref in enumerate(out_refs):
        out_ref[0] = own_ref[index]
        out_ref[1] = swapped_ref[index + 1]


def join(own, swapped):
    early, size, channels = own.shape
    return pl.pallas_call(
        join_kernel,
        in_specs=[vmem()] * 2,
        out_specs=[vmem()] * early,
        out_shape=[jax.ShapeDtypeStruct((2, size, channels), own.dtype)] * early,
        compiler_params=pltpu.CompilerParams(vmem_limit_bytes=2 * MIB),
        name="join",
    )(own, swapped)


def trade(plan, outgoing):
    masks, late, _ = plan
    devices = lax.axis_size("row") * lax.axis_size("col")

    def swap(slab, mask):
        return lax.ppermute(slab, ("row", "col"), [(i, i ^ mask) for i in range(devices)])

    slabs, (kept, passed, own) = outgoing[:late], outgoing[late:]
    swapped = swap(passed, 1)
    first = [swap(slab, mask) for slab, mask in zip(slabs, masks)]
    rest = [swap(slab, mask) for slab, mask in zip(join(own, swapped), masks[late:-1])]
    tied = lax.optimization_barrier((*first, *rest[:-late]))
    first, rest = tied[:late], [*tied[late:], *rest[-late:]]
    return [*first, *rest, kept, *[swap(slab, 1) for slab in first], swapped]


def trade_all(slabs, sets, members, outward):
    axes = ("row", "col")
    channels = slabs[0].shape[-1]
    block = slabs[0].reshape(-1, channels)
    devices = block.shape[0] // (sets * members)
    if not outward:
        block = block.reshape(sets, devices, members, channels).transpose(1, 0, 2, 3)
    block = block.reshape(devices, sets * members, channels)
    block = lax.all_to_all(block, axes, 0, 0, tiled=True)
    if outward:
        block = block.reshape(devices, sets, members, channels).transpose(1, 0, 2, 3)
    return [block.reshape(1, -1, channels)]


def grouping(rows, cols, blocks_rows, blocks_cols):
    order = np.arange(rows * cols).reshape(
        blocks_rows, rows // blocks_rows, blocks_cols, cols // blocks_cols
    )
    order = order.transpose(1, 3, 0, 2).reshape(-1)
    matrix = np.zeros((order.size, order.size), np.float32)
    matrix[np.arange(order.size), order] = 1.0
    return matrix


def shards(field, w_expand, depth_kernel, w_project, w_qkv, w_out):
    rows, cols, channels = field.shape
    tokens = rows * cols
    row_devices = lax.axis_size("row")
    col_devices = lax.axis_size("col")
    devices = row_devices * col_devices
    blocks_rows = GRID // row_devices
    blocks_cols = GRID // col_devices
    members = blocks_rows * blocks_cols
    sets_local = tokens // members // devices
    matrix = grouping(rows, cols, blocks_rows, blocks_cols)
    perm = jnp.asarray(matrix, jnp.bfloat16)
    back = jnp.asarray(matrix.T, jnp.bfloat16)

    flat = field.reshape(tokens, channels)
    pairwise = 8 <= devices <= 16 and devices & (devices - 1) == 0 and col_devices % 2 == 0
    plan = exchange_plan(row_devices, col_devices) if pairwise else ([0], 0, 1)
    row, col = lax.axis_index("row"), lax.axis_index("col")
    own = (row * col_devices + col if pairwise else row * 0).reshape(1)
    odd_row, odd_col = (row % 2).reshape(1), (col % 2).reshape(1)

    own, odd_row, odd_col, top, bottom = lax.optimization_barrier(
        (own, odd_row, odd_col, field[0], field[rows - 1])
    )
    one, two = row_edges(odd_row, top, bottom)
    one, two = swap_pairs(one, "row", 0), swap_pairs(two, "row", 1)
    normed = half_norm_of(flat)
    expanded = expand(normed, w_expand)
    tile = divisor(w_expand.shape[1] // 2, 256, LANES)
    count = w_expand.shape[1] // tile
    early = 2
    total, rim_one = inner(
        expanded, flat, depth_kernel, w_project, rows, cols, 0, early, tile
    )
    one, two, normed, expanded, total, rim_one = lax.optimization_barrier(
        (one, two, normed, expanded, total, rim_one)
    )
    up, down, one, two = column_strips(odd_row, odd_col, normed, one, two, round_up(rows + 2, 16))
    one, two = swap_pairs(one, "col", 0), swap_pairs(two, "col", 1)
    total, rim_two = inner(
        expanded, total, depth_kernel, w_project, rows, cols, early, count - early, tile
    )

    size = tokens // (len(plan[0]) * plan[2])
    mixed, *outgoing = rim(
        own, odd_col, plan, size, total, [rim_one, rim_two], up, down, one, two, w_expand,
        depth_kernel, w_project, perm, rows, cols,
    )

    def route(outgoing, outward):
        if pairwise:
            return trade(plan, outgoing)
        return trade_all(outgoing, sets_local, members, outward)

    outgoing = attend(plan, route(outgoing, True), w_qkv, sets_local)
    final = finish(own, plan, route(outgoing, False), back, w_out, mixed)
    return final.reshape(rows, cols, channels)


def solution(mesh):
    return jax.shard_map(
        shards,
        mesh=mesh,
        in_specs=(P(("field", "row"), "col", None), P(), P(), P(), P(), P()),
        out_specs=P(("field", "row"), "col", None),
        check_vma=False,
    )
```

```python
import functools
import math

import jax
import jax.numpy as jnp
import numpy as np
from jax import lax
from jax.experimental import pallas as pl
from jax.experimental.pallas import tpu as pltpu
from jax.sharding import PartitionSpec as P

HEADS = 16
GRID = 16
LANES = 128
MIB = 1024 * 1024
NT = (((1,), (1,)), ((), ()))


def layer_norm(inputs):
    average = jnp.mean(inputs, axis=-1, keepdims=True)
    centred = inputs - average
    variance = jnp.mean(centred * centred, axis=-1, keepdims=True)
    return centred * lax.rsqrt(variance + 1e-05)


def gelu_of_half(half):
    scale = math.sqrt(2.0 / math.pi)
    inner = half * (2.0 * scale + (8.0 * scale * 0.044715) * (half * half))
    return half + half * jnp.tanh(inner.astype(jnp.bfloat16)).astype(jnp.float32)


def matmul(a, b):
    return jnp.dot(a, b, preferred_element_type=jnp.float32)


def matmul_nt(a, b):
    return lax.dot_general(a, b, NT, preferred_element_type=jnp.float32)


def divisor(size, most, unit):
    best = size
    for piece in range(unit, most + 1, unit):
        if size % piece == 0:
            best = piece
    return best


def round_up(size, unit):
    return -(-size // unit) * unit


def vmem():
    return pl.BlockSpec(memory_space=pltpu.VMEM)


def half_norm(inputs):
    return (layer_norm(inputs) * 0.5).astype(jnp.bfloat16)


def half_norm_kernel(in_ref, out_ref):
    rows = in_ref.shape[0]
    step = divisor(rows, 128, 16)
    for start in range(0, rows, step):
        out_ref[start : start + step, :] = half_norm(in_ref[start : start + step, :])


def half_norm_of(inputs):
    return pl.pallas_call(
        half_norm_kernel,
        in_specs=[vmem()],
        out_specs=vmem(),
        out_shape=jax.ShapeDtypeStruct(inputs.shape, jnp.bfloat16),
        compiler_params=pltpu.CompilerParams(vmem_limit_bytes=4 * MIB),
        cost_estimate=pl.CostEstimate(
            flops=10**9, bytes_accessed=6 * inputs.size, transcendentals=inputs.shape[0]
        ),
        name="half_norm",
    )(inputs)


def choose(condition, one, two):
    flags = jnp.full((one.shape[0], 1), condition, jnp.int32) == 1
    return jnp.where(flags, one.astype(jnp.float32), two.astype(jnp.float32)).astype(one.dtype)


def edges_kernel(odd_row_ref, top_ref, bottom_ref, one_ref, two_ref):
    odd = odd_row_ref[0]
    top, bottom = half_norm(top_ref[...]), half_norm(bottom_ref[...])
    one_ref[...] = choose(odd, top, bottom)
    two_ref[...] = choose(odd, bottom, top)


def row_edges(odd_row, top, bottom):
    return pl.pallas_call(
        edges_kernel,
        in_specs=[pl.BlockSpec(memory_space=pltpu.SMEM)] + [vmem()] * 2,
        out_specs=[vmem()] * 2,
        out_shape=[jax.ShapeDtypeStruct(top.shape, jnp.bfloat16)] * 2,
        compiler_params=pltpu.CompilerParams(vmem_limit_bytes=4 * MIB),
        cost_estimate=pl.CostEstimate(
            flops=10**10, bytes_accessed=12 * top.size, transcendentals=2 * top.shape[0]
        ),
        name="row_edges",
    )(odd_row, top, bottom)


def picker(shape, pick):
    row = lax.broadcasted_iota(jnp.int32, shape, 0)
    column = lax.broadcasted_iota(jnp.int32, shape, 1)
    return jnp.where(pick(row, column), 1.0, 0.0).astype(jnp.bfloat16)


def strips_kernel(
    odd_row_ref, odd_col_ref, normed_ref, row_one_ref, row_two_ref, up_ref, down_ref, one_ref, two_ref
):
    tokens = normed_ref.shape[0]
    cols = up_ref.shape[0]
    rows = tokens // cols
    slot = one_ref.shape[0]
    odd_row, odd_col = odd_row_ref[0], odd_col_ref[0]
    up = choose(odd_row, row_one_ref[...], row_two_ref[...])
    down = choose(odd_row, row_two_ref[...], row_one_ref[...])
    up_ref[...] = up
    down_ref[...] = down
    strips = []
    for x in (0, cols - 1):
        body = picker(
            (slot, tokens), lambda i, j: (i >= 1) & (i <= rows) & (j == (i - 1) * cols + x)
        )
        head = picker((slot, cols), lambda i, j: (i == 0) & (j == x))
        foot = picker((slot, cols), lambda i, j: (i == rows + 1) & (j == x))
        strip = matmul(body, normed_ref[...]) + matmul(head, up) + matmul(foot, down)
        strips.append(strip.astype(jnp.bfloat16))
    one_ref[...] = choose(odd_col, strips[0], strips[1])
    two_ref[...] = choose(odd_col, strips[1], strips[0])


def column_strips(odd_row, odd_col, normed, row_one, row_two, slot):
    cols, channels = row_one.shape
    shapes = [(cols, channels)] * 2 + [(slot, channels)] * 2
    return pl.pallas_call(
        strips_kernel,
        in_specs=[pl.BlockSpec(memory_space=pltpu.SMEM)] * 2 + [vmem()] * 3,
        out_specs=[vmem()] * 4,
        out_shape=[jax.ShapeDtypeStruct(shape, jnp.bfloat16) for shape in shapes],
        compiler_params=pltpu.CompilerParams(vmem_limit_bytes=4 * MIB),
        name="column_strips",
    )(odd_row, odd_col, normed, row_one, row_two)


def padded_rows(tokens):
    return tokens + 16


def expand_kernel(normed_ref, weight_ref, out_ref, even_ref, odd_ref):
    tokens, tile = even_ref.shape
    width = weight_ref.shape[1]
    subs = tile // LANES

    def multiply(index, made_ref):
        lanes = pl.ds(pl.multiple_of(index * tile, tile), tile)
        made_ref[...] = matmul(normed_ref[...], weight_ref[:, lanes])

    def activate(index, made_ref):
        for sub in range(subs):
            row = (index * subs + sub) * padded_rows(tokens) + 8
            out_ref[pl.ds(pl.multiple_of(row, 8), tokens), :] = gelu_of_half(
                made_ref[:, sub * LANES : (sub + 1) * LANES]
            )

    def body(index, carry):
        multiply(2 * index + 1, odd_ref)
        activate(2 * index, even_ref)
        multiply(2 * index + 2, even_ref)
        activate(2 * index + 1, odd_ref)
        return carry

    count = width // tile
    multiply(0, even_ref)
    lax.fori_loop(0, count // 2 - 1, body, 0)
    multiply(count - 1, odd_ref)
    activate(count - 2, even_ref)
    activate(count - 1, odd_ref)


def expand(normed, w_expand):
    tokens, channels = normed.shape
    width = w_expand.shape[1]
    return pl.pallas_call(
        expand_kernel,
        in_specs=[vmem()] * 2,
        out_specs=vmem(),
        out_shape=jax.ShapeDtypeStruct((width // LANES * padded_rows(tokens), LANES), jnp.float32),
        scratch_shapes=[
            pltpu.VMEM((tokens, divisor(width // 2, 256, LANES)), jnp.float32)
        ] * 2,
        compiler_params=pltpu.CompilerParams(vmem_limit_bytes=6 * MIB),
        cost_estimate=pl.CostEstimate(
            flops=10**10,
            bytes_accessed=tokens * channels * 2 + channels * width * 2 + tokens * width * 4,
            transcendentals=tokens * width,
        ),
        name="expand",
    )(normed, w_expand)


def inner_kernel(
    expanded_ref, start_ref, depth_ref, w_project_ref, total_ref, rim_ref, even_ref, odd_ref,
    *, rows, cols, first, count,
):
    tokens = rows * cols
    tile = even_ref.shape[1]
    subs = tile // LANES
    position = lax.broadcasted_iota(jnp.int32, (8, LANES), 0)
    at_first = position == 0
    at_last = position == 7

    def clear_ends(value, low, high):
        head = jnp.where(at_first, 0.0, value[:8]) if low else value[:8]
        foot = jnp.where(at_last, 0.0, value[-8:]) if high else value[-8:]
        return jnp.concatenate([head, value[8:-8], foot], axis=0)

    def convolve(index, out_ref):
        for sub in range(subs):
            chunk = (first + index) * subs + sub
            lanes = pl.ds(pl.multiple_of(chunk * LANES, LANES), LANES)
            base = chunk * padded_rows(tokens) + 8
            here = index * subs + sub
            taps = [[0.5 * depth_ref[p, q : q + 1, lanes] for q in range(3)] for p in range(3)]
            spot = slice(sub * LANES, (sub + 1) * LANES)
            sums = {}
            for y in range(rows + 1):
                if y < rows:
                    parts = [
                        expanded_ref[pl.ds(base + (y * cols + q), cols), :] for q in (-1, 0, 1)
                    ]
                    parts[0] = clear_ends(parts[0], True, False)
                    parts[2] = clear_ends(parts[2], False, True)
                    for p in range(3):
                        target = y + 1 - p
                        if 0 <= target < rows:
                            for q in range(3):
                                term = taps[p][q] * parts[q]
                                sums[target] = sums[target] + term if target in sums else term
                if y > 0:
                    done = sums.pop(y - 1)
                    rim_ref[here, 2 * cols + y - 1 : 2 * cols + y] = done[:1]
                    rim_ref[here, 2 * cols + rows + y - 1 : 2 * cols + rows + y] = done[-1:]
                    if y in (1, rows):
                        start = 0 if y == 1 else cols
                        rim_ref[here, start : start + cols] = done
                        made = jnp.zeros_like(done)
                    else:
                        made = clear_ends(gelu_of_half(done), True, True)
                    out_ref[(y - 1) * cols : y * cols, spot] = made.astype(jnp.bfloat16)

    def project(index, in_ref, from_ref):
        piece = pl.ds(pl.multiple_of((first + index) * tile, tile), tile)
        total_ref[...] = from_ref[...] + matmul(in_ref[...], w_project_ref[piece, :])

    convolve(0, even_ref)
    project(0, even_ref, start_ref)
    convolve(1, odd_ref)

    def body(index, carry):
        convolve(2 * index, even_ref)
        project(2 * index - 1, odd_ref, total_ref)
        convolve(2 * index + 1, odd_ref)
        project(2 * index, even_ref, total_ref)
        return carry

    lax.fori_loop(1, count // 2, body, 0)
    project(count - 1, odd_ref, total_ref)


def inner(expanded, start, depth_kernel, w_project, rows, cols, first, count, tile):
    tokens, channels = start.shape
    rim = (count * tile // LANES, 2 * cols + 2 * rows, LANES)
    return pl.pallas_call(
        functools.partial(inner_kernel, rows=rows, cols=cols, first=first, count=count),
        in_specs=[vmem()] * 4,
        out_specs=[vmem()] * 2,
        out_shape=[
            jax.ShapeDtypeStruct((tokens, channels), jnp.float32),
            jax.ShapeDtypeStruct(rim, jnp.float32),
        ],
        scratch_shapes=[pltpu.VMEM((tokens, tile), jnp.bfloat16)] * 2,
        compiler_params=pltpu.CompilerParams(vmem_limit_bytes=6 * MIB),
        cost_estimate=pl.CostEstimate(
            flops=2 * 10**9 * count,
            bytes_accessed=tokens * channels * 8 + tokens * count * tile * 4,
            transcendentals=tokens * count * tile,
        ),
        name="inner",
    )(expanded, start, depth_kernel, w_project)


def rim_kernel(
    own_ref, odd_col_ref, inner_ref, *refs, rows, cols, plan, size, pieces,
):
    masks, _, sides = plan
    sent = len(outgoing_shapes(plan, size, 1))
    rim_refs, refs = refs[:pieces], refs[pieces:]
    up_ref, down_ref, one_ref, two_ref, w_expand_ref, depth_ref, w_project_ref, perm_ref = refs[:8]
    mixed_ref, slab_refs = refs[8], refs[9 : 9 + sent]
    halo_ref, active_ref, normed_ref, grouped_ref = refs[9 + sent :]
    tokens = rows * cols
    width = w_expand_ref.shape[1]
    tile = divisor(width, 512, LANES)
    subs = tile // LANES
    slot = one_ref.shape[0]
    left_start, right_start = 2 * cols, 2 * cols + slot

    odd_col = odd_col_ref[0]
    left = choose(odd_col, one_ref[...], two_ref[...])
    right = choose(odd_col, two_ref[...], one_ref[...])
    edges = jnp.concatenate([up_ref[...], down_ref[...], left, right], axis=0)

    def expand_halo(index):
        made = gelu_of_half(matmul(edges, w_expand_ref[:, index * tile : (index + 1) * tile]))
        for sub in range(subs):
            halo_ref[index * subs + sub] = made[:, sub * LANES : (sub + 1) * LANES]

    position = lax.broadcasted_iota(jnp.int32, (cols, LANES), 0)
    at_first = position == 0
    at_last = position == cols - 1

    def activate(chunk, here, sums_ref):
        lanes = slice(chunk * LANES, (chunk + 1) * LANES)
        taps = [[0.5 * depth_ref[p, q : q + 1, lanes] for q in range(3)] for p in range(3)]
        beside = []
        for q, start in ((0, left_start), (2, right_start)):
            beside.append(
                sum(taps[p][q] * halo_ref[chunk, start + p : start + p + rows] for p in range(3))
            )
        made = []
        for p, start, y in ((0, 0, 0), (2, cols, rows - 1)):
            row = halo_ref[chunk, start : start + cols]
            before = jnp.where(at_first, beside[0][y : y + 1], taps[p][0] * pltpu.roll(row, 1, 0))
            after = jnp.where(
                at_last, beside[1][y : y + 1], taps[p][2] * pltpu.roll(row, cols - 1, 0)
            )
            made.append(sums_ref[here, start : start + cols] + before + taps[p][1] * row + after)
        for index in range(2):
            start = 2 * cols + index * rows
            made.append(sums_ref[here, start : start + rows] + beside[index])
        active_ref[:, lanes] = gelu_of_half(jnp.concatenate(made, axis=0)).astype(jnp.bfloat16)

    spots = [(ref, here) for ref in rim_refs for here in range(ref.shape[0])]
    expand_halo(0)
    for index in range(width // tile):
        if (index + 1) * tile < width:
            expand_halo(index + 1)
        for chunk in range(index * subs, (index + 1) * subs):
            activate(chunk, spots[chunk][1], spots[chunk][0])

    mixed_ref[...] = inner_ref[...]
    branch = matmul(active_ref[...], w_project_ref[...])
    mixed_ref[:cols, :] += branch[:cols]
    mixed_ref[tokens - cols :, :] += branch[cols : 2 * cols]
    for y in range(1, rows - 1):
        for index, x in ((0, 0), (1, cols - 1)):
            spot = y * cols + x
            start = 2 * cols + index * rows + y
            mixed_ref[spot : spot + 1, :] += branch[start : start + 1]

    step = divisor(tokens, 128, 16)
    for start in range(0, tokens, step):
        piece = slice(start, start + step)
        normed_ref[piece, :] = layer_norm(mixed_ref[piece, :]).astype(jnp.bfloat16)
    grouped_ref[...] = matmul(perm_ref[...], normed_ref[...]).astype(jnp.bfloat16)
    for index, mask in enumerate(masks):
        for side in range(sides):
            start = pl.multiple_of((own_ref[0] ^ (mask | side)) * size, 16)
            write_block(
                plan, slab_refs, index, side, slice(None), grouped_ref[pl.ds(start, size), :]
            )


def rim(
    own, odd_col, plan, size, total, rims, up, down, one, two, w_expand, depth_kernel, w_project, perm,
    rows, cols,
):
    tokens, channels = total.shape
    width = w_expand.shape[1]
    halo_rows = 2 * cols + 2 * one.shape[0]
    sent = outgoing_shapes(plan, size, channels)
    return pl.pallas_call(
        functools.partial(
            rim_kernel, rows=rows, cols=cols, plan=plan, size=size, pieces=len(rims)
        ),
        in_specs=[pl.BlockSpec(memory_space=pltpu.SMEM)] * 2 + [vmem()] * (9 + len(rims)),
        out_specs=[vmem()] * (1 + len(sent)),
        out_shape=[jax.ShapeDtypeStruct((tokens, channels), jnp.float32)]
        + [jax.ShapeDtypeStruct(shape, jnp.bfloat16) for shape in sent],
        scratch_shapes=[
            pltpu.VMEM((width // LANES, halo_rows, LANES), jnp.float32),
            pltpu.VMEM((2 * cols + 2 * rows, width), jnp.bfloat16),
            pltpu.VMEM((tokens, channels), jnp.bfloat16),
            pltpu.VMEM((tokens, channels), jnp.bfloat16),
        ],
        compiler_params=pltpu.CompilerParams(vmem_limit_bytes=8 * MIB),
        cost_estimate=pl.CostEstimate(
            flops=2 * halo_rows * channels * width * 2 + 2 * tokens * tokens * channels,
            bytes_accessed=tokens * channels * 10 + 4 * channels * width,
            transcendentals=2 * halo_rows * width,
        ),
        name="rim",
    )(own, odd_col, total, *rims, up, down, one, two, w_expand, depth_kernel, w_project, perm)


def identity(size):
    row = lax.broadcasted_iota(jnp.int32, (size, size), 0)
    column = lax.broadcasted_iota(jnp.int32, (size, size), 1)
    return jnp.where(row == column, 1.0, 0.0).astype(jnp.bfloat16)


def attend_kernel(*refs, plan, sets, came):
    masks, _, sides = plan
    slabs = len(masks)
    _, size, channels = refs[0].shape
    in_refs, weight_ref, out_refs = refs[:came], refs[came], refs[came + 1 : -6]
    query_ref, key_ref, value_ref, turned_ref, even_ref, odd_ref = refs[-6:]
    members = size // sets
    count = slabs * sides * members
    head_width = channels // HEADS
    group_heads = LANES // head_width
    groups = channels // LANES
    factor = math.log2(math.e) / math.sqrt(head_width)
    lane = lax.broadcasted_iota(jnp.int32, (1, LANES), 1)
    masks = [
        jnp.where((lane >= j * head_width) & (lane < (j + 1) * head_width), 1.0, 0.0).astype(
            jnp.bfloat16
        )
        for j in range(group_heads)
    ]
    turn_values = identity(channels)
    block = jnp.concatenate(
        [
            read_block(plan, in_refs, index, side, slice(s * members, (s + 1) * members))
            for s in range(sets)
            for index in range(slabs)
            for side in range(sides)
        ],
        axis=0,
    )
    qkv = matmul(block, weight_ref[...]).astype(jnp.bfloat16)
    for s in range(sets):
        own_rows = slice(s * count, (s + 1) * count)
        values = matmul_nt(turn_values, qkv[own_rows, 2 * channels :]).astype(jnp.bfloat16)
        for group in range(groups):
            spot = group * LANES
            query_ref[s * groups + group] = qkv[own_rows, spot : spot + LANES]
            key_ref[s * groups + group] = qkv[own_rows, channels + spot : channels + spot + LANES]
            for j in range(group_heads):
                head = (group * group_heads + j) * head_width
                value_ref[s * groups + group, j, :head_width] = values[head : head + head_width]
                value_ref[s * groups + group, j, head_width:] = jnp.ones((16, count), jnp.bfloat16)

    def scores(index, out):
        keys = key_ref[index]
        stacked = jnp.concatenate([keys * mask for mask in masks], axis=0)
        out[...] = matmul_nt(stacked, query_ref[index])

    def weigh(index, scores_ref):
        for j in range(group_heads):
            part = scores_ref[j * count : (j + 1) * count]
            highest = jnp.max(part, axis=0, keepdims=True)
            raised = jnp.exp2(((part - highest) * factor).astype(jnp.bfloat16))
            product = matmul(value_ref[index, j], raised)
            scale = 1.0 / product[head_width : head_width + 1]
            turned_ref[index, j * head_width : (j + 1) * head_width] = (
                product[:head_width] * scale
            ).astype(jnp.bfloat16)

    total = sets * groups
    scores(0, even_ref)

    def body(pair, carry):
        scores(2 * pair + 1, odd_ref)
        weigh(2 * pair, even_ref)
        scores(jnp.minimum(2 * pair + 2, total - 1), even_ref)
        weigh(2 * pair + 1, odd_ref)
        return carry

    lax.fori_loop(0, total // 2, body, 0)
    turn_tokens = identity(count)
    for s in range(sets):
        turned = turned_ref[s * groups : (s + 1) * groups].reshape(channels, count)
        attended = matmul_nt(turn_tokens, turned).astype(jnp.bfloat16)
        for index in range(slabs):
            for side in range(sides):
                start = (index * sides + side) * members
                write_block(
                    plan, out_refs, index, side, slice(s * members, (s + 1) * members),
                    attended[start : start + members],
                )


def attend(plan, incoming, w_qkv, sets):
    masks, _, sides = plan
    _, size, channels = incoming[0].shape
    count = len(masks) * sides * size // sets
    sent = outgoing_shapes(plan, size, channels)
    head_width = channels // HEADS
    group_heads = LANES // head_width
    total = sets * channels // LANES
    return pl.pallas_call(
        functools.partial(attend_kernel, plan=plan, sets=sets, came=len(incoming)),
        in_specs=[vmem()] * (len(incoming) + 1),
        out_specs=[vmem()] * len(sent),
        out_shape=[jax.ShapeDtypeStruct(shape, jnp.bfloat16) for shape in sent],
        scratch_shapes=[
            pltpu.VMEM((total, count, LANES), jnp.bfloat16),
            pltpu.VMEM((total, count, LANES), jnp.bfloat16),
            pltpu.VMEM((total, group_heads, head_width + 16, count), jnp.bfloat16),
            pltpu.VMEM((total, LANES, count), jnp.bfloat16),
            pltpu.VMEM((group_heads * count, count), jnp.float32),
            pltpu.VMEM((group_heads * count, count), jnp.float32),
        ],
        compiler_params=pltpu.CompilerParams(vmem_limit_bytes=10 * MIB),
        cost_estimate=pl.CostEstimate(
            flops=sets * (2 * count * channels * channels * 3 + 4 * count * count * channels),
            bytes_accessed=4 * sets * count * channels + 6 * channels * channels,
            transcendentals=sets * HEADS * count * count,
        ),
        name="attend",
    )(*incoming, w_qkv)


def finish_kernel(own_ref, *refs, plan):
    masks, _, sides = plan
    in_refs, rest = refs[:-7], refs[-7:]
    back_ref, weight_ref, mixed_ref, out_ref, attended_ref, made_ref, sent = rest
    tokens = mixed_ref.shape[0]
    size = in_refs[0].shape[1]
    for index, mask in enumerate(masks):
        for side in range(sides):
            start = pl.multiple_of((own_ref[0] ^ (mask | side)) * size, 16)
            attended_ref[pl.ds(start, size), :] = read_block(
                plan, in_refs, index, side, slice(None)
            )
    step = made_ref.shape[1]
    copies = []
    for index, start in enumerate(range(0, tokens, step)):
        rows = slice(start, start + step)
        restored = matmul(back_ref[rows, :], attended_ref[...]).astype(jnp.bfloat16)
        made_ref[index] = mixed_ref[rows, :] + matmul(restored, weight_ref[...])
        copy = pltpu.make_async_copy(
            made_ref.at[index], out_ref.at[pl.ds(start, step)], sent.at[index]
        )
        copy.start()
        copies.append(copy)
    for copy in copies:
        copy.wait()


def finish(own, plan, incoming, back, w_out, mixed):
    tokens, channels = mixed.shape
    step = divisor(tokens, 256, 16)
    return pl.pallas_call(
        functools.partial(finish_kernel, plan=plan),
        in_specs=[pl.BlockSpec(memory_space=pltpu.SMEM)] + [vmem()] * (len(incoming) + 3),
        out_specs=pl.BlockSpec(memory_space=pltpu.HBM),
        out_shape=jax.ShapeDtypeStruct((tokens, channels), jnp.float32),
        scratch_shapes=[
            pltpu.VMEM((tokens, channels), jnp.bfloat16),
            pltpu.VMEM((tokens // step, step, channels), jnp.float32),
            pltpu.SemaphoreType.DMA((tokens // step,)),
        ],
        compiler_params=pltpu.CompilerParams(vmem_limit_bytes=6 * MIB),
        name="finish",
    )(own, *incoming, back, w_out, mixed)


def swap_pairs(edge, axis, start):
    pairs = [(i, i + 1) for i in range(start, lax.axis_size(axis) - 1, 2)]
    return lax.ppermute(edge, axis, pairs + [(b, a) for a, b in pairs])


def exchange_plan(row_devices, col_devices):
    devices = row_devices * col_devices
    crossing = list(range(devices - 2, devices // 2 - 1, -2))
    others = list(range(devices // 2 - 2, 0, -2))
    masks = crossing[:-1] + others[:-1] + crossing[-1:] + others[-1:] + [0]
    return masks, 2, 2


def outgoing_shapes(plan, size, channels):
    masks, late, sides = plan
    if sides == 1:
        return [(1, size, channels)]
    early = len(masks) - 1 - late
    return [(2, size, channels)] * late + [
        (1, size, channels), (early + 1, size, channels), (early, size, channels)
    ]


def write_block(plan, refs, index, side, rows, value):
    masks, late, sides = plan
    if sides == 1:
        refs[0][0, rows] = value
    elif index < late:
        refs[index][side, rows] = value
    elif index == len(masks) - 1:
        refs[late + side][0, rows] = value
    elif side == 0:
        refs[late + 2][index - late, rows] = value
    else:
        refs[late + 1][index - late + 1, rows] = value


def read_block(plan, refs, index, side, rows):
    masks, late, sides = plan
    if sides == 1:
        return refs[0][0, rows]
    if index < late:
        return refs[index + side * len(masks)][side, rows]
    if index == len(masks) - 1:
        return refs[index + side * (late + 1)][0, rows]
    return refs[index][side, rows]


def join_kernel(own_ref, swapped_ref, *out_refs):
    for index, out_ref in enumerate(out_refs):
        out_ref[0] = own_ref[index]
        out_ref[1] = swapped_ref[index + 1]


def join(own, swapped):
    early, size, channels = own.shape
    return pl.pallas_call(
        join_kernel,
        in_specs=[vmem()] * 2,
        out_specs=[vmem()] * early,
        out_shape=[jax.ShapeDtypeStruct((2, size, channels), own.dtype)] * early,
        compiler_params=pltpu.CompilerParams(vmem_limit_bytes=2 * MIB),
        name="join",
    )(own, swapped)


def trade(plan, outgoing):
    masks, late, _ = plan
    devices = lax.axis_size("row") * lax.axis_size("col")

    def swap(slab, mask):
        return lax.ppermute(slab, ("row", "col"), [(i, i ^ mask) for i in range(devices)])

    slabs, (kept, passed, own) = outgoing[:late], outgoing[late:]
    swapped = swap(passed, 1)
    first = [swap(slab, mask) for slab, mask in zip(slabs, masks)]
    rest = [swap(slab, mask) for slab, mask in zip(join(own, swapped), masks[late:-1])]
    tied = lax.optimization_barrier((*first, *rest[:-late]))
    first, rest = tied[:late], [*tied[late:], *rest[-late:]]
    return [*first, *rest, kept, *[swap(slab, 1) for slab in first], swapped]


def trade_all(slabs, sets, members, outward):
    axes = ("row", "col")
    channels = slabs[0].shape[-1]
    block = slabs[0].reshape(-1, channels)
    devices = block.shape[0] // (sets * members)
    if not outward:
        block = block.reshape(sets, devices, members, channels).transpose(1, 0, 2, 3)
    block = block.reshape(devices, sets * members, channels)
    block = lax.all_to_all(block, axes, 0, 0, tiled=True)
    if outward:
        block = block.reshape(devices, sets, members, channels).transpose(1, 0, 2, 3)
    return [block.reshape(1, -1, channels)]


def grouping(rows, cols, blocks_rows, blocks_cols):
    order = np.arange(rows * cols).reshape(
        blocks_rows, rows // blocks_rows, blocks_cols, cols // blocks_cols
    )
    order = order.transpose(1, 3, 0, 2).reshape(-1)
    matrix = np.zeros((order.size, order.size), np.float32)
    matrix[np.arange(order.size), order] = 1.0
    return matrix


def shards(field, w_expand, depth_kernel, w_project, w_qkv, w_out):
    rows, cols, channels = field.shape
    tokens = rows * cols
    row_devices = lax.axis_size("row")
    col_devices = lax.axis_size("col")
    devices = row_devices * col_devices
    blocks_rows = GRID // row_devices
    blocks_cols = GRID // col_devices
    members = blocks_rows * blocks_cols
    sets_local = tokens // members // devices
    matrix = grouping(rows, cols, blocks_rows, blocks_cols)
    perm = jnp.asarray(matrix, jnp.bfloat16)
    back = jnp.asarray(matrix.T, jnp.bfloat16)

    flat = field.reshape(tokens, channels)
    pairwise = 8 <= devices <= 16 and devices & (devices - 1) == 0 and col_devices % 2 == 0
    plan = exchange_plan(row_devices, col_devices) if pairwise else ([0], 0, 1)
    row, col = lax.axis_index("row"), lax.axis_index("col")
    own = (row * col_devices + col if pairwise else row * 0).reshape(1)
    odd_row, odd_col = (row % 2).reshape(1), (col % 2).reshape(1)

    own, odd_row, odd_col, top, bottom = lax.optimization_barrier(
        (own, odd_row, odd_col, field[0], field[rows - 1])
    )
    one, two = row_edges(odd_row, top, bottom)
    one, two = swap_pairs(one, "row", 0), swap_pairs(two, "row", 1)
    normed = half_norm_of(flat)
    expanded = expand(normed, w_expand)
    tile = divisor(w_expand.shape[1] // 2, 256, LANES)
    count = w_expand.shape[1] // tile
    early = 2
    total, rim_one = inner(
        expanded, flat, depth_kernel, w_project, rows, cols, 0, early, tile
    )
    one, two, normed, expanded, total, rim_one = lax.optimization_barrier(
        (one, two, normed, expanded, total, rim_one)
    )
    up, down, one, two = column_strips(odd_row, odd_col, normed, one, two, round_up(rows + 2, 16))
    one, two = swap_pairs(one, "col", 0), swap_pairs(two, "col", 1)
    total, rim_two = inner(
        expanded, total, depth_kernel, w_project, rows, cols, early, count - early, tile
    )

    size = tokens // (len(plan[0]) * plan[2])
    mixed, *outgoing = rim(
        own, odd_col, plan, size, total, [rim_one, rim_two], up, down, one, two, w_expand,
        depth_kernel, w_project, perm, rows, cols,
    )

    def route(outgoing, outward):
        if pairwise:
            return trade(plan, outgoing)
        return trade_all(outgoing, sets_local, members, outward)

    outgoing = attend(plan, route(outgoing, True), w_qkv, sets_local)
    final = finish(own, plan, route(outgoing, False), back, w_out, mixed)
    return final.reshape(rows, cols, channels)


def solution(mesh):
    return jax.shard_map(
        shards,
        mesh=mesh,
        in_specs=(P(("field", "row"), "col", None), P(), P(), P(), P(), P()),
        out_specs=P(("field", "row"), "col", None),
        check_vma=False,
    )
```

```python
import functools
import math

import jax
import jax.numpy as jnp
import numpy as np
from jax import lax
from jax.experimental import pallas as pl
from jax.experimental.pallas import tpu as pltpu
from jax.sharding import PartitionSpec as P

HEADS = 16
GRID = 16
LANES = 128
MIB = 1024 * 1024
NT = (((1,), (1,)), ((), ()))


def layer_norm(inputs):
    average = jnp.mean(inputs, axis=-1, keepdims=True)
    centred = inputs - average
    variance = jnp.mean(centred * centred, axis=-1, keepdims=True)
    return centred * lax.rsqrt(variance + 1e-05)


def gelu_of_half(half):
    scale = math.sqrt(2.0 / math.pi)
    inner = half * (2.0 * scale + (8.0 * scale * 0.044715) * (half * half))
    return half + half * jnp.tanh(inner)


def matmul(a, b):
    return jnp.dot(a, b, preferred_element_type=jnp.float32)


def matmul_nt(a, b):
    return lax.dot_general(a, b, NT, preferred_element_type=jnp.float32)


def divisor(size, most, unit):
    best = size
    for piece in range(unit, most + 1, unit):
        if size % piece == 0:
            best = piece
    return best


def round_up(size, unit):
    return -(-size // unit) * unit


def vmem():
    return pl.BlockSpec(memory_space=pltpu.VMEM)


def half_norm(inputs):
    return (layer_norm(inputs) * 0.5).astype(jnp.bfloat16)


def half_norm_kernel(in_ref, out_ref):
    rows = in_ref.shape[0]
    step = divisor(rows, 128, 16)
    for start in range(0, rows, step):
        out_ref[start : start + step, :] = half_norm(in_ref[start : start + step, :])


def half_norm_of(inputs):
    return pl.pallas_call(
        half_norm_kernel,
        in_specs=[vmem()],
        out_specs=vmem(),
        out_shape=jax.ShapeDtypeStruct(inputs.shape, jnp.bfloat16),
        compiler_params=pltpu.CompilerParams(vmem_limit_bytes=4 * MIB),
        cost_estimate=pl.CostEstimate(
            flops=10**9, bytes_accessed=6 * inputs.size, transcendentals=inputs.shape[0]
        ),
        name="half_norm",
    )(inputs)


def choose(condition, one, two):
    flags = jnp.full((one.shape[0], 1), condition, jnp.int32) == 1
    return jnp.where(flags, one.astype(jnp.float32), two.astype(jnp.float32)).astype(one.dtype)


def edges_kernel(odd_row_ref, top_ref, bottom_ref, one_ref, two_ref):
    odd = odd_row_ref[0]
    top, bottom = half_norm(top_ref[...]), half_norm(bottom_ref[...])
    one_ref[...] = choose(odd, top, bottom)
    two_ref[...] = choose(odd, bottom, top)


def row_edges(odd_row, top, bottom):
    return pl.pallas_call(
        edges_kernel,
        in_specs=[pl.BlockSpec(memory_space=pltpu.SMEM)] + [vmem()] * 2,
        out_specs=[vmem()] * 2,
        out_shape=[jax.ShapeDtypeStruct(top.shape, jnp.bfloat16)] * 2,
        compiler_params=pltpu.CompilerParams(vmem_limit_bytes=4 * MIB),
        cost_estimate=pl.CostEstimate(
            flops=10**10, bytes_accessed=12 * top.size, transcendentals=2 * top.shape[0]
        ),
        name="row_edges",
    )(odd_row, top, bottom)


def picker(shape, pick):
    row = lax.broadcasted_iota(jnp.int32, shape, 0)
    column = lax.broadcasted_iota(jnp.int32, shape, 1)
    return jnp.where(pick(row, column), 1.0, 0.0).astype(jnp.bfloat16)


def strips_kernel(
    odd_row_ref, odd_col_ref, normed_ref, row_one_ref, row_two_ref, up_ref, down_ref, one_ref, two_ref
):
    tokens = normed_ref.shape[0]
    cols = up_ref.shape[0]
    rows = tokens // cols
    slot = one_ref.shape[0]
    odd_row, odd_col = odd_row_ref[0], odd_col_ref[0]
    up = choose(odd_row, row_one_ref[...], row_two_ref[...])
    down = choose(odd_row, row_two_ref[...], row_one_ref[...])
    up_ref[...] = up
    down_ref[...] = down
    strips = []
    for x in (0, cols - 1):
        body = picker(
            (slot, tokens), lambda i, j: (i >= 1) & (i <= rows) & (j == (i - 1) * cols + x)
        )
        head = picker((slot, cols), lambda i, j: (i == 0) & (j == x))
        foot = picker((slot, cols), lambda i, j: (i == rows + 1) & (j == x))
        strip = matmul(body, normed_ref[...]) + matmul(head, up) + matmul(foot, down)
        strips.append(strip.astype(jnp.bfloat16))
    one_ref[...] = choose(odd_col, strips[0], strips[1])
    two_ref[...] = choose(odd_col, strips[1], strips[0])


def column_strips(odd_row, odd_col, normed, row_one, row_two, slot):
    cols, channels = row_one.shape
    shapes = [(cols, channels)] * 2 + [(slot, channels)] * 2
    return pl.pallas_call(
        strips_kernel,
        in_specs=[pl.BlockSpec(memory_space=pltpu.SMEM)] * 2 + [vmem()] * 3,
        out_specs=[vmem()] * 4,
        out_shape=[jax.ShapeDtypeStruct(shape, jnp.bfloat16) for shape in shapes],
        compiler_params=pltpu.CompilerParams(vmem_limit_bytes=4 * MIB),
        name="column_strips",
    )(odd_row, odd_col, normed, row_one, row_two)


def padded_rows(tokens):
    return tokens + 16


def expand_kernel(normed_ref, weight_ref, out_ref, even_ref, odd_ref):
    tokens, tile = even_ref.shape
    width = weight_ref.shape[1]
    subs = tile // LANES

    def multiply(index, made_ref):
        lanes = pl.ds(pl.multiple_of(index * tile, tile), tile)
        made_ref[...] = matmul(normed_ref[...], weight_ref[:, lanes])

    def activate(index, made_ref):
        for sub in range(subs):
            row = (index * subs + sub) * padded_rows(tokens) + 8
            out_ref[pl.ds(pl.multiple_of(row, 8), tokens), :] = gelu_of_half(
                made_ref[:, sub * LANES : (sub + 1) * LANES]
            )

    def body(index, carry):
        multiply(2 * index + 1, odd_ref)
        activate(2 * index, even_ref)
        multiply(2 * index + 2, even_ref)
        activate(2 * index + 1, odd_ref)
        return carry

    count = width // tile
    multiply(0, even_ref)
    lax.fori_loop(0, count // 2 - 1, body, 0)
    multiply(count - 1, odd_ref)
    activate(count - 2, even_ref)
    activate(count - 1, odd_ref)


def expand(normed, w_expand):
    tokens, channels = normed.shape
    width = w_expand.shape[1]
    return pl.pallas_call(
        expand_kernel,
        in_specs=[vmem()] * 2,
        out_specs=vmem(),
        out_shape=jax.ShapeDtypeStruct((width // LANES * padded_rows(tokens), LANES), jnp.float32),
        scratch_shapes=[
            pltpu.VMEM((tokens, divisor(width // 2, 256, LANES)), jnp.float32)
        ] * 2,
        compiler_params=pltpu.CompilerParams(vmem_limit_bytes=6 * MIB),
        cost_estimate=pl.CostEstimate(
            flops=10**10,
            bytes_accessed=tokens * channels * 2 + channels * width * 2 + tokens * width * 4,
            transcendentals=tokens * width,
        ),
        name="expand",
    )(normed, w_expand)


def inner_kernel(
    expanded_ref, start_ref, depth_ref, w_project_ref, total_ref, rim_ref, even_ref, odd_ref,
    *, rows, cols, first, count,
):
    tokens = rows * cols
    tile = even_ref.shape[1]
    subs = tile // LANES
    position = lax.broadcasted_iota(jnp.int32, (8, LANES), 0)
    at_first = position == 0
    at_last = position == 7

    def clear_ends(value, low, high):
        head = jnp.where(at_first, 0.0, value[:8]) if low else value[:8]
        foot = jnp.where(at_last, 0.0, value[-8:]) if high else value[-8:]
        return jnp.concatenate([head, value[8:-8], foot], axis=0)

    def convolve(index, out_ref):
        for sub in range(subs):
            chunk = (first + index) * subs + sub
            lanes = pl.ds(pl.multiple_of(chunk * LANES, LANES), LANES)
            base = chunk * padded_rows(tokens) + 8
            here = index * subs + sub
            taps = [[0.5 * depth_ref[p, q : q + 1, lanes] for q in range(3)] for p in range(3)]
            spot = slice(sub * LANES, (sub + 1) * LANES)
            sums = {}
            for y in range(rows + 1):
                if y < rows:
                    parts = [
                        expanded_ref[pl.ds(base + (y * cols + q), cols), :] for q in (-1, 0, 1)
                    ]
                    parts[0] = clear_ends(parts[0], True, False)
                    parts[2] = clear_ends(parts[2], False, True)
                    for p in range(3):
                        target = y + 1 - p
                        if 0 <= target < rows:
                            for q in range(3):
                                term = taps[p][q] * parts[q]
                                sums[target] = sums[target] + term if target in sums else term
                if y > 0:
                    done = sums.pop(y - 1)
                    rim_ref[here, 2 * cols + y - 1 : 2 * cols + y] = done[:1]
                    rim_ref[here, 2 * cols + rows + y - 1 : 2 * cols + rows + y] = done[-1:]
                    if y in (1, rows):
                        start = 0 if y == 1 else cols
                        rim_ref[here, start : start + cols] = done
                        made = jnp.zeros_like(done)
                    else:
                        made = clear_ends(gelu_of_half(done), True, True)
                    out_ref[(y - 1) * cols : y * cols, spot] = made.astype(jnp.bfloat16)

    def project(index, in_ref, from_ref):
        piece = pl.ds(pl.multiple_of((first + index) * tile, tile), tile)
        total_ref[...] = from_ref[...] + matmul(in_ref[...], w_project_ref[piece, :])

    convolve(0, even_ref)
    project(0, even_ref, start_ref)
    convolve(1, odd_ref)

    def body(index, carry):
        convolve(2 * index, even_ref)
        project(2 * index - 1, odd_ref, total_ref)
        convolve(2 * index + 1, odd_ref)
        project(2 * index, even_ref, total_ref)
        return carry

    lax.fori_loop(1, count // 2, body, 0)
    project(count - 1, odd_ref, total_ref)


def inner(expanded, start, depth_kernel, w_project, rows, cols, first, count, tile):
    tokens, channels = start.shape
    rim = (count * tile // LANES, 2 * cols + 2 * rows, LANES)
    return pl.pallas_call(
        functools.partial(inner_kernel, rows=rows, cols=cols, first=first, count=count),
        in_specs=[vmem()] * 4,
        out_specs=[vmem()] * 2,
        out_shape=[
            jax.ShapeDtypeStruct((tokens, channels), jnp.float32),
            jax.ShapeDtypeStruct(rim, jnp.float32),
        ],
        scratch_shapes=[pltpu.VMEM((tokens, tile), jnp.bfloat16)] * 2,
        compiler_params=pltpu.CompilerParams(vmem_limit_bytes=6 * MIB),
        cost_estimate=pl.CostEstimate(
            flops=2 * 10**9 * count,
            bytes_accessed=tokens * channels * 8 + tokens * count * tile * 4,
            transcendentals=tokens * count * tile,
        ),
        name="inner",
    )(expanded, start, depth_kernel, w_project)


def rim_kernel(
    own_ref, odd_col_ref, inner_ref, *refs, rows, cols, plan, size, pieces,
):
    masks, _, sides = plan
    sent = len(outgoing_shapes(plan, size, 1))
    rim_refs, refs = refs[:pieces], refs[pieces:]
    up_ref, down_ref, one_ref, two_ref, w_expand_ref, depth_ref, w_project_ref, perm_ref = refs[:8]
    mixed_ref, slab_refs = refs[8], refs[9 : 9 + sent]
    halo_ref, active_ref, normed_ref, grouped_ref = refs[9 + sent :]
    tokens = rows * cols
    width = w_expand_ref.shape[1]
    tile = divisor(width, 512, LANES)
    subs = tile // LANES
    slot = one_ref.shape[0]
    left_start, right_start = 2 * cols, 2 * cols + slot

    odd_col = odd_col_ref[0]
    left = choose(odd_col, one_ref[...], two_ref[...])
    right = choose(odd_col, two_ref[...], one_ref[...])
    edges = jnp.concatenate([up_ref[...], down_ref[...], left, right], axis=0)

    def expand_halo(index):
        made = gelu_of_half(matmul(edges, w_expand_ref[:, index * tile : (index + 1) * tile]))
        for sub in range(subs):
            halo_ref[index * subs + sub] = made[:, sub * LANES : (sub + 1) * LANES]

    position = lax.broadcasted_iota(jnp.int32, (cols, LANES), 0)
    at_first = position == 0
    at_last = position == cols - 1

    def activate(chunk, here, sums_ref):
        lanes = slice(chunk * LANES, (chunk + 1) * LANES)
        taps = [[0.5 * depth_ref[p, q : q + 1, lanes] for q in range(3)] for p in range(3)]
        beside = []
        for q, start in ((0, left_start), (2, right_start)):
            beside.append(
                sum(taps[p][q] * halo_ref[chunk, start + p : start + p + rows] for p in range(3))
            )
        made = []
        for p, start, y in ((0, 0, 0), (2, cols, rows - 1)):
            row = halo_ref[chunk, start : start + cols]
            before = jnp.where(at_first, beside[0][y : y + 1], taps[p][0] * pltpu.roll(row, 1, 0))
            after = jnp.where(
                at_last, beside[1][y : y + 1], taps[p][2] * pltpu.roll(row, cols - 1, 0)
            )
            made.append(sums_ref[here, start : start + cols] + before + taps[p][1] * row + after)
        for index in range(2):
            start = 2 * cols + index * rows
            made.append(sums_ref[here, start : start + rows] + beside[index])
        active_ref[:, lanes] = gelu_of_half(jnp.concatenate(made, axis=0)).astype(jnp.bfloat16)

    spots = [(ref, here) for ref in rim_refs for here in range(ref.shape[0])]
    expand_halo(0)
    for index in range(width // tile):
        if (index + 1) * tile < width:
            expand_halo(index + 1)
        for chunk in range(index * subs, (index + 1) * subs):
            activate(chunk, spots[chunk][1], spots[chunk][0])

    mixed_ref[...] = inner_ref[...]
    branch = matmul(active_ref[...], w_project_ref[...])
    mixed_ref[:cols, :] += branch[:cols]
    mixed_ref[tokens - cols :, :] += branch[cols : 2 * cols]
    for y in range(1, rows - 1):
        for index, x in ((0, 0), (1, cols - 1)):
            spot = y * cols + x
            start = 2 * cols + index * rows + y
            mixed_ref[spot : spot + 1, :] += branch[start : start + 1]

    step = divisor(tokens, 128, 16)
    for start in range(0, tokens, step):
        piece = slice(start, start + step)
        normed_ref[piece, :] = layer_norm(mixed_ref[piece, :]).astype(jnp.bfloat16)
    grouped_ref[...] = matmul(perm_ref[...], normed_ref[...]).astype(jnp.bfloat16)
    for index, mask in enumerate(masks):
        for side in range(sides):
            start = pl.multiple_of((own_ref[0] ^ (mask | side)) * size, 16)
            write_block(
                plan, slab_refs, index, side, slice(None), grouped_ref[pl.ds(start, size), :]
            )


def rim(
    own, odd_col, plan, size, total, rims, up, down, one, two, w_expand, depth_kernel, w_project, perm,
    rows, cols,
):
    tokens, channels = total.shape
    width = w_expand.shape[1]
    halo_rows = 2 * cols + 2 * one.shape[0]
    sent = outgoing_shapes(plan, size, channels)
    return pl.pallas_call(
        functools.partial(
            rim_kernel, rows=rows, cols=cols, plan=plan, size=size, pieces=len(rims)
        ),
        in_specs=[pl.BlockSpec(memory_space=pltpu.SMEM)] * 2 + [vmem()] * (9 + len(rims)),
        out_specs=[vmem()] * (1 + len(sent)),
        out_shape=[jax.ShapeDtypeStruct((tokens, channels), jnp.float32)]
        + [jax.ShapeDtypeStruct(shape, jnp.bfloat16) for shape in sent],
        scratch_shapes=[
            pltpu.VMEM((width // LANES, halo_rows, LANES), jnp.float32),
            pltpu.VMEM((2 * cols + 2 * rows, width), jnp.bfloat16),
            pltpu.VMEM((tokens, channels), jnp.bfloat16),
            pltpu.VMEM((tokens, channels), jnp.bfloat16),
        ],
        compiler_params=pltpu.CompilerParams(vmem_limit_bytes=8 * MIB),
        cost_estimate=pl.CostEstimate(
            flops=2 * halo_rows * channels * width * 2 + 2 * tokens * tokens * channels,
            bytes_accessed=tokens * channels * 10 + 4 * channels * width,
            transcendentals=2 * halo_rows * width,
        ),
        name="rim",
    )(own, odd_col, total, *rims, up, down, one, two, w_expand, depth_kernel, w_project, perm)


def identity(size):
    row = lax.broadcasted_iota(jnp.int32, (size, size), 0)
    column = lax.broadcasted_iota(jnp.int32, (size, size), 1)
    return jnp.where(row == column, 1.0, 0.0).astype(jnp.bfloat16)


def gather_blocks(plan, refs, blocks, sets):
    members = refs[0].shape[1] // sets
    return jnp.concatenate(
        [
            read_block(plan, refs, index, side, slice(s * members, (s + 1) * members))
            for s in range(sets)
            for index, side in blocks
        ],
        axis=0,
    )


def project_kernel(*refs, plan, sets):
    in_refs, weight_ref, out_ref = refs[:-2], refs[-2], refs[-1]
    block = gather_blocks(plan, in_refs, split_blocks(plan)[0], sets)
    out_ref[...] = matmul(block, weight_ref[...]).astype(jnp.bfloat16)


def project(plan, incoming, w_qkv, sets):
    soon = split_blocks(plan)[0]
    _, size, channels = incoming[0].shape
    masks, late, _ = plan
    there = [*range(late, len(masks) - 1 - late), len(masks) - 1, len(masks) + late]
    filled = [array if index in there else incoming[late] for index, array in enumerate(incoming)]
    return pl.pallas_call(
        functools.partial(project_kernel, plan=plan, sets=sets),
        in_specs=[vmem()] * (len(filled) + 1),
        out_specs=vmem(),
        out_shape=jax.ShapeDtypeStruct((len(soon) * size, w_qkv.shape[1]), jnp.bfloat16),
        compiler_params=pltpu.CompilerParams(vmem_limit_bytes=4 * MIB),
        cost_estimate=pl.CostEstimate(
            flops=2 * len(soon) * size * channels * w_qkv.shape[1],
            bytes_accessed=2 * w_qkv.size + 8 * len(soon) * size * channels,
            transcendentals=0,
        ),
        name="project",
    )(*filled, w_qkv)


def attend_kernel(*refs, plan, sets, came):
    masks, _, sides = plan
    slabs = len(masks)
    _, size, channels = refs[0].shape
    soon, rest = split_blocks(plan)
    in_refs, weight_ref, out_refs = refs[:came], refs[came], refs[came + 1 : -6]
    if soon:
        soon_ref, out_refs = out_refs[0], out_refs[1:]
    query_ref, key_ref, value_ref, turned_ref, even_ref, odd_ref = refs[-6:]
    members = size // sets
    count = slabs * sides * members
    head_width = channels // HEADS
    group_heads = LANES // head_width
    groups = channels // LANES
    factor = math.log2(math.e) / math.sqrt(head_width)
    lane = lax.broadcasted_iota(jnp.int32, (1, LANES), 1)
    masks = [
        jnp.where((lane >= j * head_width) & (lane < (j + 1) * head_width), 1.0, 0.0).astype(
            jnp.bfloat16
        )
        for j in range(group_heads)
    ]
    turn_values = identity(channels)
    block = gather_blocks(plan, in_refs, rest, sets)
    projected = matmul(block, weight_ref[...]).astype(jnp.bfloat16)
    for s in range(sets):
        near, far = len(soon) * members, len(rest) * members
        qkv = projected[s * far : (s + 1) * far]
        if soon:
            qkv = jnp.concatenate([soon_ref[s * near : (s + 1) * near, :], qkv], axis=0)
        values = matmul_nt(turn_values, qkv[:, 2 * channels :]).astype(jnp.bfloat16)
        for group in range(groups):
            spot = group * LANES
            query_ref[s * groups + group] = qkv[:, spot : spot + LANES]
            key_ref[s * groups + group] = qkv[:, channels + spot : channels + spot + LANES]
            for j in range(group_heads):
                head = (group * group_heads + j) * head_width
                value_ref[s * groups + group, j, :head_width] = values[head : head + head_width]
                value_ref[s * groups + group, j, head_width:] = jnp.ones((16, count), jnp.bfloat16)

    def scores(index, out):
        keys = key_ref[index]
        stacked = jnp.concatenate([keys * mask for mask in masks], axis=0)
        out[...] = matmul_nt(stacked, query_ref[index])

    def weigh(index, scores_ref):
        for j in range(group_heads):
            part = scores_ref[j * count : (j + 1) * count]
            highest = jnp.max(part, axis=0, keepdims=True)
            raised = jnp.exp2((part - highest) * factor).astype(jnp.bfloat16)
            product = matmul(value_ref[index, j], raised)
            scale = 1.0 / product[head_width : head_width + 1]
            turned_ref[index, j * head_width : (j + 1) * head_width] = (
                product[:head_width] * scale
            ).astype(jnp.bfloat16)

    total = sets * groups
    scores(0, even_ref)

    def body(pair, carry):
        scores(2 * pair + 1, odd_ref)
        weigh(2 * pair, even_ref)
        scores(jnp.minimum(2 * pair + 2, total - 1), even_ref)
        weigh(2 * pair + 1, odd_ref)
        return carry

    lax.fori_loop(0, total // 2, body, 0)
    turn_tokens = identity(count)
    for s in range(sets):
        turned = turned_ref[s * groups : (s + 1) * groups].reshape(channels, count)
        attended = matmul_nt(turn_tokens, turned).astype(jnp.bfloat16)
        for number, (index, side) in enumerate(soon + rest):
            write_block(
                plan, out_refs, index, side, slice(s * members, (s + 1) * members),
                attended[number * members : (number + 1) * members],
            )


def attend(plan, incoming, w_qkv, sets):
    masks, _, sides = plan
    _, size, channels = incoming[0].shape
    count = len(masks) * sides * size // sets
    sent = outgoing_shapes(plan, size, channels)
    soon = [project(plan, incoming, w_qkv, sets)] if split_blocks(plan)[0] else []
    head_width = channels // HEADS
    group_heads = LANES // head_width
    total = sets * channels // LANES
    return pl.pallas_call(
        functools.partial(attend_kernel, plan=plan, sets=sets, came=len(incoming)),
        in_specs=[vmem()] * (len(incoming) + 1 + len(soon)),
        out_specs=[vmem()] * len(sent),
        out_shape=[jax.ShapeDtypeStruct(shape, jnp.bfloat16) for shape in sent],
        scratch_shapes=[
            pltpu.VMEM((total, count, LANES), jnp.bfloat16),
            pltpu.VMEM((total, count, LANES), jnp.bfloat16),
            pltpu.VMEM((total, group_heads, head_width + 16, count), jnp.bfloat16),
            pltpu.VMEM((total, LANES, count), jnp.bfloat16),
            pltpu.VMEM((group_heads * count, count), jnp.float32),
            pltpu.VMEM((group_heads * count, count), jnp.float32),
        ],
        compiler_params=pltpu.CompilerParams(vmem_limit_bytes=10 * MIB),
        cost_estimate=pl.CostEstimate(
            flops=sets * (2 * count * channels * channels * 3 + 4 * count * count * channels),
            bytes_accessed=4 * sets * count * channels + 6 * channels * channels,
            transcendentals=sets * HEADS * count * count,
        ),
        name="attend",
    )(*incoming, w_qkv, *soon)


def finish_kernel(own_ref, *refs, plan):
    masks, _, sides = plan
    in_refs, rest = refs[:-7], refs[-7:]
    back_ref, weight_ref, mixed_ref, out_ref, attended_ref, made_ref, sent = rest
    tokens = mixed_ref.shape[0]
    size = in_refs[0].shape[1]
    for index, mask in enumerate(masks):
        for side in range(sides):
            start = pl.multiple_of((own_ref[0] ^ (mask | side)) * size, 16)
            attended_ref[pl.ds(start, size), :] = read_block(
                plan, in_refs, index, side, slice(None)
            )
    step = made_ref.shape[1]
    copies = []
    for index, start in enumerate(range(0, tokens, step)):
        rows = slice(start, start + step)
        restored = matmul(back_ref[rows, :], attended_ref[...]).astype(jnp.bfloat16)
        made_ref[index] = mixed_ref[rows, :] + matmul(restored, weight_ref[...])
        copy = pltpu.make_async_copy(
            made_ref.at[index], out_ref.at[pl.ds(start, step)], sent.at[index]
        )
        copy.start()
        copies.append(copy)
    for copy in copies:
        copy.wait()


def finish(own, plan, incoming, back, w_out, mixed):
    tokens, channels = mixed.shape
    step = divisor(tokens, 256, 16)
    return pl.pallas_call(
        functools.partial(finish_kernel, plan=plan),
        in_specs=[pl.BlockSpec(memory_space=pltpu.SMEM)] + [vmem()] * (len(incoming) + 3),
        out_specs=pl.BlockSpec(memory_space=pltpu.HBM),
        out_shape=jax.ShapeDtypeStruct((tokens, channels), jnp.float32),
        scratch_shapes=[
            pltpu.VMEM((tokens, channels), jnp.bfloat16),
            pltpu.VMEM((tokens // step, step, channels), jnp.float32),
            pltpu.SemaphoreType.DMA((tokens // step,)),
        ],
        compiler_params=pltpu.CompilerParams(vmem_limit_bytes=6 * MIB),
        name="finish",
    )(own, *incoming, back, w_out, mixed)


def swap_pairs(edge, axis, start):
    pairs = [(i, i + 1) for i in range(start, lax.axis_size(axis) - 1, 2)]
    return lax.ppermute(edge, axis, pairs + [(b, a) for a, b in pairs])


def exchange_plan(row_devices, col_devices):
    devices = row_devices * col_devices
    crossing = list(range(devices - 2, devices // 2 - 1, -2))
    others = list(range(devices // 2 - 2, 0, -2))
    masks = crossing[:-1] + others[:-1] + crossing[-1:] + others[-1:] + [0]
    return masks, 2, 2


def split_blocks(plan):
    masks, late, sides = plan
    blocks = [(index, side) for index in range(len(masks)) for side in range(sides)]
    if sides == 1:
        return [], blocks
    soon = [*range(late, len(masks) - 1 - late), len(masks) - 1]
    return [b for b in blocks if b[0] in soon], [b for b in blocks if b[0] not in soon]


def outgoing_shapes(plan, size, channels):
    masks, late, sides = plan
    if sides == 1:
        return [(1, size, channels)]
    early = len(masks) - 1 - late
    return [(2, size, channels)] * late + [
        (1, size, channels), (early + 1, size, channels), (early, size, channels)
    ]


def write_block(plan, refs, index, side, rows, value):
    masks, late, sides = plan
    if sides == 1:
        refs[0][0, rows] = value
    elif index < late:
        refs[index][side, rows] = value
    elif index == len(masks) - 1:
        refs[late + side][0, rows] = value
    elif side == 0:
        refs[late + 2][index - late, rows] = value
    else:
        refs[late + 1][index - late + 1, rows] = value


def read_block(plan, refs, index, side, rows):
    masks, late, sides = plan
    if sides == 1:
        return refs[0][0, rows]
    if index < late:
        return refs[index + side * len(masks)][side, rows]
    if index == len(masks) - 1:
        return refs[index + side * (late + 1)][0, rows]
    return refs[index][side, rows]


def join_kernel(own_ref, swapped_ref, *out_refs):
    for index, out_ref in enumerate(out_refs):
        out_ref[0] = own_ref[index]
        out_ref[1] = swapped_ref[index + 1]


def join(own, swapped):
    early, size, channels = own.shape
    return pl.pallas_call(
        join_kernel,
        in_specs=[vmem()] * 2,
        out_specs=[vmem()] * early,
        out_shape=[jax.ShapeDtypeStruct((2, size, channels), own.dtype)] * early,
        compiler_params=pltpu.CompilerParams(vmem_limit_bytes=2 * MIB),
        name="join",
    )(own, swapped)


def trade(plan, outgoing):
    masks, late, _ = plan
    devices = lax.axis_size("row") * lax.axis_size("col")

    def swap(slab, mask):
        return lax.ppermute(slab, ("row", "col"), [(i, i ^ mask) for i in range(devices)])

    slabs, (kept, passed, own) = outgoing[:late], outgoing[late:]
    swapped = swap(passed, 1)
    first = [swap(slab, mask) for slab, mask in zip(slabs, masks)]
    rest = [swap(slab, mask) for slab, mask in zip(join(own, swapped), masks[late:-1])]
    tied = lax.optimization_barrier((*first, *rest[:-late]))
    first, rest = tied[:late], [*tied[late:], *rest[-late:]]
    return [*first, *rest, kept, *[swap(slab, 1) for slab in first], swapped]


def trade_all(slabs, sets, members, outward):
    axes = ("row", "col")
    channels = slabs[0].shape[-1]
    block = slabs[0].reshape(-1, channels)
    devices = block.shape[0] // (sets * members)
    if not outward:
        block = block.reshape(sets, devices, members, channels).transpose(1, 0, 2, 3)
    block = block.reshape(devices, sets * members, channels)
    block = lax.all_to_all(block, axes, 0, 0, tiled=True)
    if outward:
        block = block.reshape(devices, sets, members, channels).transpose(1, 0, 2, 3)
    return [block.reshape(1, -1, channels)]


def grouping(rows, cols, blocks_rows, blocks_cols):
    order = np.arange(rows * cols).reshape(
        blocks_rows, rows // blocks_rows, blocks_cols, cols // blocks_cols
    )
    order = order.transpose(1, 3, 0, 2).reshape(-1)
    matrix = np.zeros((order.size, order.size), np.float32)
    matrix[np.arange(order.size), order] = 1.0
    return matrix


def shards(field, w_expand, depth_kernel, w_project, w_qkv, w_out):
    rows, cols, channels = field.shape
    tokens = rows * cols
    row_devices = lax.axis_size("row")
    col_devices = lax.axis_size("col")
    devices = row_devices * col_devices
    blocks_rows = GRID // row_devices
    blocks_cols = GRID // col_devices
    members = blocks_rows * blocks_cols
    sets_local = tokens // members // devices
    matrix = grouping(rows, cols, blocks_rows, blocks_cols)
    perm = jnp.asarray(matrix, jnp.bfloat16)
    back = jnp.asarray(matrix.T, jnp.bfloat16)

    flat = field.reshape(tokens, channels)
    pairwise = 8 <= devices <= 16 and devices & (devices - 1) == 0 and col_devices % 2 == 0
    plan = exchange_plan(row_devices, col_devices) if pairwise else ([0], 0, 1)
    row, col = lax.axis_index("row"), lax.axis_index("col")
    own = (row * col_devices + col if pairwise else row * 0).reshape(1)
    odd_row, odd_col = (row % 2).reshape(1), (col % 2).reshape(1)

    own, odd_row, odd_col, top, bottom = lax.optimization_barrier(
        (own, odd_row, odd_col, field[0], field[rows - 1])
    )
    one, two = row_edges(odd_row, top, bottom)
    one, two = swap_pairs(one, "row", 0), swap_pairs(two, "row", 1)
    normed = half_norm_of(flat)
    expanded = expand(normed, w_expand)
    tile = divisor(w_expand.shape[1] // 2, 256, LANES)
    count = w_expand.shape[1] // tile
    early = 2
    total, rim_one = inner(
        expanded, flat, depth_kernel, w_project, rows, cols, 0, early, tile
    )
    one, two, normed, expanded, total, rim_one = lax.optimization_barrier(
        (one, two, normed, expanded, total, rim_one)
    )
    up, down, one, two = column_strips(odd_row, odd_col, normed, one, two, round_up(rows + 2, 16))
    one, two = swap_pairs(one, "col", 0), swap_pairs(two, "col", 1)
    total, rim_two = inner(
        expanded, total, depth_kernel, w_project, rows, cols, early, count - early, tile
    )

    size = tokens // (len(plan[0]) * plan[2])
    mixed, *outgoing = rim(
        own, odd_col, plan, size, total, [rim_one, rim_two], up, down, one, two, w_expand,
        depth_kernel, w_project, perm, rows, cols,
    )

    def route(outgoing, outward):
        if pairwise:
            return trade(plan, outgoing)
        return trade_all(outgoing, sets_local, members, outward)

    outgoing = attend(plan, route(outgoing, True), w_qkv, sets_local)
    final = finish(own, plan, route(outgoing, False), back, w_out, mixed)
    return final.reshape(rows, cols, channels)


def solution(mesh):
    return jax.shard_map(
        shards,
        mesh=mesh,
        in_specs=(P(("field", "row"), "col", None), P(), P(), P(), P(), P()),
        out_specs=P(("field", "row"), "col", None),
        check_vma=False,
    )
```

```python
import functools
import math

import jax
import jax.numpy as jnp
import numpy as np
from jax import lax
from jax.experimental import pallas as pl
from jax.experimental.pallas import tpu as pltpu
from jax.sharding import PartitionSpec as P

HEADS = 16
GRID = 16
LANES = 128
MIB = 1024 * 1024
NT = (((1,), (1,)), ((), ()))


def layer_norm(inputs):
    average = jnp.mean(inputs, axis=-1, keepdims=True)
    centred = inputs - average
    variance = jnp.mean(centred * centred, axis=-1, keepdims=True)
    return centred * lax.rsqrt(variance + 1e-05)


def gelu_of_half(half):
    scale = math.sqrt(2.0 / math.pi)
    inner = half * (2.0 * scale + (8.0 * scale * 0.044715) * (half * half))
    return half + half * jnp.tanh(inner)


def matmul(a, b):
    return jnp.dot(a, b, preferred_element_type=jnp.float32)


def matmul_nt(a, b):
    return lax.dot_general(a, b, NT, preferred_element_type=jnp.float32)


def divisor(size, most, unit):
    best = size
    for piece in range(unit, most + 1, unit):
        if size % piece == 0:
            best = piece
    return best


def round_up(size, unit):
    return -(-size // unit) * unit


def vmem():
    return pl.BlockSpec(memory_space=pltpu.VMEM)


def half_norm(inputs):
    return (layer_norm(inputs) * 0.5).astype(jnp.bfloat16)


def half_norm_kernel(in_ref, out_ref):
    rows = in_ref.shape[0]
    step = divisor(rows, 128, 16)
    for start in range(0, rows, step):
        out_ref[start : start + step, :] = half_norm(in_ref[start : start + step, :])


def half_norm_of(inputs):
    return pl.pallas_call(
        half_norm_kernel,
        in_specs=[vmem()],
        out_specs=vmem(),
        out_shape=jax.ShapeDtypeStruct(inputs.shape, jnp.bfloat16),
        compiler_params=pltpu.CompilerParams(vmem_limit_bytes=4 * MIB),
        cost_estimate=pl.CostEstimate(
            flops=10**9, bytes_accessed=6 * inputs.size, transcendentals=inputs.shape[0]
        ),
        name="half_norm",
    )(inputs)


def choose(condition, one, two):
    flags = jnp.full((one.shape[0], 1), condition, jnp.int32) == 1
    return jnp.where(flags, one.astype(jnp.float32), two.astype(jnp.float32)).astype(one.dtype)


def edges_kernel(odd_row_ref, top_ref, bottom_ref, one_ref, two_ref):
    odd = odd_row_ref[0]
    top, bottom = half_norm(top_ref[...]), half_norm(bottom_ref[...])
    one_ref[...] = choose(odd, top, bottom)
    two_ref[...] = choose(odd, bottom, top)


def row_edges(odd_row, top, bottom):
    return pl.pallas_call(
        edges_kernel,
        in_specs=[pl.BlockSpec(memory_space=pltpu.SMEM)] + [vmem()] * 2,
        out_specs=[vmem()] * 2,
        out_shape=[jax.ShapeDtypeStruct(top.shape, jnp.bfloat16)] * 2,
        compiler_params=pltpu.CompilerParams(vmem_limit_bytes=4 * MIB),
        cost_estimate=pl.CostEstimate(
            flops=10**10, bytes_accessed=12 * top.size, transcendentals=2 * top.shape[0]
        ),
        name="row_edges",
    )(odd_row, top, bottom)


def picker(shape, pick):
    row = lax.broadcasted_iota(jnp.int32, shape, 0)
    column = lax.broadcasted_iota(jnp.int32, shape, 1)
    return jnp.where(pick(row, column), 1.0, 0.0).astype(jnp.bfloat16)


def strips_kernel(
    odd_row_ref, odd_col_ref, normed_ref, row_one_ref, row_two_ref, up_ref, down_ref, one_ref, two_ref
):
    tokens = normed_ref.shape[0]
    cols = up_ref.shape[0]
    rows = tokens // cols
    slot = one_ref.shape[0]
    odd_row, odd_col = odd_row_ref[0], odd_col_ref[0]
    up = choose(odd_row, row_one_ref[...], row_two_ref[...])
    down = choose(odd_row, row_two_ref[...], row_one_ref[...])
    up_ref[...] = up
    down_ref[...] = down
    strips = []
    for x in (0, cols - 1):
        body = picker(
            (slot, tokens), lambda i, j: (i >= 1) & (i <= rows) & (j == (i - 1) * cols + x)
        )
        head = picker((slot, cols), lambda i, j: (i == 0) & (j == x))
        foot = picker((slot, cols), lambda i, j: (i == rows + 1) & (j == x))
        strip = matmul(body, normed_ref[...]) + matmul(head, up) + matmul(foot, down)
        strips.append(strip.astype(jnp.bfloat16))
    one_ref[...] = choose(odd_col, strips[0], strips[1])
    two_ref[...] = choose(odd_col, strips[1], strips[0])


def column_strips(odd_row, odd_col, normed, row_one, row_two, slot):
    cols, channels = row_one.shape
    shapes = [(cols, channels)] * 2 + [(slot, channels)] * 2
    return pl.pallas_call(
        strips_kernel,
        in_specs=[pl.BlockSpec(memory_space=pltpu.SMEM)] * 2 + [vmem()] * 3,
        out_specs=[vmem()] * 4,
        out_shape=[jax.ShapeDtypeStruct(shape, jnp.bfloat16) for shape in shapes],
        compiler_params=pltpu.CompilerParams(vmem_limit_bytes=4 * MIB),
        name="column_strips",
    )(odd_row, odd_col, normed, row_one, row_two)


def padded_rows(tokens):
    return tokens + 16


def inner_kernel(
    odd_col_ref, normed_ref, start_ref, w_expand_ref, depth_ref, w_project_ref, total_ref, rim_ref,
    even_ref, odd_ref, even_grown_ref, odd_grown_ref, *, rows, cols, first, count,
):
    tokens = rows * cols
    tile = even_ref.shape[1]
    origin = jnp.minimum(odd_col_ref[0], 0)
    active_refs = even_ref, odd_ref
    grown_refs = even_grown_ref, odd_grown_ref
    subs = tile // LANES
    position = lax.broadcasted_iota(jnp.int32, (8, LANES), 0)
    at_first = position == 0
    at_last = position == 7

    def clear_ends(value, low, high):
        head = jnp.where(at_first, 0.0, value[:8]) if low else value[:8]
        foot = jnp.where(at_last, 0.0, value[-8:]) if high else value[-8:]
        return jnp.concatenate([head, value[8:-8], foot], axis=0)

    def grow(index):
        lanes = slice((first + index) * tile, (first + index + 1) * tile)
        made = gelu_of_half(matmul(normed_ref[...], w_expand_ref[:, lanes]))
        for sub in range(subs):
            start = sub * padded_rows(tokens) + 8
            grown_refs[index % 2][start : start + tokens, :] = made[
                :, sub * LANES : (sub + 1) * LANES
            ]

    def convolve(index):
        out_ref, grown_ref = active_refs[index % 2], grown_refs[index % 2]
        for sub in range(subs):
            chunk = (first + index) * subs + sub
            lanes = slice(chunk * LANES, (chunk + 1) * LANES)
            base = origin + sub * padded_rows(tokens) + 8
            here = index * subs + sub
            taps = [[0.5 * depth_ref[p, q : q + 1, lanes] for q in range(3)] for p in range(3)]
            spot = slice(sub * LANES, (sub + 1) * LANES)
            sums = {}
            for y in range(rows + 1):
                if y < rows:
                    parts = [
                        grown_ref[pl.ds(base + (y * cols + q), cols), :] for q in (-1, 0, 1)
                    ]
                    parts[0] = clear_ends(parts[0], True, False)
                    parts[2] = clear_ends(parts[2], False, True)
                    for p in range(3):
                        target = y + 1 - p
                        if 0 <= target < rows:
                            for q in range(3):
                                term = taps[p][q] * parts[q]
                                sums[target] = sums[target] + term if target in sums else term
                if y > 0:
                    done = sums.pop(y - 1)
                    rim_ref[here, 2 * cols + y - 1 : 2 * cols + y] = done[:1]
                    rim_ref[here, 2 * cols + rows + y - 1 : 2 * cols + rows + y] = done[-1:]
                    if y in (1, rows):
                        start = 0 if y == 1 else cols
                        rim_ref[here, start : start + cols] = done
                        made = jnp.zeros_like(done)
                    else:
                        made = clear_ends(gelu_of_half(done), True, True)
                    out_ref[(y - 1) * cols : y * cols, spot] = made.astype(jnp.bfloat16)

    def add(index):
        piece = slice((first + index) * tile, (first + index + 1) * tile)
        from_ref = total_ref if index else start_ref
        total_ref[...] = from_ref[...] + matmul(active_refs[index % 2][...], w_project_ref[piece, :])

    grow(0)
    for index in range(count):
        if index + 1 < count:
            grow(index + 1)
        convolve(index)
        if index:
            add(index - 1)
    add(count - 1)


def inner(odd_col, normed, start, w_expand, depth_kernel, w_project, rows, cols, first, count, tile):
    tokens, channels = start.shape
    rim = (count * tile // LANES, 2 * cols + 2 * rows, LANES)
    return pl.pallas_call(
        functools.partial(inner_kernel, rows=rows, cols=cols, first=first, count=count),
        in_specs=[pl.BlockSpec(memory_space=pltpu.SMEM)] + [vmem()] * 5,
        out_specs=[vmem()] * 2,
        out_shape=[
            jax.ShapeDtypeStruct((tokens, channels), jnp.float32),
            jax.ShapeDtypeStruct(rim, jnp.float32),
        ],
        scratch_shapes=[pltpu.VMEM((tokens, tile), jnp.bfloat16)] * 2
        + [pltpu.VMEM((tile // LANES * padded_rows(tokens), LANES), jnp.float32)] * 2,
        compiler_params=pltpu.CompilerParams(vmem_limit_bytes=8 * MIB),
        cost_estimate=pl.CostEstimate(
            flops=2 * 10**9 * count,
            bytes_accessed=tokens * channels * 10 + 4 * count * tile * channels,
            transcendentals=2 * tokens * count * tile,
        ),
        name="inner",
    )(odd_col, normed, start, w_expand, depth_kernel, w_project)


def rim_kernel(
    own_ref, odd_col_ref, inner_ref, *refs, rows, cols, plan, size, pieces,
):
    masks, _, sides = plan
    sent = len(outgoing_shapes(plan, size, 1))
    rim_refs, refs = refs[:pieces], refs[pieces:]
    up_ref, down_ref, one_ref, two_ref, w_expand_ref, depth_ref, w_project_ref, perm_ref = refs[:8]
    mixed_ref, slab_refs = refs[8], refs[9 : 9 + sent]
    halo_ref, active_ref, normed_ref, grouped_ref = refs[9 + sent :]
    tokens = rows * cols
    width = w_expand_ref.shape[1]
    tile = divisor(width, 512, LANES)
    subs = tile // LANES
    slot = one_ref.shape[0]
    left_start, right_start = 2 * cols, 2 * cols + slot

    odd_col = odd_col_ref[0]
    left = choose(odd_col, one_ref[...], two_ref[...])
    right = choose(odd_col, two_ref[...], one_ref[...])
    edges = jnp.concatenate([up_ref[...], down_ref[...], left, right], axis=0)

    def expand_halo(index):
        made = gelu_of_half(matmul(edges, w_expand_ref[:, index * tile : (index + 1) * tile]))
        for sub in range(subs):
            halo_ref[index * subs + sub] = made[:, sub * LANES : (sub + 1) * LANES]

    position = lax.broadcasted_iota(jnp.int32, (cols, LANES), 0)
    at_first = position == 0
    at_last = position == cols - 1

    def activate(chunk, here, sums_ref):
        lanes = slice(chunk * LANES, (chunk + 1) * LANES)
        taps = [[0.5 * depth_ref[p, q : q + 1, lanes] for q in range(3)] for p in range(3)]
        beside = []
        for q, start in ((0, left_start), (2, right_start)):
            beside.append(
                sum(taps[p][q] * halo_ref[chunk, start + p : start + p + rows] for p in range(3))
            )
        made = []
        for p, start, y in ((0, 0, 0), (2, cols, rows - 1)):
            row = halo_ref[chunk, start : start + cols]
            before = jnp.where(at_first, beside[0][y : y + 1], taps[p][0] * pltpu.roll(row, 1, 0))
            after = jnp.where(
                at_last, beside[1][y : y + 1], taps[p][2] * pltpu.roll(row, cols - 1, 0)
            )
            made.append(sums_ref[here, start : start + cols] + before + taps[p][1] * row + after)
        for index in range(2):
            start = 2 * cols + index * rows
            made.append(sums_ref[here, start : start + rows] + beside[index])
        active_ref[:, lanes] = gelu_of_half(jnp.concatenate(made, axis=0)).astype(jnp.bfloat16)

    spots = [(ref, here) for ref in rim_refs for here in range(ref.shape[0])]
    expand_halo(0)
    for index in range(width // tile):
        if (index + 1) * tile < width:
            expand_halo(index + 1)
        for chunk in range(index * subs, (index + 1) * subs):
            activate(chunk, spots[chunk][1], spots[chunk][0])

    mixed_ref[...] = inner_ref[...]
    branch = matmul(active_ref[...], w_project_ref[...])
    mixed_ref[:cols, :] += branch[:cols]
    mixed_ref[tokens - cols :, :] += branch[cols : 2 * cols]
    for y in range(1, rows - 1):
        for index, x in ((0, 0), (1, cols - 1)):
            spot = y * cols + x
            start = 2 * cols + index * rows + y
            mixed_ref[spot : spot + 1, :] += branch[start : start + 1]

    step = divisor(tokens, 128, 16)
    for start in range(0, tokens, step):
        piece = slice(start, start + step)
        normed_ref[piece, :] = layer_norm(mixed_ref[piece, :]).astype(jnp.bfloat16)
    grouped_ref[...] = matmul(perm_ref[...], normed_ref[...]).astype(jnp.bfloat16)
    for index, mask in enumerate(masks):
        for side in range(sides):
            start = pl.multiple_of((own_ref[0] ^ (mask | side)) * size, 16)
            write_block(
                plan, slab_refs, index, side, slice(None), grouped_ref[pl.ds(start, size), :]
            )


def rim(
    own, odd_col, plan, size, total, rims, up, down, one, two, w_expand, depth_kernel, w_project, perm,
    rows, cols,
):
    tokens, channels = total.shape
    width = w_expand.shape[1]
    halo_rows = 2 * cols + 2 * one.shape[0]
    sent = outgoing_shapes(plan, size, channels)
    return pl.pallas_call(
        functools.partial(
            rim_kernel, rows=rows, cols=cols, plan=plan, size=size, pieces=len(rims)
        ),
        in_specs=[pl.BlockSpec(memory_space=pltpu.SMEM)] * 2 + [vmem()] * (9 + len(rims)),
        out_specs=[vmem()] * (1 + len(sent)),
        out_shape=[jax.ShapeDtypeStruct((tokens, channels), jnp.float32)]
        + [jax.ShapeDtypeStruct(shape, jnp.bfloat16) for shape in sent],
        scratch_shapes=[
            pltpu.VMEM((width // LANES, halo_rows, LANES), jnp.float32),
            pltpu.VMEM((2 * cols + 2 * rows, width), jnp.bfloat16),
            pltpu.VMEM((tokens, channels), jnp.bfloat16),
            pltpu.VMEM((tokens, channels), jnp.bfloat16),
        ],
        compiler_params=pltpu.CompilerParams(vmem_limit_bytes=8 * MIB),
        cost_estimate=pl.CostEstimate(
            flops=2 * halo_rows * channels * width * 2 + 2 * tokens * tokens * channels,
            bytes_accessed=tokens * channels * 10 + 4 * channels * width,
            transcendentals=2 * halo_rows * width,
        ),
        name="rim",
    )(own, odd_col, total, *rims, up, down, one, two, w_expand, depth_kernel, w_project, perm)


def identity(size):
    row = lax.broadcasted_iota(jnp.int32, (size, size), 0)
    column = lax.broadcasted_iota(jnp.int32, (size, size), 1)
    return jnp.where(row == column, 1.0, 0.0).astype(jnp.bfloat16)


def gather_blocks(plan, refs, blocks, sets):
    members = refs[0].shape[1] // sets
    return jnp.concatenate(
        [
            read_block(plan, refs, index, side, slice(s * members, (s + 1) * members))
            for s in range(sets)
            for index, side in blocks
        ],
        axis=0,
    )


def project_kernel(*refs, plan, sets):
    in_refs, weight_ref, out_ref = refs[:-2], refs[-2], refs[-1]
    block = gather_blocks(plan, in_refs, split_blocks(plan)[0], sets)
    out_ref[...] = matmul(block, weight_ref[...]).astype(jnp.bfloat16)


def project(plan, incoming, w_qkv, sets):
    soon = split_blocks(plan)[0]
    _, size, channels = incoming[0].shape
    masks, late, _ = plan
    there = [*range(late, len(masks) - 1 - late), len(masks) - 1, len(masks) + late]
    filled = [array if index in there else incoming[late] for index, array in enumerate(incoming)]
    return pl.pallas_call(
        functools.partial(project_kernel, plan=plan, sets=sets),
        in_specs=[vmem()] * (len(filled) + 1),
        out_specs=vmem(),
        out_shape=jax.ShapeDtypeStruct((len(soon) * size, w_qkv.shape[1]), jnp.bfloat16),
        compiler_params=pltpu.CompilerParams(vmem_limit_bytes=4 * MIB),
        cost_estimate=pl.CostEstimate(
            flops=2 * len(soon) * size * channels * w_qkv.shape[1],
            bytes_accessed=2 * w_qkv.size + 8 * len(soon) * size * channels,
            transcendentals=0,
        ),
        name="project",
    )(*filled, w_qkv)


def attend_kernel(*refs, plan, sets, came):
    masks, _, sides = plan
    slabs = len(masks)
    _, size, channels = refs[0].shape
    soon, rest = split_blocks(plan)
    in_refs, weight_ref, out_refs = refs[:came], refs[came], refs[came + 1 : -6]
    if soon:
        soon_ref, out_refs = out_refs[0], out_refs[1:]
    query_ref, key_ref, value_ref, turned_ref, even_ref, odd_ref = refs[-6:]
    members = size // sets
    count = slabs * sides * members
    head_width = channels // HEADS
    group_heads = LANES // head_width
    groups = channels // LANES
    factor = math.log2(math.e) / math.sqrt(head_width)
    lane = lax.broadcasted_iota(jnp.int32, (1, LANES), 1)
    masks = [
        jnp.where((lane >= j * head_width) & (lane < (j + 1) * head_width), 1.0, 0.0).astype(
            jnp.bfloat16
        )
        for j in range(group_heads)
    ]
    turn_values = identity(channels)
    block = gather_blocks(plan, in_refs, rest, sets)
    projected = matmul(block, weight_ref[...]).astype(jnp.bfloat16)
    for s in range(sets):
        near, far = len(soon) * members, len(rest) * members
        qkv = projected[s * far : (s + 1) * far]
        if soon:
            qkv = jnp.concatenate([soon_ref[s * near : (s + 1) * near, :], qkv], axis=0)
        values = matmul_nt(turn_values, qkv[:, 2 * channels :]).astype(jnp.bfloat16)
        for group in range(groups):
            spot = group * LANES
            query_ref[s * groups + group] = qkv[:, spot : spot + LANES]
            key_ref[s * groups + group] = qkv[:, channels + spot : channels + spot + LANES]
            for j in range(group_heads):
                head = (group * group_heads + j) * head_width
                value_ref[s * groups + group, j, :head_width] = values[head : head + head_width]
                value_ref[s * groups + group, j, head_width:] = jnp.ones((16, count), jnp.bfloat16)

    def scores(index, out):
        keys = key_ref[index]
        stacked = jnp.concatenate([keys * mask for mask in masks], axis=0)
        out[...] = matmul_nt(stacked, query_ref[index])

    def weigh(index, scores_ref):
        for j in range(group_heads):
            part = scores_ref[j * count : (j + 1) * count]
            highest = jnp.max(part, axis=0, keepdims=True)
            raised = jnp.exp2((part - highest) * factor).astype(jnp.bfloat16)
            product = matmul(value_ref[index, j], raised)
            scale = 1.0 / product[head_width : head_width + 1]
            turned_ref[index, j * head_width : (j + 1) * head_width] = (
                product[:head_width] * scale
            ).astype(jnp.bfloat16)

    total = sets * groups
    scores(0, even_ref)

    def body(pair, carry):
        scores(2 * pair + 1, odd_ref)
        weigh(2 * pair, even_ref)
        scores(jnp.minimum(2 * pair + 2, total - 1), even_ref)
        weigh(2 * pair + 1, odd_ref)
        return carry

    lax.fori_loop(0, total // 2, body, 0)
    turn_tokens = identity(count)
    for s in range(sets):
        turned = turned_ref[s * groups : (s + 1) * groups].reshape(channels, count)
        attended = matmul_nt(turn_tokens, turned).astype(jnp.bfloat16)
        for number, (index, side) in enumerate(soon + rest):
            write_block(
                plan, out_refs, index, side, slice(s * members, (s + 1) * members),
                attended[number * members : (number + 1) * members],
            )


def attend(plan, incoming, w_qkv, sets):
    masks, _, sides = plan
    _, size, channels = incoming[0].shape
    count = len(masks) * sides * size // sets
    sent = outgoing_shapes(plan, size, channels)
    soon = [project(plan, incoming, w_qkv, sets)] if split_blocks(plan)[0] else []
    head_width = channels // HEADS
    group_heads = LANES // head_width
    total = sets * channels // LANES
    return pl.pallas_call(
        functools.partial(attend_kernel, plan=plan, sets=sets, came=len(incoming)),
        in_specs=[vmem()] * (len(incoming) + 1 + len(soon)),
        out_specs=[vmem()] * len(sent),
        out_shape=[jax.ShapeDtypeStruct(shape, jnp.bfloat16) for shape in sent],
        scratch_shapes=[
            pltpu.VMEM((total, count, LANES), jnp.bfloat16),
            pltpu.VMEM((total, count, LANES), jnp.bfloat16),
            pltpu.VMEM((total, group_heads, head_width + 16, count), jnp.bfloat16),
            pltpu.VMEM((total, LANES, count), jnp.bfloat16),
            pltpu.VMEM((group_heads * count, count), jnp.float32),
            pltpu.VMEM((group_heads * count, count), jnp.float32),
        ],
        compiler_params=pltpu.CompilerParams(vmem_limit_bytes=10 * MIB),
        cost_estimate=pl.CostEstimate(
            flops=sets * (2 * count * channels * channels * 3 + 4 * count * count * channels),
            bytes_accessed=4 * sets * count * channels + 6 * channels * channels,
            transcendentals=sets * HEADS * count * count,
        ),
        name="attend",
    )(*incoming, w_qkv, *soon)


def finish_kernel(own_ref, *refs, plan):
    masks, _, sides = plan
    in_refs, rest = refs[:-7], refs[-7:]
    back_ref, weight_ref, mixed_ref, out_ref, attended_ref, made_ref, sent = rest
    tokens = mixed_ref.shape[0]
    size = in_refs[0].shape[1]
    for index, mask in enumerate(masks):
        for side in range(sides):
            start = pl.multiple_of((own_ref[0] ^ (mask | side)) * size, 16)
            attended_ref[pl.ds(start, size), :] = read_block(
                plan, in_refs, index, side, slice(None)
            )
    step = made_ref.shape[1]
    copies = []
    for index, start in enumerate(range(0, tokens, step)):
        rows = slice(start, start + step)
        restored = matmul(back_ref[rows, :], attended_ref[...]).astype(jnp.bfloat16)
        made_ref[index] = mixed_ref[rows, :] + matmul(restored, weight_ref[...])
        copy = pltpu.make_async_copy(
            made_ref.at[index], out_ref.at[pl.ds(start, step)], sent.at[index]
        )
        copy.start()
        copies.append(copy)
    for copy in copies:
        copy.wait()


def finish(own, plan, incoming, back, w_out, mixed):
    tokens, channels = mixed.shape
    step = divisor(tokens, 256, 16)
    return pl.pallas_call(
        functools.partial(finish_kernel, plan=plan),
        in_specs=[pl.BlockSpec(memory_space=pltpu.SMEM)] + [vmem()] * (len(incoming) + 3),
        out_specs=pl.BlockSpec(memory_space=pltpu.HBM),
        out_shape=jax.ShapeDtypeStruct((tokens, channels), jnp.float32),
        scratch_shapes=[
            pltpu.VMEM((tokens, channels), jnp.bfloat16),
            pltpu.VMEM((tokens // step, step, channels), jnp.float32),
            pltpu.SemaphoreType.DMA((tokens // step,)),
        ],
        compiler_params=pltpu.CompilerParams(vmem_limit_bytes=6 * MIB),
        name="finish",
    )(own, *incoming, back, w_out, mixed)


def swap_pairs(edge, axis, start):
    pairs = [(i, i + 1) for i in range(start, lax.axis_size(axis) - 1, 2)]
    return lax.ppermute(edge, axis, pairs + [(b, a) for a, b in pairs])


def exchange_plan(row_devices, col_devices):
    devices = row_devices * col_devices
    crossing = list(range(devices - 2, devices // 2 - 1, -2))
    others = list(range(devices // 2 - 2, 0, -2))
    masks = crossing[:-1] + others[:-1] + crossing[-1:] + others[-1:] + [0]
    return masks, 2, 2


def split_blocks(plan):
    masks, late, sides = plan
    blocks = [(index, side) for index in range(len(masks)) for side in range(sides)]
    if sides == 1:
        return [], blocks
    soon = [*range(late, len(masks) - 1 - late), len(masks) - 1]
    return [b for b in blocks if b[0] in soon], [b for b in blocks if b[0] not in soon]


def outgoing_shapes(plan, size, channels):
    masks, late, sides = plan
    if sides == 1:
        return [(1, size, channels)]
    early = len(masks) - 1 - late
    return [(2, size, channels)] * late + [
        (1, size, channels), (early + 1, size, channels), (early, size, channels)
    ]


def write_block(plan, refs, index, side, rows, value):
    masks, late, sides = plan
    if sides == 1:
        refs[0][0, rows] = value
    elif index < late:
        refs[index][side, rows] = value
    elif index == len(masks) - 1:
        refs[late + side][0, rows] = value
    elif side == 0:
        refs[late + 2][index - late, rows] = value
    else:
        refs[late + 1][index - late + 1, rows] = value


def read_block(plan, refs, index, side, rows):
    masks, late, sides = plan
    if sides == 1:
        return refs[0][0, rows]
    if index < late:
        return refs[index + side * len(masks)][side, rows]
    if index == len(masks) - 1:
        return refs[index + side * (late + 1)][0, rows]
    return refs[index][side, rows]


def join_kernel(own_ref, swapped_ref, *out_refs):
    for index, out_ref in enumerate(out_refs):
        out_ref[0] = own_ref[index]
        out_ref[1] = swapped_ref[index + 1]


def join(own, swapped):
    early, size, channels = own.shape
    return pl.pallas_call(
        join_kernel,
        in_specs=[vmem()] * 2,
        out_specs=[vmem()] * early,
        out_shape=[jax.ShapeDtypeStruct((2, size, channels), own.dtype)] * early,
        compiler_params=pltpu.CompilerParams(vmem_limit_bytes=2 * MIB),
        name="join",
    )(own, swapped)


def trade(plan, outgoing):
    masks, late, _ = plan
    devices = lax.axis_size("row") * lax.axis_size("col")

    def swap(slab, mask):
        return lax.ppermute(slab, ("row", "col"), [(i, i ^ mask) for i in range(devices)])

    slabs, (kept, passed, own) = outgoing[:late], outgoing[late:]
    swapped = swap(passed, 1)
    first = [swap(slab, mask) for slab, mask in zip(slabs, masks)]
    rest = [swap(slab, mask) for slab, mask in zip(join(own, swapped), masks[late:-1])]
    tied = lax.optimization_barrier((*first, *rest[:-late]))
    first, rest = tied[:late], [*tied[late:], *rest[-late:]]
    return [*first, *rest, kept, *[swap(slab, 1) for slab in first], swapped]


def trade_all(slabs, sets, members, outward):
    axes = ("row", "col")
    channels = slabs[0].shape[-1]
    block = slabs[0].reshape(-1, channels)
    devices = block.shape[0] // (sets * members)
    if not outward:
        block = block.reshape(sets, devices, members, channels).transpose(1, 0, 2, 3)
    block = block.reshape(devices, sets * members, channels)
    block = lax.all_to_all(block, axes, 0, 0, tiled=True)
    if outward:
        block = block.reshape(devices, sets, members, channels).transpose(1, 0, 2, 3)
    return [block.reshape(1, -1, channels)]


def grouping(rows, cols, blocks_rows, blocks_cols):
    order = np.arange(rows * cols).reshape(
        blocks_rows, rows // blocks_rows, blocks_cols, cols // blocks_cols
    )
    order = order.transpose(1, 3, 0, 2).reshape(-1)
    matrix = np.zeros((order.size, order.size), np.float32)
    matrix[np.arange(order.size), order] = 1.0
    return matrix


def shards(field, w_expand, depth_kernel, w_project, w_qkv, w_out):
    rows, cols, channels = field.shape
    tokens = rows * cols
    row_devices = lax.axis_size("row")
    col_devices = lax.axis_size("col")
    devices = row_devices * col_devices
    blocks_rows = GRID // row_devices
    blocks_cols = GRID // col_devices
    members = blocks_rows * blocks_cols
    sets_local = tokens // members // devices
    matrix = grouping(rows, cols, blocks_rows, blocks_cols)
    perm = jnp.asarray(matrix, jnp.bfloat16)
    back = jnp.asarray(matrix.T, jnp.bfloat16)

    flat = field.reshape(tokens, channels)
    pairwise = 8 <= devices <= 16 and devices & (devices - 1) == 0 and col_devices % 2 == 0
    plan = exchange_plan(row_devices, col_devices) if pairwise else ([0], 0, 1)
    row, col = lax.axis_index("row"), lax.axis_index("col")
    own = (row * col_devices + col if pairwise else row * 0).reshape(1)
    odd_row, odd_col = (row % 2).reshape(1), (col % 2).reshape(1)

    own, odd_row, odd_col, top, bottom = lax.optimization_barrier(
        (own, odd_row, odd_col, field[0], field[rows - 1])
    )
    one, two = row_edges(odd_row, top, bottom)
    one, two = swap_pairs(one, "row", 0), swap_pairs(two, "row", 1)
    normed = half_norm_of(flat)
    tile = divisor(w_expand.shape[1] // 2, 256, LANES)
    count = w_expand.shape[1] // tile
    early = count // 2
    total, rim_one = inner(
        odd_col, normed, flat, w_expand, depth_kernel, w_project, rows, cols, 0, early, tile
    )
    one, two, normed, total, rim_one = lax.optimization_barrier((one, two, normed, total, rim_one))
    up, down, one, two = column_strips(odd_row, odd_col, normed, one, two, round_up(rows + 2, 16))
    one, two = swap_pairs(one, "col", 0), swap_pairs(two, "col", 1)
    total, rim_two = inner(
        odd_col, normed, total, w_expand, depth_kernel, w_project, rows, cols, early,
        count - early, tile
    )

    size = tokens // (len(plan[0]) * plan[2])
    mixed, *outgoing = rim(
        own, odd_col, plan, size, total, [rim_one, rim_two], up, down, one, two, w_expand,
        depth_kernel, w_project, perm, rows, cols,
    )

    def route(outgoing, outward):
        if pairwise:
            return trade(plan, outgoing)
        return trade_all(outgoing, sets_local, members, outward)

    outgoing = attend(plan, route(outgoing, True), w_qkv, sets_local)
    final = finish(own, plan, route(outgoing, False), back, w_out, mixed)
    return final.reshape(rows, cols, channels)


def solution(mesh):
    return jax.shard_map(
        shards,
        mesh=mesh,
        in_specs=(P(("field", "row"), "col", None), P(), P(), P(), P(), P()),
        out_specs=P(("field", "row"), "col", None),
        check_vma=False,
    )
```

```python
import functools
import math

import jax
import jax.numpy as jnp
import numpy as np
from jax import lax
from jax.experimental import pallas as pl
from jax.experimental.pallas import tpu as pltpu
from jax.sharding import PartitionSpec as P

HEADS = 16
GRID = 16
LANES = 128
MIB = 1024 * 1024
NT = (((1,), (1,)), ((), ()))


def layer_norm(inputs):
    average = jnp.mean(inputs, axis=-1, keepdims=True)
    centred = inputs - average
    variance = jnp.mean(centred * centred, axis=-1, keepdims=True)
    return centred * lax.rsqrt(variance + 1e-05)


def gelu_of_half(half):
    scale = math.sqrt(2.0 / math.pi)
    inner = half * (2.0 * scale + (8.0 * scale * 0.044715) * (half * half))
    return half + half * jnp.tanh(inner)


def matmul(a, b):
    return jnp.dot(a, b, preferred_element_type=jnp.float32)


def matmul_nt(a, b):
    return lax.dot_general(a, b, NT, preferred_element_type=jnp.float32)


def divisor(size, most, unit):
    best = size
    for piece in range(unit, most + 1, unit):
        if size % piece == 0:
            best = piece
    return best


def round_up(size, unit):
    return -(-size // unit) * unit


def vmem():
    return pl.BlockSpec(memory_space=pltpu.VMEM)


def half_norm(inputs):
    return (layer_norm(inputs) * 0.5).astype(jnp.bfloat16)


def half_norm_kernel(in_ref, out_ref):
    rows = in_ref.shape[0]
    step = divisor(rows, 128, 16)
    for start in range(0, rows, step):
        out_ref[start : start + step, :] = half_norm(in_ref[start : start + step, :])


def half_norm_of(inputs):
    return pl.pallas_call(
        half_norm_kernel,
        in_specs=[vmem()],
        out_specs=vmem(),
        out_shape=jax.ShapeDtypeStruct(inputs.shape, jnp.bfloat16),
        compiler_params=pltpu.CompilerParams(vmem_limit_bytes=4 * MIB),
        cost_estimate=pl.CostEstimate(
            flops=10**9, bytes_accessed=6 * inputs.size, transcendentals=inputs.shape[0]
        ),
        name="half_norm",
    )(inputs)


def choose(condition, one, two):
    flags = jnp.full((one.shape[0], 1), condition, jnp.int32) == 1
    return jnp.where(flags, one.astype(jnp.float32), two.astype(jnp.float32)).astype(one.dtype)


def edges_kernel(odd_row_ref, top_ref, bottom_ref, one_ref, two_ref):
    odd = odd_row_ref[0]
    top, bottom = half_norm(top_ref[...]), half_norm(bottom_ref[...])
    one_ref[...] = choose(odd, top, bottom)
    two_ref[...] = choose(odd, bottom, top)


def row_edges(odd_row, top, bottom):
    return pl.pallas_call(
        edges_kernel,
        in_specs=[pl.BlockSpec(memory_space=pltpu.SMEM)] + [vmem()] * 2,
        out_specs=[vmem()] * 2,
        out_shape=[jax.ShapeDtypeStruct(top.shape, jnp.bfloat16)] * 2,
        compiler_params=pltpu.CompilerParams(vmem_limit_bytes=4 * MIB),
        cost_estimate=pl.CostEstimate(
            flops=10**10, bytes_accessed=12 * top.size, transcendentals=2 * top.shape[0]
        ),
        name="row_edges",
    )(odd_row, top, bottom)


def picker(shape, pick):
    row = lax.broadcasted_iota(jnp.int32, shape, 0)
    column = lax.broadcasted_iota(jnp.int32, shape, 1)
    return jnp.where(pick(row, column), 1.0, 0.0).astype(jnp.bfloat16)


def strips_kernel(
    odd_row_ref, odd_col_ref, row_two_ref, row_one_ref, normed_ref, up_ref, down_ref, one_ref, two_ref
):
    tokens = normed_ref.shape[0]
    cols = up_ref.shape[0]
    rows = tokens // cols
    slot = one_ref.shape[0]
    odd_row, odd_col = odd_row_ref[0], odd_col_ref[0]
    up = choose(odd_row, row_one_ref[...], row_two_ref[...])
    down = choose(odd_row, row_two_ref[...], row_one_ref[...])
    up_ref[...] = up
    down_ref[...] = down
    strips = []
    for x in (0, cols - 1):
        body = picker(
            (slot, tokens), lambda i, j: (i >= 1) & (i <= rows) & (j == (i - 1) * cols + x)
        )
        head = picker((slot, cols), lambda i, j: (i == 0) & (j == x))
        foot = picker((slot, cols), lambda i, j: (i == rows + 1) & (j == x))
        strip = matmul(body, normed_ref[...]) + matmul(head, up) + matmul(foot, down)
        strips.append(strip.astype(jnp.bfloat16))
    one_ref[...] = choose(odd_col, strips[0], strips[1])
    two_ref[...] = choose(odd_col, strips[1], strips[0])


def column_strips(odd_row, odd_col, normed, row_one, row_two, slot):
    cols, channels = row_one.shape
    shapes = [(cols, channels)] * 2 + [(slot, channels)] * 2
    return pl.pallas_call(
        strips_kernel,
        in_specs=[pl.BlockSpec(memory_space=pltpu.SMEM)] * 2 + [vmem()] * 3,
        out_specs=[vmem()] * 4,
        out_shape=[jax.ShapeDtypeStruct(shape, jnp.bfloat16) for shape in shapes],
        compiler_params=pltpu.CompilerParams(vmem_limit_bytes=4 * MIB),
        name="column_strips",
    )(odd_row, odd_col, row_two, row_one, normed)


def padded_rows(tokens):
    return tokens + 16


def inner_kernel(
    odd_col_ref, normed_ref, start_ref, w_expand_ref, depth_ref, w_project_ref, total_ref, rim_ref,
    even_ref, odd_ref, even_grown_ref, odd_grown_ref, *, rows, cols, first, count,
):
    tokens = rows * cols
    tile = even_ref.shape[1]
    origin = jnp.minimum(odd_col_ref[0], 0)
    active_refs = even_ref, odd_ref
    grown_refs = even_grown_ref, odd_grown_ref
    subs = tile // LANES
    position = lax.broadcasted_iota(jnp.int32, (8, LANES), 0)
    at_first = position == 0
    at_last = position == 7

    def clear_ends(value, low, high):
        head = jnp.where(at_first, 0.0, value[:8]) if low else value[:8]
        foot = jnp.where(at_last, 0.0, value[-8:]) if high else value[-8:]
        return jnp.concatenate([head, value[8:-8], foot], axis=0)

    def grow(index):
        lanes = slice((first + index) * tile, (first + index + 1) * tile)
        made = gelu_of_half(matmul(normed_ref[...], w_expand_ref[:, lanes]))
        for sub in range(subs):
            start = sub * padded_rows(tokens) + 8
            grown_refs[index % 2][start : start + tokens, :] = made[
                :, sub * LANES : (sub + 1) * LANES
            ]

    def convolve(index):
        out_ref, grown_ref = active_refs[index % 2], grown_refs[index % 2]
        for sub in range(subs):
            chunk = (first + index) * subs + sub
            lanes = slice(chunk * LANES, (chunk + 1) * LANES)
            base = origin + sub * padded_rows(tokens) + 8
            here = index * subs + sub
            taps = [[0.5 * depth_ref[p, q : q + 1, lanes] for q in range(3)] for p in range(3)]
            spot = slice(sub * LANES, (sub + 1) * LANES)
            sums = {}
            for y in range(rows + 1):
                if y < rows:
                    parts = [
                        grown_ref[pl.ds(base + (y * cols + q), cols), :] for q in (-1, 0, 1)
                    ]
                    parts[0] = clear_ends(parts[0], True, False)
                    parts[2] = clear_ends(parts[2], False, True)
                    for p in range(3):
                        target = y + 1 - p
                        if 0 <= target < rows:
                            for q in range(3):
                                term = taps[p][q] * parts[q]
                                sums[target] = sums[target] + term if target in sums else term
                if y > 0:
                    done = sums.pop(y - 1)
                    rim_ref[here, 2 * cols + y - 1 : 2 * cols + y] = done[:1]
                    rim_ref[here, 2 * cols + rows + y - 1 : 2 * cols + rows + y] = done[-1:]
                    if y in (1, rows):
                        start = 0 if y == 1 else cols
                        rim_ref[here, start : start + cols] = done
                        made = jnp.zeros_like(done)
                    else:
                        made = clear_ends(gelu_of_half(done), True, True)
                    out_ref[(y - 1) * cols : y * cols, spot] = made.astype(jnp.bfloat16)

    def add(index):
        piece = slice((first + index) * tile, (first + index + 1) * tile)
        from_ref = total_ref if index else start_ref
        total_ref[...] = from_ref[...] + matmul(active_refs[index % 2][...], w_project_ref[piece, :])

    grow(0)
    for index in range(count):
        if index + 1 < count:
            grow(index + 1)
        convolve(index)
        if index:
            add(index - 1)
    add(count - 1)


def inner(odd_col, normed, start, w_expand, depth_kernel, w_project, rows, cols, first, count, tile):
    tokens, channels = start.shape
    rim = (count * tile // LANES, 2 * cols + 2 * rows, LANES)
    return pl.pallas_call(
        functools.partial(inner_kernel, rows=rows, cols=cols, first=first, count=count),
        in_specs=[pl.BlockSpec(memory_space=pltpu.SMEM)] + [vmem()] * 5,
        out_specs=[vmem()] * 2,
        out_shape=[
            jax.ShapeDtypeStruct((tokens, channels), jnp.float32),
            jax.ShapeDtypeStruct(rim, jnp.float32),
        ],
        scratch_shapes=[pltpu.VMEM((tokens, tile), jnp.bfloat16)] * 2
        + [pltpu.VMEM((tile // LANES * padded_rows(tokens), LANES), jnp.float32)] * 2,
        compiler_params=pltpu.CompilerParams(vmem_limit_bytes=8 * MIB),
        cost_estimate=pl.CostEstimate(
            flops=2 * 10**9 * count,
            bytes_accessed=tokens * channels * 10 + 4 * count * tile * channels,
            transcendentals=2 * tokens * count * tile,
        ),
        name="inner",
    )(odd_col, normed, start, w_expand, depth_kernel, w_project)


def rim_kernel(
    own_ref, odd_col_ref, inner_ref, *refs, rows, cols, plan, size, pieces,
):
    masks, _, sides = plan
    sent = len(outgoing_shapes(plan, size, 1))
    rim_refs, refs = refs[:pieces], refs[pieces:]
    up_ref, down_ref, one_ref, two_ref, w_expand_ref, depth_ref, w_project_ref, perm_ref = refs[:8]
    mixed_ref, slab_refs = refs[8], refs[9 : 9 + sent]
    halo_ref, active_ref, normed_ref, grouped_ref = refs[9 + sent :]
    tokens = rows * cols
    width = w_expand_ref.shape[1]
    tile = divisor(width, 512, LANES)
    subs = tile // LANES
    slot = one_ref.shape[0]
    left_start, right_start = 2 * cols, 2 * cols + slot

    odd_col = odd_col_ref[0]
    left = choose(odd_col, one_ref[...], two_ref[...])
    right = choose(odd_col, two_ref[...], one_ref[...])
    edges = jnp.concatenate([up_ref[...], down_ref[...], left, right], axis=0)

    def expand_halo(index):
        made = gelu_of_half(matmul(edges, w_expand_ref[:, index * tile : (index + 1) * tile]))
        for sub in range(subs):
            halo_ref[index * subs + sub] = made[:, sub * LANES : (sub + 1) * LANES]

    position = lax.broadcasted_iota(jnp.int32, (cols, LANES), 0)
    at_first = position == 0
    at_last = position == cols - 1

    def activate(chunk, here, sums_ref):
        lanes = slice(chunk * LANES, (chunk + 1) * LANES)
        taps = [[0.5 * depth_ref[p, q : q + 1, lanes] for q in range(3)] for p in range(3)]
        beside = []
        for q, start in ((0, left_start), (2, right_start)):
            beside.append(
                sum(taps[p][q] * halo_ref[chunk, start + p : start + p + rows] for p in range(3))
            )
        made = []
        for p, start, y in ((0, 0, 0), (2, cols, rows - 1)):
            row = halo_ref[chunk, start : start + cols]
            before = jnp.where(at_first, beside[0][y : y + 1], taps[p][0] * pltpu.roll(row, 1, 0))
            after = jnp.where(
                at_last, beside[1][y : y + 1], taps[p][2] * pltpu.roll(row, cols - 1, 0)
            )
            made.append(sums_ref[here, start : start + cols] + before + taps[p][1] * row + after)
        for index in range(2):
            start = 2 * cols + index * rows
            made.append(sums_ref[here, start : start + rows] + beside[index])
        active_ref[:, lanes] = gelu_of_half(jnp.concatenate(made, axis=0)).astype(jnp.bfloat16)

    spots = [(ref, here) for ref in rim_refs for here in range(ref.shape[0])]
    expand_halo(0)
    for index in range(width // tile):
        if (index + 1) * tile < width:
            expand_halo(index + 1)
        for chunk in range(index * subs, (index + 1) * subs):
            activate(chunk, spots[chunk][1], spots[chunk][0])

    mixed_ref[...] = inner_ref[...]
    branch = matmul(active_ref[...], w_project_ref[...])
    mixed_ref[:cols, :] += branch[:cols]
    mixed_ref[tokens - cols :, :] += branch[cols : 2 * cols]
    for y in range(1, rows - 1):
        for index, x in ((0, 0), (1, cols - 1)):
            spot = y * cols + x
            start = 2 * cols + index * rows + y
            mixed_ref[spot : spot + 1, :] += branch[start : start + 1]

    step = divisor(tokens, 128, 16)
    for start in range(0, tokens, step):
        piece = slice(start, start + step)
        normed_ref[piece, :] = layer_norm(mixed_ref[piece, :]).astype(jnp.bfloat16)
    grouped_ref[...] = matmul(perm_ref[...], normed_ref[...]).astype(jnp.bfloat16)
    for index, mask in enumerate(masks):
        for side in range(sides):
            start = pl.multiple_of((own_ref[0] ^ (mask | side)) * size, 16)
            write_block(
                plan, slab_refs, index, side, slice(None), grouped_ref[pl.ds(start, size), :]
            )


def rim(
    own, odd_col, plan, size, total, rims, up, down, one, two, w_expand, depth_kernel, w_project, perm,
    rows, cols,
):
    tokens, channels = total.shape
    width = w_expand.shape[1]
    halo_rows = 2 * cols + 2 * one.shape[0]
    sent = outgoing_shapes(plan, size, channels)
    return pl.pallas_call(
        functools.partial(
            rim_kernel, rows=rows, cols=cols, plan=plan, size=size, pieces=len(rims)
        ),
        in_specs=[pl.BlockSpec(memory_space=pltpu.SMEM)] * 2 + [vmem()] * (9 + len(rims)),
        out_specs=[vmem()] * (1 + len(sent)),
        out_shape=[jax.ShapeDtypeStruct((tokens, channels), jnp.float32)]
        + [jax.ShapeDtypeStruct(shape, jnp.bfloat16) for shape in sent],
        scratch_shapes=[
            pltpu.VMEM((width // LANES, halo_rows, LANES), jnp.float32),
            pltpu.VMEM((2 * cols + 2 * rows, width), jnp.bfloat16),
            pltpu.VMEM((tokens, channels), jnp.bfloat16),
            pltpu.VMEM((tokens, channels), jnp.bfloat16),
        ],
        compiler_params=pltpu.CompilerParams(vmem_limit_bytes=8 * MIB),
        cost_estimate=pl.CostEstimate(
            flops=2 * halo_rows * channels * width * 2 + 2 * tokens * tokens * channels,
            bytes_accessed=tokens * channels * 10 + 4 * channels * width,
            transcendentals=2 * halo_rows * width,
        ),
        name="rim",
    )(own, odd_col, total, *rims, up, down, one, two, w_expand, depth_kernel, w_project, perm)


def identity(size):
    row = lax.broadcasted_iota(jnp.int32, (size, size), 0)
    column = lax.broadcasted_iota(jnp.int32, (size, size), 1)
    return jnp.where(row == column, 1.0, 0.0).astype(jnp.bfloat16)


def gather_blocks(plan, refs, blocks, sets):
    members = refs[0].shape[1] // sets
    return jnp.concatenate(
        [
            read_block(plan, refs, index, side, slice(s * members, (s + 1) * members))
            for s in range(sets)
            for index, side in blocks
        ],
        axis=0,
    )


def project_kernel(*refs, plan, sets):
    in_refs, weight_ref, out_ref = refs[:-2], refs[-2], refs[-1]
    block = gather_blocks(plan, in_refs, split_blocks(plan)[0], sets)
    out_ref[...] = matmul(block, weight_ref[...]).astype(jnp.bfloat16)


def project(plan, incoming, w_qkv, sets):
    soon = split_blocks(plan)[0]
    _, size, channels = incoming[0].shape
    masks, late, _ = plan
    there = [*range(late, len(masks) - 1 - late), len(masks) - 1, len(masks) + late]
    filled = [array if index in there else incoming[late] for index, array in enumerate(incoming)]
    return pl.pallas_call(
        functools.partial(project_kernel, plan=plan, sets=sets),
        in_specs=[vmem()] * (len(filled) + 1),
        out_specs=vmem(),
        out_shape=jax.ShapeDtypeStruct((len(soon) * size, w_qkv.shape[1]), jnp.bfloat16),
        compiler_params=pltpu.CompilerParams(vmem_limit_bytes=4 * MIB),
        cost_estimate=pl.CostEstimate(
            flops=2 * len(soon) * size * channels * w_qkv.shape[1],
            bytes_accessed=2 * w_qkv.size + 8 * len(soon) * size * channels,
            transcendentals=0,
        ),
        name="project",
    )(*filled, w_qkv)


def attend_kernel(*refs, plan, sets, came):
    masks, _, sides = plan
    slabs = len(masks)
    _, size, channels = refs[0].shape
    soon, rest = split_blocks(plan)
    in_refs, weight_ref, out_refs = refs[:came], refs[came], refs[came + 1 : -6]
    if soon:
        soon_ref, out_refs = out_refs[0], out_refs[1:]
    query_ref, key_ref, value_ref, turned_ref, even_ref, odd_ref = refs[-6:]
    members = size // sets
    count = slabs * sides * members
    head_width = channels // HEADS
    group_heads = LANES // head_width
    groups = channels // LANES
    factor = math.log2(math.e) / math.sqrt(head_width)
    lane = lax.broadcasted_iota(jnp.int32, (1, LANES), 1)
    masks = [
        jnp.where((lane >= j * head_width) & (lane < (j + 1) * head_width), 1.0, 0.0).astype(
            jnp.bfloat16
        )
        for j in range(group_heads)
    ]
    turn_values = identity(channels)
    block = gather_blocks(plan, in_refs, rest, sets)
    projected = matmul(block, weight_ref[...]).astype(jnp.bfloat16)
    for s in range(sets):
        near, far = len(soon) * members, len(rest) * members
        qkv = projected[s * far : (s + 1) * far]
        if soon:
            qkv = jnp.concatenate([soon_ref[s * near : (s + 1) * near, :], qkv], axis=0)
        values = matmul_nt(turn_values, qkv[:, 2 * channels :]).astype(jnp.bfloat16)
        for group in range(groups):
            spot = group * LANES
            query_ref[s * groups + group] = qkv[:, spot : spot + LANES]
            key_ref[s * groups + group] = qkv[:, channels + spot : channels + spot + LANES]
            for j in range(group_heads):
                head = (group * group_heads + j) * head_width
                value_ref[s * groups + group, j, :head_width] = values[head : head + head_width]
                value_ref[s * groups + group, j, head_width:] = jnp.ones((16, count), jnp.bfloat16)

    def scores(index, out):
        keys = key_ref[index]
        stacked = jnp.concatenate([keys * mask for mask in masks], axis=0)
        out[...] = matmul_nt(stacked, query_ref[index])

    def weigh(index, scores_ref):
        for j in range(group_heads):
            part = scores_ref[j * count : (j + 1) * count]
            highest = jnp.max(part, axis=0, keepdims=True)
            raised = jnp.exp2((part - highest) * factor).astype(jnp.bfloat16)
            product = matmul(value_ref[index, j], raised)
            scale = 1.0 / product[head_width : head_width + 1]
            turned_ref[index, j * head_width : (j + 1) * head_width] = (
                product[:head_width] * scale
            ).astype(jnp.bfloat16)

    total = sets * groups
    scores(0, even_ref)

    def body(pair, carry):
        scores(2 * pair + 1, odd_ref)
        weigh(2 * pair, even_ref)
        scores(jnp.minimum(2 * pair + 2, total - 1), even_ref)
        weigh(2 * pair + 1, odd_ref)
        return carry

    lax.fori_loop(0, total // 2, body, 0)
    turn_tokens = identity(count)
    for s in range(sets):
        turned = turned_ref[s * groups : (s + 1) * groups].reshape(channels, count)
        attended = matmul_nt(turn_tokens, turned).astype(jnp.bfloat16)
        for number, (index, side) in enumerate(soon + rest):
            write_block(
                plan, out_refs, index, side, slice(s * members, (s + 1) * members),
                attended[number * members : (number + 1) * members],
            )


def attend(plan, incoming, w_qkv, sets):
    masks, _, sides = plan
    _, size, channels = incoming[0].shape
    count = len(masks) * sides * size // sets
    sent = outgoing_shapes(plan, size, channels)
    soon = [project(plan, incoming, w_qkv, sets)] if split_blocks(plan)[0] else []
    head_width = channels // HEADS
    group_heads = LANES // head_width
    total = sets * channels // LANES
    return pl.pallas_call(
        functools.partial(attend_kernel, plan=plan, sets=sets, came=len(incoming)),
        in_specs=[vmem()] * (len(incoming) + 1 + len(soon)),
        out_specs=[vmem()] * len(sent),
        out_shape=[jax.ShapeDtypeStruct(shape, jnp.bfloat16) for shape in sent],
        scratch_shapes=[
            pltpu.VMEM((total, count, LANES), jnp.bfloat16),
            pltpu.VMEM((total, count, LANES), jnp.bfloat16),
            pltpu.VMEM((total, group_heads, head_width + 16, count), jnp.bfloat16),
            pltpu.VMEM((total, LANES, count), jnp.bfloat16),
            pltpu.VMEM((group_heads * count, count), jnp.float32),
            pltpu.VMEM((group_heads * count, count), jnp.float32),
        ],
        compiler_params=pltpu.CompilerParams(vmem_limit_bytes=10 * MIB),
        cost_estimate=pl.CostEstimate(
            flops=sets * (2 * count * channels * channels * 3 + 4 * count * count * channels),
            bytes_accessed=4 * sets * count * channels + 6 * channels * channels,
            transcendentals=sets * HEADS * count * count,
        ),
        name="attend",
    )(*incoming, w_qkv, *soon)


def finish_kernel(own_ref, *refs, plan):
    masks, _, sides = plan
    in_refs, rest = refs[:-7], refs[-7:]
    back_ref, weight_ref, mixed_ref, out_ref, attended_ref, made_ref, sent = rest
    tokens = mixed_ref.shape[0]
    size = in_refs[0].shape[1]
    for index, mask in enumerate(masks):
        for side in range(sides):
            start = pl.multiple_of((own_ref[0] ^ (mask | side)) * size, 16)
            attended_ref[pl.ds(start, size), :] = read_block(
                plan, in_refs, index, side, slice(None)
            )
    step = made_ref.shape[1]
    copies = []
    for index, start in enumerate(range(0, tokens, step)):
        rows = slice(start, start + step)
        restored = matmul(back_ref[rows, :], attended_ref[...]).astype(jnp.bfloat16)
        made_ref[index] = mixed_ref[rows, :] + matmul(restored, weight_ref[...])
        copy = pltpu.make_async_copy(
            made_ref.at[index], out_ref.at[pl.ds(start, step)], sent.at[index]
        )
        copy.start()
        copies.append(copy)
    for copy in copies:
        copy.wait()


def finish(own, plan, incoming, back, w_out, mixed):
    tokens, channels = mixed.shape
    step = divisor(tokens, 256, 16)
    return pl.pallas_call(
        functools.partial(finish_kernel, plan=plan),
        in_specs=[pl.BlockSpec(memory_space=pltpu.SMEM)] + [vmem()] * (len(incoming) + 3),
        out_specs=pl.BlockSpec(memory_space=pltpu.HBM),
        out_shape=jax.ShapeDtypeStruct((tokens, channels), jnp.float32),
        scratch_shapes=[
            pltpu.VMEM((tokens, channels), jnp.bfloat16),
            pltpu.VMEM((tokens // step, step, channels), jnp.float32),
            pltpu.SemaphoreType.DMA((tokens // step,)),
        ],
        compiler_params=pltpu.CompilerParams(vmem_limit_bytes=6 * MIB),
        name="finish",
    )(own, *incoming, back, w_out, mixed)


def swap_pairs(edge, axis, start):
    pairs = [(i, i + 1) for i in range(start, lax.axis_size(axis) - 1, 2)]
    return lax.ppermute(edge, axis, pairs + [(b, a) for a, b in pairs])


def exchange_plan(row_devices, col_devices):
    devices = row_devices * col_devices
    crossing = list(range(devices - 2, devices // 2 - 1, -2))
    others = list(range(devices // 2 - 2, 0, -2))
    masks = crossing[:-1] + others[:-1] + crossing[-1:] + others[-1:] + [0]
    return masks, 2, 2


def split_blocks(plan):
    masks, late, sides = plan
    blocks = [(index, side) for index in range(len(masks)) for side in range(sides)]
    if sides == 1:
        return [], blocks
    soon = [*range(late, len(masks) - 1 - late), len(masks) - 1]
    return [b for b in blocks if b[0] in soon], [b for b in blocks if b[0] not in soon]


def outgoing_shapes(plan, size, channels):
    masks, late, sides = plan
    if sides == 1:
        return [(1, size, channels)]
    early = len(masks) - 1 - late
    return [(2, size, channels)] * late + [
        (1, size, channels), (early + 1, size, channels), (early, size, channels)
    ]


def write_block(plan, refs, index, side, rows, value):
    masks, late, sides = plan
    if sides == 1:
        refs[0][0, rows] = value
    elif index < late:
        refs[index][side, rows] = value
    elif index == len(masks) - 1:
        refs[late + side][0, rows] = value
    elif side == 0:
        refs[late + 2][index - late, rows] = value
    else:
        refs[late + 1][index - late + 1, rows] = value


def read_block(plan, refs, index, side, rows):
    masks, late, sides = plan
    if sides == 1:
        return refs[0][0, rows]
    if index < late:
        return refs[index + side * len(masks)][side, rows]
    if index == len(masks) - 1:
        return refs[index + side * (late + 1)][0, rows]
    return refs[index][side, rows]


def join_kernel(own_ref, swapped_ref, *out_refs):
    for index, out_ref in enumerate(out_refs):
        out_ref[0] = own_ref[index]
        out_ref[1] = swapped_ref[index + 1]


def join(own, swapped):
    early, size, channels = own.shape
    return pl.pallas_call(
        join_kernel,
        in_specs=[vmem()] * 2,
        out_specs=[vmem()] * early,
        out_shape=[jax.ShapeDtypeStruct((2, size, channels), own.dtype)] * early,
        compiler_params=pltpu.CompilerParams(vmem_limit_bytes=2 * MIB),
        name="join",
    )(own, swapped)


def trade(plan, outgoing):
    masks, late, _ = plan
    devices = lax.axis_size("row") * lax.axis_size("col")

    def swap(slab, mask):
        return lax.ppermute(slab, ("row", "col"), [(i, i ^ mask) for i in range(devices)])

    slabs, (kept, passed, own) = outgoing[:late], outgoing[late:]
    swapped = swap(passed, 1)
    first = [swap(slab, mask) for slab, mask in zip(slabs, masks)]
    rest = [swap(slab, mask) for slab, mask in zip(join(own, swapped), masks[late:-1])]
    tied = lax.optimization_barrier((*first, *rest[:-late]))
    first, rest = tied[:late], [*tied[late:], *rest[-late:]]
    return [*first, *rest, kept, *[swap(slab, 1) for slab in first], swapped]


def trade_all(slabs, sets, members, outward):
    axes = ("row", "col")
    channels = slabs[0].shape[-1]
    block = slabs[0].reshape(-1, channels)
    devices = block.shape[0] // (sets * members)
    if not outward:
        block = block.reshape(sets, devices, members, channels).transpose(1, 0, 2, 3)
    block = block.reshape(devices, sets * members, channels)
    block = lax.all_to_all(block, axes, 0, 0, tiled=True)
    if outward:
        block = block.reshape(devices, sets, members, channels).transpose(1, 0, 2, 3)
    return [block.reshape(1, -1, channels)]


def grouping(rows, cols, blocks_rows, blocks_cols):
    order = np.arange(rows * cols).reshape(
        blocks_rows, rows // blocks_rows, blocks_cols, cols // blocks_cols
    )
    order = order.transpose(1, 3, 0, 2).reshape(-1)
    matrix = np.zeros((order.size, order.size), np.float32)
    matrix[np.arange(order.size), order] = 1.0
    return matrix


def shards(field, w_expand, depth_kernel, w_project, w_qkv, w_out):
    rows, cols, channels = field.shape
    tokens = rows * cols
    row_devices = lax.axis_size("row")
    col_devices = lax.axis_size("col")
    devices = row_devices * col_devices
    blocks_rows = GRID // row_devices
    blocks_cols = GRID // col_devices
    members = blocks_rows * blocks_cols
    sets_local = tokens // members // devices
    matrix = grouping(rows, cols, blocks_rows, blocks_cols)
    perm = jnp.asarray(matrix, jnp.bfloat16)
    back = jnp.asarray(matrix.T, jnp.bfloat16)

    flat = field.reshape(tokens, channels)
    pairwise = 8 <= devices <= 16 and devices & (devices - 1) == 0 and col_devices % 2 == 0
    plan = exchange_plan(row_devices, col_devices) if pairwise else ([0], 0, 1)
    row, col = lax.axis_index("row"), lax.axis_index("col")
    own = (row * col_devices + col if pairwise else row * 0).reshape(1)
    odd_row, odd_col = (row % 2).reshape(1), (col % 2).reshape(1)

    own, odd_row, odd_col, top, bottom = lax.optimization_barrier(
        (own, odd_row, odd_col, field[0], field[rows - 1])
    )
    one, two = row_edges(odd_row, top, bottom)
    two, one = swap_pairs(two, "row", 1), swap_pairs(one, "row", 0)
    normed = half_norm_of(flat)
    tile = divisor(w_expand.shape[1] // 2, 256, LANES)
    count = w_expand.shape[1] // tile
    early = count // 2
    total, rim_one = inner(
        odd_col, normed, flat, w_expand, depth_kernel, w_project, rows, cols, 0, early, tile
    )
    two, one, normed, total, rim_one = lax.optimization_barrier((two, one, normed, total, rim_one))
    up, down, one, two = column_strips(odd_row, odd_col, normed, one, two, round_up(rows + 2, 16))
    one, two = swap_pairs(one, "col", 0), swap_pairs(two, "col", 1)
    total, rim_two = inner(
        odd_col, normed, total, w_expand, depth_kernel, w_project, rows, cols, early,
        count - early, tile
    )

    size = tokens // (len(plan[0]) * plan[2])
    mixed, *outgoing = rim(
        own, odd_col, plan, size, total, [rim_one, rim_two], up, down, one, two, w_expand,
        depth_kernel, w_project, perm, rows, cols,
    )

    def route(outgoing, outward):
        if pairwise:
            return trade(plan, outgoing)
        return trade_all(outgoing, sets_local, members, outward)

    outgoing = attend(plan, route(outgoing, True), w_qkv, sets_local)
    final = finish(own, plan, route(outgoing, False), back, w_out, mixed)
    return final.reshape(rows, cols, channels)


def solution(mesh):
    return jax.shard_map(
        shards,
        mesh=mesh,
        in_specs=(P(("field", "row"), "col", None), P(), P(), P(), P(), P()),
        out_specs=P(("field", "row"), "col", None),
        check_vma=False,
    )
```

```python
import functools
import math

import jax
import jax.numpy as jnp
import numpy as np
from jax import lax
from jax.experimental import pallas as pl
from jax.experimental.pallas import tpu as pltpu
from jax.sharding import PartitionSpec as P

HEADS = 16
GRID = 16
LANES = 128
MIB = 1024 * 1024
NT = (((1,), (1,)), ((), ()))


def layer_norm(inputs):
    average = jnp.mean(inputs, axis=-1, keepdims=True)
    centred = inputs - average
    variance = jnp.mean(centred * centred, axis=-1, keepdims=True)
    return centred * lax.rsqrt(variance + 1e-05)


def gelu_of_half(half):
    scale = math.sqrt(2.0 / math.pi)
    inner = half * (2.0 * scale + (8.0 * scale * 0.044715) * (half * half))
    return half + half * jnp.tanh(inner)


def matmul(a, b):
    return jnp.dot(a, b, preferred_element_type=jnp.float32)


def matmul_nt(a, b):
    return lax.dot_general(a, b, NT, preferred_element_type=jnp.float32)


def divisor(size, most, unit):
    best = size
    for piece in range(unit, most + 1, unit):
        if size % piece == 0:
            best = piece
    return best


def round_up(size, unit):
    return -(-size // unit) * unit


def vmem():
    return pl.BlockSpec(memory_space=pltpu.VMEM)


def half_norm(inputs):
    return (layer_norm(inputs) * 0.5).astype(jnp.bfloat16)


def half_norm_kernel(in_ref, out_ref):
    rows = in_ref.shape[0]
    step = divisor(rows, 128, 16)
    for start in range(0, rows, step):
        out_ref[start : start + step, :] = half_norm(in_ref[start : start + step, :])


def half_norm_of(inputs):
    return pl.pallas_call(
        half_norm_kernel,
        in_specs=[vmem()],
        out_specs=vmem(),
        out_shape=jax.ShapeDtypeStruct(inputs.shape, jnp.bfloat16),
        compiler_params=pltpu.CompilerParams(vmem_limit_bytes=4 * MIB),
        cost_estimate=pl.CostEstimate(
            flops=10**9, bytes_accessed=6 * inputs.size, transcendentals=inputs.shape[0]
        ),
        name="half_norm",
    )(inputs)


def choose(condition, one, two):
    flags = jnp.full((one.shape[0], 1), condition, jnp.int32) == 1
    return jnp.where(flags, one.astype(jnp.float32), two.astype(jnp.float32)).astype(one.dtype)


def edges_kernel(odd_row_ref, top_ref, bottom_ref, one_ref, two_ref):
    odd = odd_row_ref[0]
    top, bottom = half_norm(top_ref[...]), half_norm(bottom_ref[...])
    one_ref[...] = choose(odd, top, bottom)
    two_ref[...] = choose(odd, bottom, top)


def row_edges(odd_row, top, bottom):
    return pl.pallas_call(
        edges_kernel,
        in_specs=[pl.BlockSpec(memory_space=pltpu.SMEM)] + [vmem()] * 2,
        out_specs=[vmem()] * 2,
        out_shape=[jax.ShapeDtypeStruct(top.shape, jnp.bfloat16)] * 2,
        compiler_params=pltpu.CompilerParams(vmem_limit_bytes=4 * MIB),
        cost_estimate=pl.CostEstimate(
            flops=10**10, bytes_accessed=12 * top.size, transcendentals=2 * top.shape[0]
        ),
        name="row_edges",
    )(odd_row, top, bottom)


def picker(shape, pick):
    row = lax.broadcasted_iota(jnp.int32, shape, 0)
    column = lax.broadcasted_iota(jnp.int32, shape, 1)
    return jnp.where(pick(row, column), 1.0, 0.0).astype(jnp.bfloat16)


def strips_kernel(
    odd_row_ref, odd_col_ref, row_two_ref, row_one_ref, normed_ref, up_ref, down_ref, one_ref, two_ref
):
    tokens = normed_ref.shape[0]
    cols = up_ref.shape[0]
    rows = tokens // cols
    slot = one_ref.shape[0]
    odd_row, odd_col = odd_row_ref[0], odd_col_ref[0]
    up = choose(odd_row, row_one_ref[...], row_two_ref[...])
    down = choose(odd_row, row_two_ref[...], row_one_ref[...])
    up_ref[...] = up
    down_ref[...] = down
    strips = []
    for x in (0, cols - 1):
        body = picker(
            (slot, tokens), lambda i, j: (i >= 1) & (i <= rows) & (j == (i - 1) * cols + x)
        )
        head = picker((slot, cols), lambda i, j: (i == 0) & (j == x))
        foot = picker((slot, cols), lambda i, j: (i == rows + 1) & (j == x))
        strip = matmul(body, normed_ref[...]) + matmul(head, up) + matmul(foot, down)
        strips.append(strip.astype(jnp.bfloat16))
    one_ref[...] = choose(odd_col, strips[0], strips[1])
    two_ref[...] = choose(odd_col, strips[1], strips[0])


def column_strips(odd_row, odd_col, normed, row_one, row_two, slot):
    cols, channels = row_one.shape
    shapes = [(cols, channels)] * 2 + [(slot, channels)] * 2
    return pl.pallas_call(
        strips_kernel,
        in_specs=[pl.BlockSpec(memory_space=pltpu.SMEM)] * 2 + [vmem()] * 3,
        out_specs=[vmem()] * 4,
        out_shape=[jax.ShapeDtypeStruct(shape, jnp.bfloat16) for shape in shapes],
        compiler_params=pltpu.CompilerParams(vmem_limit_bytes=4 * MIB),
        name="column_strips",
    )(odd_row, odd_col, row_two, row_one, normed)


def padded_rows(tokens):
    return tokens + 16


def expand_kernel(normed_ref, weight_ref, out_ref, even_ref, odd_ref):
    tokens, tile = even_ref.shape
    width = weight_ref.shape[1]
    subs = tile // LANES

    def multiply(index, made_ref):
        lanes = pl.ds(pl.multiple_of(index * tile, tile), tile)
        made_ref[...] = matmul(normed_ref[...], weight_ref[:, lanes])

    def activate(index, made_ref):
        for sub in range(subs):
            row = (index * subs + sub) * padded_rows(tokens) + 8
            out_ref[pl.ds(pl.multiple_of(row, 8), tokens), :] = gelu_of_half(
                made_ref[:, sub * LANES : (sub + 1) * LANES]
            )

    def body(index, carry):
        multiply(2 * index + 1, odd_ref)
        activate(2 * index, even_ref)
        multiply(2 * index + 2, even_ref)
        activate(2 * index + 1, odd_ref)
        return carry

    count = width // tile
    multiply(0, even_ref)
    lax.fori_loop(0, count // 2 - 1, body, 0)
    multiply(count - 1, odd_ref)
    activate(count - 2, even_ref)
    activate(count - 1, odd_ref)


def expand(normed, w_expand):
    tokens, channels = normed.shape
    width = w_expand.shape[1]
    return pl.pallas_call(
        expand_kernel,
        in_specs=[vmem()] * 2,
        out_specs=vmem(),
        out_shape=jax.ShapeDtypeStruct((width // LANES * padded_rows(tokens), LANES), jnp.float32),
        scratch_shapes=[
            pltpu.VMEM((tokens, divisor(width // 2, 256, LANES)), jnp.float32)
        ] * 2,
        compiler_params=pltpu.CompilerParams(vmem_limit_bytes=6 * MIB),
        cost_estimate=pl.CostEstimate(
            flops=10**10,
            bytes_accessed=tokens * channels * 2 + channels * width * 2 + tokens * width * 4,
            transcendentals=tokens * width,
        ),
        name="expand",
    )(normed, w_expand)


def inner_kernel(
    expanded_ref, start_ref, depth_ref, w_project_ref, total_ref, rim_ref, even_ref, odd_ref,
    *, rows, cols, first, count,
):
    tokens = rows * cols
    tile = even_ref.shape[1]
    subs = tile // LANES
    position = lax.broadcasted_iota(jnp.int32, (8, LANES), 0)
    at_first = position == 0
    at_last = position == 7

    def clear_ends(value, low, high):
        head = jnp.where(at_first, 0.0, value[:8]) if low else value[:8]
        foot = jnp.where(at_last, 0.0, value[-8:]) if high else value[-8:]
        return jnp.concatenate([head, value[8:-8], foot], axis=0)

    def convolve(index, out_ref):
        for sub in range(subs):
            chunk = (first + index) * subs + sub
            lanes = pl.ds(pl.multiple_of(chunk * LANES, LANES), LANES)
            base = chunk * padded_rows(tokens) + 8
            here = index * subs + sub
            taps = [[0.5 * depth_ref[p, q : q + 1, lanes] for q in range(3)] for p in range(3)]
            spot = slice(sub * LANES, (sub + 1) * LANES)
            sums = {}
            for y in range(rows + 1):
                if y < rows:
                    parts = [
                        expanded_ref[pl.ds(base + (y * cols + q), cols), :] for q in (-1, 0, 1)
                    ]
                    parts[0] = clear_ends(parts[0], True, False)
                    parts[2] = clear_ends(parts[2], False, True)
                    for p in range(3):
                        target = y + 1 - p
                        if 0 <= target < rows:
                            for q in range(3):
                                term = taps[p][q] * parts[q]
                                sums[target] = sums[target] + term if target in sums else term
                if y > 0:
                    done = sums.pop(y - 1)
                    rim_ref[here, 2 * cols + y - 1 : 2 * cols + y] = done[:1]
                    rim_ref[here, 2 * cols + rows + y - 1 : 2 * cols + rows + y] = done[-1:]
                    if y in (1, rows):
                        start = 0 if y == 1 else cols
                        rim_ref[here, start : start + cols] = done
                        made = jnp.zeros_like(done)
                    else:
                        made = clear_ends(gelu_of_half(done), True, True)
                    out_ref[(y - 1) * cols : y * cols, spot] = made.astype(jnp.bfloat16)

    def project(index, in_ref, from_ref):
        piece = pl.ds(pl.multiple_of((first + index) * tile, tile), tile)
        total_ref[...] = from_ref[...] + matmul(in_ref[...], w_project_ref[piece, :])

    convolve(0, even_ref)
    project(0, even_ref, start_ref)
    convolve(1, odd_ref)

    def body(index, carry):
        convolve(2 * index, even_ref)
        project(2 * index - 1, odd_ref, total_ref)
        convolve(2 * index + 1, odd_ref)
        project(2 * index, even_ref, total_ref)
        return carry

    lax.fori_loop(1, count // 2, body, 0)
    project(count - 1, odd_ref, total_ref)


def inner(expanded, start, depth_kernel, w_project, rows, cols, first, count, tile):
    tokens, channels = start.shape
    rim = (count * tile // LANES, 2 * cols + 2 * rows, LANES)
    return pl.pallas_call(
        functools.partial(inner_kernel, rows=rows, cols=cols, first=first, count=count),
        in_specs=[vmem()] * 4,
        out_specs=[vmem()] * 2,
        out_shape=[
            jax.ShapeDtypeStruct((tokens, channels), jnp.float32),
            jax.ShapeDtypeStruct(rim, jnp.float32),
        ],
        scratch_shapes=[pltpu.VMEM((tokens, tile), jnp.bfloat16)] * 2,
        compiler_params=pltpu.CompilerParams(vmem_limit_bytes=6 * MIB),
        cost_estimate=pl.CostEstimate(
            flops=2 * 10**9 * count,
            bytes_accessed=tokens * channels * 8 + tokens * count * tile * 4,
            transcendentals=tokens * count * tile,
        ),
        name="inner",
    )(expanded, start, depth_kernel, w_project)


def rim_kernel(
    own_ref, odd_col_ref, inner_ref, *refs, rows, cols, plan, size, pieces,
):
    masks, _, sides = plan
    sent = len(outgoing_shapes(plan, size, 1))
    rim_refs, refs = refs[:pieces], refs[pieces:]
    up_ref, down_ref, one_ref, two_ref, w_expand_ref, depth_ref, w_project_ref, perm_ref = refs[:8]
    mixed_ref, slab_refs = refs[8], refs[9 : 9 + sent]
    halo_ref, active_ref, normed_ref, grouped_ref = refs[9 + sent :]
    tokens = rows * cols
    width = w_expand_ref.shape[1]
    tile = divisor(width, 512, LANES)
    subs = tile // LANES
    slot = one_ref.shape[0]
    left_start, right_start = 2 * cols, 2 * cols + slot

    odd_col = odd_col_ref[0]
    left = choose(odd_col, one_ref[...], two_ref[...])
    right = choose(odd_col, two_ref[...], one_ref[...])
    edges = jnp.concatenate([up_ref[...], down_ref[...], left, right], axis=0)

    def expand_halo(index):
        made = gelu_of_half(matmul(edges, w_expand_ref[:, index * tile : (index + 1) * tile]))
        for sub in range(subs):
            halo_ref[index * subs + sub] = made[:, sub * LANES : (sub + 1) * LANES]

    position = lax.broadcasted_iota(jnp.int32, (cols, LANES), 0)
    at_first = position == 0
    at_last = position == cols - 1

    def activate(chunk, here, sums_ref):
        lanes = slice(chunk * LANES, (chunk + 1) * LANES)
        taps = [[0.5 * depth_ref[p, q : q + 1, lanes] for q in range(3)] for p in range(3)]
        beside = []
        for q, start in ((0, left_start), (2, right_start)):
            beside.append(
                sum(taps[p][q] * halo_ref[chunk, start + p : start + p + rows] for p in range(3))
            )
        made = []
        for p, start, y in ((0, 0, 0), (2, cols, rows - 1)):
            row = halo_ref[chunk, start : start + cols]
            before = jnp.where(at_first, beside[0][y : y + 1], taps[p][0] * pltpu.roll(row, 1, 0))
            after = jnp.where(
                at_last, beside[1][y : y + 1], taps[p][2] * pltpu.roll(row, cols - 1, 0)
            )
            made.append(sums_ref[here, start : start + cols] + before + taps[p][1] * row + after)
        for index in range(2):
            start = 2 * cols + index * rows
            made.append(sums_ref[here, start : start + rows] + beside[index])
        active_ref[:, lanes] = gelu_of_half(jnp.concatenate(made, axis=0)).astype(jnp.bfloat16)

    spots = [(ref, here) for ref in rim_refs for here in range(ref.shape[0])]
    expand_halo(0)
    for index in range(width // tile):
        if (index + 1) * tile < width:
            expand_halo(index + 1)
        for chunk in range(index * subs, (index + 1) * subs):
            activate(chunk, spots[chunk][1], spots[chunk][0])

    mixed_ref[...] = inner_ref[...]
    branch = matmul(active_ref[...], w_project_ref[...])
    mixed_ref[:cols, :] += branch[:cols]
    mixed_ref[tokens - cols :, :] += branch[cols : 2 * cols]
    for y in range(1, rows - 1):
        for index, x in ((0, 0), (1, cols - 1)):
            spot = y * cols + x
            start = 2 * cols + index * rows + y
            mixed_ref[spot : spot + 1, :] += branch[start : start + 1]

    step = divisor(tokens, 128, 16)
    for start in range(0, tokens, step):
        piece = slice(start, start + step)
        normed_ref[piece, :] = layer_norm(mixed_ref[piece, :]).astype(jnp.bfloat16)
    grouped_ref[...] = matmul(perm_ref[...], normed_ref[...]).astype(jnp.bfloat16)
    for index, mask in enumerate(masks):
        for side in range(sides):
            start = pl.multiple_of((own_ref[0] ^ (mask | side)) * size, 16)
            write_block(
                plan, slab_refs, index, side, slice(None), grouped_ref[pl.ds(start, size), :]
            )


def rim(
    own, odd_col, plan, size, total, rims, up, down, one, two, w_expand, depth_kernel, w_project, perm,
    rows, cols,
):
    tokens, channels = total.shape
    width = w_expand.shape[1]
    halo_rows = 2 * cols + 2 * one.shape[0]
    sent = outgoing_shapes(plan, size, channels)
    return pl.pallas_call(
        functools.partial(
            rim_kernel, rows=rows, cols=cols, plan=plan, size=size, pieces=len(rims)
        ),
        in_specs=[pl.BlockSpec(memory_space=pltpu.SMEM)] * 2 + [vmem()] * (9 + len(rims)),
        out_specs=[vmem()] * (1 + len(sent)),
        out_shape=[jax.ShapeDtypeStruct((tokens, channels), jnp.float32)]
        + [jax.ShapeDtypeStruct(shape, jnp.bfloat16) for shape in sent],
        scratch_shapes=[
            pltpu.VMEM((width // LANES, halo_rows, LANES), jnp.float32),
            pltpu.VMEM((2 * cols + 2 * rows, width), jnp.bfloat16),
            pltpu.VMEM((tokens, channels), jnp.bfloat16),
            pltpu.VMEM((tokens, channels), jnp.bfloat16),
        ],
        compiler_params=pltpu.CompilerParams(vmem_limit_bytes=8 * MIB),
        cost_estimate=pl.CostEstimate(
            flops=2 * halo_rows * channels * width * 2 + 2 * tokens * tokens * channels,
            bytes_accessed=tokens * channels * 10 + 4 * channels * width,
            transcendentals=2 * halo_rows * width,
        ),
        name="rim",
    )(own, odd_col, total, *rims, up, down, one, two, w_expand, depth_kernel, w_project, perm)


def identity(size):
    row = lax.broadcasted_iota(jnp.int32, (size, size), 0)
    column = lax.broadcasted_iota(jnp.int32, (size, size), 1)
    return jnp.where(row == column, 1.0, 0.0).astype(jnp.bfloat16)


def gather_blocks(plan, refs, blocks, sets):
    members = refs[0].shape[1] // sets
    return jnp.concatenate(
        [
            read_block(plan, refs, index, side, slice(s * members, (s + 1) * members))
            for s in range(sets)
            for index, side in blocks
        ],
        axis=0,
    )


def project_kernel(*refs, plan, sets):
    in_refs, weight_ref, out_ref = refs[:-2], refs[-2], refs[-1]
    block = gather_blocks(plan, in_refs, split_blocks(plan)[0], sets)
    out_ref[...] = matmul(block, weight_ref[...]).astype(jnp.bfloat16)


def project(plan, incoming, w_qkv, sets):
    soon = split_blocks(plan)[0]
    _, size, channels = incoming[0].shape
    masks, late, _ = plan
    there = [*range(late, len(masks) - 1 - late), len(masks) - 1, len(masks) + late]
    filled = [array if index in there else incoming[late] for index, array in enumerate(incoming)]
    return pl.pallas_call(
        functools.partial(project_kernel, plan=plan, sets=sets),
        in_specs=[vmem()] * (len(filled) + 1),
        out_specs=vmem(),
        out_shape=jax.ShapeDtypeStruct((len(soon) * size, w_qkv.shape[1]), jnp.bfloat16),
        compiler_params=pltpu.CompilerParams(vmem_limit_bytes=4 * MIB),
        cost_estimate=pl.CostEstimate(
            flops=2 * len(soon) * size * channels * w_qkv.shape[1],
            bytes_accessed=2 * w_qkv.size + 8 * len(soon) * size * channels,
            transcendentals=0,
        ),
        name="project",
    )(*filled, w_qkv)


def attend_kernel(*refs, plan, sets, came):
    masks, _, sides = plan
    slabs = len(masks)
    _, size, channels = refs[0].shape
    soon, rest = split_blocks(plan)
    in_refs, weight_ref, out_refs = refs[:came], refs[came], refs[came + 1 : -6]
    if soon:
        soon_ref, out_refs = out_refs[0], out_refs[1:]
    query_ref, key_ref, value_ref, turned_ref, even_ref, odd_ref = refs[-6:]
    members = size // sets
    count = slabs * sides * members
    head_width = channels // HEADS
    group_heads = LANES // head_width
    groups = channels // LANES
    factor = math.log2(math.e) / math.sqrt(head_width)
    lane = lax.broadcasted_iota(jnp.int32, (1, LANES), 1)
    masks = [
        jnp.where((lane >= j * head_width) & (lane < (j + 1) * head_width), 1.0, 0.0).astype(
            jnp.bfloat16
        )
        for j in range(group_heads)
    ]
    turn_values = identity(channels)
    block = gather_blocks(plan, in_refs, rest, sets)
    projected = matmul(block, weight_ref[...]).astype(jnp.bfloat16)
    for s in range(sets):
        near, far = len(soon) * members, len(rest) * members
        qkv = projected[s * far : (s + 1) * far]
        if soon:
            qkv = jnp.concatenate([soon_ref[s * near : (s + 1) * near, :], qkv], axis=0)
        values = matmul_nt(turn_values, qkv[:, 2 * channels :]).astype(jnp.bfloat16)
        for group in range(groups):
            spot = group * LANES
            query_ref[s * groups + group] = qkv[:, spot : spot + LANES]
            key_ref[s * groups + group] = qkv[:, channels + spot : channels + spot + LANES]
            for j in range(group_heads):
                head = (group * group_heads + j) * head_width
                value_ref[s * groups + group, j, :head_width] = values[head : head + head_width]
                value_ref[s * groups + group, j, head_width:] = jnp.ones((16, count), jnp.bfloat16)

    def scores(index, out):
        keys = key_ref[index]
        stacked = jnp.concatenate([keys * mask for mask in masks], axis=0)
        out[...] = matmul_nt(stacked, query_ref[index])

    def weigh(index, scores_ref):
        for j in range(group_heads):
            part = scores_ref[j * count : (j + 1) * count]
            highest = jnp.max(part, axis=0, keepdims=True)
            raised = jnp.exp2((part - highest) * factor).astype(jnp.bfloat16)
            product = matmul(value_ref[index, j], raised)
            scale = 1.0 / product[head_width : head_width + 1]
            turned_ref[index, j * head_width : (j + 1) * head_width] = (
                product[:head_width] * scale
            ).astype(jnp.bfloat16)

    total = sets * groups
    scores(0, even_ref)

    def body(pair, carry):
        scores(2 * pair + 1, odd_ref)
        weigh(2 * pair, even_ref)
        scores(jnp.minimum(2 * pair + 2, total - 1), even_ref)
        weigh(2 * pair + 1, odd_ref)
        return carry

    lax.fori_loop(0, total // 2, body, 0)
    turn_tokens = identity(count)
    for s in range(sets):
        turned = turned_ref[s * groups : (s + 1) * groups].reshape(channels, count)
        attended = matmul_nt(turn_tokens, turned).astype(jnp.bfloat16)
        for number, (index, side) in enumerate(soon + rest):
            write_block(
                plan, out_refs, index, side, slice(s * members, (s + 1) * members),
                attended[number * members : (number + 1) * members],
            )


def attend(plan, incoming, w_qkv, sets):
    masks, _, sides = plan
    _, size, channels = incoming[0].shape
    count = len(masks) * sides * size // sets
    sent = outgoing_shapes(plan, size, channels)
    soon = [project(plan, incoming, w_qkv, sets)] if split_blocks(plan)[0] else []
    head_width = channels // HEADS
    group_heads = LANES // head_width
    total = sets * channels // LANES
    return pl.pallas_call(
        functools.partial(attend_kernel, plan=plan, sets=sets, came=len(incoming)),
        in_specs=[vmem()] * (len(incoming) + 1 + len(soon)),
        out_specs=[vmem()] * len(sent),
        out_shape=[jax.ShapeDtypeStruct(shape, jnp.bfloat16) for shape in sent],
        scratch_shapes=[
            pltpu.VMEM((total, count, LANES), jnp.bfloat16),
            pltpu.VMEM((total, count, LANES), jnp.bfloat16),
            pltpu.VMEM((total, group_heads, head_width + 16, count), jnp.bfloat16),
            pltpu.VMEM((total, LANES, count), jnp.bfloat16),
            pltpu.VMEM((group_heads * count, count), jnp.float32),
            pltpu.VMEM((group_heads * count, count), jnp.float32),
        ],
        compiler_params=pltpu.CompilerParams(vmem_limit_bytes=10 * MIB),
        cost_estimate=pl.CostEstimate(
            flops=sets * (2 * count * channels * channels * 3 + 4 * count * count * channels),
            bytes_accessed=4 * sets * count * channels + 6 * channels * channels,
            transcendentals=sets * HEADS * count * count,
        ),
        name="attend",
    )(*incoming, w_qkv, *soon)


def finish_kernel(own_ref, *refs, plan):
    masks, _, sides = plan
    in_refs, rest = refs[:-7], refs[-7:]
    back_ref, weight_ref, mixed_ref, out_ref, attended_ref, made_ref, sent = rest
    tokens = mixed_ref.shape[0]
    size = in_refs[0].shape[1]
    for index, mask in enumerate(masks):
        for side in range(sides):
            start = pl.multiple_of((own_ref[0] ^ (mask | side)) * size, 16)
            attended_ref[pl.ds(start, size), :] = read_block(
                plan, in_refs, index, side, slice(None)
            )
    step = made_ref.shape[1]
    copies = []
    for index, start in enumerate(range(0, tokens, step)):
        rows = slice(start, start + step)
        restored = matmul(back_ref[rows, :], attended_ref[...]).astype(jnp.bfloat16)
        made_ref[index] = mixed_ref[rows, :] + matmul(restored, weight_ref[...])
        copy = pltpu.make_async_copy(
            made_ref.at[index], out_ref.at[pl.ds(start, step)], sent.at[index]
        )
        copy.start()
        copies.append(copy)
    for copy in copies:
        copy.wait()


def finish(own, plan, incoming, back, w_out, mixed):
    tokens, channels = mixed.shape
    step = divisor(tokens, 256, 16)
    return pl.pallas_call(
        functools.partial(finish_kernel, plan=plan),
        in_specs=[pl.BlockSpec(memory_space=pltpu.SMEM)] + [vmem()] * (len(incoming) + 3),
        out_specs=pl.BlockSpec(memory_space=pltpu.HBM),
        out_shape=jax.ShapeDtypeStruct((tokens, channels), jnp.float32),
        scratch_shapes=[
            pltpu.VMEM((tokens, channels), jnp.bfloat16),
            pltpu.VMEM((tokens // step, step, channels), jnp.float32),
            pltpu.SemaphoreType.DMA((tokens // step,)),
        ],
        compiler_params=pltpu.CompilerParams(vmem_limit_bytes=6 * MIB),
        name="finish",
    )(own, *incoming, back, w_out, mixed)


def swap_pairs(edge, axis, start):
    pairs = [(i, i + 1) for i in range(start, lax.axis_size(axis) - 1, 2)]
    return lax.ppermute(edge, axis, pairs + [(b, a) for a, b in pairs])


def exchange_plan(row_devices, col_devices):
    devices = row_devices * col_devices
    crossing = list(range(devices - 2, devices // 2 - 1, -2))
    others = list(range(devices // 2 - 2, 0, -2))
    masks = crossing[:-1] + others[:-1] + crossing[-1:] + others[-1:] + [0]
    return masks, 2, 2


def split_blocks(plan):
    masks, late, sides = plan
    blocks = [(index, side) for index in range(len(masks)) for side in range(sides)]
    if sides == 1:
        return [], blocks
    soon = [*range(late, len(masks) - 1 - late), len(masks) - 1]
    return [b for b in blocks if b[0] in soon], [b for b in blocks if b[0] not in soon]


def outgoing_shapes(plan, size, channels):
    masks, late, sides = plan
    if sides == 1:
        return [(1, size, channels)]
    early = len(masks) - 1 - late
    return [(2, size, channels)] * late + [
        (1, size, channels), (early + 1, size, channels), (early, size, channels)
    ]


def write_block(plan, refs, index, side, rows, value):
    masks, late, sides = plan
    if sides == 1:
        refs[0][0, rows] = value
    elif index < late:
        refs[index][side, rows] = value
    elif index == len(masks) - 1:
        refs[late + side][0, rows] = value
    elif side == 0:
        refs[late + 2][index - late, rows] = value
    else:
        refs[late + 1][index - late + 1, rows] = value


def read_block(plan, refs, index, side, rows):
    masks, late, sides = plan
    if sides == 1:
        return refs[0][0, rows]
    if index < late:
        return refs[index + side * len(masks)][side, rows]
    if index == len(masks) - 1:
        return refs[index + side * (late + 1)][0, rows]
    return refs[index][side, rows]


def join_kernel(own_ref, swapped_ref, *out_refs):
    for index, out_ref in enumerate(out_refs):
        out_ref[0] = own_ref[index]
        out_ref[1] = swapped_ref[index + 1]


def join(own, swapped):
    early, size, channels = own.shape
    return pl.pallas_call(
        join_kernel,
        in_specs=[vmem()] * 2,
        out_specs=[vmem()] * early,
        out_shape=[jax.ShapeDtypeStruct((2, size, channels), own.dtype)] * early,
        compiler_params=pltpu.CompilerParams(vmem_limit_bytes=2 * MIB),
        name="join",
    )(own, swapped)


def trade(plan, outgoing):
    masks, late, _ = plan
    devices = lax.axis_size("row") * lax.axis_size("col")

    def swap(slab, mask):
        return lax.ppermute(slab, ("row", "col"), [(i, i ^ mask) for i in range(devices)])

    slabs, (kept, passed, own) = outgoing[:late], outgoing[late:]
    swapped = swap(passed, 1)
    first = [swap(slab, mask) for slab, mask in zip(slabs, masks)]
    rest = [swap(slab, mask) for slab, mask in zip(join(own, swapped), masks[late:-1])]
    tied = lax.optimization_barrier((*first, *rest[:-late]))
    first, rest = tied[:late], [*tied[late:], *rest[-late:]]
    return [*first, *rest, kept, *[swap(slab, 1) for slab in first], swapped]


def trade_all(slabs, sets, members, outward):
    axes = ("row", "col")
    channels = slabs[0].shape[-1]
    block = slabs[0].reshape(-1, channels)
    devices = block.shape[0] // (sets * members)
    if not outward:
        block = block.reshape(sets, devices, members, channels).transpose(1, 0, 2, 3)
    block = block.reshape(devices, sets * members, channels)
    block = lax.all_to_all(block, axes, 0, 0, tiled=True)
    if outward:
        block = block.reshape(devices, sets, members, channels).transpose(1, 0, 2, 3)
    return [block.reshape(1, -1, channels)]


def grouping(rows, cols, blocks_rows, blocks_cols):
    order = np.arange(rows * cols).reshape(
        blocks_rows, rows // blocks_rows, blocks_cols, cols // blocks_cols
    )
    order = order.transpose(1, 3, 0, 2).reshape(-1)
    matrix = np.zeros((order.size, order.size), np.float32)
    matrix[np.arange(order.size), order] = 1.0
    return matrix


def shards(field, w_expand, depth_kernel, w_project, w_qkv, w_out):
    rows, cols, channels = field.shape
    tokens = rows * cols
    row_devices = lax.axis_size("row")
    col_devices = lax.axis_size("col")
    devices = row_devices * col_devices
    blocks_rows = GRID // row_devices
    blocks_cols = GRID // col_devices
    members = blocks_rows * blocks_cols
    sets_local = tokens // members // devices
    matrix = grouping(rows, cols, blocks_rows, blocks_cols)
    perm = jnp.asarray(matrix, jnp.bfloat16)
    back = jnp.asarray(matrix.T, jnp.bfloat16)

    flat = field.reshape(tokens, channels)
    pairwise = 8 <= devices <= 16 and devices & (devices - 1) == 0 and col_devices % 2 == 0
    plan = exchange_plan(row_devices, col_devices) if pairwise else ([0], 0, 1)
    row, col = lax.axis_index("row"), lax.axis_index("col")
    own = (row * col_devices + col if pairwise else row * 0).reshape(1)
    odd_row, odd_col = (row % 2).reshape(1), (col % 2).reshape(1)

    own, odd_row, odd_col, top, bottom = lax.optimization_barrier(
        (own, odd_row, odd_col, field[0], field[rows - 1])
    )
    one, two = row_edges(odd_row, top, bottom)
    two, one = swap_pairs(two, "row", 1), swap_pairs(one, "row", 0)
    normed = half_norm_of(flat)
    expanded = expand(normed, w_expand)
    tile = divisor(w_expand.shape[1] // 2, 256, LANES)
    count = w_expand.shape[1] // tile
    early = 2
    total, rim_one = inner(
        expanded, flat, depth_kernel, w_project, rows, cols, 0, early, tile
    )
    two, one, normed, expanded, total, rim_one = lax.optimization_barrier(
        (two, one, normed, expanded, total, rim_one)
    )
    up, down, one, two = column_strips(odd_row, odd_col, normed, one, two, round_up(rows + 2, 16))
    one, two = swap_pairs(one, "col", 0), swap_pairs(two, "col", 1)
    total, rim_two = inner(
        expanded, total, depth_kernel, w_project, rows, cols, early, count - early, tile
    )

    size = tokens // (len(plan[0]) * plan[2])
    mixed, *outgoing = rim(
        own, odd_col, plan, size, total, [rim_one, rim_two], up, down, one, two, w_expand,
        depth_kernel, w_project, perm, rows, cols,
    )

    def route(outgoing, outward):
        if pairwise:
            return trade(plan, outgoing)
        return trade_all(outgoing, sets_local, members, outward)

    outgoing = attend(plan, route(outgoing, True), w_qkv, sets_local)
    final = finish(own, plan, route(outgoing, False), back, w_out, mixed)
    return final.reshape(rows, cols, channels)


def solution(mesh):
    return jax.shard_map(
        shards,
        mesh=mesh,
        in_specs=(P(("field", "row"), "col", None), P(), P(), P(), P(), P()),
        out_specs=P(("field", "row"), "col", None),
        check_vma=False,
    )
```

```python
import functools
import math

import jax
import jax.numpy as jnp
import numpy as np
from jax import lax
from jax.experimental import pallas as pl
from jax.experimental.pallas import tpu as pltpu
from jax.sharding import PartitionSpec as P

HEADS = 16
GRID = 16
LANES = 128
MIB = 1024 * 1024
NT = (((1,), (1,)), ((), ()))


def layer_norm(inputs):
    average = jnp.mean(inputs, axis=-1, keepdims=True)
    centred = inputs - average
    variance = jnp.mean(centred * centred, axis=-1, keepdims=True)
    return centred * lax.rsqrt(variance + 1e-05)


def gelu_of_half(half):
    scale = math.sqrt(2.0 / math.pi)
    inner = half * (2.0 * scale + (8.0 * scale * 0.044715) * (half * half))
    return half + half * jnp.tanh(inner)


def matmul(a, b):
    return jnp.dot(a, b, preferred_element_type=jnp.float32)


def matmul_nt(a, b):
    return lax.dot_general(a, b, NT, preferred_element_type=jnp.float32)


def divisor(size, most, unit):
    best = size
    for piece in range(unit, most + 1, unit):
        if size % piece == 0:
            best = piece
    return best


def round_up(size, unit):
    return -(-size // unit) * unit


def vmem():
    return pl.BlockSpec(memory_space=pltpu.VMEM)


def half_norm(inputs):
    return (layer_norm(inputs) * 0.5).astype(jnp.bfloat16)


def half_norm_kernel(in_ref, out_ref):
    rows = in_ref.shape[0]
    step = divisor(rows, 128, 16)
    for start in range(0, rows, step):
        out_ref[start : start + step, :] = half_norm(in_ref[start : start + step, :])


def half_norm_of(inputs):
    return pl.pallas_call(
        half_norm_kernel,
        in_specs=[vmem()],
        out_specs=vmem(),
        out_shape=jax.ShapeDtypeStruct(inputs.shape, jnp.bfloat16),
        compiler_params=pltpu.CompilerParams(vmem_limit_bytes=4 * MIB),
        cost_estimate=pl.CostEstimate(
            flops=10**9, bytes_accessed=6 * inputs.size, transcendentals=inputs.shape[0]
        ),
        name="half_norm",
    )(inputs)


def choose(condition, one, two):
    flags = jnp.full((one.shape[0], 1), condition, jnp.int32) == 1
    return jnp.where(flags, one.astype(jnp.float32), two.astype(jnp.float32)).astype(one.dtype)


def edges_kernel(odd_row_ref, top_ref, bottom_ref, one_ref, two_ref):
    odd = odd_row_ref[0]
    top, bottom = half_norm(top_ref[...]), half_norm(bottom_ref[...])
    one_ref[...] = choose(odd, top, bottom)
    two_ref[...] = choose(odd, bottom, top)


def row_edges(odd_row, top, bottom):
    return pl.pallas_call(
        edges_kernel,
        in_specs=[pl.BlockSpec(memory_space=pltpu.SMEM)] + [vmem()] * 2,
        out_specs=[vmem()] * 2,
        out_shape=[jax.ShapeDtypeStruct(top.shape, jnp.bfloat16)] * 2,
        compiler_params=pltpu.CompilerParams(vmem_limit_bytes=4 * MIB),
        cost_estimate=pl.CostEstimate(
            flops=10**10, bytes_accessed=12 * top.size, transcendentals=2 * top.shape[0]
        ),
        name="row_edges",
    )(odd_row, top, bottom)


def picker(shape, pick):
    row = lax.broadcasted_iota(jnp.int32, shape, 0)
    column = lax.broadcasted_iota(jnp.int32, shape, 1)
    return jnp.where(pick(row, column), 1.0, 0.0).astype(jnp.bfloat16)


def strips_kernel(
    odd_row_ref, odd_col_ref, normed_ref, row_one_ref, row_two_ref, up_ref, down_ref, one_ref, two_ref
):
    tokens = normed_ref.shape[0]
    cols = up_ref.shape[0]
    rows = tokens // cols
    slot = one_ref.shape[0]
    odd_row, odd_col = odd_row_ref[0], odd_col_ref[0]
    up = choose(odd_row, row_one_ref[...], row_two_ref[...])
    down = choose(odd_row, row_two_ref[...], row_one_ref[...])
    up_ref[...] = up
    down_ref[...] = down
    strips = []
    for x in (0, cols - 1):
        body = picker(
            (slot, tokens), lambda i, j: (i >= 1) & (i <= rows) & (j == (i - 1) * cols + x)
        )
        head = picker((slot, cols), lambda i, j: (i == 0) & (j == x))
        foot = picker((slot, cols), lambda i, j: (i == rows + 1) & (j == x))
        strip = matmul(body, normed_ref[...]) + matmul(head, up) + matmul(foot, down)
        strips.append(strip.astype(jnp.bfloat16))
    one_ref[...] = choose(odd_col, strips[0], strips[1])
    two_ref[...] = choose(odd_col, strips[1], strips[0])


def column_strips(odd_row, odd_col, normed, row_one, row_two, slot):
    cols, channels = row_one.shape
    shapes = [(cols, channels)] * 2 + [(slot, channels)] * 2
    return pl.pallas_call(
        strips_kernel,
        in_specs=[pl.BlockSpec(memory_space=pltpu.SMEM)] * 2 + [vmem()] * 3,
        out_specs=[vmem()] * 4,
        out_shape=[jax.ShapeDtypeStruct(shape, jnp.bfloat16) for shape in shapes],
        compiler_params=pltpu.CompilerParams(vmem_limit_bytes=4 * MIB),
        name="column_strips",
    )(odd_row, odd_col, normed, row_one, row_two)


def padded_rows(tokens):
    return tokens + 16


def expand_kernel(normed_ref, weight_ref, out_ref, even_ref, odd_ref):
    tokens, tile = even_ref.shape
    width = weight_ref.shape[1]
    subs = tile // LANES

    def multiply(index, made_ref):
        lanes = pl.ds(pl.multiple_of(index * tile, tile), tile)
        made_ref[...] = matmul(normed_ref[...], weight_ref[:, lanes])

    def activate(index, made_ref):
        for sub in range(subs):
            row = (index * subs + sub) * padded_rows(tokens) + 8
            out_ref[pl.ds(pl.multiple_of(row, 8), tokens), :] = gelu_of_half(
                made_ref[:, sub * LANES : (sub + 1) * LANES]
            )

    def body(index, carry):
        multiply(2 * index + 1, odd_ref)
        activate(2 * index, even_ref)
        multiply(2 * index + 2, even_ref)
        activate(2 * index + 1, odd_ref)
        return carry

    count = width // tile
    multiply(0, even_ref)
    lax.fori_loop(0, count // 2 - 1, body, 0)
    multiply(count - 1, odd_ref)
    activate(count - 2, even_ref)
    activate(count - 1, odd_ref)


def expand(normed, w_expand):
    tokens, channels = normed.shape
    width = w_expand.shape[1]
    return pl.pallas_call(
        expand_kernel,
        in_specs=[vmem()] * 2,
        out_specs=vmem(),
        out_shape=jax.ShapeDtypeStruct((width // LANES * padded_rows(tokens), LANES), jnp.float32),
        scratch_shapes=[
            pltpu.VMEM((tokens, divisor(width // 2, 256, LANES)), jnp.float32)
        ] * 2,
        compiler_params=pltpu.CompilerParams(vmem_limit_bytes=6 * MIB),
        cost_estimate=pl.CostEstimate(
            flops=10**10,
            bytes_accessed=tokens * channels * 2 + channels * width * 2 + tokens * width * 4,
            transcendentals=tokens * width,
        ),
        name="expand",
    )(normed, w_expand)


def inner_kernel(
    expanded_ref, start_ref, depth_ref, w_project_ref, total_ref, rim_ref, even_ref, odd_ref,
    *, rows, cols, first, count,
):
    tokens = rows * cols
    tile = even_ref.shape[1]
    subs = tile // LANES
    position = lax.broadcasted_iota(jnp.int32, (8, LANES), 0)
    at_first = position == 0
    at_last = position == 7

    def clear_ends(value, low, high):
        head = jnp.where(at_first, 0.0, value[:8]) if low else value[:8]
        foot = jnp.where(at_last, 0.0, value[-8:]) if high else value[-8:]
        return jnp.concatenate([head, value[8:-8], foot], axis=0)

    def convolve(index, out_ref):
        for sub in range(subs):
            chunk = (first + index) * subs + sub
            lanes = pl.ds(pl.multiple_of(chunk * LANES, LANES), LANES)
            base = chunk * padded_rows(tokens) + 8
            here = index * subs + sub
            taps = [[0.5 * depth_ref[p, q : q + 1, lanes] for q in range(3)] for p in range(3)]
            spot = slice(sub * LANES, (sub + 1) * LANES)
            sums = {}
            for y in range(rows + 1):
                if y < rows:
                    parts = [
                        expanded_ref[pl.ds(base + (y * cols + q), cols), :] for q in (-1, 0, 1)
                    ]
                    parts[0] = clear_ends(parts[0], True, False)
                    parts[2] = clear_ends(parts[2], False, True)
                    for p in range(3):
                        target = y + 1 - p
                        if 0 <= target < rows:
                            for q in range(3):
                                term = taps[p][q] * parts[q]
                                sums[target] = sums[target] + term if target in sums else term
                if y > 0:
                    done = sums.pop(y - 1)
                    rim_ref[here, 2 * cols + y - 1 : 2 * cols + y] = done[:1]
                    rim_ref[here, 2 * cols + rows + y - 1 : 2 * cols + rows + y] = done[-1:]
                    if y in (1, rows):
                        start = 0 if y == 1 else cols
                        rim_ref[here, start : start + cols] = done
                        made = jnp.zeros_like(done)
                    else:
                        made = clear_ends(gelu_of_half(done), True, True)
                    out_ref[(y - 1) * cols : y * cols, spot] = made.astype(jnp.bfloat16)

    def project(index, in_ref, from_ref):
        piece = pl.ds(pl.multiple_of((first + index) * tile, tile), tile)
        total_ref[...] = from_ref[...] + matmul(in_ref[...], w_project_ref[piece, :])

    convolve(0, even_ref)
    project(0, even_ref, start_ref)
    convolve(1, odd_ref)

    def body(index, carry):
        convolve(2 * index, even_ref)
        project(2 * index - 1, odd_ref, total_ref)
        convolve(2 * index + 1, odd_ref)
        project(2 * index, even_ref, total_ref)
        return carry

    lax.fori_loop(1, count // 2, body, 0)
    project(count - 1, odd_ref, total_ref)


def inner(expanded, start, depth_kernel, w_project, rows, cols, first, count, tile):
    tokens, channels = start.shape
    rim = (count * tile // LANES, 2 * cols + 2 * rows, LANES)
    return pl.pallas_call(
        functools.partial(inner_kernel, rows=rows, cols=cols, first=first, count=count),
        in_specs=[vmem()] * 4,
        out_specs=[vmem()] * 2,
        out_shape=[
            jax.ShapeDtypeStruct((tokens, channels), jnp.float32),
            jax.ShapeDtypeStruct(rim, jnp.float32),
        ],
        scratch_shapes=[pltpu.VMEM((tokens, tile), jnp.bfloat16)] * 2,
        compiler_params=pltpu.CompilerParams(vmem_limit_bytes=6 * MIB),
        cost_estimate=pl.CostEstimate(
            flops=2 * 10**9 * count,
            bytes_accessed=tokens * channels * 8 + tokens * count * tile * 4,
            transcendentals=tokens * count * tile,
        ),
        name="inner",
    )(expanded, start, depth_kernel, w_project)


def rim_kernel(
    own_ref, odd_col_ref, inner_ref, *refs, rows, cols, plan, size, pieces,
):
    masks, _, sides = plan
    sent = len(outgoing_shapes(plan, size, 1))
    rim_refs, refs = refs[:pieces], refs[pieces:]
    up_ref, down_ref, one_ref, two_ref, w_expand_ref, depth_ref, w_project_ref, perm_ref = refs[:8]
    mixed_ref, slab_refs = refs[8], refs[9 : 9 + sent]
    halo_ref, active_ref, normed_ref, grouped_ref = refs[9 + sent :]
    tokens = rows * cols
    width = w_expand_ref.shape[1]
    tile = divisor(width, 512, LANES)
    subs = tile // LANES
    slot = one_ref.shape[0]
    left_start, right_start = 2 * cols, 2 * cols + slot

    odd_col = odd_col_ref[0]
    left = choose(odd_col, one_ref[...], two_ref[...])
    right = choose(odd_col, two_ref[...], one_ref[...])
    edges = jnp.concatenate([up_ref[...], down_ref[...], left, right], axis=0)

    def expand_halo(index):
        made = gelu_of_half(matmul(edges, w_expand_ref[:, index * tile : (index + 1) * tile]))
        for sub in range(subs):
            halo_ref[index * subs + sub] = made[:, sub * LANES : (sub + 1) * LANES]

    position = lax.broadcasted_iota(jnp.int32, (cols, LANES), 0)
    at_first = position == 0
    at_last = position == cols - 1

    def activate(chunk, here, sums_ref):
        lanes = slice(chunk * LANES, (chunk + 1) * LANES)
        taps = [[0.5 * depth_ref[p, q : q + 1, lanes] for q in range(3)] for p in range(3)]
        beside = []
        for q, start in ((0, left_start), (2, right_start)):
            beside.append(
                sum(taps[p][q] * halo_ref[chunk, start + p : start + p + rows] for p in range(3))
            )
        made = []
        for p, start, y in ((0, 0, 0), (2, cols, rows - 1)):
            row = halo_ref[chunk, start : start + cols]
            before = jnp.where(at_first, beside[0][y : y + 1], taps[p][0] * pltpu.roll(row, 1, 0))
            after = jnp.where(
                at_last, beside[1][y : y + 1], taps[p][2] * pltpu.roll(row, cols - 1, 0)
            )
            made.append(sums_ref[here, start : start + cols] + before + taps[p][1] * row + after)
        for index in range(2):
            start = 2 * cols + index * rows
            made.append(sums_ref[here, start : start + rows] + beside[index])
        active_ref[:, lanes] = gelu_of_half(jnp.concatenate(made, axis=0)).astype(jnp.bfloat16)

    spots = [(ref, here) for ref in rim_refs for here in range(ref.shape[0])]
    expand_halo(0)
    for index in range(width // tile):
        if (index + 1) * tile < width:
            expand_halo(index + 1)
        for chunk in range(index * subs, (index + 1) * subs):
            activate(chunk, spots[chunk][1], spots[chunk][0])

    mixed_ref[...] = inner_ref[...]
    branch = matmul(active_ref[...], w_project_ref[...])
    mixed_ref[:cols, :] += branch[:cols]
    mixed_ref[tokens - cols :, :] += branch[cols : 2 * cols]
    for y in range(1, rows - 1):
        for index, x in ((0, 0), (1, cols - 1)):
            spot = y * cols + x
            start = 2 * cols + index * rows + y
            mixed_ref[spot : spot + 1, :] += branch[start : start + 1]

    step = divisor(tokens, 128, 16)
    for start in range(0, tokens, step):
        piece = slice(start, start + step)
        normed_ref[piece, :] = layer_norm(mixed_ref[piece, :]).astype(jnp.bfloat16)
    grouped_ref[...] = matmul(perm_ref[...], normed_ref[...]).astype(jnp.bfloat16)
    for index, mask in enumerate(masks):
        for side in range(sides):
            start = pl.multiple_of((own_ref[0] ^ (mask | side)) * size, 16)
            write_block(
                plan, slab_refs, index, side, slice(None), grouped_ref[pl.ds(start, size), :]
            )


def rim(
    own, odd_col, plan, size, total, rims, up, down, one, two, w_expand, depth_kernel, w_project, perm,
    rows, cols,
):
    tokens, channels = total.shape
    width = w_expand.shape[1]
    halo_rows = 2 * cols + 2 * one.shape[0]
    sent = outgoing_shapes(plan, size, channels)
    return pl.pallas_call(
        functools.partial(
            rim_kernel, rows=rows, cols=cols, plan=plan, size=size, pieces=len(rims)
        ),
        in_specs=[pl.BlockSpec(memory_space=pltpu.SMEM)] * 2 + [vmem()] * (9 + len(rims)),
        out_specs=[vmem()] * (1 + len(sent)),
        out_shape=[jax.ShapeDtypeStruct((tokens, channels), jnp.float32)]
        + [jax.ShapeDtypeStruct(shape, jnp.bfloat16) for shape in sent],
        scratch_shapes=[
            pltpu.VMEM((width // LANES, halo_rows, LANES), jnp.float32),
            pltpu.VMEM((2 * cols + 2 * rows, width), jnp.bfloat16),
            pltpu.VMEM((tokens, channels), jnp.bfloat16),
            pltpu.VMEM((tokens, channels), jnp.bfloat16),
        ],
        compiler_params=pltpu.CompilerParams(vmem_limit_bytes=8 * MIB),
        cost_estimate=pl.CostEstimate(
            flops=2 * halo_rows * channels * width * 2 + 2 * tokens * tokens * channels,
            bytes_accessed=tokens * channels * 10 + 4 * channels * width,
            transcendentals=2 * halo_rows * width,
        ),
        name="rim",
    )(own, odd_col, total, *rims, up, down, one, two, w_expand, depth_kernel, w_project, perm)


def identity(size):
    row = lax.broadcasted_iota(jnp.int32, (size, size), 0)
    column = lax.broadcasted_iota(jnp.int32, (size, size), 1)
    return jnp.where(row == column, 1.0, 0.0).astype(jnp.bfloat16)


def gather_blocks(plan, refs, blocks, sets):
    members = refs[0].shape[1] // sets
    return jnp.concatenate(
        [
            read_block(plan, refs, index, side, slice(s * members, (s + 1) * members))
            for s in range(sets)
            for index, side in blocks
        ],
        axis=0,
    )


def project_kernel(*refs, plan, sets):
    in_refs, weight_ref, out_ref = refs[:-2], refs[-2], refs[-1]
    block = gather_blocks(plan, in_refs, split_blocks(plan)[0], sets)
    out_ref[...] = matmul(block, weight_ref[...]).astype(jnp.bfloat16)


def project(plan, incoming, w_qkv, sets):
    soon = split_blocks(plan)[0]
    _, size, channels = incoming[0].shape
    masks, late, _ = plan
    there = [*range(late, len(masks) - 1 - late), len(masks) - 1, len(masks) + late]
    filled = [array if index in there else incoming[late] for index, array in enumerate(incoming)]
    return pl.pallas_call(
        functools.partial(project_kernel, plan=plan, sets=sets),
        in_specs=[vmem()] * (len(filled) + 1),
        out_specs=vmem(),
        out_shape=jax.ShapeDtypeStruct((len(soon) * size, w_qkv.shape[1]), jnp.bfloat16),
        compiler_params=pltpu.CompilerParams(vmem_limit_bytes=4 * MIB),
        cost_estimate=pl.CostEstimate(
            flops=2 * len(soon) * size * channels * w_qkv.shape[1],
            bytes_accessed=2 * w_qkv.size + 8 * len(soon) * size * channels,
            transcendentals=0,
        ),
        name="project",
    )(*filled, w_qkv)


def attend_kernel(*refs, plan, sets, came):
    masks, _, sides = plan
    slabs = len(masks)
    _, size, channels = refs[0].shape
    soon, rest = split_blocks(plan)
    in_refs, weight_ref, out_refs = refs[:came], refs[came], refs[came + 1 : -6]
    if soon:
        soon_ref, out_refs = out_refs[0], out_refs[1:]
    query_ref, key_ref, value_ref, turned_ref, even_ref, odd_ref = refs[-6:]
    members = size // sets
    count = slabs * sides * members
    head_width = channels // HEADS
    group_heads = LANES // head_width
    groups = channels // LANES
    factor = math.log2(math.e) / math.sqrt(head_width)
    lane = lax.broadcasted_iota(jnp.int32, (1, LANES), 1)
    masks = [
        jnp.where((lane >= j * head_width) & (lane < (j + 1) * head_width), 1.0, 0.0).astype(
            jnp.bfloat16
        )
        for j in range(group_heads)
    ]
    turn_values = identity(channels)
    block = gather_blocks(plan, in_refs, rest, sets)
    projected = matmul(block, weight_ref[...]).astype(jnp.bfloat16)
    for s in range(sets):
        near, far = len(soon) * members, len(rest) * members
        qkv = projected[s * far : (s + 1) * far]
        if soon:
            qkv = jnp.concatenate([soon_ref[s * near : (s + 1) * near, :], qkv], axis=0)
        values = matmul_nt(turn_values, qkv[:, 2 * channels :]).astype(jnp.bfloat16)
        for group in range(groups):
            spot = group * LANES
            query_ref[s * groups + group] = qkv[:, spot : spot + LANES]
            key_ref[s * groups + group] = qkv[:, channels + spot : channels + spot + LANES]
            for j in range(group_heads):
                head = (group * group_heads + j) * head_width
                value_ref[s * groups + group, j, :head_width] = values[head : head + head_width]
                value_ref[s * groups + group, j, head_width:] = jnp.ones((16, count), jnp.bfloat16)

    def scores(index, out):
        keys = key_ref[index]
        stacked = jnp.concatenate([keys * mask for mask in masks], axis=0)
        out[...] = matmul_nt(stacked, query_ref[index])

    def weigh(index, scores_ref):
        for j in range(group_heads):
            part = scores_ref[j * count : (j + 1) * count]
            highest = jnp.max(part, axis=0, keepdims=True)
            raised = jnp.exp2((part - highest) * factor).astype(jnp.bfloat16)
            product = matmul(value_ref[index, j], raised)
            scale = 1.0 / product[head_width : head_width + 1]
            turned_ref[index, j * head_width : (j + 1) * head_width] = (
                product[:head_width] * scale
            ).astype(jnp.bfloat16)

    total = sets * groups
    scores(0, even_ref)

    def body(pair, carry):
        scores(2 * pair + 1, odd_ref)
        weigh(2 * pair, even_ref)
        scores(jnp.minimum(2 * pair + 2, total - 1), even_ref)
        weigh(2 * pair + 1, odd_ref)
        return carry

    lax.fori_loop(0, total // 2, body, 0)
    turn_tokens = identity(count)
    for s in range(sets):
        turned = turned_ref[s * groups : (s + 1) * groups].reshape(channels, count)
        attended = matmul_nt(turn_tokens, turned).astype(jnp.bfloat16)
        for number, (index, side) in enumerate(soon + rest):
            write_block(
                plan, out_refs, index, side, slice(s * members, (s + 1) * members),
                attended[number * members : (number + 1) * members],
            )


def attend(plan, incoming, w_qkv, sets):
    masks, _, sides = plan
    _, size, channels = incoming[0].shape
    count = len(masks) * sides * size // sets
    sent = outgoing_shapes(plan, size, channels)
    soon = [project(plan, incoming, w_qkv, sets)] if split_blocks(plan)[0] else []
    head_width = channels // HEADS
    group_heads = LANES // head_width
    total = sets * channels // LANES
    return pl.pallas_call(
        functools.partial(attend_kernel, plan=plan, sets=sets, came=len(incoming)),
        in_specs=[vmem()] * (len(incoming) + 1 + len(soon)),
        out_specs=[vmem()] * len(sent),
        out_shape=[jax.ShapeDtypeStruct(shape, jnp.bfloat16) for shape in sent],
        scratch_shapes=[
            pltpu.VMEM((total, count, LANES), jnp.bfloat16),
            pltpu.VMEM((total, count, LANES), jnp.bfloat16),
            pltpu.VMEM((total, group_heads, head_width + 16, count), jnp.bfloat16),
            pltpu.VMEM((total, LANES, count), jnp.bfloat16),
            pltpu.VMEM((group_heads * count, count), jnp.float32),
            pltpu.VMEM((group_heads * count, count), jnp.float32),
        ],
        compiler_params=pltpu.CompilerParams(vmem_limit_bytes=10 * MIB),
        cost_estimate=pl.CostEstimate(
            flops=sets * (2 * count * channels * channels * 3 + 4 * count * count * channels),
            bytes_accessed=4 * sets * count * channels + 6 * channels * channels,
            transcendentals=sets * HEADS * count * count,
        ),
        name="attend",
    )(*incoming, w_qkv, *soon)


def finish_kernel(own_ref, *refs, plan):
    masks, _, sides = plan
    in_refs, rest = refs[:-7], refs[-7:]
    back_ref, weight_ref, mixed_ref, out_ref, attended_ref, made_ref, sent = rest
    tokens = mixed_ref.shape[0]
    size = in_refs[0].shape[1]
    for index, mask in enumerate(masks):
        for side in range(sides):
            start = pl.multiple_of((own_ref[0] ^ (mask | side)) * size, 16)
            attended_ref[pl.ds(start, size), :] = read_block(
                plan, in_refs, index, side, slice(None)
            )
    step = made_ref.shape[1]
    copies = []
    for index, start in enumerate(range(0, tokens, step)):
        rows = slice(start, start + step)
        restored = matmul(back_ref[rows, :], attended_ref[...]).astype(jnp.bfloat16)
        made_ref[index] = mixed_ref[rows, :] + matmul(restored, weight_ref[...])
        copy = pltpu.make_async_copy(
            made_ref.at[index], out_ref.at[pl.ds(start, step)], sent.at[index]
        )
        copy.start()
        copies.append(copy)
    for copy in copies:
        copy.wait()


def finish(own, plan, incoming, back, w_out, mixed):
    tokens, channels = mixed.shape
    step = divisor(tokens, 256, 16)
    return pl.pallas_call(
        functools.partial(finish_kernel, plan=plan),
        in_specs=[pl.BlockSpec(memory_space=pltpu.SMEM)] + [vmem()] * (len(incoming) + 3),
        out_specs=pl.BlockSpec(memory_space=pltpu.HBM),
        out_shape=jax.ShapeDtypeStruct((tokens, channels), jnp.float32),
        scratch_shapes=[
            pltpu.VMEM((tokens, channels), jnp.bfloat16),
            pltpu.VMEM((tokens // step, step, channels), jnp.float32),
            pltpu.SemaphoreType.DMA((tokens // step,)),
        ],
        compiler_params=pltpu.CompilerParams(vmem_limit_bytes=6 * MIB),
        name="finish",
    )(own, *incoming, back, w_out, mixed)


def swap_pairs(edge, axis, start):
    pairs = [(i, i + 1) for i in range(start, lax.axis_size(axis) - 1, 2)]
    return lax.ppermute(edge, axis, pairs + [(b, a) for a, b in pairs])


def exchange_plan(row_devices, col_devices):
    devices = row_devices * col_devices
    crossing = list(range(devices // 2, devices, 2))
    others = list(range(devices // 2 - 2, 0, -2))
    masks = crossing[:-1] + others[:-1] + crossing[-1:] + others[-1:] + [0]
    return masks, 2, 2


def split_blocks(plan):
    masks, late, sides = plan
    blocks = [(index, side) for index in range(len(masks)) for side in range(sides)]
    if sides == 1:
        return [], blocks
    soon = [*range(late, len(masks) - 1 - late), len(masks) - 1]
    return [b for b in blocks if b[0] in soon], [b for b in blocks if b[0] not in soon]


def outgoing_shapes(plan, size, channels):
    masks, late, sides = plan
    if sides == 1:
        return [(1, size, channels)]
    early = len(masks) - 1 - late
    return [(2, size, channels)] * late + [
        (1, size, channels), (early + 1, size, channels), (early, size, channels)
    ]


def write_block(plan, refs, index, side, rows, value):
    masks, late, sides = plan
    if sides == 1:
        refs[0][0, rows] = value
    elif index < late:
        refs[index][side, rows] = value
    elif index == len(masks) - 1:
        refs[late + side][0, rows] = value
    elif side == 0:
        refs[late + 2][index - late, rows] = value
    else:
        refs[late + 1][index - late + 1, rows] = value


def read_block(plan, refs, index, side, rows):
    masks, late, sides = plan
    if sides == 1:
        return refs[0][0, rows]
    if index < late:
        return refs[index + side * len(masks)][side, rows]
    if index == len(masks) - 1:
        return refs[index + side * (late + 1)][0, rows]
    return refs[index][side, rows]


def join_kernel(own_ref, swapped_ref, *out_refs):
    for index, out_ref in enumerate(out_refs):
        out_ref[0] = own_ref[index]
        out_ref[1] = swapped_ref[index + 1]


def join(own, swapped):
    early, size, channels = own.shape
    return pl.pallas_call(
        join_kernel,
        in_specs=[vmem()] * 2,
        out_specs=[vmem()] * early,
        out_shape=[jax.ShapeDtypeStruct((2, size, channels), own.dtype)] * early,
        compiler_params=pltpu.CompilerParams(vmem_limit_bytes=2 * MIB),
        name="join",
    )(own, swapped)


def trade(plan, outgoing):
    masks, late, _ = plan
    devices = lax.axis_size("row") * lax.axis_size("col")

    def swap(slab, mask):
        return lax.ppermute(slab, ("row", "col"), [(i, i ^ mask) for i in range(devices)])

    slabs, (kept, passed, own) = outgoing[:late], outgoing[late:]
    swapped = swap(passed, 1)
    first = [swap(slab, mask) for slab, mask in zip(slabs, masks)]
    rest = [swap(slab, mask) for slab, mask in zip(join(own, swapped), masks[late:-1])]
    tied = lax.optimization_barrier((*first, *rest[:-late]))
    first, rest = tied[:late], [*tied[late:], *rest[-late:]]
    return [*first, *rest, kept, *[swap(slab, 1) for slab in first], swapped]


def trade_all(slabs, sets, members, outward):
    axes = ("row", "col")
    channels = slabs[0].shape[-1]
    block = slabs[0].reshape(-1, channels)
    devices = block.shape[0] // (sets * members)
    if not outward:
        block = block.reshape(sets, devices, members, channels).transpose(1, 0, 2, 3)
    block = block.reshape(devices, sets * members, channels)
    block = lax.all_to_all(block, axes, 0, 0, tiled=True)
    if outward:
        block = block.reshape(devices, sets, members, channels).transpose(1, 0, 2, 3)
    return [block.reshape(1, -1, channels)]


def grouping(rows, cols, blocks_rows, blocks_cols):
    order = np.arange(rows * cols).reshape(
        blocks_rows, rows // blocks_rows, blocks_cols, cols // blocks_cols
    )
    order = order.transpose(1, 3, 0, 2).reshape(-1)
    matrix = np.zeros((order.size, order.size), np.float32)
    matrix[np.arange(order.size), order] = 1.0
    return matrix


def shards(field, w_expand, depth_kernel, w_project, w_qkv, w_out):
    rows, cols, channels = field.shape
    tokens = rows * cols
    row_devices = lax.axis_size("row")
    col_devices = lax.axis_size("col")
    devices = row_devices * col_devices
    blocks_rows = GRID // row_devices
    blocks_cols = GRID // col_devices
    members = blocks_rows * blocks_cols
    sets_local = tokens // members // devices
    matrix = grouping(rows, cols, blocks_rows, blocks_cols)
    perm = jnp.asarray(matrix, jnp.bfloat16)
    back = jnp.asarray(matrix.T, jnp.bfloat16)

    flat = field.reshape(tokens, channels)
    pairwise = 8 <= devices <= 16 and devices & (devices - 1) == 0 and col_devices % 2 == 0
    plan = exchange_plan(row_devices, col_devices) if pairwise else ([0], 0, 1)
    row, col = lax.axis_index("row"), lax.axis_index("col")
    own = (row * col_devices + col if pairwise else row * 0).reshape(1)
    odd_row, odd_col = (row % 2).reshape(1), (col % 2).reshape(1)

    own, odd_row, odd_col, top, bottom = lax.optimization_barrier(
        (own, odd_row, odd_col, field[0], field[rows - 1])
    )
    one, two = row_edges(odd_row, top, bottom)
    one, two = swap_pairs(one, "row", 0), swap_pairs(two, "row", 1)
    normed = half_norm_of(flat)
    expanded = expand(normed, w_expand)
    tile = divisor(w_expand.shape[1] // 2, 256, LANES)
    count = w_expand.shape[1] // tile
    early = 2
    total, rim_one = inner(
        expanded, flat, depth_kernel, w_project, rows, cols, 0, early, tile
    )
    one, two, normed, expanded, total, rim_one = lax.optimization_barrier(
        (one, two, normed, expanded, total, rim_one)
    )
    up, down, one, two = column_strips(odd_row, odd_col, normed, one, two, round_up(rows + 2, 16))
    one, two = swap_pairs(one, "col", 0), swap_pairs(two, "col", 1)
    total, rim_two = inner(
        expanded, total, depth_kernel, w_project, rows, cols, early, count - early, tile
    )

    size = tokens // (len(plan[0]) * plan[2])
    mixed, *outgoing = rim(
        own, odd_col, plan, size, total, [rim_one, rim_two], up, down, one, two, w_expand,
        depth_kernel, w_project, perm, rows, cols,
    )

    def route(outgoing, outward):
        if pairwise:
            return trade(plan, outgoing)
        return trade_all(outgoing, sets_local, members, outward)

    outgoing = attend(plan, route(outgoing, True), w_qkv, sets_local)
    final = finish(own, plan, route(outgoing, False), back, w_out, mixed)
    return final.reshape(rows, cols, channels)


def solution(mesh):
    return jax.shard_map(
        shards,
        mesh=mesh,
        in_specs=(P(("field", "row"), "col", None), P(), P(), P(), P(), P()),
        out_specs=P(("field", "row"), "col", None),
        check_vma=False,
    )
```

```python
import functools
import math

import jax
import jax.numpy as jnp
import numpy as np
from jax import lax
from jax.experimental import pallas as pl
from jax.experimental.pallas import tpu as pltpu
from jax.sharding import PartitionSpec as P

HEADS = 16
GRID = 16
LANES = 128
MIB = 1024 * 1024
NT = (((1,), (1,)), ((), ()))


def layer_norm(inputs):
    average = jnp.mean(inputs, axis=-1, keepdims=True)
    centred = inputs - average
    variance = jnp.mean(centred * centred, axis=-1, keepdims=True)
    return centred * lax.rsqrt(variance + 1e-05)


def gelu_of_half(half):
    scale = math.sqrt(2.0 / math.pi)
    inner = half * (2.0 * scale + (8.0 * scale * 0.044715) * (half * half))
    return half + half * jnp.tanh(inner)


def matmul(a, b):
    return jnp.dot(a, b, preferred_element_type=jnp.float32)


def matmul_nt(a, b):
    return lax.dot_general(a, b, NT, preferred_element_type=jnp.float32)


def divisor(size, most, unit):
    best = size
    for piece in range(unit, most + 1, unit):
        if size % piece == 0:
            best = piece
    return best


def round_up(size, unit):
    return -(-size // unit) * unit


def vmem():
    return pl.BlockSpec(memory_space=pltpu.VMEM)


def half_norm(inputs):
    return (layer_norm(inputs) * 0.5).astype(jnp.bfloat16)


def half_norm_kernel(in_ref, out_ref):
    rows = in_ref.shape[0]
    step = divisor(rows, 128, 16)
    for start in range(0, rows, step):
        out_ref[start : start + step, :] = half_norm(in_ref[start : start + step, :])


def half_norm_of(inputs):
    return pl.pallas_call(
        half_norm_kernel,
        in_specs=[vmem()],
        out_specs=vmem(),
        out_shape=jax.ShapeDtypeStruct(inputs.shape, jnp.bfloat16),
        compiler_params=pltpu.CompilerParams(vmem_limit_bytes=4 * MIB),
        cost_estimate=pl.CostEstimate(
            flops=10**9, bytes_accessed=6 * inputs.size, transcendentals=inputs.shape[0]
        ),
        name="half_norm",
    )(inputs)


def choose(condition, one, two):
    flags = jnp.full((one.shape[0], 1), condition, jnp.int32) == 1
    return jnp.where(flags, one.astype(jnp.float32), two.astype(jnp.float32)).astype(one.dtype)


def edges_kernel(odd_row_ref, top_ref, bottom_ref, one_ref, two_ref):
    odd = odd_row_ref[0]
    top, bottom = half_norm(top_ref[...]), half_norm(bottom_ref[...])
    one_ref[...] = choose(odd, top, bottom)
    two_ref[...] = choose(odd, bottom, top)


def row_edges(odd_row, top, bottom):
    return pl.pallas_call(
        edges_kernel,
        in_specs=[pl.BlockSpec(memory_space=pltpu.SMEM)] + [vmem()] * 2,
        out_specs=[vmem()] * 2,
        out_shape=[jax.ShapeDtypeStruct(top.shape, jnp.bfloat16)] * 2,
        compiler_params=pltpu.CompilerParams(vmem_limit_bytes=4 * MIB),
        cost_estimate=pl.CostEstimate(
            flops=10**10, bytes_accessed=12 * top.size, transcendentals=2 * top.shape[0]
        ),
        name="row_edges",
    )(odd_row, top, bottom)


def picker(shape, pick):
    row = lax.broadcasted_iota(jnp.int32, shape, 0)
    column = lax.broadcasted_iota(jnp.int32, shape, 1)
    return jnp.where(pick(row, column), 1.0, 0.0).astype(jnp.bfloat16)


def strips_kernel(
    odd_row_ref, odd_col_ref, normed_ref, row_one_ref, row_two_ref, up_ref, down_ref, one_ref, two_ref
):
    tokens = normed_ref.shape[0]
    cols = up_ref.shape[0]
    rows = tokens // cols
    slot = one_ref.shape[0]
    odd_row, odd_col = odd_row_ref[0], odd_col_ref[0]
    up = choose(odd_row, row_one_ref[...], row_two_ref[...])
    down = choose(odd_row, row_two_ref[...], row_one_ref[...])
    up_ref[...] = up
    down_ref[...] = down
    strips = []
    for x in (0, cols - 1):
        body = picker(
            (slot, tokens), lambda i, j: (i >= 1) & (i <= rows) & (j == (i - 1) * cols + x)
        )
        head = picker((slot, cols), lambda i, j: (i == 0) & (j == x))
        foot = picker((slot, cols), lambda i, j: (i == rows + 1) & (j == x))
        strip = matmul(body, normed_ref[...]) + matmul(head, up) + matmul(foot, down)
        strips.append(strip.astype(jnp.bfloat16))
    one_ref[...] = choose(odd_col, strips[0], strips[1])
    two_ref[...] = choose(odd_col, strips[1], strips[0])


def column_strips(odd_row, odd_col, normed, row_one, row_two, slot):
    cols, channels = row_one.shape
    shapes = [(cols, channels)] * 2 + [(slot, channels)] * 2
    return pl.pallas_call(
        strips_kernel,
        in_specs=[pl.BlockSpec(memory_space=pltpu.SMEM)] * 2 + [vmem()] * 3,
        out_specs=[vmem()] * 4,
        out_shape=[jax.ShapeDtypeStruct(shape, jnp.bfloat16) for shape in shapes],
        compiler_params=pltpu.CompilerParams(vmem_limit_bytes=4 * MIB),
        name="column_strips",
    )(odd_row, odd_col, normed, row_one, row_two)


def padded_rows(tokens):
    return tokens + 16


def expand_kernel(normed_ref, weight_ref, out_ref, even_ref, odd_ref):
    tokens, tile = even_ref.shape
    width = weight_ref.shape[1]
    subs = tile // LANES

    def multiply(index, made_ref):
        lanes = pl.ds(pl.multiple_of(index * tile, tile), tile)
        made_ref[...] = matmul(normed_ref[...], weight_ref[:, lanes])

    def activate(index, made_ref):
        for sub in range(subs):
            row = (index * subs + sub) * padded_rows(tokens) + 8
            out_ref[pl.ds(pl.multiple_of(row, 8), tokens), :] = gelu_of_half(
                made_ref[:, sub * LANES : (sub + 1) * LANES]
            )

    def body(index, carry):
        multiply(2 * index + 1, odd_ref)
        activate(2 * index, even_ref)
        multiply(2 * index + 2, even_ref)
        activate(2 * index + 1, odd_ref)
        return carry

    count = width // tile
    multiply(0, even_ref)
    lax.fori_loop(0, count // 2 - 1, body, 0)
    multiply(count - 1, odd_ref)
    activate(count - 2, even_ref)
    activate(count - 1, odd_ref)


def expand(normed, w_expand):
    tokens, channels = normed.shape
    width = w_expand.shape[1]
    return pl.pallas_call(
        expand_kernel,
        in_specs=[vmem()] * 2,
        out_specs=vmem(),
        out_shape=jax.ShapeDtypeStruct((width // LANES * padded_rows(tokens), LANES), jnp.float32),
        scratch_shapes=[
            pltpu.VMEM((tokens, divisor(width // 2, 256, LANES)), jnp.float32)
        ] * 2,
        compiler_params=pltpu.CompilerParams(vmem_limit_bytes=6 * MIB),
        cost_estimate=pl.CostEstimate(
            flops=10**10,
            bytes_accessed=tokens * channels * 2 + channels * width * 2 + tokens * width * 4,
            transcendentals=tokens * width,
        ),
        name="expand",
    )(normed, w_expand)


def inner_kernel(
    expanded_ref, start_ref, depth_ref, w_project_ref, total_ref, rim_ref, even_ref, odd_ref,
    *, rows, cols, first, count,
):
    tokens = rows * cols
    tile = even_ref.shape[1]
    subs = tile // LANES
    position = lax.broadcasted_iota(jnp.int32, (8, LANES), 0)
    at_first = position == 0
    at_last = position == 7

    def clear_ends(value, low, high):
        head = jnp.where(at_first, 0.0, value[:8]) if low else value[:8]
        foot = jnp.where(at_last, 0.0, value[-8:]) if high else value[-8:]
        return jnp.concatenate([head, value[8:-8], foot], axis=0)

    def convolve(index, out_ref):
        for sub in range(subs):
            chunk = (first + index) * subs + sub
            lanes = pl.ds(pl.multiple_of(chunk * LANES, LANES), LANES)
            base = chunk * padded_rows(tokens) + 8
            here = index * subs + sub
            taps = [[0.5 * depth_ref[p, q : q + 1, lanes] for q in range(3)] for p in range(3)]
            spot = slice(sub * LANES, (sub + 1) * LANES)
            sums = {}
            for y in range(rows + 1):
                if y < rows:
                    parts = [
                        expanded_ref[pl.ds(base + (y * cols + q), cols), :] for q in (-1, 0, 1)
                    ]
                    parts[0] = clear_ends(parts[0], True, False)
                    parts[2] = clear_ends(parts[2], False, True)
                    for p in range(3):
                        target = y + 1 - p
                        if 0 <= target < rows:
                            for q in range(3):
                                term = taps[p][q] * parts[q]
                                sums[target] = sums[target] + term if target in sums else term
                if y > 0:
                    done = sums.pop(y - 1)
                    rim_ref[here, 2 * cols + y - 1 : 2 * cols + y] = done[:1]
                    rim_ref[here, 2 * cols + rows + y - 1 : 2 * cols + rows + y] = done[-1:]
                    if y in (1, rows):
                        start = 0 if y == 1 else cols
                        rim_ref[here, start : start + cols] = done
                        made = jnp.zeros_like(done)
                    else:
                        made = clear_ends(gelu_of_half(done), True, True)
                    out_ref[(y - 1) * cols : y * cols, spot] = made.astype(jnp.bfloat16)

    def project(index, in_ref, from_ref):
        piece = pl.ds(pl.multiple_of((first + index) * tile, tile), tile)
        total_ref[...] = from_ref[...] + matmul(in_ref[...], w_project_ref[piece, :])

    convolve(0, even_ref)
    project(0, even_ref, start_ref)
    convolve(1, odd_ref)

    def body(index, carry):
        convolve(2 * index, even_ref)
        project(2 * index - 1, odd_ref, total_ref)
        convolve(2 * index + 1, odd_ref)
        project(2 * index, even_ref, total_ref)
        return carry

    lax.fori_loop(1, count // 2, body, 0)
    project(count - 1, odd_ref, total_ref)


def inner(expanded, start, depth_kernel, w_project, rows, cols, first, count, tile):
    tokens, channels = start.shape
    rim = (count * tile // LANES, 2 * cols + 2 * rows, LANES)
    return pl.pallas_call(
        functools.partial(inner_kernel, rows=rows, cols=cols, first=first, count=count),
        in_specs=[vmem()] * 4,
        out_specs=[vmem()] * 2,
        out_shape=[
            jax.ShapeDtypeStruct((tokens, channels), jnp.float32),
            jax.ShapeDtypeStruct(rim, jnp.float32),
        ],
        scratch_shapes=[pltpu.VMEM((tokens, tile), jnp.bfloat16)] * 2,
        compiler_params=pltpu.CompilerParams(vmem_limit_bytes=6 * MIB),
        cost_estimate=pl.CostEstimate(
            flops=2 * 10**9 * count,
            bytes_accessed=tokens * channels * 8 + tokens * count * tile * 4,
            transcendentals=tokens * count * tile,
        ),
        name="inner",
    )(expanded, start, depth_kernel, w_project)


def rim_kernel(
    own_ref, odd_col_ref, inner_ref, *refs, rows, cols, plan, size, pieces,
):
    masks, _, sides = plan
    sent = len(outgoing_shapes(plan, size, 1))
    rim_refs, refs = refs[:pieces], refs[pieces:]
    up_ref, down_ref, one_ref, two_ref, w_expand_ref, depth_ref, w_project_ref, perm_ref = refs[:8]
    mixed_ref, slab_refs = refs[8], refs[9 : 9 + sent]
    halo_ref, active_ref, normed_ref, grouped_ref = refs[9 + sent :]
    tokens = rows * cols
    width = w_expand_ref.shape[1]
    tile = divisor(width, 512, LANES)
    subs = tile // LANES
    slot = one_ref.shape[0]
    left_start, right_start = 2 * cols, 2 * cols + slot

    odd_col = odd_col_ref[0]
    left = choose(odd_col, one_ref[...], two_ref[...])
    right = choose(odd_col, two_ref[...], one_ref[...])
    edges = jnp.concatenate([up_ref[...], down_ref[...], left, right], axis=0)

    def expand_halo(index):
        made = gelu_of_half(matmul(edges, w_expand_ref[:, index * tile : (index + 1) * tile]))
        for sub in range(subs):
            halo_ref[index * subs + sub] = made[:, sub * LANES : (sub + 1) * LANES]

    position = lax.broadcasted_iota(jnp.int32, (cols, LANES), 0)
    at_first = position == 0
    at_last = position == cols - 1

    def activate(chunk, here, sums_ref):
        lanes = slice(chunk * LANES, (chunk + 1) * LANES)
        taps = [[0.5 * depth_ref[p, q : q + 1, lanes] for q in range(3)] for p in range(3)]
        beside = []
        for q, start in ((0, left_start), (2, right_start)):
            beside.append(
                sum(taps[p][q] * halo_ref[chunk, start + p : start + p + rows] for p in range(3))
            )
        made = []
        for p, start, y in ((0, 0, 0), (2, cols, rows - 1)):
            row = halo_ref[chunk, start : start + cols]
            before = jnp.where(at_first, beside[0][y : y + 1], taps[p][0] * pltpu.roll(row, 1, 0))
            after = jnp.where(
                at_last, beside[1][y : y + 1], taps[p][2] * pltpu.roll(row, cols - 1, 0)
            )
            made.append(sums_ref[here, start : start + cols] + before + taps[p][1] * row + after)
        for index in range(2):
            start = 2 * cols + index * rows
            made.append(sums_ref[here, start : start + rows] + beside[index])
        active_ref[:, lanes] = gelu_of_half(jnp.concatenate(made, axis=0)).astype(jnp.bfloat16)

    spots = [(ref, here) for ref in rim_refs for here in range(ref.shape[0])]
    expand_halo(0)
    for index in range(width // tile):
        if (index + 1) * tile < width:
            expand_halo(index + 1)
        for chunk in range(index * subs, (index + 1) * subs):
            activate(chunk, spots[chunk][1], spots[chunk][0])

    mixed_ref[...] = inner_ref[...]
    branch = matmul(active_ref[...], w_project_ref[...])
    mixed_ref[:cols, :] += branch[:cols]
    mixed_ref[tokens - cols :, :] += branch[cols : 2 * cols]
    for y in range(1, rows - 1):
        for index, x in ((0, 0), (1, cols - 1)):
            spot = y * cols + x
            start = 2 * cols + index * rows + y
            mixed_ref[spot : spot + 1, :] += branch[start : start + 1]

    step = divisor(tokens, 128, 16)
    for start in range(0, tokens, step):
        piece = slice(start, start + step)
        normed_ref[piece, :] = layer_norm(mixed_ref[piece, :]).astype(jnp.bfloat16)
    grouped_ref[...] = matmul(perm_ref[...], normed_ref[...]).astype(jnp.bfloat16)
    for index, mask in enumerate(masks):
        for side in range(sides):
            start = pl.multiple_of((own_ref[0] ^ (mask | side)) * size, 16)
            write_block(
                plan, slab_refs, index, side, slice(None), grouped_ref[pl.ds(start, size), :]
            )


def rim(
    own, odd_col, plan, size, total, rims, up, down, one, two, w_expand, depth_kernel, w_project, perm,
    rows, cols,
):
    tokens, channels = total.shape
    width = w_expand.shape[1]
    halo_rows = 2 * cols + 2 * one.shape[0]
    sent = outgoing_shapes(plan, size, channels)
    return pl.pallas_call(
        functools.partial(
            rim_kernel, rows=rows, cols=cols, plan=plan, size=size, pieces=len(rims)
        ),
        in_specs=[pl.BlockSpec(memory_space=pltpu.SMEM)] * 2 + [vmem()] * (9 + len(rims)),
        out_specs=[vmem()] * (1 + len(sent)),
        out_shape=[jax.ShapeDtypeStruct((tokens, channels), jnp.float32)]
        + [jax.ShapeDtypeStruct(shape, jnp.bfloat16) for shape in sent],
        scratch_shapes=[
            pltpu.VMEM((width // LANES, halo_rows, LANES), jnp.float32),
            pltpu.VMEM((2 * cols + 2 * rows, width), jnp.bfloat16),
            pltpu.VMEM((tokens, channels), jnp.bfloat16),
            pltpu.VMEM((tokens, channels), jnp.bfloat16),
        ],
        compiler_params=pltpu.CompilerParams(vmem_limit_bytes=8 * MIB),
        cost_estimate=pl.CostEstimate(
            flops=2 * halo_rows * channels * width * 2 + 2 * tokens * tokens * channels,
            bytes_accessed=tokens * channels * 10 + 4 * channels * width,
            transcendentals=2 * halo_rows * width,
        ),
        name="rim",
    )(own, odd_col, total, *rims, up, down, one, two, w_expand, depth_kernel, w_project, perm)


def identity(size):
    row = lax.broadcasted_iota(jnp.int32, (size, size), 0)
    column = lax.broadcasted_iota(jnp.int32, (size, size), 1)
    return jnp.where(row == column, 1.0, 0.0).astype(jnp.bfloat16)


def gather_blocks(plan, refs, blocks, sets):
    members = refs[0].shape[1] // sets
    return jnp.concatenate(
        [
            read_block(plan, refs, index, side, slice(s * members, (s + 1) * members))
            for s in range(sets)
            for index, side in blocks
        ],
        axis=0,
    )


def project_kernel(*refs, plan, sets):
    in_refs, weight_ref, out_ref = refs[:-2], refs[-2], refs[-1]
    block = gather_blocks(plan, in_refs, split_blocks(plan)[0], sets)
    out_ref[...] = matmul(block, weight_ref[...]).astype(jnp.bfloat16)


def project(plan, incoming, w_qkv, sets):
    soon = split_blocks(plan)[0]
    _, size, channels = incoming[0].shape
    masks, late, _ = plan
    there = [*range(late, len(masks) - 1 - late), len(masks) - 1, len(masks) + late]
    filled = [array if index in there else incoming[late] for index, array in enumerate(incoming)]
    return pl.pallas_call(
        functools.partial(project_kernel, plan=plan, sets=sets),
        in_specs=[vmem()] * (len(filled) + 1),
        out_specs=vmem(),
        out_shape=jax.ShapeDtypeStruct((len(soon) * size, w_qkv.shape[1]), jnp.bfloat16),
        compiler_params=pltpu.CompilerParams(vmem_limit_bytes=4 * MIB),
        cost_estimate=pl.CostEstimate(
            flops=2 * len(soon) * size * channels * w_qkv.shape[1],
            bytes_accessed=2 * w_qkv.size + 8 * len(soon) * size * channels,
            transcendentals=0,
        ),
        name="project",
    )(*filled, w_qkv)


def attend_kernel(*refs, plan, sets, came):
    masks, _, sides = plan
    slabs = len(masks)
    _, size, channels = refs[0].shape
    soon, rest = split_blocks(plan)
    in_refs, weight_ref, out_refs = refs[:came], refs[came], refs[came + 1 : -6]
    if soon:
        soon_ref, out_refs = out_refs[0], out_refs[1:]
    query_ref, key_ref, value_ref, turned_ref, even_ref, odd_ref = refs[-6:]
    members = size // sets
    count = slabs * sides * members
    head_width = channels // HEADS
    group_heads = LANES // head_width
    groups = channels // LANES
    factor = math.log2(math.e) / math.sqrt(head_width)
    lane = lax.broadcasted_iota(jnp.int32, (1, LANES), 1)
    masks = [
        jnp.where((lane >= j * head_width) & (lane < (j + 1) * head_width), 1.0, 0.0).astype(
            jnp.bfloat16
        )
        for j in range(group_heads)
    ]
    turn_values = identity(channels)
    block = gather_blocks(plan, in_refs, rest, sets)
    projected = matmul(block, weight_ref[...]).astype(jnp.bfloat16)
    for s in range(sets):
        near, far = len(soon) * members, len(rest) * members
        qkv = projected[s * far : (s + 1) * far]
        if soon:
            qkv = jnp.concatenate([soon_ref[s * near : (s + 1) * near, :], qkv], axis=0)
        values = matmul_nt(turn_values, qkv[:, 2 * channels :]).astype(jnp.bfloat16)
        for group in range(groups):
            spot = group * LANES
            query_ref[s * groups + group] = qkv[:, spot : spot + LANES]
            key_ref[s * groups + group] = qkv[:, channels + spot : channels + spot + LANES]
            for j in range(group_heads):
                head = (group * group_heads + j) * head_width
                value_ref[s * groups + group, j, :head_width] = values[head : head + head_width]
                value_ref[s * groups + group, j, head_width:] = jnp.ones((16, count), jnp.bfloat16)

    def scores(index, out):
        keys = key_ref[index]
        stacked = jnp.concatenate([keys * mask for mask in masks], axis=0)
        out[...] = matmul_nt(stacked, query_ref[index])

    def weigh(index, scores_ref):
        for j in range(group_heads):
            part = scores_ref[j * count : (j + 1) * count]
            highest = jnp.max(part, axis=0, keepdims=True)
            raised = jnp.exp2((part - highest) * factor).astype(jnp.bfloat16)
            product = matmul(value_ref[index, j], raised)
            scale = 1.0 / product[head_width : head_width + 1]
            turned_ref[index, j * head_width : (j + 1) * head_width] = (
                product[:head_width] * scale
            ).astype(jnp.bfloat16)

    total = sets * groups
    scores(0, even_ref)

    def body(pair, carry):
        scores(2 * pair + 1, odd_ref)
        weigh(2 * pair, even_ref)
        scores(jnp.minimum(2 * pair + 2, total - 1), even_ref)
        weigh(2 * pair + 1, odd_ref)
        return carry

    lax.fori_loop(0, total // 2, body, 0)
    turn_tokens = identity(count)
    for s in range(sets):
        turned = turned_ref[s * groups : (s + 1) * groups].reshape(channels, count)
        attended = matmul_nt(turn_tokens, turned).astype(jnp.bfloat16)
        for number, (index, side) in enumerate(soon + rest):
            write_block(
                plan, out_refs, index, side, slice(s * members, (s + 1) * members),
                attended[number * members : (number + 1) * members],
            )


def attend(plan, incoming, w_qkv, sets):
    masks, _, sides = plan
    _, size, channels = incoming[0].shape
    count = len(masks) * sides * size // sets
    sent = outgoing_shapes(plan, size, channels)
    soon = [project(plan, incoming, w_qkv, sets)] if split_blocks(plan)[0] else []
    head_width = channels // HEADS
    group_heads = LANES // head_width
    total = sets * channels // LANES
    return pl.pallas_call(
        functools.partial(attend_kernel, plan=plan, sets=sets, came=len(incoming)),
        in_specs=[vmem()] * (len(incoming) + 1 + len(soon)),
        out_specs=[vmem()] * len(sent),
        out_shape=[jax.ShapeDtypeStruct(shape, jnp.bfloat16) for shape in sent],
        scratch_shapes=[
            pltpu.VMEM((total, count, LANES), jnp.bfloat16),
            pltpu.VMEM((total, count, LANES), jnp.bfloat16),
            pltpu.VMEM((total, group_heads, head_width + 16, count), jnp.bfloat16),
            pltpu.VMEM((total, LANES, count), jnp.bfloat16),
            pltpu.VMEM((group_heads * count, count), jnp.float32),
            pltpu.VMEM((group_heads * count, count), jnp.float32),
        ],
        compiler_params=pltpu.CompilerParams(vmem_limit_bytes=10 * MIB),
        cost_estimate=pl.CostEstimate(
            flops=sets * (2 * count * channels * channels * 3 + 4 * count * count * channels),
            bytes_accessed=4 * sets * count * channels + 6 * channels * channels,
            transcendentals=sets * HEADS * count * count,
        ),
        name="attend",
    )(*incoming, w_qkv, *soon)


def finish_kernel(own_ref, *refs, plan):
    masks, _, sides = plan
    in_refs, rest = refs[:-7], refs[-7:]
    back_ref, weight_ref, mixed_ref, out_ref, attended_ref, made_ref, sent = rest
    tokens = mixed_ref.shape[0]
    size = in_refs[0].shape[1]
    for index, mask in enumerate(masks):
        for side in range(sides):
            start = pl.multiple_of((own_ref[0] ^ (mask | side)) * size, 16)
            attended_ref[pl.ds(start, size), :] = read_block(
                plan, in_refs, index, side, slice(None)
            )
    step = made_ref.shape[1]
    copies = []
    for index, start in enumerate(range(0, tokens, step)):
        rows = slice(start, start + step)
        restored = matmul(back_ref[rows, :], attended_ref[...]).astype(jnp.bfloat16)
        made_ref[index] = mixed_ref[rows, :] + matmul(restored, weight_ref[...])
        copy = pltpu.make_async_copy(
            made_ref.at[index], out_ref.at[pl.ds(start, step)], sent.at[index]
        )
        copy.start()
        copies.append(copy)
    for copy in copies:
        copy.wait()


def finish(own, plan, incoming, back, w_out, mixed):
    tokens, channels = mixed.shape
    step = divisor(tokens, 256, 16)
    return pl.pallas_call(
        functools.partial(finish_kernel, plan=plan),
        in_specs=[pl.BlockSpec(memory_space=pltpu.SMEM)] + [vmem()] * (len(incoming) + 3),
        out_specs=pl.BlockSpec(memory_space=pltpu.HBM),
        out_shape=jax.ShapeDtypeStruct((tokens, channels), jnp.float32),
        scratch_shapes=[
            pltpu.VMEM((tokens, channels), jnp.bfloat16),
            pltpu.VMEM((tokens // step, step, channels), jnp.float32),
            pltpu.SemaphoreType.DMA((tokens // step,)),
        ],
        compiler_params=pltpu.CompilerParams(vmem_limit_bytes=6 * MIB),
        name="finish",
    )(own, *incoming, back, w_out, mixed)


def swap_pairs(edge, axis, start):
    pairs = [(i, i + 1) for i in range(start, lax.axis_size(axis) - 1, 2)]
    return lax.ppermute(edge, axis, pairs + [(b, a) for a, b in pairs])


def exchange_plan(row_devices, col_devices):
    devices = row_devices * col_devices
    crossing = list(range(devices - 2, devices // 2 - 1, -2))
    others = list(range(devices // 2 - 2, 0, -2))
    masks = crossing[:-1] + others[:-1] + crossing[-1:] + others[-1:] + [0]
    return masks, 2, 2


def split_blocks(plan):
    masks, late, sides = plan
    blocks = [(index, side) for index in range(len(masks)) for side in range(sides)]
    if sides == 1:
        return [], blocks
    soon = [*range(late, len(masks) - 1 - late), len(masks) - 1]
    return [b for b in blocks if b[0] in soon], [b for b in blocks if b[0] not in soon]


def outgoing_shapes(plan, size, channels):
    masks, late, sides = plan
    if sides == 1:
        return [(1, size, channels)]
    early = len(masks) - 1 - late
    return [(2, size, channels)] * late + [
        (1, size, channels), (early + 1, size, channels), (early, size, channels)
    ]


def write_block(plan, refs, index, side, rows, value):
    masks, late, sides = plan
    if sides == 1:
        refs[0][0, rows] = value
    elif index < late:
        refs[index][side, rows] = value
    elif index == len(masks) - 1:
        refs[late + side][0, rows] = value
    elif side == 0:
        refs[late + 2][index - late, rows] = value
    else:
        refs[late + 1][index - late + 1, rows] = value


def read_block(plan, refs, index, side, rows):
    masks, late, sides = plan
    if sides == 1:
        return refs[0][0, rows]
    if index < late:
        return refs[index + side * len(masks)][side, rows]
    if index == len(masks) - 1:
        return refs[index + side * (late + 1)][0, rows]
    return refs[index][side, rows]


def join_kernel(own_ref, swapped_ref, *out_refs):
    for index, out_ref in enumerate(out_refs):
        out_ref[0] = own_ref[index]
        out_ref[1] = swapped_ref[index + 1]


def join(own, swapped):
    early, size, channels = own.shape
    return pl.pallas_call(
        join_kernel,
        in_specs=[vmem()] * 2,
        out_specs=[vmem()] * early,
        out_shape=[jax.ShapeDtypeStruct((2, size, channels), own.dtype)] * early,
        compiler_params=pltpu.CompilerParams(vmem_limit_bytes=2 * MIB),
        name="join",
    )(own, swapped)


def trade(plan, outgoing):
    masks, late, _ = plan
    devices = lax.axis_size("row") * lax.axis_size("col")

    def swap(slab, mask):
        return lax.ppermute(slab, ("row", "col"), [(i, i ^ mask) for i in range(devices)])

    slabs, (kept, passed, own) = outgoing[:late], outgoing[late:]
    swapped = swap(passed, 1)
    first = [swap(slab, mask) for slab, mask in zip(slabs, masks)]
    rest = [swap(slab, mask) for slab, mask in zip(join(own, swapped), masks[late:-1])]
    tied = lax.optimization_barrier((*first, *rest[:-late]))
    first, rest = tied[:late], [*tied[late:], *rest[-late:]]
    return [*first, *rest, kept, *[swap(slab, 1) for slab in first], swapped]


def trade_all(slabs, sets, members, outward):
    axes = ("row", "col")
    channels = slabs[0].shape[-1]
    block = slabs[0].reshape(-1, channels)
    devices = block.shape[0] // (sets * members)
    if not outward:
        block = block.reshape(sets, devices, members, channels).transpose(1, 0, 2, 3)
    block = block.reshape(devices, sets * members, channels)
    block = lax.all_to_all(block, axes, 0, 0, tiled=True)
    if outward:
        block = block.reshape(devices, sets, members, channels).transpose(1, 0, 2, 3)
    return [block.reshape(1, -1, channels)]


def grouping(rows, cols, blocks_rows, blocks_cols):
    order = np.arange(rows * cols).reshape(
        blocks_rows, rows // blocks_rows, blocks_cols, cols // blocks_cols
    )
    order = order.transpose(1, 3, 0, 2).reshape(-1)
    matrix = np.zeros((order.size, order.size), np.float32)
    matrix[np.arange(order.size), order] = 1.0
    return matrix


def shards(field, w_expand, depth_kernel, w_project, w_qkv, w_out):
    rows, cols, channels = field.shape
    tokens = rows * cols
    row_devices = lax.axis_size("row")
    col_devices = lax.axis_size("col")
    devices = row_devices * col_devices
    blocks_rows = GRID // row_devices
    blocks_cols = GRID // col_devices
    members = blocks_rows * blocks_cols
    sets_local = tokens // members // devices
    matrix = grouping(rows, cols, blocks_rows, blocks_cols)
    perm = jnp.asarray(matrix, jnp.bfloat16)
    back = jnp.asarray(matrix.T, jnp.bfloat16)

    flat = field.reshape(tokens, channels)
    pairwise = 8 <= devices <= 16 and devices & (devices - 1) == 0 and col_devices % 2 == 0
    plan = exchange_plan(row_devices, col_devices) if pairwise else ([0], 0, 1)
    row, col = lax.axis_index("row"), lax.axis_index("col")
    own = (row * col_devices + col if pairwise else row * 0).reshape(1)
    odd_row, odd_col = (row % 2).reshape(1), (col % 2).reshape(1)

    own, odd_row, odd_col, top, bottom = lax.optimization_barrier(
        (own, odd_row, odd_col, field[0], field[rows - 1])
    )
    one, two = row_edges(odd_row, top, bottom)
    one, two = swap_pairs(one, "row", 0), swap_pairs(two, "row", 1)
    normed = half_norm_of(flat)
    expanded = expand(normed, w_expand)
    tile = divisor(w_expand.shape[1] // 2, 256, LANES)
    count = w_expand.shape[1] // tile
    early = count // 4 * 2
    total, rim_one = inner(
        expanded, flat, depth_kernel, w_project, rows, cols, 0, early, tile
    )
    one, two, normed, expanded, total, rim_one = lax.optimization_barrier(
        (one, two, normed, expanded, total, rim_one)
    )
    up, down, one, two = column_strips(odd_row, odd_col, normed, one, two, round_up(rows + 2, 16))
    one, two = swap_pairs(one, "col", 0), swap_pairs(two, "col", 1)
    total, rim_two = inner(
        expanded, total, depth_kernel, w_project, rows, cols, early, count - early, tile
    )

    size = tokens // (len(plan[0]) * plan[2])
    mixed, *outgoing = rim(
        own, odd_col, plan, size, total, [rim_one, rim_two], up, down, one, two, w_expand,
        depth_kernel, w_project, perm, rows, cols,
    )

    def route(outgoing, outward):
        if pairwise:
            return trade(plan, outgoing)
        return trade_all(outgoing, sets_local, members, outward)

    outgoing = attend(plan, route(outgoing, True), w_qkv, sets_local)
    final = finish(own, plan, route(outgoing, False), back, w_out, mixed)
    return final.reshape(rows, cols, channels)


def solution(mesh):
    return jax.shard_map(
        shards,
        mesh=mesh,
        in_specs=(P(("field", "row"), "col", None), P(), P(), P(), P(), P()),
        out_specs=P(("field", "row"), "col", None),
        check_vma=False,
    )
```
